32 devices in a mesh: energy: 8 (over y, x, core), space: 4 (over z).
Axes of the slice: x: 2, y: 2, z: 4, core: 2. Of those that a mesh axis runs over, the one named last changes fastest.
Arguments:
- g_lesser: bfloat16 [8, 2, 4, 512, 512], P('energy', None, 'space'), may hold values from -6 to 6, as said below
- w_lesser: bfloat16 [8, 2, 4, 512, 512], P('energy', None, 'space'), may hold values from -6 to 6, as said below
- g_retarded: bfloat16 [8, 2, 4, 4, 512, 512], P('energy', None, 'space'), may hold values from -0.1875 to 0.1875
- energy_index: int32 [8], replicated, may hold values from 0 to 7, each once
Outputs:
- sigma_lesser: bfloat16 [8, 2, 4, 512, 512], P('energy', None, 'space')
- delta_green: bfloat16 [8, 2, 4, 512, 512], P('energy', None, 'space')
The draws below stay inside these ranges and needn't reach their ends.
Inputs may be any that keep to these rules, and one draw needn't show every extreme that they name: `g_lesser`: anti-Hermitian in every diagonal block at every energy: element (j, i) of component 0 is minus element (i, j), of component 1 equal to it. `w_lesser`: anti-Hermitian in every diagonal block at every energy: element (j, i) of component 0 is minus element (i, j), of component 1 equal to it. `energy_index`: each grid point once.
All inputs are finite; a program needn't handle non-finite values.
Results may differ from the reference program's by a relative error of at most 0.013.
Values may be sent and summed in bfloat16 or wider, within the bound.
No kernel may reach another device: no remote copies, remote signals or barrier semaphores. Data moves between devices by JAX's collectives and lax.ppermute only.
A program may use at most 128 MiB of HBM per device.

```python
import jax
import jax.numpy as jnp
from jax import lax

B = 512
NE = 8
NB = 4


def anti_hermitian(key):
    first_key, second_key = jax.random.split(key, 2)
    block_shape = (NE, NB, B, B)
    noise_real = jax.random.normal(first_key, block_shape, jnp.float32)
    noise_imag = jax.random.normal(second_key, block_shape, jnp.float32)
    real_part = (noise_real - jnp.swapaxes(noise_real, -1, -2)) * 0.70710678
    imag_part = (noise_imag + jnp.swapaxes(noise_imag, -1, -2)) * 0.70710678
    stacked = jnp.stack([real_part, imag_part], axis=1)
    return jnp.clip(stacked, -6.0, 6.0).astype(jnp.bfloat16)


def draw_g_lesser(key, part):
    return anti_hermitian(jax.random.fold_in(key, 11))


def draw_w_lesser(key, part):
    return anti_hermitian(jax.random.fold_in(key, 23))


def shard_levels(key, shape, cuts, low, high):
    level = 1.0
    for dim, parts in cuts:
        draws = jax.random.uniform(jax.random.fold_in(jax.random.fold_in(key, 6), dim), (parts,), jnp.float32, low / len(cuts), high / len(cuts))
        level = level * jnp.repeat(jnp.exp(draws), shape[dim] // parts).reshape((-1,) + (1,) * (len(shape) - 1 - dim))
    return level


def bell_draw(own_key, extent, deviation, reach, shards=(), held_as=jnp.bfloat16):
    factor_of = shard_levels(own_key, extent, shards, -0.22, 0.18) if shards else 1.0
    drawn = jax.random.normal(own_key, extent, jnp.float32) * deviation * factor_of
    return jnp.minimum(jnp.maximum(drawn, -reach), reach).astype(held_as)


def setup_inputs(seed: int = 0) -> dict:
    streams_of = jax.random.split(jax.random.key(seed), 5)
    return {
        "g_lesser": draw_g_lesser(jax.random.fold_in(streams_of[4], 71), 0),
        "w_lesser": draw_w_lesser(jax.random.fold_in(streams_of[4], 71), 0),
        "g_retarded": bell_draw(streams_of[2], (NE, 2, NB, NB, B, B), (2 * B) ** -0.5, 0.1875, ((0, 8), (2, 4))),
        "energy_index": jax.random.permutation(streams_of[3], NE).astype(jnp.int32),
    }


def convolve_block(operands):
    green, screen = operands
    green_c = green[:, 0].astype(jnp.float32) + 1j * green[:, 1].astype(jnp.float32)
    screen_c = screen[:, 0].astype(jnp.float32) + 1j * screen[:, 1].astype(jnp.float32)
    green_hat = jnp.fft.fft(green_c, n=2 * NE, axis=0)
    screen_hat = jnp.fft.fft(screen_c, n=2 * NE, axis=0)
    product = jnp.fft.ifft(green_hat * screen_hat, axis=0)[NE // 2:NE // 2 + NE]
    sigma_c = 1j * (NE ** -0.5) * product
    return jnp.stack([jnp.real(sigma_c), jnp.imag(sigma_c)], axis=1).astype(jnp.bfloat16)


def two_sided(operands):
    sigma_e, retarded = operands
    sig_real = sigma_e[0].astype(jnp.float32)
    sig_imag = sigma_e[1].astype(jnp.float32)
    ret_real = retarded[0].astype(jnp.float32)
    ret_imag = retarded[1].astype(jnp.float32)
    left_real = jnp.einsum('skij,kjl->skil', ret_real, sig_real) - jnp.einsum('skij,kjl->skil', ret_imag, sig_imag)
    left_imag = jnp.einsum('skij,kjl->skil', ret_real, sig_imag) + jnp.einsum('skij,kjl->skil', ret_imag, sig_real)
    left_real = lax.optimization_barrier(left_real.astype(jnp.bfloat16)).astype(jnp.float32)
    left_imag = lax.optimization_barrier(left_imag.astype(jnp.bfloat16)).astype(jnp.float32)
    out_real = jnp.einsum('skil,skml->sim', left_real, ret_real) + jnp.einsum('skil,skml->sim', left_imag, ret_imag)
    out_imag = jnp.einsum('skil,skml->sim', left_imag, ret_real) - jnp.einsum('skil,skml->sim', left_real, ret_imag)
    return jnp.stack([out_real, out_imag], axis=0).astype(jnp.bfloat16)


def reference(g_lesser, w_lesser, g_retarded, energy_index):
    to_grid = jnp.argsort(energy_index).astype(jnp.int32)
    green_grid = jnp.moveaxis(g_lesser[to_grid], 2, 0)
    screen_grid = jnp.moveaxis(w_lesser[to_grid], 2, 0)
    sigma_grid = lax.map(convolve_block, (green_grid, screen_grid))
    sigma_lesser = jnp.moveaxis(sigma_grid, 0, 2)[energy_index.astype(jnp.int32)]
    delta_green = lax.map(two_sided, (sigma_lesser, g_retarded))
    return sigma_lesser, delta_green
```

```python
import functools

import jax
import jax.numpy as jnp
from jax import lax
from jax.experimental import pallas as pl
from jax.experimental.pallas import tpu as pltpu
from jax.sharding import PartitionSpec as P


VMEM = pltpu.MemorySpace.VMEM
SMEM = pltpu.MemorySpace.SMEM


def vmem(count):
    return [pl.BlockSpec(memory_space=VMEM)] * count


def params(mib):
    return pltpu.CompilerParams(vmem_limit_bytes=mib * 2**20)


def grid_of(shape, row_offset=0):
    rows = lax.broadcasted_iota(jnp.int32, shape, 0) + row_offset
    cols = lax.broadcasted_iota(jnp.int32, shape, 1)
    return rows, cols


def pack_kernel(green, screen, cross, tri):
    half = green.shape[-1] // 2
    rows, cols = grid_of((half, half))
    upper = rows < cols
    diagonal = rows == cols
    for place, source in enumerate((green, screen)):
        a_re = source[0, 0, 0, :half, :half].astype(jnp.float32)
        a_im = source[0, 1, 0, :half, :half].astype(jnp.float32)
        d_re = source[0, 0, 0, half:, half:].astype(jnp.float32)
        d_im = source[0, 1, 0, half:, half:].astype(jnp.float32)
        t_re = jnp.where(upper, a_re, jnp.where(diagonal, a_im, d_re)).astype(jnp.bfloat16)
        t_im = jnp.where(upper, a_im, d_im).astype(jnp.bfloat16)
        c_re = source[0, 0, 0, :half, half:]
        c_im = source[0, 1, 0, :half, half:]
        shape = cross.shape[:1] + cross.shape[3:]
        cross[:, place, 0] = c_re.reshape(shape)
        cross[:, place, 1] = c_im.reshape(shape)
        tri[:, place, 0] = t_re.reshape(shape)
        tri[:, place, 1] = t_im.reshape(shape)


def pack(green, screen, parts):
    half = green.shape[-1] // 2
    out = jax.ShapeDtypeStruct((parts, 2, 2, half // parts, half), jnp.bfloat16)
    return pl.pallas_call(
        pack_kernel,
        out_shape=(out, out),
        in_specs=vmem(2),
        out_specs=tuple(vmem(2)),
        compiler_params=params(24),
    )(green, screen)


def split_rows(packed, groups):
    _, fields, comps, half, width = packed.shape
    shaped = packed.reshape(fields, comps, groups, half // groups, width)
    return jnp.moveaxis(shaped, 2, 0)


def conv_kernel(has_diagonal, index, offset, pieces, out, green, screen, place):
    count, _, _, rows, width = pieces.shape

    def scatter(stored, carry):
        point = index[stored]
        place[point] = stored
        green[point] = pieces[stored, 0].astype(jnp.float32)
        screen[point] = pieces[stored, 1].astype(jnp.float32)
        return carry

    unroll = count <= 16
    lax.fori_loop(0, count, scatter, 0, unroll=unroll)
    scale = count**-0.5
    zero = jnp.zeros((rows, width), jnp.float32)

    def one(point, carry):
        total = point + count // 2

        def term(first, sums):
            both_re, both_im, mixed = sums
            g_re = green[first, 0]
            g_im = green[first, 1]
            w_re = screen[total - first, 0]
            w_im = screen[total - first, 1]
            return (
                both_re + g_re * w_re,
                both_im + g_im * w_im,
                mixed + g_re * w_im + g_im * w_re,
            )

        if unroll:
            sums = (zero, zero, zero)
            for first in range(max(0, total - count + 1), min(count - 1, total) + 1):
                sums = term(first, sums)
        else:
            low = jnp.maximum(0, total - count + 1)
            high = jnp.minimum(count - 1, total) + 1
            sums = lax.fori_loop(low, high, term, (zero, zero, zero))
        both_re, both_im, mixed = sums
        s_re = -scale * mixed
        s_im = scale * (both_re - both_im)
        if has_diagonal:
            at_rows, at_cols = grid_of((rows, width), offset[0])
            diagonal = at_rows == at_cols
            s_re = jnp.where(diagonal, -scale * both_re, s_re)
            s_im = jnp.where(diagonal, -scale * both_im, s_im)
        stored = place[point]
        out[stored, 0] = s_re.astype(jnp.bfloat16)
        out[stored, 1] = s_im.astype(jnp.bfloat16)
        return carry

    if unroll:
        for point in range(count):
            one(point, 0)
    else:
        lax.fori_loop(0, count, one, 0)


def convolve(pieces, energy_index, row_offset, has_diagonal):
    count, _, _, rows, width = pieces.shape
    smem = pl.BlockSpec(memory_space=SMEM)
    return pl.pallas_call(
        functools.partial(conv_kernel, has_diagonal),
        out_shape=jax.ShapeDtypeStruct((count, 2, rows, width), jnp.bfloat16),
        in_specs=[smem, smem] + vmem(1),
        out_specs=vmem(1)[0],
        scratch_shapes=[
            pltpu.VMEM((count, 2, rows, width), jnp.float32),
            pltpu.VMEM((count, 2, rows, width), jnp.float32),
            pltpu.SMEM((count,), jnp.int32),
        ],
        compiler_params=params(24),
    )(energy_index, row_offset, pieces)


def squares(cross, tri):
    half = cross.shape[-1]
    shape = (half, half)
    return (
        cross[:, 0].reshape(shape),
        cross[:, 1].reshape(shape),
        tri[:, 0].reshape(shape),
        tri[:, 1].reshape(shape),
    )


def dot(a, b):
    return jnp.dot(a, b, preferred_element_type=jnp.float32)


def dot_t(a, b):
    return lax.dot_general(a, b, (((1,), (1,)), ((), ())), preferred_element_type=jnp.float32)


def product(cross, tri, retarded):
    c_re, c_im, t_re, t_im = squares(cross, tri)
    half = c_re.shape[0]
    rows, cols = grid_of((half, half))
    tr = t_re.astype(jnp.float32)
    ti = t_im.astype(jnp.float32)
    diagonal = rows == cols
    a_re = jnp.where(rows < cols, tr, 0.0).astype(jnp.bfloat16)
    a_im = jnp.where(rows < cols, ti, jnp.where(diagonal, 0.5 * tr, 0.0)).astype(jnp.bfloat16)
    d_re = jnp.where(rows > cols, tr, 0.0).astype(jnp.bfloat16)
    d_im = jnp.where(rows > cols, ti, jnp.where(diagonal, 0.5 * ti, 0.0)).astype(jnp.bfloat16)
    g_re = retarded[0]
    g_im = retarded[1]
    near = jnp.concatenate([g_re[:, :half], g_im[:, :half]], axis=1)
    far = jnp.concatenate([g_re, g_im], axis=1)
    l_re = jnp.concatenate(
        [
            dot(near, jnp.concatenate([a_re, -a_im], axis=0)),
            dot(far, jnp.concatenate([c_re, d_re, -c_im, -d_im], axis=0)),
        ],
        axis=1,
    ).astype(jnp.bfloat16)
    l_im = jnp.concatenate(
        [
            dot(near, jnp.concatenate([a_im, a_re], axis=0)),
            dot(far, jnp.concatenate([c_im, d_im, c_re, d_re], axis=0)),
        ],
        axis=1,
    ).astype(jnp.bfloat16)
    x_re = dot_t(jnp.concatenate([l_re, l_im], axis=1), far)
    x_im = dot_t(jnp.concatenate([l_im, -l_re], axis=1), far)
    return x_re, x_im


def own_kernel(where, cross, tri, retarded, sigma, total, block, sem):
    copy = pltpu.make_async_copy(retarded.at[0, :, 0, where[0]], block, sem)
    copy.start()
    c_re, c_im, t_re, t_im = squares(cross, tri)
    half = c_re.shape[0]
    rows, cols = grid_of((half, half))
    upper = rows < cols
    diagonal = rows == cols
    tr = t_re.astype(jnp.float32)
    ti = t_im.astype(jnp.float32)
    trt = tr.T
    tit = ti.T
    zero = jnp.zeros_like(tr)
    bf = jnp.bfloat16
    sigma[0, 0, 0, :half, half:] = c_re
    sigma[0, 1, 0, :half, half:] = c_im
    sigma[0, 0, 0, half:, :half] = (-(c_re.astype(jnp.float32).T)).astype(bf)
    sigma[0, 1, 0, half:, :half] = c_im.astype(jnp.float32).T.astype(bf)
    sigma[0, 0, 0, :half, :half] = jnp.where(upper, tr, jnp.where(diagonal, zero, -trt)).astype(bf)
    sigma[0, 1, 0, :half, :half] = jnp.where(upper, ti, jnp.where(diagonal, tr, tit)).astype(bf)
    sigma[0, 0, 0, half:, half:] = jnp.where(upper, -trt, jnp.where(diagonal, zero, tr)).astype(bf)
    sigma[0, 1, 0, half:, half:] = jnp.where(upper, tit, ti).astype(bf)
    copy.wait()
    x_re, x_im = product(cross, tri, block)
    total[0] = x_re
    total[1] = x_im


def step_kernel(last, where, u_cross, u_tri, d_cross, d_tri, retarded, total, out, blocks, sems, *scratch):
    sides = ((u_cross, u_tri), (d_cross, d_tri))
    held = scratch[0] if last else out

    def copy_of(side):
        return pltpu.make_async_copy(
            retarded.at[0, :, 0, where[2 * side]], blocks.at[side], sems.at[side]
        )

    for side in range(2):

        @pl.when(where[2 * side + 1] == 1)
        def _():
            copy_of(side).start()

    held[...] = total[...]
    for side, (cross, tri) in enumerate(sides):

        @pl.when(where[2 * side + 1] == 1)
        def _():
            copy_of(side).wait()
            x_re, x_im = product(cross, tri, blocks.at[side])
            held[0] += x_re
            held[1] += x_im

    if last:
        x_re = held[0]
        x_im = held[1]
        out[0, 0, 0] = (x_re - x_re.T).astype(jnp.bfloat16)
        out[0, 1, 0] = (x_im + x_im.T).astype(jnp.bfloat16)


def cost(blocks, width):
    return pl.CostEstimate(flops=blocks * 14 * width**3, bytes_accessed=blocks * 8 * width**2, transcendentals=0)


def own_product(where, cross, tri, retarded):
    width = retarded.shape[-1]
    return pl.pallas_call(
        own_kernel,
        out_shape=(
            jax.ShapeDtypeStruct((1, 2, 1, width, width), jnp.bfloat16),
            jax.ShapeDtypeStruct((2, width, width), jnp.float32),
        ),
        in_specs=[pl.BlockSpec(memory_space=SMEM)] + vmem(2) + [pl.BlockSpec(memory_space=pl.ANY)],
        out_specs=tuple(vmem(2)),
        scratch_shapes=[pltpu.VMEM((2, width, width), jnp.bfloat16), pltpu.SemaphoreType.DMA],
        compiler_params=params(40),
        cost_estimate=cost(1, width),
    )(where, cross, tri, retarded)


def step_product(where, up, down, retarded, total, last):
    width = retarded.shape[-1]
    if last:
        shape = jax.ShapeDtypeStruct((1, 2, 1, width, width), jnp.bfloat16)
    else:
        shape = jax.ShapeDtypeStruct((2, width, width), jnp.float32)
    scratch = [pltpu.VMEM((2, 2, width, width), jnp.bfloat16), pltpu.SemaphoreType.DMA((2,))]
    if last:
        scratch.append(pltpu.VMEM((2, width, width), jnp.float32))
    return pl.pallas_call(
        functools.partial(step_kernel, last),
        out_shape=shape,
        in_specs=[pl.BlockSpec(memory_space=SMEM)]
        + vmem(4)
        + [pl.BlockSpec(memory_space=pl.ANY)]
        + vmem(1),
        out_specs=vmem(1)[0],
        scratch_shapes=scratch,
        compiler_params=params(40),
        cost_estimate=cost(1, width),
    )(where, *up, *down, retarded, total)


def exchange(pieces):
    return lax.all_to_all(pieces, "energy", split_axis=0, concat_axis=0, tiled=True)


def shards(g_lesser, w_lesser, g_retarded, energy_index):
    width = g_lesser.shape[-1]
    half = width // 2
    groups = lax.axis_size("energy")
    chain = lax.axis_size("space")
    here = lax.axis_index("space")
    rows = half // groups
    aligned = rows % 16 == 0
    cross, tri = pack(g_lesser, w_lesser, groups if aligned else 1)
    if not aligned:
        cross, tri = split_rows(cross, groups), split_rows(tri, groups)
    offset = (lax.axis_index("energy") * rows).astype(jnp.int32).reshape(1)
    own = []
    for pieces, has_diagonal in ((cross, False), (tri, True)):
        shares = convolve(exchange(pieces), energy_index, offset, has_diagonal)
        mine = exchange(shares)
        if not aligned:
            mine = jnp.moveaxis(mine, 0, 1).reshape(1, 2, half, half)
        own.append(mine)

    def flags(step):
        below = here - step
        above = here + step
        return jnp.stack(
            [
                jnp.maximum(below, 0),
                (below >= 0).astype(jnp.int32),
                jnp.minimum(above, chain - 1),
                (above < chain).astype(jnp.int32),
            ]
        ).astype(jnp.int32)

    up = list(own)
    down = list(own)
    arrived = []
    for step in range(1, chain):
        rise = [(i, i + 1) for i in range(step - 1, chain - 1)]
        fall = [(i + 1, i) for i in range(chain - step)]
        up = [lax.ppermute(piece, "space", rise) for piece in up]
        down = [lax.ppermute(piece, "space", fall) for piece in down]
        arrived.append((tuple(up), tuple(down)))

    sigma_lesser, total = own_product(flags(0), *own, g_retarded)
    for step in range(1, chain):
        up, down = arrived[step - 1]
        total = step_product(flags(step), up, down, g_retarded, total, step == chain - 1)
    return (sigma_lesser, total)


def solution(mesh):
    return jax.shard_map(
        shards,
        mesh=mesh,
        in_specs=(
            P("energy", None, "space", None, None),
            P("energy", None, "space", None, None),
            P("energy", None, "space", None, None, None),
            P(),
        ),
        out_specs=(P("energy", None, "space", None, None), P("energy", None, "space", None, None)),
        check_vma=False,
    )
```

```python
import functools

import jax
import jax.numpy as jnp
from jax import lax
from jax.experimental import pallas as pl
from jax.experimental.pallas import tpu as pltpu
from jax.sharding import PartitionSpec as P


VMEM = pltpu.MemorySpace.VMEM
SMEM = pltpu.MemorySpace.SMEM


def vmem(count):
    return [pl.BlockSpec(memory_space=VMEM)] * count


def params(mib):
    return pltpu.CompilerParams(vmem_limit_bytes=mib * 2**20)


def grid_of(shape, row_offset=0):
    rows = lax.broadcasted_iota(jnp.int32, shape, 0) + row_offset
    cols = lax.broadcasted_iota(jnp.int32, shape, 1)
    return rows, cols


def pack_kernel(green, screen, cross, tri):
    half = green.shape[-1] // 2
    rows, cols = grid_of((half, half))
    upper = rows < cols
    diagonal = rows == cols
    for place, source in enumerate((green, screen)):
        a_re = source[0, 0, 0, :half, :half].astype(jnp.float32)
        a_im = source[0, 1, 0, :half, :half].astype(jnp.float32)
        d_re = source[0, 0, 0, half:, half:].astype(jnp.float32)
        d_im = source[0, 1, 0, half:, half:].astype(jnp.float32)
        t_re = jnp.where(upper, a_re, jnp.where(diagonal, a_im, d_re)).astype(jnp.bfloat16)
        t_im = jnp.where(upper, a_im, d_im).astype(jnp.bfloat16)
        c_re = source[0, 0, 0, :half, half:]
        c_im = source[0, 1, 0, :half, half:]
        shape = cross.shape[:1] + cross.shape[3:]
        cross[:, place, 0] = c_re.reshape(shape)
        cross[:, place, 1] = c_im.reshape(shape)
        tri[:, place, 0] = t_re.reshape(shape)
        tri[:, place, 1] = t_im.reshape(shape)


def pack(green, screen, parts):
    half = green.shape[-1] // 2
    out = jax.ShapeDtypeStruct((parts, 2, 2, half // parts, half), jnp.bfloat16)
    return pl.pallas_call(
        pack_kernel,
        out_shape=(out, out),
        in_specs=vmem(2),
        out_specs=tuple(vmem(2)),
        compiler_params=params(24),
    )(green, screen)


def split_rows(packed, groups):
    _, fields, comps, half, width = packed.shape
    shaped = packed.reshape(fields, comps, groups, half // groups, width)
    return jnp.moveaxis(shaped, 2, 0)


def conv_kernel(has_diagonal, index, offset, pieces, out, green, screen, place):
    count, _, _, rows, width = pieces.shape

    def scatter(stored, carry):
        point = index[stored]
        place[point] = stored
        green[point] = pieces[stored, 0].astype(jnp.float32)
        screen[point] = pieces[stored, 1].astype(jnp.float32)
        return carry

    unroll = count <= 16
    lax.fori_loop(0, count, scatter, 0, unroll=unroll)
    scale = count**-0.5
    zero = jnp.zeros((rows, width), jnp.float32)

    def one(point, carry):
        total = point + count // 2

        def term(first, sums):
            both_re, both_im, mixed = sums
            g_re = green[first, 0]
            g_im = green[first, 1]
            w_re = screen[total - first, 0]
            w_im = screen[total - first, 1]
            return (
                both_re + g_re * w_re,
                both_im + g_im * w_im,
                mixed + g_re * w_im + g_im * w_re,
            )

        if unroll:
            sums = (zero, zero, zero)
            for first in range(max(0, total - count + 1), min(count - 1, total) + 1):
                sums = term(first, sums)
        else:
            low = jnp.maximum(0, total - count + 1)
            high = jnp.minimum(count - 1, total) + 1
            sums = lax.fori_loop(low, high, term, (zero, zero, zero))
        both_re, both_im, mixed = sums
        s_re = -scale * mixed
        s_im = scale * (both_re - both_im)
        if has_diagonal:
            at_rows, at_cols = grid_of((rows, width), offset[0])
            diagonal = at_rows == at_cols
            s_re = jnp.where(diagonal, -scale * both_re, s_re)
            s_im = jnp.where(diagonal, -scale * both_im, s_im)
        stored = place[point]
        out[stored, 0] = s_re.astype(jnp.bfloat16)
        out[stored, 1] = s_im.astype(jnp.bfloat16)
        return carry

    if unroll:
        for point in range(count):
            one(point, 0)
    else:
        lax.fori_loop(0, count, one, 0)


def convolve(pieces, energy_index, row_offset, has_diagonal):
    count, _, _, rows, width = pieces.shape
    smem = pl.BlockSpec(memory_space=SMEM)
    return pl.pallas_call(
        functools.partial(conv_kernel, has_diagonal),
        out_shape=jax.ShapeDtypeStruct((count, 2, rows, width), jnp.bfloat16),
        in_specs=[smem, smem] + vmem(1),
        out_specs=vmem(1)[0],
        scratch_shapes=[
            pltpu.VMEM((count, 2, rows, width), jnp.float32),
            pltpu.VMEM((count, 2, rows, width), jnp.float32),
            pltpu.SMEM((count,), jnp.int32),
        ],
        compiler_params=params(24),
    )(energy_index, row_offset, pieces)


def pack_pieces_kernel(groups, me, green, screen, *rest):
    outs = rest[:groups]
    held, tri, sems = rest[groups:]
    copies = []
    for place, source in enumerate((green, screen)):
        for comp in range(2):
            copy = pltpu.make_async_copy(
                source.at[0, comp, 0], held.at[place, comp], sems.at[place, comp]
            )
            copy.start()
            copies.append(copy)
    half = held.shape[-1] // 2
    rows, cols = grid_of((half, half))
    upper = rows < cols
    diagonal = rows == cols
    share = half // groups
    for copy in copies:
        copy.wait()
    for place in range(2):
        a_re = held[place, 0, :half, :half].astype(jnp.float32)
        a_im = held[place, 1, :half, :half].astype(jnp.float32)
        d_re = held[place, 0, half:, half:].astype(jnp.float32)
        d_im = held[place, 1, half:, half:].astype(jnp.float32)
        t_re = jnp.where(upper, a_re, jnp.where(diagonal, a_im, d_re))
        t_im = jnp.where(upper, a_im, d_im)
        tri[place, 0] = t_re.astype(jnp.bfloat16)
        tri[place, 1] = t_im.astype(jnp.bfloat16)
    for d in range(groups):
        lines = pl.ds(pl.multiple_of((me[0] ^ d) * share, share), share)
        for place in range(2):
            for comp in range(2):
                outs[d][place, 0, comp] = held[place, comp, lines, half:]
                outs[d][place, 1, comp] = tri[place, comp, lines, :]


def pack_pieces(me, green, screen, groups):
    width = green.shape[-1]
    half = width // 2
    piece = jax.ShapeDtypeStruct((2, 2, 2, half // groups, half), jnp.bfloat16)
    return pl.pallas_call(
        functools.partial(pack_pieces_kernel, groups),
        out_shape=(piece,) * groups,
        in_specs=[pl.BlockSpec(memory_space=SMEM)] + [pl.BlockSpec(memory_space=pltpu.MemorySpace.HBM)] * 2,
        out_specs=tuple(vmem(groups)),
        scratch_shapes=[
            pltpu.VMEM((2, 2, width, width), jnp.bfloat16),
            pltpu.VMEM((2, 2, half, half), jnp.bfloat16),
            pltpu.SemaphoreType.DMA((2, 2)),
        ],
        compiler_params=params(52),
    )(me, green, screen)


def conv_pieces_kernel(groups, me, index, *rest):
    pieces = rest[:groups]
    outs = rest[groups : 2 * groups]
    green, screen, sums = rest[2 * groups :]
    _, _, rows, width = sums.shape[1:]
    for d in range(groups):
        point = index[me[0] ^ d]
        green[point] = pieces[d][0]
        screen[point] = pieces[d][1]
    scale = groups**-0.5
    tall = 16
    for square in range(2):
        for first_row in range(0, rows, tall):
            for first_col in range(0, width, 128):
                at = (slice(first_row, first_row + tall), slice(first_col, first_col + 128))

                def load(source, point, comp):
                    return source[(point, square, comp) + at].astype(jnp.float32)

                g = [[load(green, p, c) for c in range(2)] for p in range(groups)]
                w = [[load(screen, p, c) for c in range(2)] for p in range(groups)]
                if square == 1:
                    at_rows, at_cols = grid_of((tall, 128), me[0] * rows + first_row)
                    diagonal = at_rows == at_cols + first_col
                for point in range(groups):
                    total = point + groups // 2
                    both_re = both_im = mixed = None
                    for p in range(max(0, total - groups + 1), min(groups - 1, total) + 1):
                        q = total - p
                        re = g[p][0] * w[q][0]
                        im = g[p][1] * w[q][1]
                        mix = g[p][0] * w[q][1] + g[p][1] * w[q][0]
                        both_re = re if both_re is None else both_re + re
                        both_im = im if both_im is None else both_im + im
                        mixed = mix if mixed is None else mixed + mix
                    s_re = -scale * mixed
                    s_im = scale * (both_re - both_im)
                    if square == 1:
                        s_re = jnp.where(diagonal, -scale * both_re, s_re)
                        s_im = jnp.where(diagonal, -scale * both_im, s_im)
                    sums[(point, square, 0) + at] = s_re.astype(jnp.bfloat16)
                    sums[(point, square, 1) + at] = s_im.astype(jnp.bfloat16)
    for d in range(groups):
        outs[d][...] = sums[index[me[0] ^ d]]


def conv_pieces(me, energy_index, pieces):
    groups = len(pieces)
    shape = pieces[0].shape[1:]
    smem = pl.BlockSpec(memory_space=SMEM)
    return pl.pallas_call(
        functools.partial(conv_pieces_kernel, groups),
        out_shape=(jax.ShapeDtypeStruct(shape, jnp.bfloat16),) * groups,
        in_specs=[smem, smem] + vmem(groups),
        out_specs=tuple(vmem(groups)),
        scratch_shapes=[pltpu.VMEM((groups,) + shape, jnp.bfloat16)] * 3,
        compiler_params=params(32),
    )(me, energy_index, *pieces)


def join_kernel(groups, me, *rest):
    pieces = rest[:groups]
    cross, tri = rest[groups:]
    share = pieces[0].shape[2]
    for d in range(groups):
        lines = pl.ds(pl.multiple_of((me[0] ^ d) * share, share), share)
        for comp in range(2):
            cross[comp, lines, :] = pieces[d][0, comp]
            tri[comp, lines, :] = pieces[d][1, comp]


def join(me, pieces):
    half = pieces[0].shape[-1]
    out = jax.ShapeDtypeStruct((2, half, half), jnp.bfloat16)
    return pl.pallas_call(
        functools.partial(join_kernel, len(pieces)),
        out_shape=(out, out),
        in_specs=[pl.BlockSpec(memory_space=SMEM)] + vmem(len(pieces)),
        out_specs=tuple(vmem(2)),
        compiler_params=params(32),
    )(me, *pieces)


def swap(pieces):
    groups = len(pieces)
    order = sorted(range(1, groups), key=lambda d: (-bin(d & ~1).count("1"), d))
    got = {0: pieces[0]}
    for d in order:
        got[d] = lax.ppermute(pieces[d], "energy", [(i, i ^ d) for i in range(groups)])
    return [got[d] for d in range(groups)]


def gather_paired(g_lesser, w_lesser, energy_index, groups):
    me = lax.axis_index("energy").astype(jnp.int32).reshape(1)
    pieces = swap(pack_pieces(me, g_lesser, w_lesser, groups))
    return join(me, swap(conv_pieces(me, energy_index, pieces)))


def gather_shared(g_lesser, w_lesser, energy_index, groups):
    half = g_lesser.shape[-1] // 2
    rows = half // groups
    cross, tri = (split_rows(packed, groups) for packed in pack(g_lesser, w_lesser, 1))
    offset = (lax.axis_index("energy") * rows).astype(jnp.int32).reshape(1)
    own = []
    for pieces, has_diagonal in ((cross, False), (tri, True)):
        shares = convolve(exchange(pieces), energy_index, offset, has_diagonal)
        own.append(jnp.moveaxis(exchange(shares), 0, 1).reshape(2, half, half))
    return own


def squares(cross, tri):
    return cross[0], cross[1], tri[0], tri[1]


def dot(a, b):
    return jnp.dot(a, b, preferred_element_type=jnp.float32)


def dot_t(a, b):
    return lax.dot_general(a, b, (((1,), (1,)), ((), ())), preferred_element_type=jnp.float32)


def product(cross, tri, retarded):
    c_re, c_im, t_re, t_im = squares(cross, tri)
    half = c_re.shape[0]
    rows, cols = grid_of((half, half))
    tr = t_re.astype(jnp.float32)
    ti = t_im.astype(jnp.float32)
    diagonal = rows == cols
    a_re = jnp.where(rows < cols, tr, 0.0).astype(jnp.bfloat16)
    a_im = jnp.where(rows < cols, ti, jnp.where(diagonal, 0.5 * tr, 0.0)).astype(jnp.bfloat16)
    d_re = jnp.where(rows > cols, tr, 0.0).astype(jnp.bfloat16)
    d_im = jnp.where(rows > cols, ti, jnp.where(diagonal, 0.5 * ti, 0.0)).astype(jnp.bfloat16)
    g_re = retarded[0]
    g_im = retarded[1]
    near = jnp.concatenate([g_re[:, :half], g_im[:, :half]], axis=1)
    far = jnp.concatenate([g_re, g_im], axis=1)
    l_re = jnp.concatenate(
        [
            dot(near, jnp.concatenate([a_re, -a_im], axis=0)),
            dot(far, jnp.concatenate([c_re, d_re, -c_im, -d_im], axis=0)),
        ],
        axis=1,
    ).astype(jnp.bfloat16)
    l_im = jnp.concatenate(
        [
            dot(near, jnp.concatenate([a_im, a_re], axis=0)),
            dot(far, jnp.concatenate([c_im, d_im, c_re, d_re], axis=0)),
        ],
        axis=1,
    ).astype(jnp.bfloat16)
    x_re = dot_t(jnp.concatenate([l_re, l_im], axis=1), far)
    x_im = dot_t(jnp.concatenate([l_im, -l_re], axis=1), far)
    return x_re, x_im


def own_kernel(where, cross, tri, retarded, sigma, total, block, sem):
    copy = pltpu.make_async_copy(retarded.at[0, :, 0, where[0]], block, sem)
    copy.start()
    c_re, c_im, t_re, t_im = squares(cross, tri)
    half = c_re.shape[0]
    rows, cols = grid_of((half, half))
    upper = rows < cols
    diagonal = rows == cols
    tr = t_re.astype(jnp.float32)
    ti = t_im.astype(jnp.float32)
    trt = tr.T
    tit = ti.T
    zero = jnp.zeros_like(tr)
    bf = jnp.bfloat16
    sigma[0, 0, 0, :half, half:] = c_re
    sigma[0, 1, 0, :half, half:] = c_im
    sigma[0, 0, 0, half:, :half] = (-(c_re.astype(jnp.float32).T)).astype(bf)
    sigma[0, 1, 0, half:, :half] = c_im.astype(jnp.float32).T.astype(bf)
    sigma[0, 0, 0, :half, :half] = jnp.where(upper, tr, jnp.where(diagonal, zero, -trt)).astype(bf)
    sigma[0, 1, 0, :half, :half] = jnp.where(upper, ti, jnp.where(diagonal, tr, tit)).astype(bf)
    sigma[0, 0, 0, half:, half:] = jnp.where(upper, -trt, jnp.where(diagonal, zero, tr)).astype(bf)
    sigma[0, 1, 0, half:, half:] = jnp.where(upper, tit, ti).astype(bf)
    copy.wait()
    x_re, x_im = product(cross, tri, block)
    total[0] = x_re
    total[1] = x_im


def step_kernel(last, where, u_cross, u_tri, d_cross, d_tri, retarded, total, out, blocks, sems, *scratch):
    sides = ((u_cross, u_tri), (d_cross, d_tri))
    held = scratch[0] if last else out

    def copy_of(side):
        return pltpu.make_async_copy(
            retarded.at[0, :, 0, where[2 * side]], blocks.at[side], sems.at[side]
        )

    for side in range(2):

        @pl.when(where[2 * side + 1] == 1)
        def _():
            copy_of(side).start()

    held[...] = total[...]
    for side, (cross, tri) in enumerate(sides):

        @pl.when(where[2 * side + 1] == 1)
        def _():
            copy_of(side).wait()
            x_re, x_im = product(cross, tri, blocks.at[side])
            held[0] += x_re
            held[1] += x_im

    if last:
        x_re = held[0]
        x_im = held[1]
        out[0, 0, 0] = (x_re - x_re.T).astype(jnp.bfloat16)
        out[0, 1, 0] = (x_im + x_im.T).astype(jnp.bfloat16)


def cost(blocks, width):
    return pl.CostEstimate(flops=blocks * 14 * width**3, bytes_accessed=blocks * 8 * width**2, transcendentals=0)


def own_product(where, cross, tri, retarded):
    width = retarded.shape[-1]
    return pl.pallas_call(
        own_kernel,
        out_shape=(
            jax.ShapeDtypeStruct((1, 2, 1, width, width), jnp.bfloat16),
            jax.ShapeDtypeStruct((2, width, width), jnp.float32),
        ),
        in_specs=[pl.BlockSpec(memory_space=SMEM)] + vmem(2) + [pl.BlockSpec(memory_space=pltpu.MemorySpace.HBM)],
        out_specs=tuple(vmem(2)),
        scratch_shapes=[pltpu.VMEM((2, width, width), jnp.bfloat16), pltpu.SemaphoreType.DMA],
        compiler_params=params(48),
        cost_estimate=cost(1, width),
    )(where, cross, tri, retarded)


def step_product(where, up, down, retarded, total, last):
    width = retarded.shape[-1]
    if last:
        shape = jax.ShapeDtypeStruct((1, 2, 1, width, width), jnp.bfloat16)
    else:
        shape = jax.ShapeDtypeStruct((2, width, width), jnp.float32)
    scratch = [pltpu.VMEM((2, 2, width, width), jnp.bfloat16), pltpu.SemaphoreType.DMA((2,))]
    if last:
        scratch.append(pltpu.VMEM((2, width, width), jnp.float32))
    return pl.pallas_call(
        functools.partial(step_kernel, last),
        out_shape=shape,
        in_specs=[pl.BlockSpec(memory_space=SMEM)]
        + vmem(4)
        + [pl.BlockSpec(memory_space=pltpu.MemorySpace.HBM)]
        + vmem(1),
        out_specs=vmem(1)[0],
        scratch_shapes=scratch,
        compiler_params=params(48),
        cost_estimate=cost(1, width),
    )(where, *up, *down, retarded, total)


def exchange(pieces):
    return lax.all_to_all(pieces, "energy", split_axis=0, concat_axis=0, tiled=True)


def shards(g_lesser, w_lesser, g_retarded, energy_index):
    width = g_lesser.shape[-1]
    groups = lax.axis_size("energy")
    chain = lax.axis_size("space")
    here = lax.axis_index("space")
    paired = groups & (groups - 1) == 0 and (width // 2 // groups) % 16 == 0
    gather = gather_paired if paired else gather_shared
    own = gather(g_lesser, w_lesser, energy_index, groups)

    def flags(step):
        below = here - step
        above = here + step
        return jnp.stack(
            [
                jnp.maximum(below, 0),
                (below >= 0).astype(jnp.int32),
                jnp.minimum(above, chain - 1),
                (above < chain).astype(jnp.int32),
            ]
        ).astype(jnp.int32)

    up = list(own)
    down = list(own)
    arrived = []
    for step in range(1, chain):
        rise = [(i, i + 1) for i in range(step - 1, chain - 1)]
        fall = [(i + 1, i) for i in range(chain - step)]
        up = [lax.ppermute(piece, "space", rise) for piece in up]
        down = [lax.ppermute(piece, "space", fall) for piece in down]
        arrived.append((tuple(up), tuple(down)))

    sigma_lesser, total = own_product(flags(0), *own, g_retarded)
    for step in range(1, chain):
        up, down = arrived[step - 1]
        total = step_product(flags(step), up, down, g_retarded, total, step == chain - 1)
    return (sigma_lesser, total)


def solution(mesh):
    return jax.shard_map(
        shards,
        mesh=mesh,
        in_specs=(
            P("energy", None, "space", None, None),
            P("energy", None, "space", None, None),
            P("energy", None, "space", None, None, None),
            P(),
        ),
        out_specs=(P("energy", None, "space", None, None), P("energy", None, "space", None, None)),
        check_vma=False,
    )
```

```python
import functools

import jax
import jax.numpy as jnp
from jax import lax
from jax.experimental import pallas as pl
from jax.experimental.pallas import tpu as pltpu
from jax.sharding import PartitionSpec as P


VMEM = pltpu.MemorySpace.VMEM
SMEM = pltpu.MemorySpace.SMEM


def vmem(count):
    return [pl.BlockSpec(memory_space=VMEM)] * count


def params(mib):
    return pltpu.CompilerParams(vmem_limit_bytes=mib * 2**20)


def grid_of(shape, row_offset=0):
    rows = lax.broadcasted_iota(jnp.int32, shape, 0) + row_offset
    cols = lax.broadcasted_iota(jnp.int32, shape, 1)
    return rows, cols


def pack_kernel(green, screen, cross, tri):
    half = green.shape[-1] // 2
    rows, cols = grid_of((half, half))
    upper = rows < cols
    diagonal = rows == cols
    for place, source in enumerate((green, screen)):
        a_re = source[0, 0, 0, :half, :half].astype(jnp.float32)
        a_im = source[0, 1, 0, :half, :half].astype(jnp.float32)
        d_re = source[0, 0, 0, half:, half:].astype(jnp.float32)
        d_im = source[0, 1, 0, half:, half:].astype(jnp.float32)
        t_re = jnp.where(upper, a_re, jnp.where(diagonal, a_im, d_re)).astype(jnp.bfloat16)
        t_im = jnp.where(upper, a_im, d_im).astype(jnp.bfloat16)
        c_re = source[0, 0, 0, :half, half:]
        c_im = source[0, 1, 0, :half, half:]
        shape = cross.shape[:1] + cross.shape[3:]
        cross[:, place, 0] = c_re.reshape(shape)
        cross[:, place, 1] = c_im.reshape(shape)
        tri[:, place, 0] = t_re.reshape(shape)
        tri[:, place, 1] = t_im.reshape(shape)


def pack(green, screen, parts):
    half = green.shape[-1] // 2
    out = jax.ShapeDtypeStruct((parts, 2, 2, half // parts, half), jnp.bfloat16)
    return pl.pallas_call(
        pack_kernel,
        out_shape=(out, out),
        in_specs=vmem(2),
        out_specs=tuple(vmem(2)),
        compiler_params=params(24),
    )(green, screen)


def split_rows(packed, groups):
    _, fields, comps, half, width = packed.shape
    shaped = packed.reshape(fields, comps, groups, half // groups, width)
    return jnp.moveaxis(shaped, 2, 0)


def conv_kernel(has_diagonal, index, offset, pieces, out, green, screen, place):
    count, _, _, rows, width = pieces.shape

    def scatter(stored, carry):
        point = index[stored]
        place[point] = stored
        green[point] = pieces[stored, 0].astype(jnp.float32)
        screen[point] = pieces[stored, 1].astype(jnp.float32)
        return carry

    unroll = count <= 16
    lax.fori_loop(0, count, scatter, 0, unroll=unroll)
    scale = count**-0.5
    zero = jnp.zeros((rows, width), jnp.float32)

    def one(point, carry):
        total = point + count // 2

        def term(first, sums):
            both_re, both_im, mixed = sums
            g_re = green[first, 0]
            g_im = green[first, 1]
            w_re = screen[total - first, 0]
            w_im = screen[total - first, 1]
            return (
                both_re + g_re * w_re,
                both_im + g_im * w_im,
                mixed + g_re * w_im + g_im * w_re,
            )

        if unroll:
            sums = (zero, zero, zero)
            for first in range(max(0, total - count + 1), min(count - 1, total) + 1):
                sums = term(first, sums)
        else:
            low = jnp.maximum(0, total - count + 1)
            high = jnp.minimum(count - 1, total) + 1
            sums = lax.fori_loop(low, high, term, (zero, zero, zero))
        both_re, both_im, mixed = sums
        s_re = -scale * mixed
        s_im = scale * (both_re - both_im)
        if has_diagonal:
            at_rows, at_cols = grid_of((rows, width), offset[0])
            diagonal = at_rows == at_cols
            s_re = jnp.where(diagonal, -scale * both_re, s_re)
            s_im = jnp.where(diagonal, -scale * both_im, s_im)
        stored = place[point]
        out[stored, 0] = s_re.astype(jnp.bfloat16)
        out[stored, 1] = s_im.astype(jnp.bfloat16)
        return carry

    if unroll:
        for point in range(count):
            one(point, 0)
    else:
        lax.fori_loop(0, count, one, 0)


def convolve(pieces, energy_index, row_offset, has_diagonal):
    count, _, _, rows, width = pieces.shape
    smem = pl.BlockSpec(memory_space=SMEM)
    return pl.pallas_call(
        functools.partial(conv_kernel, has_diagonal),
        out_shape=jax.ShapeDtypeStruct((count, 2, rows, width), jnp.bfloat16),
        in_specs=[smem, smem] + vmem(1),
        out_specs=vmem(1)[0],
        scratch_shapes=[
            pltpu.VMEM((count, 2, rows, width), jnp.float32),
            pltpu.VMEM((count, 2, rows, width), jnp.float32),
            pltpu.SMEM((count,), jnp.int32),
        ],
        compiler_params=params(24),
    )(energy_index, row_offset, pieces)


def pack_pieces_kernel(groups, me, green, screen, *rest):
    outs = rest[:groups]
    held, tri, sems = rest[groups:]
    copies = []
    for place, source in enumerate((green, screen)):
        for comp in range(2):
            copy = pltpu.make_async_copy(
                source.at[0, comp, 0], held.at[place, comp], sems.at[place, comp]
            )
            copy.start()
            copies.append(copy)
    half = held.shape[-1] // 2
    rows, cols = grid_of((half, half))
    upper = rows < cols
    diagonal = rows == cols
    share = half // groups
    for copy in copies:
        copy.wait()
    for place in range(2):
        a_re = held[place, 0, :half, :half].astype(jnp.float32)
        a_im = held[place, 1, :half, :half].astype(jnp.float32)
        d_re = held[place, 0, half:, half:].astype(jnp.float32)
        d_im = held[place, 1, half:, half:].astype(jnp.float32)
        t_re = jnp.where(upper, a_re, jnp.where(diagonal, a_im, d_re))
        t_im = jnp.where(upper, a_im, d_im)
        tri[place, 0] = t_re.astype(jnp.bfloat16)
        tri[place, 1] = t_im.astype(jnp.bfloat16)
    for d in range(groups):
        lines = pl.ds(pl.multiple_of((me[0] ^ d) * share, share), share)
        for place in range(2):
            for comp in range(2):
                outs[d][place, 0, comp] = held[place, comp, lines, half:]
                outs[d][place, 1, comp] = tri[place, comp, lines, :]


def pack_pieces(me, green, screen, groups):
    width = green.shape[-1]
    half = width // 2
    piece = jax.ShapeDtypeStruct((2, 2, 2, half // groups, half), jnp.bfloat16)
    return pl.pallas_call(
        functools.partial(pack_pieces_kernel, groups),
        out_shape=(piece,) * groups,
        in_specs=[pl.BlockSpec(memory_space=SMEM)] + [pl.BlockSpec(memory_space=pltpu.MemorySpace.HBM)] * 2,
        out_specs=tuple(vmem(groups)),
        scratch_shapes=[
            pltpu.VMEM((2, 2, width, width), jnp.bfloat16),
            pltpu.VMEM((2, 2, half, half), jnp.bfloat16),
            pltpu.SemaphoreType.DMA((2, 2)),
        ],
        compiler_params=params(52),
    )(me, green, screen)


def conv_pieces_kernel(groups, me, index, *rest):
    pieces = rest[:groups]
    outs = rest[groups : 2 * groups]
    green, screen, sums = rest[2 * groups :]
    _, _, rows, width = sums.shape[1:]
    for d in range(groups):
        point = index[me[0] ^ d]
        green[point] = pieces[d][0]
        screen[point] = pieces[d][1]
    scale = groups**-0.5
    tall = 16
    for square in range(2):
        for first_row in range(0, rows, tall):
            for first_col in range(0, width, 128):
                at = (slice(first_row, first_row + tall), slice(first_col, first_col + 128))

                def load(source, point, comp):
                    return source[(point, square, comp) + at].astype(jnp.float32)

                g = [[load(green, p, c) for c in range(2)] for p in range(groups)]
                w = [[load(screen, p, c) for c in range(2)] for p in range(groups)]
                if square == 1:
                    at_rows, at_cols = grid_of((tall, 128), me[0] * rows + first_row)
                    diagonal = at_rows == at_cols + first_col
                for point in range(groups):
                    total = point + groups // 2
                    both_re = both_im = mixed = None
                    for p in range(max(0, total - groups + 1), min(groups - 1, total) + 1):
                        q = total - p
                        re = g[p][0] * w[q][0]
                        im = g[p][1] * w[q][1]
                        mix = g[p][0] * w[q][1] + g[p][1] * w[q][0]
                        both_re = re if both_re is None else both_re + re
                        both_im = im if both_im is None else both_im + im
                        mixed = mix if mixed is None else mixed + mix
                    s_re = -scale * mixed
                    s_im = scale * (both_re - both_im)
                    if square == 1:
                        s_re = jnp.where(diagonal, -scale * both_re, s_re)
                        s_im = jnp.where(diagonal, -scale * both_im, s_im)
                    sums[(point, square, 0) + at] = s_re.astype(jnp.bfloat16)
                    sums[(point, square, 1) + at] = s_im.astype(jnp.bfloat16)
    for d in range(groups):
        outs[d][...] = sums[index[me[0] ^ d]]


def conv_pieces(me, energy_index, pieces):
    groups = len(pieces)
    shape = pieces[0].shape[1:]
    smem = pl.BlockSpec(memory_space=SMEM)
    return pl.pallas_call(
        functools.partial(conv_pieces_kernel, groups),
        out_shape=(jax.ShapeDtypeStruct(shape, jnp.bfloat16),) * groups,
        in_specs=[smem, smem] + vmem(groups),
        out_specs=tuple(vmem(groups)),
        scratch_shapes=[pltpu.VMEM((groups,) + shape, jnp.bfloat16)] * 3,
        compiler_params=params(32),
    )(me, energy_index, *pieces)


def join_kernel(groups, me, *rest):
    pieces = rest[:groups]
    cross, tri = rest[groups:]
    share = pieces[0].shape[2]
    for d in range(groups):
        lines = pl.ds(pl.multiple_of((me[0] ^ d) * share, share), share)
        for comp in range(2):
            cross[comp, lines, :] = pieces[d][0, comp]
            tri[comp, lines, :] = pieces[d][1, comp]


def join(me, pieces):
    half = pieces[0].shape[-1]
    out = jax.ShapeDtypeStruct((2, half, half), jnp.bfloat16)
    return pl.pallas_call(
        functools.partial(join_kernel, len(pieces)),
        out_shape=(out, out),
        in_specs=[pl.BlockSpec(memory_space=SMEM)] + vmem(len(pieces)),
        out_specs=tuple(vmem(2)),
        compiler_params=params(32),
    )(me, *pieces)


def swap(pieces):
    groups = len(pieces)
    order = sorted(range(1, groups), key=lambda d: (-bin(d & ~1).count("1"), d))
    got = {0: pieces[0]}
    for d in order:
        got[d] = lax.ppermute(pieces[d], "energy", [(i, i ^ d) for i in range(groups)])
    return [got[d] for d in range(groups)]


def gather_paired(g_lesser, w_lesser, energy_index, groups):
    me = lax.axis_index("energy").astype(jnp.int32).reshape(1)
    pieces = swap(pack_pieces(me, g_lesser, w_lesser, groups))
    return join(me, swap(conv_pieces(me, energy_index, pieces)))


def gather_shared(g_lesser, w_lesser, energy_index, groups):
    half = g_lesser.shape[-1] // 2
    rows = half // groups
    cross, tri = (split_rows(packed, groups) for packed in pack(g_lesser, w_lesser, 1))
    offset = (lax.axis_index("energy") * rows).astype(jnp.int32).reshape(1)
    own = []
    for pieces, has_diagonal in ((cross, False), (tri, True)):
        shares = convolve(exchange(pieces), energy_index, offset, has_diagonal)
        own.append(jnp.moveaxis(exchange(shares), 0, 1).reshape(2, half, half))
    return own


def squares(cross, tri):
    return cross[0], cross[1], tri[0], tri[1]


def dot(a, b):
    return jnp.dot(a, b, preferred_element_type=jnp.float32)


def dot_t(a, b):
    return lax.dot_general(a, b, (((1,), (1,)), ((), ())), preferred_element_type=jnp.float32)


def product(cross, tri, retarded):
    c_re, c_im, t_re, t_im = squares(cross, tri)
    half = c_re.shape[0]
    rows, cols = grid_of((half, half))
    tr = t_re.astype(jnp.float32)
    ti = t_im.astype(jnp.float32)
    diagonal = rows == cols
    a_re = jnp.where(rows < cols, tr, 0.0).astype(jnp.bfloat16)
    a_im = jnp.where(rows < cols, ti, jnp.where(diagonal, 0.5 * tr, 0.0)).astype(jnp.bfloat16)
    d_re = jnp.where(rows > cols, tr, 0.0).astype(jnp.bfloat16)
    d_im = jnp.where(rows > cols, ti, jnp.where(diagonal, 0.5 * ti, 0.0)).astype(jnp.bfloat16)
    g_re = retarded[0]
    g_im = retarded[1]
    near = jnp.concatenate([g_re[:, :half], g_im[:, :half]], axis=1)
    far = jnp.concatenate([g_re, g_im], axis=1)
    l_re = jnp.concatenate(
        [
            dot(near, jnp.concatenate([a_re, -a_im], axis=0)),
            dot(far, jnp.concatenate([c_re, d_re, -c_im, -d_im], axis=0)),
        ],
        axis=1,
    ).astype(jnp.bfloat16)
    l_im = jnp.concatenate(
        [
            dot(near, jnp.concatenate([a_im, a_re], axis=0)),
            dot(far, jnp.concatenate([c_im, d_im, c_re, d_re], axis=0)),
        ],
        axis=1,
    ).astype(jnp.bfloat16)
    x_re = dot_t(jnp.concatenate([l_re, l_im], axis=1), far)
    x_im = dot_t(jnp.concatenate([l_im, -l_re], axis=1), far)
    return x_re, x_im


def own_kernel(where, cross, tri, retarded, sigma, total, block, sem):
    copy = pltpu.make_async_copy(retarded.at[0, :, 0, where[0]], block, sem)
    copy.start()
    c_re, c_im, t_re, t_im = squares(cross, tri)
    half = c_re.shape[0]
    rows, cols = grid_of((half, half))
    upper = rows < cols
    diagonal = rows == cols
    tr = t_re.astype(jnp.float32)
    ti = t_im.astype(jnp.float32)
    trt = tr.T
    tit = ti.T
    zero = jnp.zeros_like(tr)
    bf = jnp.bfloat16
    sigma[0, 0, 0, :half, half:] = c_re
    sigma[0, 1, 0, :half, half:] = c_im
    sigma[0, 0, 0, half:, :half] = (-(c_re.astype(jnp.float32).T)).astype(bf)
    sigma[0, 1, 0, half:, :half] = c_im.astype(jnp.float32).T.astype(bf)
    sigma[0, 0, 0, :half, :half] = jnp.where(upper, tr, jnp.where(diagonal, zero, -trt)).astype(bf)
    sigma[0, 1, 0, :half, :half] = jnp.where(upper, ti, jnp.where(diagonal, tr, tit)).astype(bf)
    sigma[0, 0, 0, half:, half:] = jnp.where(upper, -trt, jnp.where(diagonal, zero, tr)).astype(bf)
    sigma[0, 1, 0, half:, half:] = jnp.where(upper, tit, ti).astype(bf)
    copy.wait()
    total[0], total[1] = product(cross, tri, block)


def step_kernel(count, last, ahead, where, *rest):
    if last:
        block, total = rest[:2]
        sources = rest[2 : 2 + 2 * count]
        out = rest[-1]
    else:
        sources = rest[: 2 * count]
        rest = rest[2 * count :]
    if last:
        pass
    elif ahead:
        retarded, total, out, later, block, sems = rest
        fetch = pltpu.make_async_copy(retarded.at[0, :, 0, where[0]], block, sems.at[0])
        fetch.start()
        prefetch = pltpu.make_async_copy(retarded.at[0, :, 0, where[2]], later, sems.at[1])
        prefetch.start()
        fetch.wait()
    else:
        retarded, total, out, block, sems = rest
        fetch = pltpu.make_async_copy(retarded.at[0, :, 0, where[0]], block, sems.at[0])
        fetch.start()
        fetch.wait()
    for pick in range(count):

        @pl.when(where[1] == pick)
        def _():
            cross, tri = sources[pick], sources[count + pick]
            x_re, x_im = product(cross, tri, block)
            x_re += total[0]
            x_im += total[1]
            if last:
                out[0, 0, 0] = (x_re - x_re.T).astype(jnp.bfloat16)
                out[0, 1, 0] = (x_im + x_im.T).astype(jnp.bfloat16)
            else:
                out[0] = x_re
                out[1] = x_im

    if ahead:
        prefetch.wait()


def cost(width):
    return pl.CostEstimate(flops=14 * width**3, bytes_accessed=8 * width**2, transcendentals=0)


HBM = pltpu.MemorySpace.HBM


def own_product(block, own, retarded):
    width = retarded.shape[-1]
    return pl.pallas_call(
        own_kernel,
        out_shape=(
            jax.ShapeDtypeStruct((1, 2, 1, width, width), jnp.bfloat16),
            jax.ShapeDtypeStruct((2, width, width), jnp.float32),
        ),
        in_specs=[pl.BlockSpec(memory_space=SMEM)] + vmem(2) + [pl.BlockSpec(memory_space=HBM)],
        out_specs=tuple(vmem(2)),
        scratch_shapes=[pltpu.VMEM((2, width, width), jnp.bfloat16), pltpu.SemaphoreType.DMA],
        compiler_params=params(48),
        cost_estimate=cost(width),
    )(block.reshape(1), *own, retarded)


def step_product(block, pick, sources, retarded, total, later=None):
    width = retarded.shape[-1]
    flat = [source[part] for part in range(2) for source in sources]
    ahead = later is not None
    numbers = jnp.stack([block, pick] + ([later] if ahead else []))
    total_shape = jax.ShapeDtypeStruct((2, width, width), jnp.float32)
    block_shape = jax.ShapeDtypeStruct((2, width, width), jnp.bfloat16)
    return pl.pallas_call(
        functools.partial(step_kernel, len(sources), False, ahead),
        out_shape=(total_shape, block_shape) if ahead else total_shape,
        in_specs=[pl.BlockSpec(memory_space=SMEM)]
        + vmem(len(flat))
        + [pl.BlockSpec(memory_space=HBM)]
        + vmem(1),
        out_specs=tuple(vmem(2)) if ahead else vmem(1)[0],
        scratch_shapes=[pltpu.VMEM((2, width, width), jnp.bfloat16), pltpu.SemaphoreType.DMA((2,))],
        compiler_params=params(46),
        cost_estimate=cost(width),
    )(numbers, *flat, retarded, total)


def last_product(pick, sources, block, total):
    width = block.shape[-1]
    flat = [source[part] for part in range(2) for source in sources]
    return pl.pallas_call(
        functools.partial(step_kernel, len(sources), True, False),
        out_shape=jax.ShapeDtypeStruct((1, 2, 1, width, width), jnp.bfloat16),
        in_specs=[pl.BlockSpec(memory_space=SMEM)] + vmem(len(flat) + 2),
        out_specs=vmem(1)[0],
        compiler_params=params(48),
        cost_estimate=cost(width),
    )(jnp.stack([pick, pick]), block, total, *flat)


def exchange(pieces):
    return lax.all_to_all(pieces, "energy", split_axis=0, concat_axis=0, tiled=True)


def shards(g_lesser, w_lesser, g_retarded, energy_index):
    width = g_lesser.shape[-1]
    groups = lax.axis_size("energy")
    chain = lax.axis_size("space")
    here = lax.axis_index("space")
    paired = groups & (groups - 1) == 0 and (width // 2 // groups) % 16 == 0
    gather = gather_paired if paired else gather_shared
    own = gather(g_lesser, w_lesser, energy_index, groups)
    here = here.astype(jnp.int32)
    if chain == 4:
        return around_line(here, own, g_retarded)
    everyone = [lax.all_gather(part, "space") for part in own]
    sigma_lesser, total = own_product(here, own, g_retarded)
    zero = jnp.int32(0)

    def source(block):
        return tuple(lax.dynamic_index_in_dim(part, block, 0, False) for part in everyone)

    for step in range(1, chain - 1):
        block = (here + step) % chain
        later = (block + 1) % chain
        total, held = step_product(block, zero, [source(block)], g_retarded, total, later)
    return (sigma_lesser, last_product(zero, [source(later)], held, total))


def around_line(here, own, retarded):
    outer = [(0, 1), (1, 0), (2, 3), (3, 2)]
    inner = [(1, 2), (2, 1)]

    def swap(part, pairs):
        return lax.ppermute(part, "space", pairs)

    end = ((here == 0) | (here == 3)).astype(jnp.int32)
    sigma_lesser, total = own_product(here, own, retarded)
    first, second, third, fourth, fifth = [], [], [], [], []
    for part in own:
        first.append(swap(part, outer))
        second.append(swap(part, inner))
        if part is own[0]:
            ready, total = lax.optimization_barrier((first[-1], total))
        else:
            ready = first[-1]
        third.append(swap(ready, inner))
        fourth.append(swap(second[-1], outer))
    zero = jnp.int32(0)
    total = step_product(here ^ 1, zero, [first], retarded, total)
    near, far = here ^ 2, 3 - here
    for part in range(2):
        if part == 0:
            ready, total = lax.optimization_barrier((third[0], total))
        else:
            ready = third[1]
        fifth.append(swap(ready, outer))
    total, held = step_product(
        jnp.where(end == 1, near, far), end, [second, fourth], retarded, total, jnp.where(end == 1, far, near)
    )
    delta = last_product(end, [third, fifth], held, total)
    return (sigma_lesser, delta)


def solution(mesh):
    return jax.shard_map(
        shards,
        mesh=mesh,
        in_specs=(
            P("energy", None, "space", None, None),
            P("energy", None, "space", None, None),
            P("energy", None, "space", None, None, None),
            P(),
        ),
        out_specs=(P("energy", None, "space", None, None), P("energy", None, "space", None, None)),
        check_vma=False,
    )
```

```python
import functools

import jax
import jax.numpy as jnp
from jax import lax
from jax.experimental import pallas as pl
from jax.experimental.pallas import tpu as pltpu
from jax.sharding import PartitionSpec as P


VMEM = pltpu.MemorySpace.VMEM
SMEM = pltpu.MemorySpace.SMEM
HBM = pltpu.MemorySpace.HBM

SMALL = pl.CostEstimate(flops=1, bytes_accessed=1, transcendentals=0)


def vmem(count):
    return [pl.BlockSpec(memory_space=VMEM)] * count


def params(mib):
    return pltpu.CompilerParams(vmem_limit_bytes=mib * 2**20)


def grid_of(shape, row_offset=0):
    rows = lax.broadcasted_iota(jnp.int32, shape, 0) + row_offset
    cols = lax.broadcasted_iota(jnp.int32, shape, 1)
    return rows, cols


def pack_kernel(green, screen, cross, tri):
    half = green.shape[-1] // 2
    rows, cols = grid_of((half, half))
    upper = rows < cols
    diagonal = rows == cols
    for place, source in enumerate((green, screen)):
        a_re = source[0, 0, 0, :half, :half].astype(jnp.float32)
        a_im = source[0, 1, 0, :half, :half].astype(jnp.float32)
        d_re = source[0, 0, 0, half:, half:].astype(jnp.float32)
        d_im = source[0, 1, 0, half:, half:].astype(jnp.float32)
        t_re = jnp.where(upper, a_re, jnp.where(diagonal, a_im, d_re)).astype(jnp.bfloat16)
        t_im = jnp.where(upper, a_im, d_im).astype(jnp.bfloat16)
        c_re = source[0, 0, 0, :half, half:]
        c_im = source[0, 1, 0, :half, half:]
        shape = cross.shape[:1] + cross.shape[3:]
        cross[:, place, 0] = c_re.reshape(shape)
        cross[:, place, 1] = c_im.reshape(shape)
        tri[:, place, 0] = t_re.reshape(shape)
        tri[:, place, 1] = t_im.reshape(shape)


def pack(green, screen, parts):
    half = green.shape[-1] // 2
    out = jax.ShapeDtypeStruct((parts, 2, 2, half // parts, half), jnp.bfloat16)
    return pl.pallas_call(
        pack_kernel,
        out_shape=(out, out),
        in_specs=vmem(2),
        out_specs=tuple(vmem(2)),
        compiler_params=params(24),
    )(green, screen)


def split_rows(packed, groups):
    _, fields, comps, half, width = packed.shape
    shaped = packed.reshape(fields, comps, groups, half // groups, width)
    return jnp.moveaxis(shaped, 2, 0)


def conv_kernel(has_diagonal, index, offset, pieces, out, green, screen, place):
    count, _, _, rows, width = pieces.shape

    def scatter(stored, carry):
        point = index[stored]
        place[point] = stored
        green[point] = pieces[stored, 0].astype(jnp.float32)
        screen[point] = pieces[stored, 1].astype(jnp.float32)
        return carry

    unroll = count <= 16
    lax.fori_loop(0, count, scatter, 0, unroll=unroll)
    scale = count**-0.5
    zero = jnp.zeros((rows, width), jnp.float32)

    def one(point, carry):
        total = point + count // 2

        def term(first, sums):
            both_re, both_im, mixed = sums
            g_re = green[first, 0]
            g_im = green[first, 1]
            w_re = screen[total - first, 0]
            w_im = screen[total - first, 1]
            return (
                both_re + g_re * w_re,
                both_im + g_im * w_im,
                mixed + g_re * w_im + g_im * w_re,
            )

        if unroll:
            sums = (zero, zero, zero)
            for first in range(max(0, total - count + 1), min(count - 1, total) + 1):
                sums = term(first, sums)
        else:
            low = jnp.maximum(0, total - count + 1)
            high = jnp.minimum(count - 1, total) + 1
            sums = lax.fori_loop(low, high, term, (zero, zero, zero))
        both_re, both_im, mixed = sums
        s_re = -scale * mixed
        s_im = scale * (both_re - both_im)
        if has_diagonal:
            at_rows, at_cols = grid_of((rows, width), offset[0])
            diagonal = at_rows == at_cols
            s_re = jnp.where(diagonal, -scale * both_re, s_re)
            s_im = jnp.where(diagonal, -scale * both_im, s_im)
        stored = place[point]
        out[stored, 0] = s_re.astype(jnp.bfloat16)
        out[stored, 1] = s_im.astype(jnp.bfloat16)
        return carry

    if unroll:
        for point in range(count):
            one(point, 0)
    else:
        lax.fori_loop(0, count, one, 0)


def convolve(pieces, energy_index, row_offset, has_diagonal):
    count, _, _, rows, width = pieces.shape
    smem = pl.BlockSpec(memory_space=SMEM)
    return pl.pallas_call(
        functools.partial(conv_kernel, has_diagonal),
        out_shape=jax.ShapeDtypeStruct((count, 2, rows, width), jnp.bfloat16),
        in_specs=[smem, smem] + vmem(1),
        out_specs=vmem(1)[0],
        scratch_shapes=[
            pltpu.VMEM((count, 2, rows, width), jnp.float32),
            pltpu.VMEM((count, 2, rows, width), jnp.float32),
            pltpu.SMEM((count,), jnp.int32),
        ],
        compiler_params=params(24),
    )(energy_index, row_offset, pieces)


def share_of(me, d, rows):
    return pl.ds(pl.multiple_of((lax.shift_right_logical(me, 1) ^ d) * rows, rows), rows)


def cut_cross_kernel(chips, me, green, screen, *rest):
    outs, sems = rest[:chips], rest[chips]
    half = green.shape[-1] // 2
    rows = half // chips
    copies = []
    for d in range(chips):
        for field, source in enumerate((green, screen)):
            part = source.at[0, :, 0, share_of(me[0], d, rows), half:]
            copies.append(pltpu.make_async_copy(part, outs[d].at[field], sems.at[d, field]))
            copies[-1].start()
    for copy in copies:
        copy.wait()


def cut_tri_kernel(chips, me, green, screen, *rest):
    outs = rest[:chips]
    near, far, sems = rest[chips:]
    half = near.shape[-1]
    rows = half // chips
    copies = []
    for field, source in enumerate((green, screen)):
        for place, (held, lines) in enumerate(((near, slice(0, half)), (far, slice(half, None)))):
            copy = pltpu.make_async_copy(
                source.at[0, :, 0, lines, lines], held.at[field], sems.at[field, place]
            )
            copy.start()
            copies.append(copy)
    for copy in copies:
        copy.wait()
    at_rows, at_cols = grid_of((rows, half))
    for d in range(chips):
        lines = share_of(me[0], d, rows)
        here = at_rows + (lax.shift_right_logical(me[0], 1) ^ d) * rows
        upper = here < at_cols
        diagonal = here == at_cols
        for field in range(2):
            a_re = near[field, 0, lines, :].astype(jnp.float32)
            a_im = near[field, 1, lines, :].astype(jnp.float32)
            d_re = far[field, 0, lines, :].astype(jnp.float32)
            d_im = far[field, 1, lines, :].astype(jnp.float32)
            t_re = jnp.where(upper, a_re, jnp.where(diagonal, a_im, d_re))
            outs[d][field, 0] = t_re.astype(jnp.bfloat16)
            outs[d][field, 1] = jnp.where(upper, a_im, d_im).astype(jnp.bfloat16)


def cut(me, green, screen, chips, tri):
    half = green.shape[-1] // 2
    piece = jax.ShapeDtypeStruct((2, 2, half // chips, half), jnp.bfloat16)
    squares_held = [pltpu.VMEM((2, 2, half, half), jnp.bfloat16)] * 2
    scratch = squares_held + [pltpu.SemaphoreType.DMA((2, 2))] if tri else [pltpu.SemaphoreType.DMA((chips, 2))]
    return pl.pallas_call(
        functools.partial(cut_tri_kernel if tri else cut_cross_kernel, chips),
        out_shape=(piece,) * chips,
        in_specs=[pl.BlockSpec(memory_space=SMEM)] + [pl.BlockSpec(memory_space=HBM)] * 2,
        out_specs=tuple(vmem(chips)),
        scratch_shapes=scratch,
        compiler_params=params(56),
        cost_estimate=SMALL,
    )(me, green, screen)


def bind_kernel(*refs):
    for place, piece in enumerate(refs[:-1]):
        refs[-1][place] = piece[...]


def bind(pieces):
    shape = (len(pieces),) + pieces[0].shape
    return pl.pallas_call(
        bind_kernel,
        out_shape=jax.ShapeDtypeStruct(shape, jnp.bfloat16),
        in_specs=vmem(len(pieces)),
        out_specs=vmem(1)[0],
        compiler_params=params(32),
        cost_estimate=SMALL,
    )(*pieces)


def conv_pieces_kernel(chips, has_diagonal, me, index, *rest):
    same = rest[:chips]
    beside, other = rest[chips : chips + 2]
    outs = rest[chips + 2 : 2 * chips + 2]
    green, screen, sums, place = rest[2 * chips + 2 :]
    groups = 2 * chips
    rows, width = sums.shape[2:]
    for core in range(2):
        for d in range(chips):
            stored = me[0] ^ (2 * d + core)
            point = index[stored]
            place[point] = stored
            if core == 0:
                green[point] = same[d][0]
                screen[point] = same[d][1]
            elif d == 0:
                green[point] = beside[0]
                screen[point] = beside[1]
            else:
                green[point] = other[d - 1, 0]
                screen[point] = other[d - 1, 1]
    scale = groups**-0.5
    tall = 16
    for point in range(groups):

        @pl.when(((place[point] ^ me[0]) & 1) == 0)
        def _():
            total = point + groups // 2
            for first_row in range(0, rows, tall):
                for first_col in range(0, width, 128):
                    at = (slice(first_row, first_row + tall), slice(first_col, first_col + 128))
                    both_re = both_im = mixed = None
                    for p in range(max(0, total - groups + 1), min(groups - 1, total) + 1):
                        g_re = green[(p, 0) + at].astype(jnp.float32)
                        g_im = green[(p, 1) + at].astype(jnp.float32)
                        w_re = screen[(total - p, 0) + at].astype(jnp.float32)
                        w_im = screen[(total - p, 1) + at].astype(jnp.float32)
                        re = g_re * w_re
                        im = g_im * w_im
                        mix = g_re * w_im + g_im * w_re
                        both_re = re if both_re is None else both_re + re
                        both_im = im if both_im is None else both_im + im
                        mixed = mix if mixed is None else mixed + mix
                    s_re = -scale * mixed
                    s_im = scale * (both_re - both_im)
                    if has_diagonal:
                        first = lax.shift_right_logical(me[0], 1) * rows + first_row
                        at_rows, at_cols = grid_of((tall, 128), first)
                        diagonal = at_rows == at_cols + first_col
                        s_re = jnp.where(diagonal, -scale * both_re, s_re)
                        s_im = jnp.where(diagonal, -scale * both_im, s_im)
                    sums[(point, 0) + at] = s_re.astype(jnp.bfloat16)
                    sums[(point, 1) + at] = s_im.astype(jnp.bfloat16)

    for d in range(chips):
        outs[d][...] = sums[index[me[0] ^ (2 * d)]]


def conv_pieces(me, energy_index, same, beside, other, has_diagonal):
    chips = len(same)
    shape = same[0].shape[1:]
    smem = pl.BlockSpec(memory_space=SMEM)
    return pl.pallas_call(
        functools.partial(conv_pieces_kernel, chips, has_diagonal),
        out_shape=(jax.ShapeDtypeStruct(shape, jnp.bfloat16),) * chips,
        in_specs=[smem, smem] + vmem(chips + 2),
        out_specs=tuple(vmem(chips)),
        scratch_shapes=[pltpu.VMEM((2 * chips,) + shape, jnp.bfloat16)] * 3
        + [pltpu.SMEM((2 * chips,), jnp.int32)],
        compiler_params=params(32),
        cost_estimate=SMALL,
    )(me, energy_index, *same, beside, other)


def join_kernel(chips, me, *rest):
    pieces, out = rest[:chips], rest[chips]
    rows = pieces[0].shape[1]
    for d in range(chips):
        out[:, share_of(me[0], d, rows), :] = pieces[d][...]


def join(me, pieces):
    half = pieces[0].shape[-1]
    return pl.pallas_call(
        functools.partial(join_kernel, len(pieces)),
        out_shape=jax.ShapeDtypeStruct((2, half, half), jnp.bfloat16),
        in_specs=[pl.BlockSpec(memory_space=SMEM)] + vmem(len(pieces)),
        out_specs=vmem(1)[0],
        compiler_params=params(32),
        cost_estimate=SMALL,
    )(me, *pieces)


def swap(piece, d, groups):
    return lax.ppermute(piece, "energy", [(i, i ^ d) for i in range(groups)]) if d else piece


def after(value, *earlier):
    return lax.optimization_barrier((value, earlier))[0]


def gather_paired(g_lesser, w_lesser, energy_index, groups, send=lambda part: ()):
    me = lax.axis_index("energy").astype(jnp.int32).reshape(1)
    chips = groups // 2

    def over(pieces):
        return [swap(pieces[d], 2 * d, groups) for d in range(chips)]

    cross, tri = (cut(me, g_lesser, w_lesser, chips, which) for which in (False, True))
    same_cross, same_tri = over(cross), over(tri)
    beside_cross, beside_tri = swap(cross[0], 1, groups), swap(tri[0], 1, groups)
    other = swap(bind(after(same_cross[1:], tri[0])), 1, groups)
    shares = over(conv_pieces(me, energy_index, same_cross, beside_cross, other, False))
    own_cross = join(me, after(shares, same_tri[1:], beside_tri))
    sent = send(own_cross)
    other = swap(bind(after(same_tri[1:], own_cross)), 1, groups)
    shares = over(conv_pieces(me, energy_index, same_tri, beside_tri, other, True))
    own_tri = join(me, after(shares, sent))
    return own_cross, own_tri


def gather_shared(g_lesser, w_lesser, energy_index, groups):
    half = g_lesser.shape[-1] // 2
    rows = half // groups
    cross, tri = (split_rows(packed, groups) for packed in pack(g_lesser, w_lesser, 1))
    offset = (lax.axis_index("energy") * rows).astype(jnp.int32).reshape(1)
    own = []
    for pieces, has_diagonal in ((cross, False), (tri, True)):
        shares = convolve(exchange(pieces), energy_index, offset, has_diagonal)
        own.append(jnp.moveaxis(exchange(shares), 0, 1).reshape(2, half, half))
    return own


def squares(cross, tri):
    return cross[0], cross[1], tri[0], tri[1]


def dot(a, b):
    return jnp.dot(a, b, preferred_element_type=jnp.float32)


def dot_t(a, b):
    return lax.dot_general(a, b, (((1,), (1,)), ((), ())), preferred_element_type=jnp.float32)


def product(cross, tri, retarded):
    c_re, c_im, t_re, t_im = squares(cross, tri)
    half = c_re.shape[0]
    rows, cols = grid_of((half, half))
    tr = t_re.astype(jnp.float32)
    ti = t_im.astype(jnp.float32)
    diagonal = rows == cols
    a_re = jnp.where(rows < cols, tr, 0.0).astype(jnp.bfloat16)
    a_im = jnp.where(rows < cols, ti, jnp.where(diagonal, 0.5 * tr, 0.0)).astype(jnp.bfloat16)
    d_re = jnp.where(rows > cols, tr, 0.0).astype(jnp.bfloat16)
    d_im = jnp.where(rows > cols, ti, jnp.where(diagonal, 0.5 * ti, 0.0)).astype(jnp.bfloat16)
    g_re = retarded[0]
    g_im = retarded[1]
    near = jnp.concatenate([g_re[:, :half], g_im[:, :half]], axis=1)
    far = jnp.concatenate([g_re, g_im], axis=1)
    l_re = jnp.concatenate(
        [
            dot(near, jnp.concatenate([a_re, -a_im], axis=0)),
            dot(far, jnp.concatenate([c_re, d_re, -c_im, -d_im], axis=0)),
        ],
        axis=1,
    ).astype(jnp.bfloat16)
    l_im = jnp.concatenate(
        [
            dot(near, jnp.concatenate([a_im, a_re], axis=0)),
            dot(far, jnp.concatenate([c_im, d_im, c_re, d_re], axis=0)),
        ],
        axis=1,
    ).astype(jnp.bfloat16)
    x_re = dot_t(jnp.concatenate([l_re, l_im], axis=1), far)
    x_im = dot_t(jnp.concatenate([l_im, -l_re], axis=1), far)
    return x_re, x_im


def own_kernel(where, cross, tri, retarded, sigma, total, block, sem):
    copy = pltpu.make_async_copy(retarded.at[0, :, 0, where[0]], block, sem)
    copy.start()
    c_re, c_im, t_re, t_im = squares(cross, tri)
    half = c_re.shape[0]
    rows, cols = grid_of((half, half))
    upper = rows < cols
    diagonal = rows == cols
    tr = t_re.astype(jnp.float32)
    ti = t_im.astype(jnp.float32)
    trt = tr.T
    tit = ti.T
    zero = jnp.zeros_like(tr)
    bf = jnp.bfloat16
    sigma[0, 0, 0, :half, half:] = c_re
    sigma[0, 1, 0, :half, half:] = c_im
    sigma[0, 0, 0, half:, :half] = (-(c_re.astype(jnp.float32).T)).astype(bf)
    sigma[0, 1, 0, half:, :half] = c_im.astype(jnp.float32).T.astype(bf)
    sigma[0, 0, 0, :half, :half] = jnp.where(upper, tr, jnp.where(diagonal, zero, -trt)).astype(bf)
    sigma[0, 1, 0, :half, :half] = jnp.where(upper, ti, jnp.where(diagonal, tr, tit)).astype(bf)
    sigma[0, 0, 0, half:, half:] = jnp.where(upper, -trt, jnp.where(diagonal, zero, tr)).astype(bf)
    sigma[0, 1, 0, half:, half:] = jnp.where(upper, tit, ti).astype(bf)
    copy.wait()
    total[0], total[1] = product(cross, tri, block)


def step_kernel(count, last, ahead, where, *rest):
    if last:
        block, total = rest[:2]
        sources = rest[2 : 2 + 2 * count]
        out = rest[-1]
    else:
        sources = rest[: 2 * count]
        rest = rest[2 * count :]
    if last:
        pass
    elif ahead:
        retarded, total, out, later, block, sems = rest
        fetch = pltpu.make_async_copy(retarded.at[0, :, 0, where[0]], block, sems.at[0])
        fetch.start()
        prefetch = pltpu.make_async_copy(retarded.at[0, :, 0, where[2]], later, sems.at[1])
        prefetch.start()
        fetch.wait()
    else:
        retarded, total, out, block, sems = rest
        fetch = pltpu.make_async_copy(retarded.at[0, :, 0, where[0]], block, sems.at[0])
        fetch.start()
        fetch.wait()
    for pick in range(count):

        @pl.when(where[1] == pick)
        def _():
            cross, tri = sources[pick], sources[count + pick]
            x_re, x_im = product(cross, tri, block)
            x_re += total[0]
            x_im += total[1]
            if last:
                out[0, 0, 0] = (x_re - x_re.T).astype(jnp.bfloat16)
                out[0, 1, 0] = (x_im + x_im.T).astype(jnp.bfloat16)
            else:
                out[0] = x_re
                out[1] = x_im

    if ahead:
        prefetch.wait()


def cost(width):
    return pl.CostEstimate(flops=14 * width**3, bytes_accessed=8 * width**2, transcendentals=0)


def own_product(block, own, retarded):
    width = retarded.shape[-1]
    return pl.pallas_call(
        own_kernel,
        out_shape=(
            jax.ShapeDtypeStruct((1, 2, 1, width, width), jnp.bfloat16),
            jax.ShapeDtypeStruct((2, width, width), jnp.float32),
        ),
        in_specs=[pl.BlockSpec(memory_space=SMEM)] + vmem(2) + [pl.BlockSpec(memory_space=HBM)],
        out_specs=tuple(vmem(2)),
        scratch_shapes=[pltpu.VMEM((2, width, width), jnp.bfloat16), pltpu.SemaphoreType.DMA],
        compiler_params=params(48),
        cost_estimate=cost(width),
    )(block.reshape(1), *own, retarded)


def step_product(block, pick, sources, retarded, total, later=None):
    width = retarded.shape[-1]
    flat = [source[part] for part in range(2) for source in sources]
    ahead = later is not None
    numbers = jnp.stack([block, pick] + ([later] if ahead else []))
    total_shape = jax.ShapeDtypeStruct((2, width, width), jnp.float32)
    block_shape = jax.ShapeDtypeStruct((2, width, width), jnp.bfloat16)
    return pl.pallas_call(
        functools.partial(step_kernel, len(sources), False, ahead),
        out_shape=(total_shape, block_shape) if ahead else total_shape,
        in_specs=[pl.BlockSpec(memory_space=SMEM)]
        + vmem(len(flat))
        + [pl.BlockSpec(memory_space=HBM)]
        + vmem(1),
        out_specs=tuple(vmem(2)) if ahead else vmem(1)[0],
        scratch_shapes=[pltpu.VMEM((2, width, width), jnp.bfloat16), pltpu.SemaphoreType.DMA((2,))],
        compiler_params=params(46),
        cost_estimate=cost(width),
    )(numbers, *flat, retarded, total)


def last_product(pick, sources, block, total):
    width = block.shape[-1]
    flat = [source[part] for part in range(2) for source in sources]
    return pl.pallas_call(
        functools.partial(step_kernel, len(sources), True, False),
        out_shape=jax.ShapeDtypeStruct((1, 2, 1, width, width), jnp.bfloat16),
        in_specs=[pl.BlockSpec(memory_space=SMEM)] + vmem(len(flat) + 2),
        out_specs=vmem(1)[0],
        compiler_params=params(48),
        cost_estimate=cost(width),
    )(jnp.stack([pick, pick]), block, total, *flat)


def exchange(pieces):
    return lax.all_to_all(pieces, "energy", split_axis=0, concat_axis=0, tiled=True)


def shards(g_lesser, w_lesser, g_retarded, energy_index):
    width = g_lesser.shape[-1]
    groups = lax.axis_size("energy")
    chain = lax.axis_size("space")
    here = lax.axis_index("space")
    paired = groups >= 4 and groups & (groups - 1) == 0 and (width // groups) % 16 == 0
    here = here.astype(jnp.int32)
    if chain == 4:
        return around_line(here, paired, g_lesser, w_lesser, energy_index, groups, g_retarded)
    gather = gather_paired if paired else gather_shared
    own = gather(g_lesser, w_lesser, energy_index, groups)
    everyone = [lax.all_gather(part, "space") for part in own]
    sigma_lesser, total = own_product(here, own, g_retarded)
    zero = jnp.int32(0)

    def source(block):
        return tuple(lax.dynamic_index_in_dim(part, block, 0, False) for part in everyone)

    for step in range(1, chain - 1):
        block = (here + step) % chain
        later = (block + 1) % chain
        total, held = step_product(block, zero, [source(block)], g_retarded, total, later)
    return (sigma_lesser, last_product(zero, [source(later)], held, total))


def around_line(here, paired, g_lesser, w_lesser, energy_index, groups, retarded):
    outer = [(0, 1), (1, 0), (2, 3), (3, 2)]
    inner = [(1, 2), (2, 1)]

    def swap(part, pairs):
        return lax.ppermute(part, "space", pairs)

    end = ((here == 0) | (here == 3)).astype(jnp.int32)
    first, second, third, fourth = [], [], [], []

    def send(part):
        first.append(swap(part, outer))
        second.append(swap(part, inner))
        return first[-1], second[-1]

    if paired:
        own = gather_paired(g_lesser, w_lesser, energy_index, groups, send)
        send(own[1])
    else:
        own = gather_shared(g_lesser, w_lesser, energy_index, groups)
        send(own[0]), send(own[1])
    sigma_lesser, total = own_product(here, own, retarded)
    third.append(swap(first[0], inner))
    fourth.append(swap(second[0], outer))
    third.append(swap(after(first[1], fourth[0], total), inner))
    fourth.append(swap(second[1], outer))
    fifth = [swap(part, outer) for part in third]
    zero = jnp.int32(0)
    total = step_product(here ^ 1, zero, [first], retarded, total)
    near, far = here ^ 2, 3 - here
    total, held = step_product(
        jnp.where(end == 1, near, far), end, [second, fourth], retarded, total, jnp.where(end == 1, far, near)
    )
    delta = last_product(end, [third, fifth], held, total)
    return (sigma_lesser, delta)


def solution(mesh):
    return jax.shard_map(
        shards,
        mesh=mesh,
        in_specs=(
            P("energy", None, "space", None, None),
            P("energy", None, "space", None, None),
            P("energy", None, "space", None, None, None),
            P(),
        ),
        out_specs=(P("energy", None, "space", None, None), P("energy", None, "space", None, None)),
        check_vma=False,
    )
```

```python
import functools

import jax
import jax.numpy as jnp
from jax import lax
from jax.experimental import pallas as pl
from jax.experimental.pallas import tpu as pltpu
from jax.sharding import PartitionSpec as P


VMEM = pltpu.MemorySpace.VMEM
SMEM = pltpu.MemorySpace.SMEM
HBM = pltpu.MemorySpace.HBM

SMALL = pl.CostEstimate(flops=1, bytes_accessed=1, transcendentals=0)


def vmem(count):
    return [pl.BlockSpec(memory_space=VMEM)] * count


def params(mib):
    return pltpu.CompilerParams(vmem_limit_bytes=mib * 2**20)


def grid_of(shape, row_offset=0):
    rows = lax.broadcasted_iota(jnp.int32, shape, 0) + row_offset
    cols = lax.broadcasted_iota(jnp.int32, shape, 1)
    return rows, cols


def pack_kernel(green, screen, cross, tri):
    half = green.shape[-1] // 2
    rows, cols = grid_of((half, half))
    upper = rows < cols
    diagonal = rows == cols
    for place, source in enumerate((green, screen)):
        a_re = source[0, 0, 0, :half, :half].astype(jnp.float32)
        a_im = source[0, 1, 0, :half, :half].astype(jnp.float32)
        d_re = source[0, 0, 0, half:, half:].astype(jnp.float32)
        d_im = source[0, 1, 0, half:, half:].astype(jnp.float32)
        t_re = jnp.where(upper, a_re, jnp.where(diagonal, a_im, d_re)).astype(jnp.bfloat16)
        t_im = jnp.where(upper, a_im, d_im).astype(jnp.bfloat16)
        c_re = source[0, 0, 0, :half, half:]
        c_im = source[0, 1, 0, :half, half:]
        shape = cross.shape[:1] + cross.shape[3:]
        cross[:, place, 0] = c_re.reshape(shape)
        cross[:, place, 1] = c_im.reshape(shape)
        tri[:, place, 0] = t_re.reshape(shape)
        tri[:, place, 1] = t_im.reshape(shape)


def pack(green, screen, parts):
    half = green.shape[-1] // 2
    out = jax.ShapeDtypeStruct((parts, 2, 2, half // parts, half), jnp.bfloat16)
    return pl.pallas_call(
        pack_kernel,
        out_shape=(out, out),
        in_specs=vmem(2),
        out_specs=tuple(vmem(2)),
        compiler_params=params(24),
    )(green, screen)


def split_rows(packed, groups):
    _, fields, comps, half, width = packed.shape
    shaped = packed.reshape(fields, comps, groups, half // groups, width)
    return jnp.moveaxis(shaped, 2, 0)


def conv_kernel(has_diagonal, index, offset, pieces, out, green, screen, place):
    count, _, _, rows, width = pieces.shape

    def scatter(stored, carry):
        point = index[stored]
        place[point] = stored
        green[point] = pieces[stored, 0].astype(jnp.float32)
        screen[point] = pieces[stored, 1].astype(jnp.float32)
        return carry

    unroll = count <= 16
    lax.fori_loop(0, count, scatter, 0, unroll=unroll)
    scale = count**-0.5
    zero = jnp.zeros((rows, width), jnp.float32)

    def one(point, carry):
        total = point + count // 2

        def term(first, sums):
            both_re, both_im, mixed = sums
            g_re = green[first, 0]
            g_im = green[first, 1]
            w_re = screen[total - first, 0]
            w_im = screen[total - first, 1]
            return (
                both_re + g_re * w_re,
                both_im + g_im * w_im,
                mixed + g_re * w_im + g_im * w_re,
            )

        if unroll:
            sums = (zero, zero, zero)
            for first in range(max(0, total - count + 1), min(count - 1, total) + 1):
                sums = term(first, sums)
        else:
            low = jnp.maximum(0, total - count + 1)
            high = jnp.minimum(count - 1, total) + 1
            sums = lax.fori_loop(low, high, term, (zero, zero, zero))
        both_re, both_im, mixed = sums
        s_re = -scale * mixed
        s_im = scale * (both_re - both_im)
        if has_diagonal:
            at_rows, at_cols = grid_of((rows, width), offset[0])
            diagonal = at_rows == at_cols
            s_re = jnp.where(diagonal, -scale * both_re, s_re)
            s_im = jnp.where(diagonal, -scale * both_im, s_im)
        stored = place[point]
        out[stored, 0] = s_re.astype(jnp.bfloat16)
        out[stored, 1] = s_im.astype(jnp.bfloat16)
        return carry

    if unroll:
        for point in range(count):
            one(point, 0)
    else:
        lax.fori_loop(0, count, one, 0)


def convolve(pieces, energy_index, row_offset, has_diagonal):
    count, _, _, rows, width = pieces.shape
    smem = pl.BlockSpec(memory_space=SMEM)
    return pl.pallas_call(
        functools.partial(conv_kernel, has_diagonal),
        out_shape=jax.ShapeDtypeStruct((count, 2, rows, width), jnp.bfloat16),
        in_specs=[smem, smem] + vmem(1),
        out_specs=vmem(1)[0],
        scratch_shapes=[
            pltpu.VMEM((count, 2, rows, width), jnp.float32),
            pltpu.VMEM((count, 2, rows, width), jnp.float32),
            pltpu.SMEM((count,), jnp.int32),
        ],
        compiler_params=params(24),
    )(energy_index, row_offset, pieces)


def share_of(me, d, rows):
    return pl.ds(pl.multiple_of((lax.shift_right_logical(me, 1) ^ d) * rows, rows), rows)


def cut_cross_kernel(chips, me, green, screen, *rest):
    outs, sems = rest[:chips], rest[chips]
    half = green.shape[-1] // 2
    rows = half // chips
    copies = []
    for d in range(chips):
        for field, source in enumerate((green, screen)):
            part = source.at[0, :, 0, share_of(me[0], d, rows), half:]
            copies.append(pltpu.make_async_copy(part, outs[d].at[field], sems.at[d, field]))
            copies[-1].start()
    for copy in copies:
        copy.wait()


def cut_tri_kernel(chips, me, green, screen, *rest):
    outs = rest[:chips]
    near, far, sems = rest[chips:]
    half = near.shape[-1]
    rows = half // chips
    copies = []
    for field, source in enumerate((green, screen)):
        for place, (held, lines) in enumerate(((near, slice(0, half)), (far, slice(half, None)))):
            copy = pltpu.make_async_copy(
                source.at[0, :, 0, lines, lines], held.at[field], sems.at[field, place]
            )
            copy.start()
            copies.append(copy)
    for copy in copies:
        copy.wait()
    at_rows, at_cols = grid_of((rows, half))
    for d in range(chips):
        lines = share_of(me[0], d, rows)
        here = at_rows + (lax.shift_right_logical(me[0], 1) ^ d) * rows
        upper = here < at_cols
        diagonal = here == at_cols
        for field in range(2):
            a_re = near[field, 0, lines, :].astype(jnp.float32)
            a_im = near[field, 1, lines, :].astype(jnp.float32)
            d_re = far[field, 0, lines, :].astype(jnp.float32)
            d_im = far[field, 1, lines, :].astype(jnp.float32)
            t_re = jnp.where(upper, a_re, jnp.where(diagonal, a_im, d_re))
            outs[d][field, 0] = t_re.astype(jnp.bfloat16)
            outs[d][field, 1] = jnp.where(upper, a_im, d_im).astype(jnp.bfloat16)


def cut(me, green, screen, chips, tri):
    half = green.shape[-1] // 2
    piece = jax.ShapeDtypeStruct((2, 2, half // chips, half), jnp.bfloat16)
    squares_held = [pltpu.VMEM((2, 2, half, half), jnp.bfloat16)] * 2
    scratch = squares_held + [pltpu.SemaphoreType.DMA((2, 2))] if tri else [pltpu.SemaphoreType.DMA((chips, 2))]
    return pl.pallas_call(
        functools.partial(cut_tri_kernel if tri else cut_cross_kernel, chips),
        out_shape=(piece,) * chips,
        in_specs=[pl.BlockSpec(memory_space=SMEM)] + [pl.BlockSpec(memory_space=HBM)] * 2,
        out_specs=tuple(vmem(chips)),
        scratch_shapes=scratch,
        compiler_params=params(56),
        cost_estimate=SMALL,
    )(me, green, screen)


def bind_kernel(*refs):
    for place, piece in enumerate(refs[:-1]):
        refs[-1][place] = piece[...]


def bind(pieces):
    shape = (len(pieces),) + pieces[0].shape
    return pl.pallas_call(
        bind_kernel,
        out_shape=jax.ShapeDtypeStruct(shape, jnp.bfloat16),
        in_specs=vmem(len(pieces)),
        out_specs=vmem(1)[0],
        compiler_params=params(32),
        cost_estimate=SMALL,
    )(*pieces)


def conv_pieces_kernel(chips, has_diagonal, me, index, *rest):
    same = rest[:chips]
    beside, other = rest[chips : chips + 2]
    outs = rest[chips + 2 : 2 * chips + 2]
    green, screen, sums, place = rest[2 * chips + 2 :]
    groups = 2 * chips
    rows, width = sums.shape[2:]
    for core in range(2):
        for d in range(chips):
            stored = me[0] ^ (2 * d + core)
            point = index[stored]
            place[point] = stored
            if core == 0:
                green[point] = same[d][0]
                screen[point] = same[d][1]
            elif d == 0:
                green[point] = beside[0]
                screen[point] = beside[1]
            else:
                green[point] = other[d - 1, 0]
                screen[point] = other[d - 1, 1]
    scale = groups**-0.5
    tall = 16
    for point in range(groups):

        @pl.when(((place[point] ^ me[0]) & 1) == 0)
        def _():
            total = point + groups // 2
            for first_row in range(0, rows, tall):
                for first_col in range(0, width, 128):
                    at = (slice(first_row, first_row + tall), slice(first_col, first_col + 128))
                    both_re = both_im = mixed = None
                    for p in range(max(0, total - groups + 1), min(groups - 1, total) + 1):
                        g_re = green[(p, 0) + at].astype(jnp.float32)
                        g_im = green[(p, 1) + at].astype(jnp.float32)
                        w_re = screen[(total - p, 0) + at].astype(jnp.float32)
                        w_im = screen[(total - p, 1) + at].astype(jnp.float32)
                        re = g_re * w_re
                        im = g_im * w_im
                        mix = g_re * w_im + g_im * w_re
                        both_re = re if both_re is None else both_re + re
                        both_im = im if both_im is None else both_im + im
                        mixed = mix if mixed is None else mixed + mix
                    s_re = -scale * mixed
                    s_im = scale * (both_re - both_im)
                    if has_diagonal:
                        first = lax.shift_right_logical(me[0], 1) * rows + first_row
                        at_rows, at_cols = grid_of((tall, 128), first)
                        diagonal = at_rows == at_cols + first_col
                        s_re = jnp.where(diagonal, -scale * both_re, s_re)
                        s_im = jnp.where(diagonal, -scale * both_im, s_im)
                    sums[(point, 0) + at] = s_re.astype(jnp.bfloat16)
                    sums[(point, 1) + at] = s_im.astype(jnp.bfloat16)

    for d in range(chips):
        outs[d][...] = sums[index[me[0] ^ (2 * d)]]


def conv_pieces(me, energy_index, same, beside, other, has_diagonal):
    chips = len(same)
    shape = same[0].shape[1:]
    smem = pl.BlockSpec(memory_space=SMEM)
    return pl.pallas_call(
        functools.partial(conv_pieces_kernel, chips, has_diagonal),
        out_shape=(jax.ShapeDtypeStruct(shape, jnp.bfloat16),) * chips,
        in_specs=[smem, smem] + vmem(chips + 2),
        out_specs=tuple(vmem(chips)),
        scratch_shapes=[pltpu.VMEM((2 * chips,) + shape, jnp.bfloat16)] * 3
        + [pltpu.SMEM((2 * chips,), jnp.int32)],
        compiler_params=params(32),
        cost_estimate=SMALL,
    )(me, energy_index, *same, beside, other)


def join_kernel(chips, me, *rest):
    pieces, out = rest[:chips], rest[chips]
    rows = pieces[0].shape[1]
    for d in range(chips):
        out[:, share_of(me[0], d, rows), :] = pieces[d][...]


def join(me, pieces):
    half = pieces[0].shape[-1]
    return pl.pallas_call(
        functools.partial(join_kernel, len(pieces)),
        out_shape=jax.ShapeDtypeStruct((2, half, half), jnp.bfloat16),
        in_specs=[pl.BlockSpec(memory_space=SMEM)] + vmem(len(pieces)),
        out_specs=vmem(1)[0],
        compiler_params=params(32),
        cost_estimate=SMALL,
    )(me, *pieces)


def swap(piece, d, groups):
    return lax.ppermute(piece, "energy", [(i, i ^ d) for i in range(groups)]) if d else piece


def after(value, *earlier):
    return lax.optimization_barrier((value, earlier))[0]


def gather_paired(g_lesser, w_lesser, energy_index, groups, send=lambda part: ()):
    me = lax.axis_index("energy").astype(jnp.int32).reshape(1)
    chips = groups // 2

    def over(pieces):
        return [swap(pieces[d], 2 * d, groups) for d in range(chips)]

    cross, tri = (cut(me, g_lesser, w_lesser, chips, which) for which in (False, True))
    same_cross, same_tri = over(cross), over(tri)
    beside_cross, beside_tri = swap(cross[0], 1, groups), swap(tri[0], 1, groups)
    other = swap(bind(after(same_cross[1:], tri[0])), 1, groups)
    other = after(other, same_tri[-1])
    shares = over(conv_pieces(me, energy_index, same_cross, beside_cross, other, False))
    own_cross = join(me, after(shares, same_tri[1:], beside_tri))
    sent = send(own_cross)
    other = swap(bind(after(same_tri[1:], own_cross)), 1, groups)
    shares = over(conv_pieces(me, energy_index, same_tri, beside_tri, other, True))
    own_tri = join(me, after(shares, sent))
    return own_cross, own_tri


def gather_shared(g_lesser, w_lesser, energy_index, groups):
    half = g_lesser.shape[-1] // 2
    rows = half // groups
    cross, tri = (split_rows(packed, groups) for packed in pack(g_lesser, w_lesser, 1))
    offset = (lax.axis_index("energy") * rows).astype(jnp.int32).reshape(1)
    own = []
    for pieces, has_diagonal in ((cross, False), (tri, True)):
        shares = convolve(exchange(pieces), energy_index, offset, has_diagonal)
        own.append(jnp.moveaxis(exchange(shares), 0, 1).reshape(2, half, half))
    return own


def squares(cross, tri):
    return cross[0], cross[1], tri[0], tri[1]


def dot(a, b):
    return jnp.dot(a, b, preferred_element_type=jnp.float32)


def dot_t(a, b):
    return lax.dot_general(a, b, (((1,), (1,)), ((), ())), preferred_element_type=jnp.float32)


def product(cross, tri, retarded):
    c_re, c_im, t_re, t_im = squares(cross, tri)
    half = c_re.shape[0]
    rows, cols = grid_of((half, half))
    tr = t_re.astype(jnp.float32)
    ti = t_im.astype(jnp.float32)
    diagonal = rows == cols
    a_re = jnp.where(rows < cols, tr, 0.0).astype(jnp.bfloat16)
    a_im = jnp.where(rows < cols, ti, jnp.where(diagonal, 0.5 * tr, 0.0)).astype(jnp.bfloat16)
    d_re = jnp.where(rows > cols, tr, 0.0).astype(jnp.bfloat16)
    d_im = jnp.where(rows > cols, ti, jnp.where(diagonal, 0.5 * ti, 0.0)).astype(jnp.bfloat16)
    g_re = retarded[0]
    g_im = retarded[1]
    near = jnp.concatenate([g_re[:, :half], g_im[:, :half]], axis=1)
    far = jnp.concatenate([g_re, g_im], axis=1)
    l_re = jnp.concatenate(
        [
            dot(near, jnp.concatenate([a_re, -a_im], axis=0)),
            dot(far, jnp.concatenate([c_re, d_re, -c_im, -d_im], axis=0)),
        ],
        axis=1,
    ).astype(jnp.bfloat16)
    l_im = jnp.concatenate(
        [
            dot(near, jnp.concatenate([a_im, a_re], axis=0)),
            dot(far, jnp.concatenate([c_im, d_im, c_re, d_re], axis=0)),
        ],
        axis=1,
    ).astype(jnp.bfloat16)
    x_re = dot_t(jnp.concatenate([l_re, l_im], axis=1), far)
    x_im = dot_t(jnp.concatenate([l_im, -l_re], axis=1), far)
    return x_re, x_im


def own_kernel(where, cross, tri, retarded, sigma, total, block, sem):
    copy = pltpu.make_async_copy(retarded.at[0, :, 0, where[0]], block, sem)
    copy.start()
    c_re, c_im, t_re, t_im = squares(cross, tri)
    half = c_re.shape[0]
    rows, cols = grid_of((half, half))
    upper = rows < cols
    diagonal = rows == cols
    tr = t_re.astype(jnp.float32)
    ti = t_im.astype(jnp.float32)
    trt = tr.T
    tit = ti.T
    zero = jnp.zeros_like(tr)
    bf = jnp.bfloat16
    sigma[0, 0, 0, :half, half:] = c_re
    sigma[0, 1, 0, :half, half:] = c_im
    sigma[0, 0, 0, half:, :half] = (-(c_re.astype(jnp.float32).T)).astype(bf)
    sigma[0, 1, 0, half:, :half] = c_im.astype(jnp.float32).T.astype(bf)
    sigma[0, 0, 0, :half, :half] = jnp.where(upper, tr, jnp.where(diagonal, zero, -trt)).astype(bf)
    sigma[0, 1, 0, :half, :half] = jnp.where(upper, ti, jnp.where(diagonal, tr, tit)).astype(bf)
    sigma[0, 0, 0, half:, half:] = jnp.where(upper, -trt, jnp.where(diagonal, zero, tr)).astype(bf)
    sigma[0, 1, 0, half:, half:] = jnp.where(upper, tit, ti).astype(bf)
    copy.wait()
    total[0], total[1] = product(cross, tri, block)


def step_kernel(count, last, ahead, where, *rest):
    if last:
        block, total = rest[:2]
        sources = rest[2 : 2 + 2 * count]
        out = rest[-1]
    else:
        sources = rest[: 2 * count]
        rest = rest[2 * count :]
    if last:
        pass
    elif ahead:
        retarded, total, out, later, block, sems = rest
        fetch = pltpu.make_async_copy(retarded.at[0, :, 0, where[0]], block, sems.at[0])
        fetch.start()
        prefetch = pltpu.make_async_copy(retarded.at[0, :, 0, where[2]], later, sems.at[1])
        prefetch.start()
        fetch.wait()
    else:
        retarded, total, out, block, sems = rest
        fetch = pltpu.make_async_copy(retarded.at[0, :, 0, where[0]], block, sems.at[0])
        fetch.start()
        fetch.wait()
    for pick in range(count):

        @pl.when(where[1] == pick)
        def _():
            cross, tri = sources[pick], sources[count + pick]
            x_re, x_im = product(cross, tri, block)
            x_re += total[0]
            x_im += total[1]
            if last:
                out[0, 0, 0] = (x_re - x_re.T).astype(jnp.bfloat16)
                out[0, 1, 0] = (x_im + x_im.T).astype(jnp.bfloat16)
            else:
                out[0] = x_re
                out[1] = x_im

    if ahead:
        prefetch.wait()


def cost(width):
    return pl.CostEstimate(flops=14 * width**3, bytes_accessed=8 * width**2, transcendentals=0)


def own_product(block, own, retarded):
    width = retarded.shape[-1]
    return pl.pallas_call(
        own_kernel,
        out_shape=(
            jax.ShapeDtypeStruct((1, 2, 1, width, width), jnp.bfloat16),
            jax.ShapeDtypeStruct((2, width, width), jnp.float32),
        ),
        in_specs=[pl.BlockSpec(memory_space=SMEM)] + vmem(2) + [pl.BlockSpec(memory_space=HBM)],
        out_specs=tuple(vmem(2)),
        scratch_shapes=[pltpu.VMEM((2, width, width), jnp.bfloat16), pltpu.SemaphoreType.DMA],
        compiler_params=params(48),
        cost_estimate=cost(width),
    )(block.reshape(1), *own, retarded)


def step_product(block, pick, sources, retarded, total, later=None):
    width = retarded.shape[-1]
    flat = [source[part] for part in range(2) for source in sources]
    ahead = later is not None
    numbers = jnp.stack([block, pick] + ([later] if ahead else []))
    total_shape = jax.ShapeDtypeStruct((2, width, width), jnp.float32)
    block_shape = jax.ShapeDtypeStruct((2, width, width), jnp.bfloat16)
    return pl.pallas_call(
        functools.partial(step_kernel, len(sources), False, ahead),
        out_shape=(total_shape, block_shape) if ahead else total_shape,
        in_specs=[pl.BlockSpec(memory_space=SMEM)]
        + vmem(len(flat))
        + [pl.BlockSpec(memory_space=HBM)]
        + vmem(1),
        out_specs=tuple(vmem(2)) if ahead else vmem(1)[0],
        scratch_shapes=[pltpu.VMEM((2, width, width), jnp.bfloat16), pltpu.SemaphoreType.DMA((2,))],
        compiler_params=params(46),
        cost_estimate=cost(width),
    )(numbers, *flat, retarded, total)


def last_product(pick, sources, block, total):
    width = block.shape[-1]
    flat = [source[part] for part in range(2) for source in sources]
    return pl.pallas_call(
        functools.partial(step_kernel, len(sources), True, False),
        out_shape=jax.ShapeDtypeStruct((1, 2, 1, width, width), jnp.bfloat16),
        in_specs=[pl.BlockSpec(memory_space=SMEM)] + vmem(len(flat) + 2),
        out_specs=vmem(1)[0],
        compiler_params=params(48),
        cost_estimate=cost(width),
    )(jnp.stack([pick, pick]), block, total, *flat)


def exchange(pieces):
    return lax.all_to_all(pieces, "energy", split_axis=0, concat_axis=0, tiled=True)


def shards(g_lesser, w_lesser, g_retarded, energy_index):
    width = g_lesser.shape[-1]
    groups = lax.axis_size("energy")
    chain = lax.axis_size("space")
    here = lax.axis_index("space")
    paired = groups >= 4 and groups & (groups - 1) == 0 and (width // groups) % 16 == 0
    here = here.astype(jnp.int32)
    if chain == 4:
        return around_line(here, paired, g_lesser, w_lesser, energy_index, groups, g_retarded)
    gather = gather_paired if paired else gather_shared
    own = gather(g_lesser, w_lesser, energy_index, groups)
    everyone = [lax.all_gather(part, "space") for part in own]
    sigma_lesser, total = own_product(here, own, g_retarded)
    zero = jnp.int32(0)

    def source(block):
        return tuple(lax.dynamic_index_in_dim(part, block, 0, False) for part in everyone)

    for step in range(1, chain - 1):
        block = (here + step) % chain
        later = (block + 1) % chain
        total, held = step_product(block, zero, [source(block)], g_retarded, total, later)
    return (sigma_lesser, last_product(zero, [source(later)], held, total))


def around_line(here, paired, g_lesser, w_lesser, energy_index, groups, retarded):
    outer = [(0, 1), (1, 0), (2, 3), (3, 2)]
    inner = [(0, 0), (1, 2), (2, 1), (3, 3)]

    def swap(part, pairs):
        return lax.ppermute(part, "space", pairs)

    end = ((here == 0) | (here == 3)).astype(jnp.int32)
    first, second, third, fourth = [], [], [], []

    def send(part):
        first.append(swap(part, outer))
        second.append(swap(part, inner))
        return first[-1], second[-1]

    if paired:
        own = gather_paired(g_lesser, w_lesser, energy_index, groups, send)
        send(own[1])
    else:
        own = gather_shared(g_lesser, w_lesser, energy_index, groups)
        send(own[0]), send(own[1])
    third.append(swap(first[0], inner))
    sigma_lesser, total = own_product(here, own, retarded)
    fourth.append(swap(second[0], outer))
    third.append(swap(after(first[1], fourth[0], total), inner))
    fourth.append(swap(second[1], outer))
    fifth = [swap(part, outer) for part in third]
    zero = jnp.int32(0)
    total = step_product(here ^ 1, zero, [first], retarded, total)
    near, far = here ^ 2, 3 - here
    total, held = step_product(
        jnp.where(end == 1, near, far), end, [second, fourth], retarded, total, jnp.where(end == 1, far, near)
    )
    delta = last_product(end, [third, fifth], held, total)
    return (sigma_lesser, delta)


def solution(mesh):
    return jax.shard_map(
        shards,
        mesh=mesh,
        in_specs=(
            P("energy", None, "space", None, None),
            P("energy", None, "space", None, None),
            P("energy", None, "space", None, None, None),
            P(),
        ),
        out_specs=(P("energy", None, "space", None, None), P("energy", None, "space", None, None)),
        check_vma=False,
    )
```

```python
import functools

import jax
import jax.numpy as jnp
from jax import lax
from jax.experimental import pallas as pl
from jax.experimental.pallas import tpu as pltpu
from jax.sharding import PartitionSpec as P


VMEM = pltpu.MemorySpace.VMEM
SMEM = pltpu.MemorySpace.SMEM
HBM = pltpu.MemorySpace.HBM

SMALL = pl.CostEstimate(flops=1, bytes_accessed=1, transcendentals=0)


def vmem(count):
    return [pl.BlockSpec(memory_space=VMEM)] * count


def params(mib):
    return pltpu.CompilerParams(vmem_limit_bytes=mib * 2**20)


def grid_of(shape, row_offset=0):
    rows = lax.broadcasted_iota(jnp.int32, shape, 0) + row_offset
    cols = lax.broadcasted_iota(jnp.int32, shape, 1)
    return rows, cols


def pack_kernel(green, screen, cross, tri):
    half = green.shape[-1] // 2
    rows, cols = grid_of((half, half))
    upper = rows < cols
    diagonal = rows == cols
    for place, source in enumerate((green, screen)):
        a_re = source[0, 0, 0, :half, :half].astype(jnp.float32)
        a_im = source[0, 1, 0, :half, :half].astype(jnp.float32)
        d_re = source[0, 0, 0, half:, half:].astype(jnp.float32)
        d_im = source[0, 1, 0, half:, half:].astype(jnp.float32)
        t_re = jnp.where(upper, a_re, jnp.where(diagonal, a_im, d_re)).astype(jnp.bfloat16)
        t_im = jnp.where(upper, a_im, d_im).astype(jnp.bfloat16)
        c_re = source[0, 0, 0, :half, half:]
        c_im = source[0, 1, 0, :half, half:]
        shape = cross.shape[:1] + cross.shape[3:]
        cross[:, place, 0] = c_re.reshape(shape)
        cross[:, place, 1] = c_im.reshape(shape)
        tri[:, place, 0] = t_re.reshape(shape)
        tri[:, place, 1] = t_im.reshape(shape)


def pack(green, screen, parts):
    half = green.shape[-1] // 2
    out = jax.ShapeDtypeStruct((parts, 2, 2, half // parts, half), jnp.bfloat16)
    return pl.pallas_call(
        pack_kernel,
        out_shape=(out, out),
        in_specs=vmem(2),
        out_specs=tuple(vmem(2)),
        compiler_params=params(24),
    )(green, screen)


def split_rows(packed, groups):
    _, fields, comps, half, width = packed.shape
    shaped = packed.reshape(fields, comps, groups, half // groups, width)
    return jnp.moveaxis(shaped, 2, 0)


def conv_kernel(has_diagonal, index, offset, pieces, out, green, screen, place):
    count, _, _, rows, width = pieces.shape

    def scatter(stored, carry):
        point = index[stored]
        place[point] = stored
        green[point] = pieces[stored, 0].astype(jnp.float32)
        screen[point] = pieces[stored, 1].astype(jnp.float32)
        return carry

    unroll = count <= 16
    lax.fori_loop(0, count, scatter, 0, unroll=unroll)
    scale = count**-0.5
    zero = jnp.zeros((rows, width), jnp.float32)

    def one(point, carry):
        total = point + count // 2

        def term(first, sums):
            both_re, both_im, mixed = sums
            g_re = green[first, 0]
            g_im = green[first, 1]
            w_re = screen[total - first, 0]
            w_im = screen[total - first, 1]
            return (
                both_re + g_re * w_re,
                both_im + g_im * w_im,
                mixed + g_re * w_im + g_im * w_re,
            )

        if unroll:
            sums = (zero, zero, zero)
            for first in range(max(0, total - count + 1), min(count - 1, total) + 1):
                sums = term(first, sums)
        else:
            low = jnp.maximum(0, total - count + 1)
            high = jnp.minimum(count - 1, total) + 1
            sums = lax.fori_loop(low, high, term, (zero, zero, zero))
        both_re, both_im, mixed = sums
        s_re = -scale * mixed
        s_im = scale * (both_re - both_im)
        if has_diagonal:
            at_rows, at_cols = grid_of((rows, width), offset[0])
            diagonal = at_rows == at_cols
            s_re = jnp.where(diagonal, -scale * both_re, s_re)
            s_im = jnp.where(diagonal, -scale * both_im, s_im)
        stored = place[point]
        out[stored, 0] = s_re.astype(jnp.bfloat16)
        out[stored, 1] = s_im.astype(jnp.bfloat16)
        return carry

    if unroll:
        for point in range(count):
            one(point, 0)
    else:
        lax.fori_loop(0, count, one, 0)


def convolve(pieces, energy_index, row_offset, has_diagonal):
    count, _, _, rows, width = pieces.shape
    smem = pl.BlockSpec(memory_space=SMEM)
    return pl.pallas_call(
        functools.partial(conv_kernel, has_diagonal),
        out_shape=jax.ShapeDtypeStruct((count, 2, rows, width), jnp.bfloat16),
        in_specs=[smem, smem] + vmem(1),
        out_specs=vmem(1)[0],
        scratch_shapes=[
            pltpu.VMEM((count, 2, rows, width), jnp.float32),
            pltpu.VMEM((count, 2, rows, width), jnp.float32),
            pltpu.SMEM((count,), jnp.int32),
        ],
        compiler_params=params(24),
    )(energy_index, row_offset, pieces)


def share_of(me, d, rows):
    return pl.ds(pl.multiple_of((lax.shift_right_logical(me, 1) ^ d) * rows, rows), rows)


def cut_cross_kernel(chips, me, green, screen, *rest):
    outs, sems = rest[:chips], rest[chips]
    half = green.shape[-1] // 2
    rows = half // chips
    copies = []
    for d in range(chips):
        for field, source in enumerate((green, screen)):
            part = source.at[0, :, 0, share_of(me[0], d, rows), half:]
            copies.append(pltpu.make_async_copy(part, outs[d].at[field], sems.at[d, field]))
            copies[-1].start()
    for copy in copies:
        copy.wait()


def cut_tri_kernel(chips, me, green, screen, *rest):
    outs = rest[:chips]
    near, far, sems = rest[chips:]
    half = near.shape[-1]
    rows = half // chips
    copies = []
    for field, source in enumerate((green, screen)):
        for place, (held, lines) in enumerate(((near, slice(0, half)), (far, slice(half, None)))):
            copy = pltpu.make_async_copy(
                source.at[0, :, 0, lines, lines], held.at[field], sems.at[field, place]
            )
            copy.start()
            copies.append(copy)
    for copy in copies:
        copy.wait()
    at_rows, at_cols = grid_of((rows, half))
    for d in range(chips):
        lines = share_of(me[0], d, rows)
        here = at_rows + (lax.shift_right_logical(me[0], 1) ^ d) * rows
        upper = here < at_cols
        diagonal = here == at_cols
        for field in range(2):
            a_re = near[field, 0, lines, :].astype(jnp.float32)
            a_im = near[field, 1, lines, :].astype(jnp.float32)
            d_re = far[field, 0, lines, :].astype(jnp.float32)
            d_im = far[field, 1, lines, :].astype(jnp.float32)
            t_re = jnp.where(upper, a_re, jnp.where(diagonal, a_im, d_re))
            outs[d][field, 0] = t_re.astype(jnp.bfloat16)
            outs[d][field, 1] = jnp.where(upper, a_im, d_im).astype(jnp.bfloat16)


def cut(me, green, screen, chips, tri):
    half = green.shape[-1] // 2
    piece = jax.ShapeDtypeStruct((2, 2, half // chips, half), jnp.bfloat16)
    squares_held = [pltpu.VMEM((2, 2, half, half), jnp.bfloat16)] * 2
    scratch = squares_held + [pltpu.SemaphoreType.DMA((2, 2))] if tri else [pltpu.SemaphoreType.DMA((chips, 2))]
    return pl.pallas_call(
        functools.partial(cut_tri_kernel if tri else cut_cross_kernel, chips),
        out_shape=(piece,) * chips,
        in_specs=[pl.BlockSpec(memory_space=SMEM)] + [pl.BlockSpec(memory_space=HBM)] * 2,
        out_specs=tuple(vmem(chips)),
        scratch_shapes=scratch,
        compiler_params=params(56),
        cost_estimate=SMALL,
    )(me, green, screen)


def bind_kernel(*refs):
    for place, piece in enumerate(refs[:-1]):
        refs[-1][place] = piece[...]


def bind(pieces):
    shape = (len(pieces),) + pieces[0].shape
    return pl.pallas_call(
        bind_kernel,
        out_shape=jax.ShapeDtypeStruct(shape, jnp.bfloat16),
        in_specs=vmem(len(pieces)),
        out_specs=vmem(1)[0],
        compiler_params=params(32),
        cost_estimate=SMALL,
    )(*pieces)


def conv_pieces_kernel(chips, has_diagonal, me, index, *rest):
    same = rest[:chips]
    beside, other = rest[chips : chips + 2]
    outs = rest[chips + 2 : 2 * chips + 2]
    green, screen, sums, place = rest[2 * chips + 2 :]
    groups = 2 * chips
    rows, width = sums.shape[2:]
    for core in range(2):
        for d in range(chips):
            stored = me[0] ^ (2 * d + core)
            point = index[stored]
            place[point] = stored
            if core == 0:
                green[point] = same[d][0]
                screen[point] = same[d][1]
            elif d == 0:
                green[point] = beside[0]
                screen[point] = beside[1]
            else:
                green[point] = other[d - 1, 0]
                screen[point] = other[d - 1, 1]
    scale = groups**-0.5
    tall = 16
    for point in range(groups):

        @pl.when(((place[point] ^ me[0]) & 1) == 0)
        def _():
            total = point + groups // 2
            for first_row in range(0, rows, tall):
                for first_col in range(0, width, 128):
                    at = (slice(first_row, first_row + tall), slice(first_col, first_col + 128))
                    both_re = both_im = mixed = None
                    for p in range(max(0, total - groups + 1), min(groups - 1, total) + 1):
                        g_re = green[(p, 0) + at].astype(jnp.float32)
                        g_im = green[(p, 1) + at].astype(jnp.float32)
                        w_re = screen[(total - p, 0) + at].astype(jnp.float32)
                        w_im = screen[(total - p, 1) + at].astype(jnp.float32)
                        re = g_re * w_re
                        im = g_im * w_im
                        mix = g_re * w_im + g_im * w_re
                        both_re = re if both_re is None else both_re + re
                        both_im = im if both_im is None else both_im + im
                        mixed = mix if mixed is None else mixed + mix
                    s_re = -scale * mixed
                    s_im = scale * (both_re - both_im)
                    if has_diagonal:
                        first = lax.shift_right_logical(me[0], 1) * rows + first_row
                        at_rows, at_cols = grid_of((tall, 128), first)
                        diagonal = at_rows == at_cols + first_col
                        s_re = jnp.where(diagonal, -scale * both_re, s_re)
                        s_im = jnp.where(diagonal, -scale * both_im, s_im)
                    sums[(point, 0) + at] = s_re.astype(jnp.bfloat16)
                    sums[(point, 1) + at] = s_im.astype(jnp.bfloat16)

    for d in range(chips):
        outs[d][...] = sums[index[me[0] ^ (2 * d)]]


def conv_pieces(me, energy_index, same, beside, other, has_diagonal):
    chips = len(same)
    shape = same[0].shape[1:]
    smem = pl.BlockSpec(memory_space=SMEM)
    return pl.pallas_call(
        functools.partial(conv_pieces_kernel, chips, has_diagonal),
        out_shape=(jax.ShapeDtypeStruct(shape, jnp.bfloat16),) * chips,
        in_specs=[smem, smem] + vmem(chips + 2),
        out_specs=tuple(vmem(chips)),
        scratch_shapes=[pltpu.VMEM((2 * chips,) + shape, jnp.bfloat16)] * 3
        + [pltpu.SMEM((2 * chips,), jnp.int32)],
        compiler_params=params(32),
        cost_estimate=SMALL,
    )(me, energy_index, *same, beside, other)


def join_kernel(chips, me, *rest):
    pieces, out = rest[:chips], rest[chips]
    rows = pieces[0].shape[1]
    for d in range(chips):
        out[:, share_of(me[0], d, rows), :] = pieces[d][...]


def join(me, pieces):
    half = pieces[0].shape[-1]
    return pl.pallas_call(
        functools.partial(join_kernel, len(pieces)),
        out_shape=jax.ShapeDtypeStruct((2, half, half), jnp.bfloat16),
        in_specs=[pl.BlockSpec(memory_space=SMEM)] + vmem(len(pieces)),
        out_specs=vmem(1)[0],
        compiler_params=params(32),
        cost_estimate=SMALL,
    )(me, *pieces)


def swap(piece, d, groups):
    return lax.ppermute(piece, "energy", [(i, i ^ d) for i in range(groups)]) if d else piece


def after(value, *earlier):
    return lax.optimization_barrier((value, earlier))[0]


def gather_paired(g_lesser, w_lesser, energy_index, groups, send=lambda part: ()):
    me = lax.axis_index("energy").astype(jnp.int32).reshape(1)
    chips = groups // 2

    def over(pieces):
        return [swap(pieces[d], 2 * d, groups) for d in range(chips)]

    cross, tri = (cut(me, g_lesser, w_lesser, chips, which) for which in (False, True))
    same = over(cross)
    other = swap(bind(after(same[1:], tri[0])), 1, groups)
    mine = conv_pieces(me, energy_index, same, swap(cross[0], 1, groups), other, False)
    shares = over(mine)
    own_cross = join(me, shares)
    sent = send(own_cross)
    tri = after(tri, shares[1])
    same = over(tri)
    other = swap(bind(after(same[1:], own_cross)), 1, groups)
    mine = conv_pieces(me, energy_index, same, swap(tri[0], 1, groups), other, True)
    own_tri = join(me, after(over(mine), sent))
    return own_cross, own_tri


def gather_shared(g_lesser, w_lesser, energy_index, groups):
    half = g_lesser.shape[-1] // 2
    rows = half // groups
    cross, tri = (split_rows(packed, groups) for packed in pack(g_lesser, w_lesser, 1))
    offset = (lax.axis_index("energy") * rows).astype(jnp.int32).reshape(1)
    own = []
    for pieces, has_diagonal in ((cross, False), (tri, True)):
        shares = convolve(exchange(pieces), energy_index, offset, has_diagonal)
        own.append(jnp.moveaxis(exchange(shares), 0, 1).reshape(2, half, half))
    return own


def squares(cross, tri):
    return cross[0], cross[1], tri[0], tri[1]


def dot(a, b):
    return jnp.dot(a, b, preferred_element_type=jnp.float32)


def dot_t(a, b):
    return lax.dot_general(a, b, (((1,), (1,)), ((), ())), preferred_element_type=jnp.float32)


def product(cross, tri, retarded):
    c_re, c_im, t_re, t_im = squares(cross, tri)
    half = c_re.shape[0]
    rows, cols = grid_of((half, half))
    tr = t_re.astype(jnp.float32)
    ti = t_im.astype(jnp.float32)
    diagonal = rows == cols
    a_re = jnp.where(rows < cols, tr, 0.0).astype(jnp.bfloat16)
    a_im = jnp.where(rows < cols, ti, jnp.where(diagonal, 0.5 * tr, 0.0)).astype(jnp.bfloat16)
    d_re = jnp.where(rows > cols, tr, 0.0).astype(jnp.bfloat16)
    d_im = jnp.where(rows > cols, ti, jnp.where(diagonal, 0.5 * ti, 0.0)).astype(jnp.bfloat16)
    g_re = retarded[0]
    g_im = retarded[1]
    near = jnp.concatenate([g_re[:, :half], g_im[:, :half]], axis=1)
    far = jnp.concatenate([g_re, g_im], axis=1)
    l_re = jnp.concatenate(
        [
            dot(near, jnp.concatenate([a_re, -a_im], axis=0)),
            dot(far, jnp.concatenate([c_re, d_re, -c_im, -d_im], axis=0)),
        ],
        axis=1,
    ).astype(jnp.bfloat16)
    l_im = jnp.concatenate(
        [
            dot(near, jnp.concatenate([a_im, a_re], axis=0)),
            dot(far, jnp.concatenate([c_im, d_im, c_re, d_re], axis=0)),
        ],
        axis=1,
    ).astype(jnp.bfloat16)
    x_re = dot_t(jnp.concatenate([l_re, l_im], axis=1), far)
    x_im = dot_t(jnp.concatenate([l_im, -l_re], axis=1), far)
    return x_re, x_im


def own_kernel(where, cross, tri, retarded, sigma, total, block, sem):
    copy = pltpu.make_async_copy(retarded.at[0, :, 0, where[0]], block, sem)
    copy.start()
    c_re, c_im, t_re, t_im = squares(cross, tri)
    half = c_re.shape[0]
    rows, cols = grid_of((half, half))
    upper = rows < cols
    diagonal = rows == cols
    tr = t_re.astype(jnp.float32)
    ti = t_im.astype(jnp.float32)
    trt = tr.T
    tit = ti.T
    zero = jnp.zeros_like(tr)
    bf = jnp.bfloat16
    sigma[0, 0, 0, :half, half:] = c_re
    sigma[0, 1, 0, :half, half:] = c_im
    sigma[0, 0, 0, half:, :half] = (-(c_re.astype(jnp.float32).T)).astype(bf)
    sigma[0, 1, 0, half:, :half] = c_im.astype(jnp.float32).T.astype(bf)
    sigma[0, 0, 0, :half, :half] = jnp.where(upper, tr, jnp.where(diagonal, zero, -trt)).astype(bf)
    sigma[0, 1, 0, :half, :half] = jnp.where(upper, ti, jnp.where(diagonal, tr, tit)).astype(bf)
    sigma[0, 0, 0, half:, half:] = jnp.where(upper, -trt, jnp.where(diagonal, zero, tr)).astype(bf)
    sigma[0, 1, 0, half:, half:] = jnp.where(upper, tit, ti).astype(bf)
    copy.wait()
    total[0], total[1] = product(cross, tri, block)


def step_kernel(count, last, ahead, where, *rest):
    if last:
        block, total = rest[:2]
        sources = rest[2 : 2 + 2 * count]
        out = rest[-1]
    else:
        sources = rest[: 2 * count]
        rest = rest[2 * count :]
    if last:
        pass
    elif ahead:
        retarded, total, out, later, block, sems = rest
        fetch = pltpu.make_async_copy(retarded.at[0, :, 0, where[0]], block, sems.at[0])
        fetch.start()
        prefetch = pltpu.make_async_copy(retarded.at[0, :, 0, where[2]], later, sems.at[1])
        prefetch.start()
        fetch.wait()
    else:
        retarded, total, out, block, sems = rest
        fetch = pltpu.make_async_copy(retarded.at[0, :, 0, where[0]], block, sems.at[0])
        fetch.start()
        fetch.wait()
    for pick in range(count):

        @pl.when(where[1] == pick)
        def _():
            cross, tri = sources[pick], sources[count + pick]
            x_re, x_im = product(cross, tri, block)
            x_re += total[0]
            x_im += total[1]
            if last:
                out[0, 0, 0] = (x_re - x_re.T).astype(jnp.bfloat16)
                out[0, 1, 0] = (x_im + x_im.T).astype(jnp.bfloat16)
            else:
                out[0] = x_re
                out[1] = x_im

    if ahead:
        prefetch.wait()


def cost(width):
    return pl.CostEstimate(flops=14 * width**3, bytes_accessed=8 * width**2, transcendentals=0)


def own_product(block, own, retarded):
    width = retarded.shape[-1]
    return pl.pallas_call(
        own_kernel,
        out_shape=(
            jax.ShapeDtypeStruct((1, 2, 1, width, width), jnp.bfloat16),
            jax.ShapeDtypeStruct((2, width, width), jnp.float32),
        ),
        in_specs=[pl.BlockSpec(memory_space=SMEM)] + vmem(2) + [pl.BlockSpec(memory_space=HBM)],
        out_specs=tuple(vmem(2)),
        scratch_shapes=[pltpu.VMEM((2, width, width), jnp.bfloat16), pltpu.SemaphoreType.DMA],
        compiler_params=params(48),
        cost_estimate=cost(width),
    )(block.reshape(1), *own, retarded)


def step_product(block, pick, sources, retarded, total, later=None):
    width = retarded.shape[-1]
    flat = [source[part] for part in range(2) for source in sources]
    ahead = later is not None
    numbers = jnp.stack([block, pick] + ([later] if ahead else []))
    total_shape = jax.ShapeDtypeStruct((2, width, width), jnp.float32)
    block_shape = jax.ShapeDtypeStruct((2, width, width), jnp.bfloat16)
    return pl.pallas_call(
        functools.partial(step_kernel, len(sources), False, ahead),
        out_shape=(total_shape, block_shape) if ahead else total_shape,
        in_specs=[pl.BlockSpec(memory_space=SMEM)]
        + vmem(len(flat))
        + [pl.BlockSpec(memory_space=HBM)]
        + vmem(1),
        out_specs=tuple(vmem(2)) if ahead else vmem(1)[0],
        scratch_shapes=[pltpu.VMEM((2, width, width), jnp.bfloat16), pltpu.SemaphoreType.DMA((2,))],
        compiler_params=params(46),
        cost_estimate=cost(width),
    )(numbers, *flat, retarded, total)


def last_product(pick, sources, block, total):
    width = block.shape[-1]
    flat = [source[part] for part in range(2) for source in sources]
    return pl.pallas_call(
        functools.partial(step_kernel, len(sources), True, False),
        out_shape=jax.ShapeDtypeStruct((1, 2, 1, width, width), jnp.bfloat16),
        in_specs=[pl.BlockSpec(memory_space=SMEM)] + vmem(len(flat) + 2),
        out_specs=vmem(1)[0],
        compiler_params=params(48),
        cost_estimate=cost(width),
    )(jnp.stack([pick, pick]), block, total, *flat)


def exchange(pieces):
    return lax.all_to_all(pieces, "energy", split_axis=0, concat_axis=0, tiled=True)


def shards(g_lesser, w_lesser, g_retarded, energy_index):
    width = g_lesser.shape[-1]
    groups = lax.axis_size("energy")
    chain = lax.axis_size("space")
    here = lax.axis_index("space")
    paired = groups >= 4 and groups & (groups - 1) == 0 and (width // groups) % 16 == 0
    here = here.astype(jnp.int32)
    if chain == 4:
        return around_line(here, paired, g_lesser, w_lesser, energy_index, groups, g_retarded)
    gather = gather_paired if paired else gather_shared
    own = gather(g_lesser, w_lesser, energy_index, groups)
    everyone = [lax.all_gather(part, "space") for part in own]
    sigma_lesser, total = own_product(here, own, g_retarded)
    zero = jnp.int32(0)

    def source(block):
        return tuple(lax.dynamic_index_in_dim(part, block, 0, False) for part in everyone)

    for step in range(1, chain - 1):
        block = (here + step) % chain
        later = (block + 1) % chain
        total, held = step_product(block, zero, [source(block)], g_retarded, total, later)
    return (sigma_lesser, last_product(zero, [source(later)], held, total))


def around_line(here, paired, g_lesser, w_lesser, energy_index, groups, retarded):
    def swap(part, bits):
        return lax.ppermute(part, "space", [(i, i ^ bits) for i in range(4)])

    first, second = [], []

    def send(part):
        second.append(swap(part, 3))
        first.append(swap(part, 1))
        return first[-1], second[-1]

    if paired:
        own = gather_paired(g_lesser, w_lesser, energy_index, groups, send)
        send(own[1])
    else:
        own = gather_shared(g_lesser, w_lesser, energy_index, groups)
        send(own[0]), send(own[1])
    third = [swap(part, 1) for part in second]
    zero = jnp.int32(0)
    sigma_lesser, total = own_product(here, own, retarded)
    total = step_product(here ^ 1, zero, [first], retarded, total)
    total, held = step_product(here ^ 3, zero, [second], retarded, total, here ^ 2)
    delta = last_product(zero, [third], held, total)
    return (sigma_lesser, delta)


def solution(mesh):
    return jax.shard_map(
        shards,
        mesh=mesh,
        in_specs=(
            P("energy", None, "space", None, None),
            P("energy", None, "space", None, None),
            P("energy", None, "space", None, None, None),
            P(),
        ),
        out_specs=(P("energy", None, "space", None, None), P("energy", None, "space", None, None)),
        check_vma=False,
    )
```

```python
import functools

import jax
import jax.numpy as jnp
from jax import lax
from jax.experimental import pallas as pl
from jax.experimental.pallas import tpu as pltpu
from jax.sharding import PartitionSpec as P


VMEM = pltpu.MemorySpace.VMEM
SMEM = pltpu.MemorySpace.SMEM
HBM = pltpu.MemorySpace.HBM

SMALL = pl.CostEstimate(flops=1, bytes_accessed=1, transcendentals=0)


def vmem(count):
    return [pl.BlockSpec(memory_space=VMEM)] * count


def params(mib):
    return pltpu.CompilerParams(vmem_limit_bytes=mib * 2**20)


def grid_of(shape, row_offset=0):
    rows = lax.broadcasted_iota(jnp.int32, shape, 0) + row_offset
    cols = lax.broadcasted_iota(jnp.int32, shape, 1)
    return rows, cols


def pack_kernel(green, screen, cross, tri):
    half = green.shape[-1] // 2
    rows, cols = grid_of((half, half))
    upper = rows < cols
    diagonal = rows == cols
    for place, source in enumerate((green, screen)):
        a_re = source[0, 0, 0, :half, :half].astype(jnp.float32)
        a_im = source[0, 1, 0, :half, :half].astype(jnp.float32)
        d_re = source[0, 0, 0, half:, half:].astype(jnp.float32)
        d_im = source[0, 1, 0, half:, half:].astype(jnp.float32)
        t_re = jnp.where(upper, a_re, jnp.where(diagonal, a_im, d_re)).astype(jnp.bfloat16)
        t_im = jnp.where(upper, a_im, d_im).astype(jnp.bfloat16)
        c_re = source[0, 0, 0, :half, half:]
        c_im = source[0, 1, 0, :half, half:]
        shape = cross.shape[:1] + cross.shape[3:]
        cross[:, place, 0] = c_re.reshape(shape)
        cross[:, place, 1] = c_im.reshape(shape)
        tri[:, place, 0] = t_re.reshape(shape)
        tri[:, place, 1] = t_im.reshape(shape)


def pack(green, screen, parts):
    half = green.shape[-1] // 2
    out = jax.ShapeDtypeStruct((parts, 2, 2, half // parts, half), jnp.bfloat16)
    return pl.pallas_call(
        pack_kernel,
        out_shape=(out, out),
        in_specs=vmem(2),
        out_specs=tuple(vmem(2)),
        compiler_params=params(24),
    )(green, screen)


def split_rows(packed, groups):
    _, fields, comps, half, width = packed.shape
    shaped = packed.reshape(fields, comps, groups, half // groups, width)
    return jnp.moveaxis(shaped, 2, 0)


def conv_kernel(has_diagonal, index, offset, pieces, out, green, screen, place):
    count, _, _, rows, width = pieces.shape

    def scatter(stored, carry):
        point = index[stored]
        place[point] = stored
        green[point] = pieces[stored, 0].astype(jnp.float32)
        screen[point] = pieces[stored, 1].astype(jnp.float32)
        return carry

    unroll = count <= 16
    lax.fori_loop(0, count, scatter, 0, unroll=unroll)
    scale = count**-0.5
    zero = jnp.zeros((rows, width), jnp.float32)

    def one(point, carry):
        total = point + count // 2

        def term(first, sums):
            both_re, both_im, mixed = sums
            g_re = green[first, 0]
            g_im = green[first, 1]
            w_re = screen[total - first, 0]
            w_im = screen[total - first, 1]
            return (
                both_re + g_re * w_re,
                both_im + g_im * w_im,
                mixed + g_re * w_im + g_im * w_re,
            )

        if unroll:
            sums = (zero, zero, zero)
            for first in range(max(0, total - count + 1), min(count - 1, total) + 1):
                sums = term(first, sums)
        else:
            low = jnp.maximum(0, total - count + 1)
            high = jnp.minimum(count - 1, total) + 1
            sums = lax.fori_loop(low, high, term, (zero, zero, zero))
        both_re, both_im, mixed = sums
        s_re = -scale * mixed
        s_im = scale * (both_re - both_im)
        if has_diagonal:
            at_rows, at_cols = grid_of((rows, width), offset[0])
            diagonal = at_rows == at_cols
            s_re = jnp.where(diagonal, -scale * both_re, s_re)
            s_im = jnp.where(diagonal, -scale * both_im, s_im)
        stored = place[point]
        out[stored, 0] = s_re.astype(jnp.bfloat16)
        out[stored, 1] = s_im.astype(jnp.bfloat16)
        return carry

    if unroll:
        for point in range(count):
            one(point, 0)
    else:
        lax.fori_loop(0, count, one, 0)


def convolve(pieces, energy_index, row_offset, has_diagonal):
    count, _, _, rows, width = pieces.shape
    smem = pl.BlockSpec(memory_space=SMEM)
    return pl.pallas_call(
        functools.partial(conv_kernel, has_diagonal),
        out_shape=jax.ShapeDtypeStruct((count, 2, rows, width), jnp.bfloat16),
        in_specs=[smem, smem] + vmem(1),
        out_specs=vmem(1)[0],
        scratch_shapes=[
            pltpu.VMEM((count, 2, rows, width), jnp.float32),
            pltpu.VMEM((count, 2, rows, width), jnp.float32),
            pltpu.SMEM((count,), jnp.int32),
        ],
        compiler_params=params(24),
    )(energy_index, row_offset, pieces)


def share_of(me, d, rows):
    return pl.ds(pl.multiple_of((lax.shift_right_logical(me, 1) ^ d) * rows, rows), rows)


def cut_kernel(chips, me, green, screen, *rest):
    outs = rest[:chips]
    near, far, sems, cross_sems = rest[chips:]
    half = near.shape[-1]
    rows = half // chips
    copies = []
    for field, source in enumerate((green, screen)):
        for place, (held, lines) in enumerate(((near, slice(0, half)), (far, slice(half, None)))):
            copy = pltpu.make_async_copy(
                source.at[0, :, 0, lines, lines], held.at[field], sems.at[field, place]
            )
            copy.start()
            copies.append(copy)
    cross_copies = []
    for d in range(chips):
        for field, source in enumerate((green, screen)):
            part = source.at[0, :, 0, share_of(me[0], d, rows), half:]
            copy = pltpu.make_async_copy(part, outs[d].at[0, field], cross_sems.at[d, field])
            copy.start()
            cross_copies.append(copy)
    at_rows, at_cols = grid_of((rows, half))
    for field in range(2):
        for copy in copies[2 * field : 2 * field + 2]:
            copy.wait()
        for d in range(chips):
            lines = share_of(me[0], d, rows)
            here = at_rows + (lax.shift_right_logical(me[0], 1) ^ d) * rows
            upper = here < at_cols
            diagonal = here == at_cols
            a_re = near[field, 0, lines, :].astype(jnp.float32)
            a_im = near[field, 1, lines, :].astype(jnp.float32)
            d_re = far[field, 0, lines, :].astype(jnp.float32)
            d_im = far[field, 1, lines, :].astype(jnp.float32)
            t_re = jnp.where(upper, a_re, jnp.where(diagonal, a_im, d_re))
            outs[d][1, field, 0] = t_re.astype(jnp.bfloat16)
            outs[d][1, field, 1] = jnp.where(upper, a_im, d_im).astype(jnp.bfloat16)
    for copy in cross_copies:
        copy.wait()


def cut(me, green, screen, chips):
    half = green.shape[-1] // 2
    piece = jax.ShapeDtypeStruct((2, 2, 2, half // chips, half), jnp.bfloat16)
    return pl.pallas_call(
        functools.partial(cut_kernel, chips),
        out_shape=(piece,) * chips,
        in_specs=[pl.BlockSpec(memory_space=SMEM)] + [pl.BlockSpec(memory_space=HBM)] * 2,
        out_specs=tuple(vmem(chips)),
        scratch_shapes=[pltpu.VMEM((2, 2, half, half), jnp.bfloat16)] * 2
        + [pltpu.SemaphoreType.DMA((2, 2)), pltpu.SemaphoreType.DMA((chips, 2))],
        compiler_params=params(52),
        cost_estimate=SMALL,
    )(me, green, screen)


def bind_kernel(part, *refs):
    for place, piece in enumerate(refs[:-1]):
        refs[-1][place] = piece[part]


def bind(pieces, part):
    shape = (len(pieces),) + pieces[0].shape[1:]
    return pl.pallas_call(
        functools.partial(bind_kernel, part),
        out_shape=jax.ShapeDtypeStruct(shape, jnp.bfloat16),
        in_specs=vmem(len(pieces)),
        out_specs=vmem(1)[0],
        compiler_params=params(32),
        cost_estimate=SMALL,
    )(*pieces)


def conv_pieces_kernel(chips, part, me, index, *rest):
    same = rest[:chips]
    beside, other = rest[chips : chips + 2]
    outs = rest[chips + 2 : 2 * chips + 2]
    green, screen, sums, place = rest[2 * chips + 2 :]
    groups = 2 * chips
    rows, width = sums.shape[2:]
    for core in range(2):
        for d in range(chips):
            stored = me[0] ^ (2 * d + core)
            point = index[stored]
            place[point] = stored
            if core == 0:
                green[point] = same[d][part, 0]
                screen[point] = same[d][part, 1]
            elif d == 0:
                green[point] = beside[part, 0]
                screen[point] = beside[part, 1]
            else:
                green[point] = other[d - 1, 0]
                screen[point] = other[d - 1, 1]
    scale = groups**-0.5
    tall = 16
    for point in range(groups):

        @pl.when(((place[point] ^ me[0]) & 1) == 0)
        def _():
            total = point + groups // 2
            for first_row in range(0, rows, tall):
                for first_col in range(0, width, 128):
                    at = (slice(first_row, first_row + tall), slice(first_col, first_col + 128))
                    both_re = both_im = mixed = None
                    for p in range(max(0, total - groups + 1), min(groups - 1, total) + 1):
                        g_re = green[(p, 0) + at].astype(jnp.float32)
                        g_im = green[(p, 1) + at].astype(jnp.float32)
                        w_re = screen[(total - p, 0) + at].astype(jnp.float32)
                        w_im = screen[(total - p, 1) + at].astype(jnp.float32)
                        re = g_re * w_re
                        im = g_im * w_im
                        mix = g_re * w_im + g_im * w_re
                        both_re = re if both_re is None else both_re + re
                        both_im = im if both_im is None else both_im + im
                        mixed = mix if mixed is None else mixed + mix
                    s_re = -scale * mixed
                    s_im = scale * (both_re - both_im)
                    if part == 1:
                        first = lax.shift_right_logical(me[0], 1) * rows + first_row
                        at_rows, at_cols = grid_of((tall, 128), first)
                        diagonal = at_rows == at_cols + first_col
                        s_re = jnp.where(diagonal, -scale * both_re, s_re)
                        s_im = jnp.where(diagonal, -scale * both_im, s_im)
                    sums[(point, 0) + at] = s_re.astype(jnp.bfloat16)
                    sums[(point, 1) + at] = s_im.astype(jnp.bfloat16)

    for d in range(chips):
        outs[d][...] = sums[index[me[0] ^ (2 * d)]]


def conv_pieces(me, energy_index, same, beside, other, part):
    chips = len(same)
    shape = same[0].shape[2:]
    smem = pl.BlockSpec(memory_space=SMEM)
    return pl.pallas_call(
        functools.partial(conv_pieces_kernel, chips, part),
        out_shape=(jax.ShapeDtypeStruct(shape, jnp.bfloat16),) * chips,
        in_specs=[smem, smem] + vmem(chips + 2),
        out_specs=tuple(vmem(chips)),
        scratch_shapes=[pltpu.VMEM((2 * chips,) + shape, jnp.bfloat16)] * 3
        + [pltpu.SMEM((2 * chips,), jnp.int32)],
        compiler_params=params(32),
        cost_estimate=SMALL,
    )(me, energy_index, *same, beside, other)


def join_kernel(chips, me, *rest):
    pieces, out = rest[:chips], rest[chips]
    rows = pieces[0].shape[1]
    for d in range(chips):
        out[:, share_of(me[0], d, rows), :] = pieces[d][...]


def join(me, pieces):
    half = pieces[0].shape[-1]
    return pl.pallas_call(
        functools.partial(join_kernel, len(pieces)),
        out_shape=jax.ShapeDtypeStruct((2, half, half), jnp.bfloat16),
        in_specs=[pl.BlockSpec(memory_space=SMEM)] + vmem(len(pieces)),
        out_specs=vmem(1)[0],
        compiler_params=params(32),
        cost_estimate=SMALL,
    )(me, *pieces)


def swap(piece, d, groups):
    return lax.ppermute(piece, "energy", [(i, i ^ d) for i in range(groups)]) if d else piece


def after(value, *earlier):
    return lax.optimization_barrier((value, earlier))[0]


def gather_paired(g_lesser, w_lesser, energy_index, groups, send=lambda part: ()):
    me = lax.axis_index("energy").astype(jnp.int32).reshape(1)
    chips = groups // 2

    def over(pieces):
        return [swap(pieces[d], 2 * d, groups) for d in range(chips)]

    pieces = cut(me, g_lesser, w_lesser, chips)
    same = over(pieces)
    beside = swap(pieces[0], 1, groups)
    bound = [bind(after(same[1:], beside), part) for part in range(2)]
    other = [swap(piece, 1, groups) for piece in bound]
    mine = conv_pieces(me, energy_index, same, beside, other[0], 0)
    shares = over(mine)
    own_cross = join(me, shares)
    sent = send(own_cross)
    mine = conv_pieces(me, energy_index, same, beside, after(other[1], own_cross), 1)
    own_tri = join(me, after(over(mine), sent[1:]))
    return own_cross, own_tri


def gather_shared(g_lesser, w_lesser, energy_index, groups):
    half = g_lesser.shape[-1] // 2
    rows = half // groups
    cross, tri = (split_rows(packed, groups) for packed in pack(g_lesser, w_lesser, 1))
    offset = (lax.axis_index("energy") * rows).astype(jnp.int32).reshape(1)
    own = []
    for pieces, has_diagonal in ((cross, False), (tri, True)):
        shares = convolve(exchange(pieces), energy_index, offset, has_diagonal)
        own.append(jnp.moveaxis(exchange(shares), 0, 1).reshape(2, half, half))
    return own


def squares(cross, tri):
    return cross[0], cross[1], tri[0], tri[1]


def dot(a, b):
    return jnp.dot(a, b, preferred_element_type=jnp.float32)


def dot_t(a, b):
    return lax.dot_general(a, b, (((1,), (1,)), ((), ())), preferred_element_type=jnp.float32)


def product(cross, tri, retarded):
    c_re, c_im, t_re, t_im = squares(cross, tri)
    half = c_re.shape[0]
    rows, cols = grid_of((half, half))
    tr = t_re.astype(jnp.float32)
    ti = t_im.astype(jnp.float32)
    diagonal = rows == cols
    a_re = jnp.where(rows < cols, tr, 0.0).astype(jnp.bfloat16)
    a_im = jnp.where(rows < cols, ti, jnp.where(diagonal, 0.5 * tr, 0.0)).astype(jnp.bfloat16)
    d_re = jnp.where(rows > cols, tr, 0.0).astype(jnp.bfloat16)
    d_im = jnp.where(rows > cols, ti, jnp.where(diagonal, 0.5 * ti, 0.0)).astype(jnp.bfloat16)
    g_re = retarded[0]
    g_im = retarded[1]
    near = jnp.concatenate([g_re[:, :half], g_im[:, :half]], axis=1)
    far = jnp.concatenate([g_re, g_im], axis=1)
    l_re = jnp.concatenate(
        [
            dot(near, jnp.concatenate([a_re, -a_im], axis=0)),
            dot(far, jnp.concatenate([c_re, d_re, -c_im, -d_im], axis=0)),
        ],
        axis=1,
    ).astype(jnp.bfloat16)
    l_im = jnp.concatenate(
        [
            dot(near, jnp.concatenate([a_im, a_re], axis=0)),
            dot(far, jnp.concatenate([c_im, d_im, c_re, d_re], axis=0)),
        ],
        axis=1,
    ).astype(jnp.bfloat16)
    x_re = dot_t(jnp.concatenate([l_re, l_im], axis=1), far)
    x_im = dot_t(jnp.concatenate([l_im, -l_re], axis=1), far)
    return x_re, x_im


def own_kernel(where, cross, tri, retarded, sigma, total, block, sem):
    copy = pltpu.make_async_copy(retarded.at[0, :, 0, where[0]], block, sem)
    copy.start()
    c_re, c_im, t_re, t_im = squares(cross, tri)
    half = c_re.shape[0]
    rows, cols = grid_of((half, half))
    upper = rows < cols
    diagonal = rows == cols
    tr = t_re.astype(jnp.float32)
    ti = t_im.astype(jnp.float32)
    trt = tr.T
    tit = ti.T
    zero = jnp.zeros_like(tr)
    bf = jnp.bfloat16
    sigma[0, 0, 0, :half, half:] = c_re
    sigma[0, 1, 0, :half, half:] = c_im
    sigma[0, 0, 0, half:, :half] = (-(c_re.astype(jnp.float32).T)).astype(bf)
    sigma[0, 1, 0, half:, :half] = c_im.astype(jnp.float32).T.astype(bf)
    sigma[0, 0, 0, :half, :half] = jnp.where(upper, tr, jnp.where(diagonal, zero, -trt)).astype(bf)
    sigma[0, 1, 0, :half, :half] = jnp.where(upper, ti, jnp.where(diagonal, tr, tit)).astype(bf)
    sigma[0, 0, 0, half:, half:] = jnp.where(upper, -trt, jnp.where(diagonal, zero, tr)).astype(bf)
    sigma[0, 1, 0, half:, half:] = jnp.where(upper, tit, ti).astype(bf)
    copy.wait()
    total[0], total[1] = product(cross, tri, block)


def step_kernel(count, last, ahead, where, *rest):
    if last:
        block, total = rest[:2]
        sources = rest[2 : 2 + 2 * count]
        out = rest[-1]
    else:
        sources = rest[: 2 * count]
        rest = rest[2 * count :]
    if last:
        pass
    elif ahead:
        retarded, total, out, later, block, sems = rest
        fetch = pltpu.make_async_copy(retarded.at[0, :, 0, where[0]], block, sems.at[0])
        fetch.start()
        prefetch = pltpu.make_async_copy(retarded.at[0, :, 0, where[2]], later, sems.at[1])
        prefetch.start()
        fetch.wait()
    else:
        retarded, total, out, block, sems = rest
        fetch = pltpu.make_async_copy(retarded.at[0, :, 0, where[0]], block, sems.at[0])
        fetch.start()
        fetch.wait()
    for pick in range(count):

        @pl.when(where[1] == pick)
        def _():
            cross, tri = sources[pick], sources[count + pick]
            x_re, x_im = product(cross, tri, block)
            x_re += total[0]
            x_im += total[1]
            if last:
                out[0, 0, 0] = (x_re - x_re.T).astype(jnp.bfloat16)
                out[0, 1, 0] = (x_im + x_im.T).astype(jnp.bfloat16)
            else:
                out[0] = x_re
                out[1] = x_im

    if ahead:
        prefetch.wait()


def cost(width):
    return pl.CostEstimate(flops=14 * width**3, bytes_accessed=8 * width**2, transcendentals=0)


def own_product(block, own, retarded):
    width = retarded.shape[-1]
    return pl.pallas_call(
        own_kernel,
        out_shape=(
            jax.ShapeDtypeStruct((1, 2, 1, width, width), jnp.bfloat16),
            jax.ShapeDtypeStruct((2, width, width), jnp.float32),
        ),
        in_specs=[pl.BlockSpec(memory_space=SMEM)] + vmem(2) + [pl.BlockSpec(memory_space=HBM)],
        out_specs=tuple(vmem(2)),
        scratch_shapes=[pltpu.VMEM((2, width, width), jnp.bfloat16), pltpu.SemaphoreType.DMA],
        compiler_params=params(48),
        cost_estimate=cost(width),
    )(block.reshape(1), *own, retarded)


def step_product(block, pick, sources, retarded, total, later=None):
    width = retarded.shape[-1]
    flat = [source[part] for part in range(2) for source in sources]
    ahead = later is not None
    numbers = jnp.stack([block, pick] + ([later] if ahead else []))
    total_shape = jax.ShapeDtypeStruct((2, width, width), jnp.float32)
    block_shape = jax.ShapeDtypeStruct((2, width, width), jnp.bfloat16)
    return pl.pallas_call(
        functools.partial(step_kernel, len(sources), False, ahead),
        out_shape=(total_shape, block_shape) if ahead else total_shape,
        in_specs=[pl.BlockSpec(memory_space=SMEM)]
        + vmem(len(flat))
        + [pl.BlockSpec(memory_space=HBM)]
        + vmem(1),
        out_specs=tuple(vmem(2)) if ahead else vmem(1)[0],
        scratch_shapes=[pltpu.VMEM((2, width, width), jnp.bfloat16), pltpu.SemaphoreType.DMA((2,))],
        compiler_params=params(46),
        cost_estimate=cost(width),
    )(numbers, *flat, retarded, total)


def last_product(pick, sources, block, total):
    width = block.shape[-1]
    flat = [source[part] for part in range(2) for source in sources]
    return pl.pallas_call(
        functools.partial(step_kernel, len(sources), True, False),
        out_shape=jax.ShapeDtypeStruct((1, 2, 1, width, width), jnp.bfloat16),
        in_specs=[pl.BlockSpec(memory_space=SMEM)] + vmem(len(flat) + 2),
        out_specs=vmem(1)[0],
        compiler_params=params(48),
        cost_estimate=cost(width),
    )(jnp.stack([pick, pick]), block, total, *flat)


def exchange(pieces):
    return lax.all_to_all(pieces, "energy", split_axis=0, concat_axis=0, tiled=True)


def shards(g_lesser, w_lesser, g_retarded, energy_index):
    width = g_lesser.shape[-1]
    groups = lax.axis_size("energy")
    chain = lax.axis_size("space")
    here = lax.axis_index("space")
    paired = groups >= 4 and groups & (groups - 1) == 0 and (width // groups) % 16 == 0
    here = here.astype(jnp.int32)
    if chain == 4:
        return around_line(here, paired, g_lesser, w_lesser, energy_index, groups, g_retarded)
    gather = gather_paired if paired else gather_shared
    own = gather(g_lesser, w_lesser, energy_index, groups)
    everyone = [lax.all_gather(part, "space") for part in own]
    sigma_lesser, total = own_product(here, own, g_retarded)
    zero = jnp.int32(0)

    def source(block):
        return tuple(lax.dynamic_index_in_dim(part, block, 0, False) for part in everyone)

    for step in range(1, chain - 1):
        block = (here + step) % chain
        later = (block + 1) % chain
        total, held = step_product(block, zero, [source(block)], g_retarded, total, later)
    return (sigma_lesser, last_product(zero, [source(later)], held, total))


def around_line(here, paired, g_lesser, w_lesser, energy_index, groups, retarded):
    def swap(part, bits):
        return lax.ppermute(part, "space", [(i, i ^ bits) for i in range(4)])

    first, second = [], []

    def send(part):
        second.append(swap(part, 3))
        first.append(swap(part, 1))
        return first[-1], second[-1]

    if paired:
        own = gather_paired(g_lesser, w_lesser, energy_index, groups, send)
        send(own[1])
    else:
        own = gather_shared(g_lesser, w_lesser, energy_index, groups)
        send(own[0]), send(own[1])
    third = [swap(part, 1) for part in second]
    zero = jnp.int32(0)
    sigma_lesser, total = own_product(here, own, retarded)
    total = step_product(here ^ 1, zero, [first], retarded, total)
    total, held = step_product(here ^ 3, zero, [second], retarded, total, here ^ 2)
    delta = last_product(zero, [third], held, total)
    return (sigma_lesser, delta)


def solution(mesh):
    return jax.shard_map(
        shards,
        mesh=mesh,
        in_specs=(
            P("energy", None, "space", None, None),
            P("energy", None, "space", None, None),
            P("energy", None, "space", None, None, None),
            P(),
        ),
        out_specs=(P("energy", None, "space", None, None), P("energy", None, "space", None, None)),
        check_vma=False,
    )
```

```python
import functools

import jax
import jax.numpy as jnp
from jax import lax
from jax.experimental import pallas as pl
from jax.experimental.pallas import tpu as pltpu
from jax.sharding import PartitionSpec as P


VMEM = pltpu.MemorySpace.VMEM
SMEM = pltpu.MemorySpace.SMEM
HBM = pltpu.MemorySpace.HBM

SMALL = pl.CostEstimate(flops=1, bytes_accessed=1, transcendentals=0)


def vmem(count):
    return [pl.BlockSpec(memory_space=VMEM)] * count


def params(mib):
    return pltpu.CompilerParams(vmem_limit_bytes=mib * 2**20)


def grid_of(shape, row_offset=0):
    rows = lax.broadcasted_iota(jnp.int32, shape, 0) + row_offset
    cols = lax.broadcasted_iota(jnp.int32, shape, 1)
    return rows, cols


def pack_kernel(green, screen, cross, tri):
    half = green.shape[-1] // 2
    rows, cols = grid_of((half, half))
    upper = rows < cols
    diagonal = rows == cols
    for place, source in enumerate((green, screen)):
        a_re = source[0, 0, 0, :half, :half].astype(jnp.float32)
        a_im = source[0, 1, 0, :half, :half].astype(jnp.float32)
        d_re = source[0, 0, 0, half:, half:].astype(jnp.float32)
        d_im = source[0, 1, 0, half:, half:].astype(jnp.float32)
        t_re = jnp.where(upper, a_re, jnp.where(diagonal, a_im, d_re)).astype(jnp.bfloat16)
        t_im = jnp.where(upper, a_im, d_im).astype(jnp.bfloat16)
        c_re = source[0, 0, 0, :half, half:]
        c_im = source[0, 1, 0, :half, half:]
        shape = cross.shape[:1] + cross.shape[3:]
        cross[:, place, 0] = c_re.reshape(shape)
        cross[:, place, 1] = c_im.reshape(shape)
        tri[:, place, 0] = t_re.reshape(shape)
        tri[:, place, 1] = t_im.reshape(shape)


def pack(green, screen, parts):
    half = green.shape[-1] // 2
    out = jax.ShapeDtypeStruct((parts, 2, 2, half // parts, half), jnp.bfloat16)
    return pl.pallas_call(
        pack_kernel,
        out_shape=(out, out),
        in_specs=vmem(2),
        out_specs=tuple(vmem(2)),
        compiler_params=params(24),
    )(green, screen)


def split_rows(packed, groups):
    _, fields, comps, half, width = packed.shape
    shaped = packed.reshape(fields, comps, groups, half // groups, width)
    return jnp.moveaxis(shaped, 2, 0)


def conv_kernel(has_diagonal, index, offset, pieces, out, green, screen, place):
    count, _, _, rows, width = pieces.shape

    def scatter(stored, carry):
        point = index[stored]
        place[point] = stored
        green[point] = pieces[stored, 0].astype(jnp.float32)
        screen[point] = pieces[stored, 1].astype(jnp.float32)
        return carry

    unroll = count <= 16
    lax.fori_loop(0, count, scatter, 0, unroll=unroll)
    scale = count**-0.5
    zero = jnp.zeros((rows, width), jnp.float32)

    def one(point, carry):
        total = point + count // 2

        def term(first, sums):
            both_re, both_im, mixed = sums
            g_re = green[first, 0]
            g_im = green[first, 1]
            w_re = screen[total - first, 0]
            w_im = screen[total - first, 1]
            return (
                both_re + g_re * w_re,
                both_im + g_im * w_im,
                mixed + g_re * w_im + g_im * w_re,
            )

        if unroll:
            sums = (zero, zero, zero)
            for first in range(max(0, total - count + 1), min(count - 1, total) + 1):
                sums = term(first, sums)
        else:
            low = jnp.maximum(0, total - count + 1)
            high = jnp.minimum(count - 1, total) + 1
            sums = lax.fori_loop(low, high, term, (zero, zero, zero))
        both_re, both_im, mixed = sums
        s_re = -scale * mixed
        s_im = scale * (both_re - both_im)
        if has_diagonal:
            at_rows, at_cols = grid_of((rows, width), offset[0])
            diagonal = at_rows == at_cols
            s_re = jnp.where(diagonal, -scale * both_re, s_re)
            s_im = jnp.where(diagonal, -scale * both_im, s_im)
        stored = place[point]
        out[stored, 0] = s_re.astype(jnp.bfloat16)
        out[stored, 1] = s_im.astype(jnp.bfloat16)
        return carry

    if unroll:
        for point in range(count):
            one(point, 0)
    else:
        lax.fori_loop(0, count, one, 0)


def convolve(pieces, energy_index, row_offset, has_diagonal):
    count, _, _, rows, width = pieces.shape
    smem = pl.BlockSpec(memory_space=SMEM)
    return pl.pallas_call(
        functools.partial(conv_kernel, has_diagonal),
        out_shape=jax.ShapeDtypeStruct((count, 2, rows, width), jnp.bfloat16),
        in_specs=[smem, smem] + vmem(1),
        out_specs=vmem(1)[0],
        scratch_shapes=[
            pltpu.VMEM((count, 2, rows, width), jnp.float32),
            pltpu.VMEM((count, 2, rows, width), jnp.float32),
            pltpu.SMEM((count,), jnp.int32),
        ],
        compiler_params=params(24),
    )(energy_index, row_offset, pieces)


def share_of(me, d, rows):
    return pl.ds(pl.multiple_of((lax.shift_right_logical(me, 1) ^ d) * rows, rows), rows)


def cut_kernel(chips, me, green, screen, *rest):
    outs = rest[:chips]
    near, far, sems, cross_sems = rest[chips:]
    half = near.shape[-1]
    rows = half // chips
    copies = []
    for field, source in enumerate((green, screen)):
        for place, (held, lines) in enumerate(((near, slice(0, half)), (far, slice(half, None)))):
            copy = pltpu.make_async_copy(
                source.at[0, :, 0, lines, lines], held.at[field], sems.at[field, place]
            )
            copy.start()
            copies.append(copy)
    cross_copies = []
    for d in range(chips):
        for field, source in enumerate((green, screen)):
            part = source.at[0, :, 0, share_of(me[0], d, rows), half:]
            copy = pltpu.make_async_copy(part, outs[d].at[0, field], cross_sems.at[d, field])
            copy.start()
            cross_copies.append(copy)
    at_rows, at_cols = grid_of((rows, half))
    for field in range(2):
        for copy in copies[2 * field : 2 * field + 2]:
            copy.wait()
        for d in range(chips):
            lines = share_of(me[0], d, rows)
            here = at_rows + (lax.shift_right_logical(me[0], 1) ^ d) * rows
            upper = here < at_cols
            diagonal = here == at_cols
            a_re = near[field, 0, lines, :].astype(jnp.float32)
            a_im = near[field, 1, lines, :].astype(jnp.float32)
            d_re = far[field, 0, lines, :].astype(jnp.float32)
            d_im = far[field, 1, lines, :].astype(jnp.float32)
            t_re = jnp.where(upper, a_re, jnp.where(diagonal, a_im, d_re))
            outs[d][1, field, 0] = t_re.astype(jnp.bfloat16)
            outs[d][1, field, 1] = jnp.where(upper, a_im, d_im).astype(jnp.bfloat16)
    for copy in cross_copies:
        copy.wait()


def cut(me, green, screen, chips):
    half = green.shape[-1] // 2
    piece = jax.ShapeDtypeStruct((2, 2, 2, half // chips, half), jnp.bfloat16)
    return pl.pallas_call(
        functools.partial(cut_kernel, chips),
        out_shape=(piece,) * chips,
        in_specs=[pl.BlockSpec(memory_space=SMEM)] + [pl.BlockSpec(memory_space=HBM)] * 2,
        out_specs=tuple(vmem(chips)),
        scratch_shapes=[pltpu.VMEM((2, 2, half, half), jnp.bfloat16)] * 2
        + [pltpu.SemaphoreType.DMA((2, 2)), pltpu.SemaphoreType.DMA((chips, 2))],
        compiler_params=params(52),
        cost_estimate=SMALL,
    )(me, green, screen)


def bind_kernel(part, *refs):
    for place, piece in enumerate(refs[:-1]):
        refs[-1][place] = piece[part]


def bind(pieces, part):
    shape = (len(pieces),) + pieces[0].shape[1:]
    return pl.pallas_call(
        functools.partial(bind_kernel, part),
        out_shape=jax.ShapeDtypeStruct(shape, jnp.bfloat16),
        in_specs=vmem(len(pieces)),
        out_specs=vmem(1)[0],
        compiler_params=params(32),
        cost_estimate=SMALL,
    )(*pieces)


def conv_pieces_kernel(chips, part, me, index, *rest):
    same = rest[:chips][::-1]
    beside, other = rest[chips : chips + 2]
    outs = rest[chips + 2 : 2 * chips + 2]
    green, screen, sums, place = rest[2 * chips + 2 :]
    groups = 2 * chips
    rows, width = sums.shape[2:]
    for core in range(2):
        for d in range(chips):
            stored = me[0] ^ (2 * d + core)
            point = index[stored]
            place[point] = stored
            if core == 0:
                green[point] = same[d][part, 0]
                screen[point] = same[d][part, 1]
            elif d == 0:
                green[point] = beside[part, 0]
                screen[point] = beside[part, 1]
            else:
                green[point] = other[chips - 1 - d, 0]
                screen[point] = other[chips - 1 - d, 1]
    scale = groups**-0.5
    tall = 16
    for point in range(groups):

        @pl.when(((place[point] ^ me[0]) & 1) == 0)
        def _():
            total = point + groups // 2
            for first_row in range(0, rows, tall):
                for first_col in range(0, width, 128):
                    at = (slice(first_row, first_row + tall), slice(first_col, first_col + 128))
                    both_re = both_im = mixed = None
                    for p in range(max(0, total - groups + 1), min(groups - 1, total) + 1):
                        g_re = green[(p, 0) + at].astype(jnp.float32)
                        g_im = green[(p, 1) + at].astype(jnp.float32)
                        w_re = screen[(total - p, 0) + at].astype(jnp.float32)
                        w_im = screen[(total - p, 1) + at].astype(jnp.float32)
                        re = g_re * w_re
                        im = g_im * w_im
                        mix = g_re * w_im + g_im * w_re
                        both_re = re if both_re is None else both_re + re
                        both_im = im if both_im is None else both_im + im
                        mixed = mix if mixed is None else mixed + mix
                    s_re = -scale * mixed
                    s_im = scale * (both_re - both_im)
                    if part == 1:
                        first = lax.shift_right_logical(me[0], 1) * rows + first_row
                        at_rows, at_cols = grid_of((tall, 128), first)
                        diagonal = at_rows == at_cols + first_col
                        s_re = jnp.where(diagonal, -scale * both_re, s_re)
                        s_im = jnp.where(diagonal, -scale * both_im, s_im)
                    sums[(point, 0) + at] = s_re.astype(jnp.bfloat16)
                    sums[(point, 1) + at] = s_im.astype(jnp.bfloat16)

    for d in range(chips):
        outs[d][...] = sums[index[me[0] ^ (2 * d)]]


def conv_pieces(me, energy_index, same, beside, other, part):
    chips = len(same)
    shape = same[0].shape[2:]
    smem = pl.BlockSpec(memory_space=SMEM)
    return pl.pallas_call(
        functools.partial(conv_pieces_kernel, chips, part),
        out_shape=(jax.ShapeDtypeStruct(shape, jnp.bfloat16),) * chips,
        in_specs=[smem, smem] + vmem(chips + 2),
        out_specs=tuple(vmem(chips)),
        scratch_shapes=[pltpu.VMEM((2 * chips,) + shape, jnp.bfloat16)] * 3
        + [pltpu.SMEM((2 * chips,), jnp.int32)],
        compiler_params=params(32),
        cost_estimate=SMALL,
    )(me, energy_index, *same[::-1], beside, other)


def join_kernel(chips, me, *rest):
    pieces, out = rest[:chips][::-1], rest[chips]
    rows = pieces[0].shape[1]
    for d in range(chips):
        out[:, share_of(me[0], d, rows), :] = pieces[d][...]


def join(me, pieces):
    half = pieces[0].shape[-1]
    return pl.pallas_call(
        functools.partial(join_kernel, len(pieces)),
        out_shape=jax.ShapeDtypeStruct((2, half, half), jnp.bfloat16),
        in_specs=[pl.BlockSpec(memory_space=SMEM)] + vmem(len(pieces)),
        out_specs=vmem(1)[0],
        compiler_params=params(32),
        cost_estimate=SMALL,
    )(me, *pieces[::-1])


def swap(piece, d, groups):
    return lax.ppermute(piece, "energy", [(i, i ^ d) for i in range(groups)]) if d else piece


def after(value, *earlier):
    return lax.optimization_barrier((value, earlier))[0]


def gather_paired(g_lesser, w_lesser, energy_index, groups, send=lambda part: ()):
    me = lax.axis_index("energy").astype(jnp.int32).reshape(1)
    chips = groups // 2

    def over(pieces):
        return [swap(pieces[d], 2 * d, groups) for d in range(chips)]

    pieces = cut(me, g_lesser, w_lesser, chips)
    same = over(pieces)
    beside = swap(pieces[0], 1, groups)
    bound = [bind(after(same[:0:-1], beside), part) for part in range(2)]
    other = [swap(piece, 1, groups) for piece in bound]
    mine = conv_pieces(me, energy_index, same, beside, other[0], 0)
    shares = over(mine)
    own_cross = join(me, shares)
    sent = send(own_cross)
    mine = conv_pieces(me, energy_index, same, beside, after(other[1], own_cross), 1)
    own_tri = join(me, after(over(mine), sent[1:]))
    return own_cross, own_tri


def gather_shared(g_lesser, w_lesser, energy_index, groups):
    half = g_lesser.shape[-1] // 2
    rows = half // groups
    cross, tri = (split_rows(packed, groups) for packed in pack(g_lesser, w_lesser, 1))
    offset = (lax.axis_index("energy") * rows).astype(jnp.int32).reshape(1)
    own = []
    for pieces, has_diagonal in ((cross, False), (tri, True)):
        shares = convolve(exchange(pieces), energy_index, offset, has_diagonal)
        own.append(jnp.moveaxis(exchange(shares), 0, 1).reshape(2, half, half))
    return own


def squares(cross, tri):
    return cross[0], cross[1], tri[0], tri[1]


def dot(a, b):
    return jnp.dot(a, b, preferred_element_type=jnp.float32)


def dot_t(a, b):
    return lax.dot_general(a, b, (((1,), (1,)), ((), ())), preferred_element_type=jnp.float32)


def product(cross, tri, retarded):
    c_re, c_im, t_re, t_im = squares(cross, tri)
    half = c_re.shape[0]
    rows, cols = grid_of((half, half))
    tr = t_re.astype(jnp.float32)
    ti = t_im.astype(jnp.float32)
    diagonal = rows == cols
    a_re = jnp.where(rows < cols, tr, 0.0).astype(jnp.bfloat16)
    a_im = jnp.where(rows < cols, ti, jnp.where(diagonal, 0.5 * tr, 0.0)).astype(jnp.bfloat16)
    d_re = jnp.where(rows > cols, tr, 0.0).astype(jnp.bfloat16)
    d_im = jnp.where(rows > cols, ti, jnp.where(diagonal, 0.5 * ti, 0.0)).astype(jnp.bfloat16)
    g_re = retarded[0]
    g_im = retarded[1]
    near = jnp.concatenate([g_re[:, :half], g_im[:, :half]], axis=1)
    far = jnp.concatenate([g_re, g_im], axis=1)
    l_re = jnp.concatenate(
        [
            dot(near, jnp.concatenate([a_re, -a_im], axis=0)),
            dot(far, jnp.concatenate([c_re, d_re, -c_im, -d_im], axis=0)),
        ],
        axis=1,
    ).astype(jnp.bfloat16)
    l_im = jnp.concatenate(
        [
            dot(near, jnp.concatenate([a_im, a_re], axis=0)),
            dot(far, jnp.concatenate([c_im, d_im, c_re, d_re], axis=0)),
        ],
        axis=1,
    ).astype(jnp.bfloat16)
    left = jnp.concatenate(
        [jnp.concatenate([l_re, l_im], axis=1), jnp.concatenate([l_im, -l_re], axis=1)], axis=0
    )
    x = dot_t(left, far)
    return x[: 2 * half], x[2 * half :]


def own_kernel(where, cross, tri, retarded, sigma, total, block, sem):
    copy = pltpu.make_async_copy(retarded.at[0, :, 0, where[0]], block, sem)
    copy.start()
    c_re, c_im, t_re, t_im = squares(cross, tri)
    half = c_re.shape[0]
    rows, cols = grid_of((half, half))
    upper = rows < cols
    diagonal = rows == cols
    tr = t_re.astype(jnp.float32)
    ti = t_im.astype(jnp.float32)
    trt = tr.T
    tit = ti.T
    zero = jnp.zeros_like(tr)
    bf = jnp.bfloat16
    sigma[0, 0, 0, :half, half:] = c_re
    sigma[0, 1, 0, :half, half:] = c_im
    sigma[0, 0, 0, half:, :half] = (-(c_re.astype(jnp.float32).T)).astype(bf)
    sigma[0, 1, 0, half:, :half] = c_im.astype(jnp.float32).T.astype(bf)
    sigma[0, 0, 0, :half, :half] = jnp.where(upper, tr, jnp.where(diagonal, zero, -trt)).astype(bf)
    sigma[0, 1, 0, :half, :half] = jnp.where(upper, ti, jnp.where(diagonal, tr, tit)).astype(bf)
    sigma[0, 0, 0, half:, half:] = jnp.where(upper, -trt, jnp.where(diagonal, zero, tr)).astype(bf)
    sigma[0, 1, 0, half:, half:] = jnp.where(upper, tit, ti).astype(bf)
    copy.wait()
    total[0], total[1] = product(cross, tri, block)


def step_kernel(count, last, ahead, where, *rest):
    if last:
        block, total = rest[:2]
        sources = rest[2 : 2 + 2 * count]
        out = rest[-1]
    else:
        sources = rest[: 2 * count]
        rest = rest[2 * count :]
    if last:
        pass
    elif ahead:
        retarded, total, out, later, block, sems = rest
        fetch = pltpu.make_async_copy(retarded.at[0, :, 0, where[0]], block, sems.at[0])
        fetch.start()
        prefetch = pltpu.make_async_copy(retarded.at[0, :, 0, where[2]], later, sems.at[1])
        prefetch.start()
        fetch.wait()
    else:
        retarded, total, out, block, sems = rest
        fetch = pltpu.make_async_copy(retarded.at[0, :, 0, where[0]], block, sems.at[0])
        fetch.start()
        fetch.wait()
    for pick in range(count):

        @pl.when(where[1] == pick)
        def _():
            cross, tri = sources[pick], sources[count + pick]
            x_re, x_im = product(cross, tri, block)
            x_re += total[0]
            x_im += total[1]
            if last:
                out[0, 0, 0] = (x_re - x_re.T).astype(jnp.bfloat16)
                out[0, 1, 0] = (x_im + x_im.T).astype(jnp.bfloat16)
            else:
                out[0] = x_re
                out[1] = x_im

    if ahead:
        prefetch.wait()


def cost(width):
    return pl.CostEstimate(flops=14 * width**3, bytes_accessed=8 * width**2, transcendentals=0)


def own_product(block, own, retarded):
    width = retarded.shape[-1]
    return pl.pallas_call(
        own_kernel,
        out_shape=(
            jax.ShapeDtypeStruct((1, 2, 1, width, width), jnp.bfloat16),
            jax.ShapeDtypeStruct((2, width, width), jnp.float32),
        ),
        in_specs=[pl.BlockSpec(memory_space=SMEM)] + vmem(2) + [pl.BlockSpec(memory_space=HBM)],
        out_specs=tuple(vmem(2)),
        scratch_shapes=[pltpu.VMEM((2, width, width), jnp.bfloat16), pltpu.SemaphoreType.DMA],
        compiler_params=params(48),
        cost_estimate=cost(width),
    )(block.reshape(1), *own, retarded)


def step_product(block, pick, sources, retarded, total, later=None):
    width = retarded.shape[-1]
    flat = [source[part] for part in range(2) for source in sources]
    ahead = later is not None
    numbers = jnp.stack([block, pick] + ([later] if ahead else []))
    total_shape = jax.ShapeDtypeStruct((2, width, width), jnp.float32)
    block_shape = jax.ShapeDtypeStruct((2, width, width), jnp.bfloat16)
    return pl.pallas_call(
        functools.partial(step_kernel, len(sources), False, ahead),
        out_shape=(total_shape, block_shape) if ahead else total_shape,
        in_specs=[pl.BlockSpec(memory_space=SMEM)]
        + vmem(len(flat))
        + [pl.BlockSpec(memory_space=HBM)]
        + vmem(1),
        out_specs=tuple(vmem(2)) if ahead else vmem(1)[0],
        scratch_shapes=[pltpu.VMEM((2, width, width), jnp.bfloat16), pltpu.SemaphoreType.DMA((2,))],
        compiler_params=params(46),
        cost_estimate=cost(width),
    )(numbers, *flat, retarded, total)


def last_product(pick, sources, block, total):
    width = block.shape[-1]
    flat = [source[part] for part in range(2) for source in sources]
    return pl.pallas_call(
        functools.partial(step_kernel, len(sources), True, False),
        out_shape=jax.ShapeDtypeStruct((1, 2, 1, width, width), jnp.bfloat16),
        in_specs=[pl.BlockSpec(memory_space=SMEM)] + vmem(len(flat) + 2),
        out_specs=vmem(1)[0],
        compiler_params=params(48),
        cost_estimate=cost(width),
    )(jnp.stack([pick, pick]), block, total, *flat)


def exchange(pieces):
    return lax.all_to_all(pieces, "energy", split_axis=0, concat_axis=0, tiled=True)


def shards(g_lesser, w_lesser, g_retarded, energy_index):
    width = g_lesser.shape[-1]
    groups = lax.axis_size("energy")
    chain = lax.axis_size("space")
    here = lax.axis_index("space")
    paired = groups >= 4 and groups & (groups - 1) == 0 and (width // groups) % 16 == 0
    here = here.astype(jnp.int32)
    if chain == 4:
        return around_line(here, paired, g_lesser, w_lesser, energy_index, groups, g_retarded)
    gather = gather_paired if paired else gather_shared
    own = gather(g_lesser, w_lesser, energy_index, groups)
    everyone = [lax.all_gather(part, "space") for part in own]
    sigma_lesser, total = own_product(here, own, g_retarded)
    zero = jnp.int32(0)

    def source(block):
        return tuple(lax.dynamic_index_in_dim(part, block, 0, False) for part in everyone)

    for step in range(1, chain - 1):
        block = (here + step) % chain
        later = (block + 1) % chain
        total, held = step_product(block, zero, [source(block)], g_retarded, total, later)
    return (sigma_lesser, last_product(zero, [source(later)], held, total))


def around_line(here, paired, g_lesser, w_lesser, energy_index, groups, retarded):
    def swap(part, bits):
        return lax.ppermute(part, "space", [(i, i ^ bits) for i in range(4)])

    first, second = [], []

    def send(part):
        second.append(swap(part, 3))
        first.append(swap(part, 1))
        return first[-1], second[-1]

    if paired:
        own = gather_paired(g_lesser, w_lesser, energy_index, groups, send)
        send(own[1])
    else:
        own = gather_shared(g_lesser, w_lesser, energy_index, groups)
        send(own[0]), send(own[1])
    zero = jnp.int32(0)
    sigma_lesser, total = own_product(here, own, retarded)
    total = step_product(here ^ 1, zero, [first], retarded, total)
    third = [swap(after(second[0], first[0]), 1), swap(after(second[1], total), 1)]
    total, held = step_product(here ^ 3, zero, [second], retarded, total, here ^ 2)
    delta = last_product(zero, [third], held, total)
    return (sigma_lesser, delta)


def solution(mesh):
    return jax.shard_map(
        shards,
        mesh=mesh,
        in_specs=(
            P("energy", None, "space", None, None),
            P("energy", None, "space", None, None),
            P("energy", None, "space", None, None, None),
            P(),
        ),
        out_specs=(P("energy", None, "space", None, None), P("energy", None, "space", None, None)),
        check_vma=False,
    )
```

```python
import functools

import jax
import jax.numpy as jnp
from jax import lax
from jax.experimental import pallas as pl
from jax.experimental.pallas import tpu as pltpu
from jax.sharding import PartitionSpec as P


VMEM = pltpu.MemorySpace.VMEM
SMEM = pltpu.MemorySpace.SMEM
HBM = pltpu.MemorySpace.HBM

SMALL = pl.CostEstimate(flops=1, bytes_accessed=1, transcendentals=0)


def vmem(count):
    return [pl.BlockSpec(memory_space=VMEM)] * count


def params(mib):
    return pltpu.CompilerParams(vmem_limit_bytes=mib * 2**20)


def grid_of(shape, row_offset=0):
    rows = lax.broadcasted_iota(jnp.int32, shape, 0) + row_offset
    cols = lax.broadcasted_iota(jnp.int32, shape, 1)
    return rows, cols


def pack_kernel(green, screen, cross, tri):
    half = green.shape[-1] // 2
    rows, cols = grid_of((half, half))
    upper = rows < cols
    diagonal = rows == cols
    for place, source in enumerate((green, screen)):
        a_re = source[0, 0, 0, :half, :half].astype(jnp.float32)
        a_im = source[0, 1, 0, :half, :half].astype(jnp.float32)
        d_re = source[0, 0, 0, half:, half:].astype(jnp.float32)
        d_im = source[0, 1, 0, half:, half:].astype(jnp.float32)
        t_re = jnp.where(upper, a_re, jnp.where(diagonal, a_im, d_re)).astype(jnp.bfloat16)
        t_im = jnp.where(upper, a_im, d_im).astype(jnp.bfloat16)
        c_re = source[0, 0, 0, :half, half:]
        c_im = source[0, 1, 0, :half, half:]
        shape = cross.shape[:1] + cross.shape[3:]
        cross[:, place, 0] = c_re.reshape(shape)
        cross[:, place, 1] = c_im.reshape(shape)
        tri[:, place, 0] = t_re.reshape(shape)
        tri[:, place, 1] = t_im.reshape(shape)


def pack(green, screen, parts):
    half = green.shape[-1] // 2
    out = jax.ShapeDtypeStruct((parts, 2, 2, half // parts, half), jnp.bfloat16)
    return pl.pallas_call(
        pack_kernel,
        out_shape=(out, out),
        in_specs=vmem(2),
        out_specs=tuple(vmem(2)),
        compiler_params=params(24),
    )(green, screen)


def split_rows(packed, groups):
    _, fields, comps, half, width = packed.shape
    shaped = packed.reshape(fields, comps, groups, half // groups, width)
    return jnp.moveaxis(shaped, 2, 0)


def conv_kernel(has_diagonal, index, offset, pieces, out, green, screen, place):
    count, _, _, rows, width = pieces.shape

    def scatter(stored, carry):
        point = index[stored]
        place[point] = stored
        green[point] = pieces[stored, 0].astype(jnp.float32)
        screen[point] = pieces[stored, 1].astype(jnp.float32)
        return carry

    unroll = count <= 16
    lax.fori_loop(0, count, scatter, 0, unroll=unroll)
    scale = count**-0.5
    zero = jnp.zeros((rows, width), jnp.float32)

    def one(point, carry):
        total = point + count // 2

        def term(first, sums):
            both_re, both_im, mixed = sums
            g_re = green[first, 0]
            g_im = green[first, 1]
            w_re = screen[total - first, 0]
            w_im = screen[total - first, 1]
            return (
                both_re + g_re * w_re,
                both_im + g_im * w_im,
                mixed + g_re * w_im + g_im * w_re,
            )

        if unroll:
            sums = (zero, zero, zero)
            for first in range(max(0, total - count + 1), min(count - 1, total) + 1):
                sums = term(first, sums)
        else:
            low = jnp.maximum(0, total - count + 1)
            high = jnp.minimum(count - 1, total) + 1
            sums = lax.fori_loop(low, high, term, (zero, zero, zero))
        both_re, both_im, mixed = sums
        s_re = -scale * mixed
        s_im = scale * (both_re - both_im)
        if has_diagonal:
            at_rows, at_cols = grid_of((rows, width), offset[0])
            diagonal = at_rows == at_cols
            s_re = jnp.where(diagonal, -scale * both_re, s_re)
            s_im = jnp.where(diagonal, -scale * both_im, s_im)
        stored = place[point]
        out[stored, 0] = s_re.astype(jnp.bfloat16)
        out[stored, 1] = s_im.astype(jnp.bfloat16)
        return carry

    if unroll:
        for point in range(count):
            one(point, 0)
    else:
        lax.fori_loop(0, count, one, 0)


def convolve(pieces, energy_index, row_offset, has_diagonal):
    count, _, _, rows, width = pieces.shape
    smem = pl.BlockSpec(memory_space=SMEM)
    return pl.pallas_call(
        functools.partial(conv_kernel, has_diagonal),
        out_shape=jax.ShapeDtypeStruct((count, 2, rows, width), jnp.bfloat16),
        in_specs=[smem, smem] + vmem(1),
        out_specs=vmem(1)[0],
        scratch_shapes=[
            pltpu.VMEM((count, 2, rows, width), jnp.float32),
            pltpu.VMEM((count, 2, rows, width), jnp.float32),
            pltpu.SMEM((count,), jnp.int32),
        ],
        compiler_params=params(24),
    )(energy_index, row_offset, pieces)


def share_of(me, d, rows):
    return pl.ds(pl.multiple_of((lax.shift_right_logical(me, 1) ^ d) * rows, rows), rows)


def cut_cross_kernel(chips, me, green, screen, *rest):
    outs, sems = rest[:chips], rest[chips]
    half = green.shape[-1] // 2
    rows = half // chips
    copies = []
    for d in range(chips):
        for field, source in enumerate((green, screen)):
            part = source.at[0, :, 0, share_of(me[0], d, rows), half:]
            copies.append(pltpu.make_async_copy(part, outs[d].at[field], sems.at[d, field]))
            copies[-1].start()
    for copy in copies:
        copy.wait()


def cut_tri_kernel(chips, me, green, screen, *rest):
    outs = rest[:chips]
    near, far, sems = rest[chips:]
    half = near.shape[-1]
    rows = half // chips
    copies = []
    for field, source in enumerate((green, screen)):
        for place, (held, lines) in enumerate(((near, slice(0, half)), (far, slice(half, None)))):
            copy = pltpu.make_async_copy(
                source.at[0, :, 0, lines, lines], held.at[field], sems.at[field, place]
            )
            copy.start()
            copies.append(copy)
    for copy in copies:
        copy.wait()
    at_rows, at_cols = grid_of((rows, half))
    for d in range(chips):
        lines = share_of(me[0], d, rows)
        here = at_rows + (lax.shift_right_logical(me[0], 1) ^ d) * rows
        upper = here < at_cols
        diagonal = here == at_cols
        for field in range(2):
            a_re = near[field, 0, lines, :].astype(jnp.float32)
            a_im = near[field, 1, lines, :].astype(jnp.float32)
            d_re = far[field, 0, lines, :].astype(jnp.float32)
            d_im = far[field, 1, lines, :].astype(jnp.float32)
            t_re = jnp.where(upper, a_re, jnp.where(diagonal, a_im, d_re))
            outs[d][field, 0] = t_re.astype(jnp.bfloat16)
            outs[d][field, 1] = jnp.where(upper, a_im, d_im).astype(jnp.bfloat16)


def cut(me, green, screen, chips, tri):
    half = green.shape[-1] // 2
    piece = jax.ShapeDtypeStruct((2, 2, half // chips, half), jnp.bfloat16)
    squares_held = [pltpu.VMEM((2, 2, half, half), jnp.bfloat16)] * 2
    scratch = squares_held + [pltpu.SemaphoreType.DMA((2, 2))] if tri else [pltpu.SemaphoreType.DMA((chips, 2))]
    return pl.pallas_call(
        functools.partial(cut_tri_kernel if tri else cut_cross_kernel, chips),
        out_shape=(piece,) * chips,
        in_specs=[pl.BlockSpec(memory_space=SMEM)] + [pl.BlockSpec(memory_space=HBM)] * 2,
        out_specs=tuple(vmem(chips)),
        scratch_shapes=scratch,
        compiler_params=params(56),
        cost_estimate=SMALL,
    )(me, green, screen)


def bind_kernel(*refs):
    for place, piece in enumerate(refs[:-1]):
        refs[-1][place] = piece[...]


def bind(pieces):
    shape = (len(pieces),) + pieces[0].shape
    return pl.pallas_call(
        bind_kernel,
        out_shape=jax.ShapeDtypeStruct(shape, jnp.bfloat16),
        in_specs=vmem(len(pieces)),
        out_specs=vmem(1)[0],
        compiler_params=params(32),
        cost_estimate=SMALL,
    )(*pieces)


def conv_pieces_kernel(chips, has_diagonal, me, index, *rest):
    same = rest[:chips][::-1]
    beside, other = rest[chips : chips + 2]
    outs = rest[chips + 2 : 2 * chips + 2]
    green, screen, sums, place = rest[2 * chips + 2 :]
    groups = 2 * chips
    rows, width = sums.shape[2:]
    for core in range(2):
        for d in range(chips):
            stored = me[0] ^ (2 * d + core)
            point = index[stored]
            place[point] = stored
            if core == 0:
                green[point] = same[d][0]
                screen[point] = same[d][1]
            elif d == 0:
                green[point] = beside[0]
                screen[point] = beside[1]
            else:
                green[point] = other[chips - 1 - d, 0]
                screen[point] = other[chips - 1 - d, 1]
    scale = groups**-0.5
    tall = 16
    for point in range(groups):

        @pl.when(((place[point] ^ me[0]) & 1) == 0)
        def _():
            total = point + groups // 2
            for first_row in range(0, rows, tall):
                for first_col in range(0, width, 128):
                    at = (slice(first_row, first_row + tall), slice(first_col, first_col + 128))
                    both_re = both_im = mixed = None
                    for p in range(max(0, total - groups + 1), min(groups - 1, total) + 1):
                        g_re = green[(p, 0) + at].astype(jnp.float32)
                        g_im = green[(p, 1) + at].astype(jnp.float32)
                        w_re = screen[(total - p, 0) + at].astype(jnp.float32)
                        w_im = screen[(total - p, 1) + at].astype(jnp.float32)
                        re = g_re * w_re
                        im = g_im * w_im
                        mix = g_re * w_im + g_im * w_re
                        both_re = re if both_re is None else both_re + re
                        both_im = im if both_im is None else both_im + im
                        mixed = mix if mixed is None else mixed + mix
                    s_re = -scale * mixed
                    s_im = scale * (both_re - both_im)
                    if has_diagonal:
                        first = lax.shift_right_logical(me[0], 1) * rows + first_row
                        at_rows, at_cols = grid_of((tall, 128), first)
                        diagonal = at_rows == at_cols + first_col
                        s_re = jnp.where(diagonal, -scale * both_re, s_re)
                        s_im = jnp.where(diagonal, -scale * both_im, s_im)
                    sums[(point, 0) + at] = s_re.astype(jnp.bfloat16)
                    sums[(point, 1) + at] = s_im.astype(jnp.bfloat16)

    for d in range(chips):
        outs[d][...] = sums[index[me[0] ^ (2 * d)]]


def conv_pieces(me, energy_index, same, beside, other, has_diagonal):
    chips = len(same)
    shape = same[0].shape[1:]
    smem = pl.BlockSpec(memory_space=SMEM)
    return pl.pallas_call(
        functools.partial(conv_pieces_kernel, chips, has_diagonal),
        out_shape=(jax.ShapeDtypeStruct(shape, jnp.bfloat16),) * chips,
        in_specs=[smem, smem] + vmem(chips + 2),
        out_specs=tuple(vmem(chips)),
        scratch_shapes=[pltpu.VMEM((2 * chips,) + shape, jnp.bfloat16)] * 3
        + [pltpu.SMEM((2 * chips,), jnp.int32)],
        compiler_params=params(32),
        cost_estimate=SMALL,
    )(me, energy_index, *same[::-1], beside, other)


def join_kernel(chips, me, *rest):
    pieces, out = rest[:chips][::-1], rest[chips]
    rows = pieces[0].shape[1]
    for d in range(chips):
        out[:, share_of(me[0], d, rows), :] = pieces[d][...]


def join(me, pieces):
    half = pieces[0].shape[-1]
    return pl.pallas_call(
        functools.partial(join_kernel, len(pieces)),
        out_shape=jax.ShapeDtypeStruct((2, half, half), jnp.bfloat16),
        in_specs=[pl.BlockSpec(memory_space=SMEM)] + vmem(len(pieces)),
        out_specs=vmem(1)[0],
        compiler_params=params(32),
        cost_estimate=SMALL,
    )(me, *pieces[::-1])


def swap(piece, d, groups):
    return lax.ppermute(piece, "energy", [(i, i ^ d) for i in range(groups)]) if d else piece


def after(value, *earlier):
    return lax.optimization_barrier((value, earlier))[0]


def gather_paired(g_lesser, w_lesser, energy_index, groups, send=lambda part: ()):
    me = lax.axis_index("energy").astype(jnp.int32).reshape(1)
    chips = groups // 2

    def over(pieces):
        return [swap(pieces[d], 2 * d, groups) for d in range(chips)]

    cross, tri = (cut(me, g_lesser, w_lesser, chips, which) for which in (False, True))
    same_cross, same_tri = over(cross), over(tri)
    beside_cross, beside_tri = swap(cross[0], 1, groups), swap(tri[0], 1, groups)
    other = swap(bind(after(same_cross[:0:-1], tri[0])), 1, groups)
    mine = conv_pieces(me, energy_index, same_cross, beside_cross, other, False)
    own_cross = join(me, after(over(mine), same_tri[:0:-1], beside_tri))
    sent = send(own_cross)
    other = swap(bind(after(same_tri[:0:-1], own_cross)), 1, groups)
    mine = conv_pieces(me, energy_index, same_tri, beside_tri, other, True)
    own_tri = join(me, after(over(mine), sent))
    return own_cross, own_tri


def gather_shared(g_lesser, w_lesser, energy_index, groups):
    half = g_lesser.shape[-1] // 2
    rows = half // groups
    cross, tri = (split_rows(packed, groups) for packed in pack(g_lesser, w_lesser, 1))
    offset = (lax.axis_index("energy") * rows).astype(jnp.int32).reshape(1)
    own = []
    for pieces, has_diagonal in ((cross, False), (tri, True)):
        shares = convolve(exchange(pieces), energy_index, offset, has_diagonal)
        own.append(jnp.moveaxis(exchange(shares), 0, 1).reshape(2, half, half))
    return own


def squares(cross, tri):
    return cross[0], cross[1], tri[0], tri[1]


def dot(a, b):
    return jnp.dot(a, b, preferred_element_type=jnp.float32)


def dot_t(a, b):
    return lax.dot_general(a, b, (((1,), (1,)), ((), ())), preferred_element_type=jnp.float32)


def product(cross, tri, retarded):
    c_re, c_im, t_re, t_im = squares(cross, tri)
    half = c_re.shape[0]
    rows, cols = grid_of((half, half))
    tr = t_re.astype(jnp.float32)
    ti = t_im.astype(jnp.float32)
    diagonal = rows == cols
    a_re = jnp.where(rows < cols, tr, 0.0).astype(jnp.bfloat16)
    a_im = jnp.where(rows < cols, ti, jnp.where(diagonal, 0.5 * tr, 0.0)).astype(jnp.bfloat16)
    d_re = jnp.where(rows > cols, tr, 0.0).astype(jnp.bfloat16)
    d_im = jnp.where(rows > cols, ti, jnp.where(diagonal, 0.5 * ti, 0.0)).astype(jnp.bfloat16)
    g_re = retarded[0]
    g_im = retarded[1]
    near = jnp.concatenate([g_re[:, :half], g_im[:, :half]], axis=1)
    far = jnp.concatenate([g_re, g_im], axis=1)
    l_re = jnp.concatenate(
        [
            dot(near, jnp.concatenate([a_re, -a_im], axis=0)),
            dot(far, jnp.concatenate([c_re, d_re, -c_im, -d_im], axis=0)),
        ],
        axis=1,
    ).astype(jnp.bfloat16)
    l_im = jnp.concatenate(
        [
            dot(near, jnp.concatenate([a_im, a_re], axis=0)),
            dot(far, jnp.concatenate([c_im, d_im, c_re, d_re], axis=0)),
        ],
        axis=1,
    ).astype(jnp.bfloat16)
    x_re = dot_t(jnp.concatenate([l_re, l_im], axis=1), far)
    x_im = dot_t(jnp.concatenate([l_im, -l_re], axis=1), far)
    return x_re, x_im


def own_kernel(where, cross, tri, retarded, sigma, total, block, sem):
    copy = pltpu.make_async_copy(retarded.at[0, :, 0, where[0]], block, sem)
    copy.start()
    c_re, c_im, t_re, t_im = squares(cross, tri)
    half = c_re.shape[0]
    rows, cols = grid_of((half, half))
    upper = rows < cols
    diagonal = rows == cols
    tr = t_re.astype(jnp.float32)
    ti = t_im.astype(jnp.float32)
    trt = tr.T
    tit = ti.T
    zero = jnp.zeros_like(tr)
    bf = jnp.bfloat16
    sigma[0, 0, 0, :half, half:] = c_re
    sigma[0, 1, 0, :half, half:] = c_im
    sigma[0, 0, 0, half:, :half] = (-(c_re.astype(jnp.float32).T)).astype(bf)
    sigma[0, 1, 0, half:, :half] = c_im.astype(jnp.float32).T.astype(bf)
    sigma[0, 0, 0, :half, :half] = jnp.where(upper, tr, jnp.where(diagonal, zero, -trt)).astype(bf)
    sigma[0, 1, 0, :half, :half] = jnp.where(upper, ti, jnp.where(diagonal, tr, tit)).astype(bf)
    sigma[0, 0, 0, half:, half:] = jnp.where(upper, -trt, jnp.where(diagonal, zero, tr)).astype(bf)
    sigma[0, 1, 0, half:, half:] = jnp.where(upper, tit, ti).astype(bf)
    copy.wait()
    total[0], total[1] = product(cross, tri, block)


def step_kernel(count, last, ahead, where, *rest):
    if last:
        block, total = rest[:2]
        sources = rest[2 : 2 + 2 * count]
        out = rest[-1]
    else:
        sources = rest[: 2 * count]
        rest = rest[2 * count :]
    if last:
        pass
    elif ahead:
        retarded, total, out, later, block, sems = rest
        fetch = pltpu.make_async_copy(retarded.at[0, :, 0, where[0]], block, sems.at[0])
        fetch.start()
        prefetch = pltpu.make_async_copy(retarded.at[0, :, 0, where[2]], later, sems.at[1])
        prefetch.start()
        fetch.wait()
    else:
        retarded, total, out, block, sems = rest
        fetch = pltpu.make_async_copy(retarded.at[0, :, 0, where[0]], block, sems.at[0])
        fetch.start()
        fetch.wait()
    for pick in range(count):

        @pl.when(where[1] == pick)
        def _():
            cross, tri = sources[pick], sources[count + pick]
            x_re, x_im = product(cross, tri, block)
            x_re += total[0]
            x_im += total[1]
            if last:
                out[0, 0, 0] = (x_re - x_re.T).astype(jnp.bfloat16)
                out[0, 1, 0] = (x_im + x_im.T).astype(jnp.bfloat16)
            else:
                out[0] = x_re
                out[1] = x_im

    if ahead:
        prefetch.wait()


def cost(width):
    return pl.CostEstimate(flops=14 * width**3, bytes_accessed=8 * width**2, transcendentals=0)


def own_product(block, own, retarded):
    width = retarded.shape[-1]
    return pl.pallas_call(
        own_kernel,
        out_shape=(
            jax.ShapeDtypeStruct((1, 2, 1, width, width), jnp.bfloat16),
            jax.ShapeDtypeStruct((2, width, width), jnp.float32),
        ),
        in_specs=[pl.BlockSpec(memory_space=SMEM)] + vmem(2) + [pl.BlockSpec(memory_space=HBM)],
        out_specs=tuple(vmem(2)),
        scratch_shapes=[pltpu.VMEM((2, width, width), jnp.bfloat16), pltpu.SemaphoreType.DMA],
        compiler_params=params(48),
        cost_estimate=cost(width),
    )(block.reshape(1), *own, retarded)


def step_product(block, pick, sources, retarded, total, later=None):
    width = retarded.shape[-1]
    flat = [source[part] for part in range(2) for source in sources]
    ahead = later is not None
    numbers = jnp.stack([block, pick] + ([later] if ahead else []))
    total_shape = jax.ShapeDtypeStruct((2, width, width), jnp.float32)
    block_shape = jax.ShapeDtypeStruct((2, width, width), jnp.bfloat16)
    return pl.pallas_call(
        functools.partial(step_kernel, len(sources), False, ahead),
        out_shape=(total_shape, block_shape) if ahead else total_shape,
        in_specs=[pl.BlockSpec(memory_space=SMEM)]
        + vmem(len(flat))
        + [pl.BlockSpec(memory_space=HBM)]
        + vmem(1),
        out_specs=tuple(vmem(2)) if ahead else vmem(1)[0],
        scratch_shapes=[pltpu.VMEM((2, width, width), jnp.bfloat16), pltpu.SemaphoreType.DMA((2,))],
        compiler_params=params(46),
        cost_estimate=cost(width),
    )(numbers, *flat, retarded, total)


def last_product(pick, sources, block, total):
    width = block.shape[-1]
    flat = [source[part] for part in range(2) for source in sources]
    return pl.pallas_call(
        functools.partial(step_kernel, len(sources), True, False),
        out_shape=jax.ShapeDtypeStruct((1, 2, 1, width, width), jnp.bfloat16),
        in_specs=[pl.BlockSpec(memory_space=SMEM)] + vmem(len(flat) + 2),
        out_specs=vmem(1)[0],
        compiler_params=params(48),
        cost_estimate=cost(width),
    )(jnp.stack([pick, pick]), block, total, *flat)


def exchange(pieces):
    return lax.all_to_all(pieces, "energy", split_axis=0, concat_axis=0, tiled=True)


def shards(g_lesser, w_lesser, g_retarded, energy_index):
    width = g_lesser.shape[-1]
    groups = lax.axis_size("energy")
    chain = lax.axis_size("space")
    here = lax.axis_index("space")
    paired = groups >= 4 and groups & (groups - 1) == 0 and (width // groups) % 16 == 0
    here = here.astype(jnp.int32)
    if chain == 4:
        return around_line(here, paired, g_lesser, w_lesser, energy_index, groups, g_retarded)
    gather = gather_paired if paired else gather_shared
    own = gather(g_lesser, w_lesser, energy_index, groups)
    everyone = [lax.all_gather(part, "space") for part in own]
    sigma_lesser, total = own_product(here, own, g_retarded)
    zero = jnp.int32(0)

    def source(block):
        return tuple(lax.dynamic_index_in_dim(part, block, 0, False) for part in everyone)

    for step in range(1, chain - 1):
        block = (here + step) % chain
        later = (block + 1) % chain
        total, held = step_product(block, zero, [source(block)], g_retarded, total, later)
    return (sigma_lesser, last_product(zero, [source(later)], held, total))


def around_line(here, paired, g_lesser, w_lesser, energy_index, groups, retarded):
    def swap(part, bits):
        return lax.ppermute(part, "space", [(i, i ^ bits) for i in range(4)])

    first, second = [], []

    def send(part):
        second.append(swap(part, 3))
        first.append(swap(part, 1))
        return first[-1], second[-1]

    if paired:
        own = gather_paired(g_lesser, w_lesser, energy_index, groups, send)
        send(own[1])
    else:
        own = gather_shared(g_lesser, w_lesser, energy_index, groups)
        send(own[0]), send(own[1])
    zero = jnp.int32(0)
    sigma_lesser, total = own_product(here, own, retarded)
    third = [swap(after(second[0], total), 1)]
    total = step_product(here ^ 1, zero, [first], retarded, total)
    third.append(swap(after(second[1], total), 1))
    total, held = step_product(here ^ 3, zero, [second], retarded, total, here ^ 2)
    delta = last_product(zero, [third], held, total)
    return (sigma_lesser, delta)


def solution(mesh):
    return jax.shard_map(
        shards,
        mesh=mesh,
        in_specs=(
            P("energy", None, "space", None, None),
            P("energy", None, "space", None, None),
            P("energy", None, "space", None, None, None),
            P(),
        ),
        out_specs=(P("energy", None, "space", None, None), P("energy", None, "space", None, None)),
        check_vma=False,
    )
```

```python
import functools

import jax
import jax.numpy as jnp
from jax import lax
from jax.experimental import pallas as pl
from jax.experimental.pallas import tpu as pltpu
from jax.sharding import PartitionSpec as P


VMEM = pltpu.MemorySpace.VMEM
SMEM = pltpu.MemorySpace.SMEM
HBM = pltpu.MemorySpace.HBM

SMALL = pl.CostEstimate(flops=1, bytes_accessed=1, transcendentals=0)


def vmem(count):
    return [pl.BlockSpec(memory_space=VMEM)] * count


def params(mib):
    return pltpu.CompilerParams(vmem_limit_bytes=mib * 2**20)


def grid_of(shape, row_offset=0):
    rows = lax.broadcasted_iota(jnp.int32, shape, 0) + row_offset
    cols = lax.broadcasted_iota(jnp.int32, shape, 1)
    return rows, cols


def pack_kernel(green, screen, cross, tri):
    half = green.shape[-1] // 2
    rows, cols = grid_of((half, half))
    upper = rows < cols
    diagonal = rows == cols
    for place, source in enumerate((green, screen)):
        a_re = source[0, 0, 0, :half, :half].astype(jnp.float32)
        a_im = source[0, 1, 0, :half, :half].astype(jnp.float32)
        d_re = source[0, 0, 0, half:, half:].astype(jnp.float32)
        d_im = source[0, 1, 0, half:, half:].astype(jnp.float32)
        t_re = jnp.where(upper, a_re, jnp.where(diagonal, a_im, d_re)).astype(jnp.bfloat16)
        t_im = jnp.where(upper, a_im, d_im).astype(jnp.bfloat16)
        c_re = source[0, 0, 0, :half, half:]
        c_im = source[0, 1, 0, :half, half:]
        shape = cross.shape[:1] + cross.shape[3:]
        cross[:, place, 0] = c_re.reshape(shape)
        cross[:, place, 1] = c_im.reshape(shape)
        tri[:, place, 0] = t_re.reshape(shape)
        tri[:, place, 1] = t_im.reshape(shape)


def pack(green, screen, parts):
    half = green.shape[-1] // 2
    out = jax.ShapeDtypeStruct((parts, 2, 2, half // parts, half), jnp.bfloat16)
    return pl.pallas_call(
        pack_kernel,
        out_shape=(out, out),
        in_specs=vmem(2),
        out_specs=tuple(vmem(2)),
        compiler_params=params(24),
    )(green, screen)


def split_rows(packed, groups):
    _, fields, comps, half, width = packed.shape
    shaped = packed.reshape(fields, comps, groups, half // groups, width)
    return jnp.moveaxis(shaped, 2, 0)


def conv_kernel(has_diagonal, index, offset, pieces, out, green, screen, place):
    count, _, _, rows, width = pieces.shape

    def scatter(stored, carry):
        point = index[stored]
        place[point] = stored
        green[point] = pieces[stored, 0].astype(jnp.float32)
        screen[point] = pieces[stored, 1].astype(jnp.float32)
        return carry

    unroll = count <= 16
    lax.fori_loop(0, count, scatter, 0, unroll=unroll)
    scale = count**-0.5
    zero = jnp.zeros((rows, width), jnp.float32)

    def one(point, carry):
        total = point + count // 2

        def term(first, sums):
            both_re, both_im, mixed = sums
            g_re = green[first, 0]
            g_im = green[first, 1]
            w_re = screen[total - first, 0]
            w_im = screen[total - first, 1]
            return (
                both_re + g_re * w_re,
                both_im + g_im * w_im,
                mixed + g_re * w_im + g_im * w_re,
            )

        if unroll:
            sums = (zero, zero, zero)
            for first in range(max(0, total - count + 1), min(count - 1, total) + 1):
                sums = term(first, sums)
        else:
            low = jnp.maximum(0, total - count + 1)
            high = jnp.minimum(count - 1, total) + 1
            sums = lax.fori_loop(low, high, term, (zero, zero, zero))
        both_re, both_im, mixed = sums
        s_re = -scale * mixed
        s_im = scale * (both_re - both_im)
        if has_diagonal:
            at_rows, at_cols = grid_of((rows, width), offset[0])
            diagonal = at_rows == at_cols
            s_re = jnp.where(diagonal, -scale * both_re, s_re)
            s_im = jnp.where(diagonal, -scale * both_im, s_im)
        stored = place[point]
        out[stored, 0] = s_re.astype(jnp.bfloat16)
        out[stored, 1] = s_im.astype(jnp.bfloat16)
        return carry

    if unroll:
        for point in range(count):
            one(point, 0)
    else:
        lax.fori_loop(0, count, one, 0)


def convolve(pieces, energy_index, row_offset, has_diagonal):
    count, _, _, rows, width = pieces.shape
    smem = pl.BlockSpec(memory_space=SMEM)
    return pl.pallas_call(
        functools.partial(conv_kernel, has_diagonal),
        out_shape=jax.ShapeDtypeStruct((count, 2, rows, width), jnp.bfloat16),
        in_specs=[smem, smem] + vmem(1),
        out_specs=vmem(1)[0],
        scratch_shapes=[
            pltpu.VMEM((count, 2, rows, width), jnp.float32),
            pltpu.VMEM((count, 2, rows, width), jnp.float32),
            pltpu.SMEM((count,), jnp.int32),
        ],
        compiler_params=params(24),
    )(energy_index, row_offset, pieces)


def share_of(me, d, rows):
    return pl.ds(pl.multiple_of((lax.shift_right_logical(me, 1) ^ d) * rows, rows), rows)


def cut_kernel(chips, me, green, screen, *rest):
    outs = rest[:chips]
    near, far, sems, cross_sems = rest[chips:]
    half = near.shape[-1]
    rows = half // chips
    copies = []
    for field, source in enumerate((green, screen)):
        for place, (held, lines) in enumerate(((near, slice(0, half)), (far, slice(half, None)))):
            copy = pltpu.make_async_copy(
                source.at[0, :, 0, lines, lines], held.at[field], sems.at[field, place]
            )
            copy.start()
            copies.append(copy)
    cross_copies = []
    for d in range(chips):
        for field, source in enumerate((green, screen)):
            part = source.at[0, :, 0, share_of(me[0], d, rows), half:]
            copy = pltpu.make_async_copy(part, outs[d].at[0, field], cross_sems.at[d, field])
            copy.start()
            cross_copies.append(copy)
    at_rows, at_cols = grid_of((rows, half))
    for field in range(2):
        for copy in copies[2 * field : 2 * field + 2]:
            copy.wait()
        for d in range(chips):
            lines = share_of(me[0], d, rows)
            here = at_rows + (lax.shift_right_logical(me[0], 1) ^ d) * rows
            upper = here < at_cols
            diagonal = here == at_cols
            a_re = near[field, 0, lines, :].astype(jnp.float32)
            a_im = near[field, 1, lines, :].astype(jnp.float32)
            d_re = far[field, 0, lines, :].astype(jnp.float32)
            d_im = far[field, 1, lines, :].astype(jnp.float32)
            t_re = jnp.where(upper, a_re, jnp.where(diagonal, a_im, d_re))
            outs[d][1, field, 0] = t_re.astype(jnp.bfloat16)
            outs[d][1, field, 1] = jnp.where(upper, a_im, d_im).astype(jnp.bfloat16)
    for copy in cross_copies:
        copy.wait()


def cut(me, green, screen, chips):
    half = green.shape[-1] // 2
    piece = jax.ShapeDtypeStruct((2, 2, 2, half // chips, half), jnp.bfloat16)
    return pl.pallas_call(
        functools.partial(cut_kernel, chips),
        out_shape=(piece,) * chips,
        in_specs=[pl.BlockSpec(memory_space=SMEM)] + [pl.BlockSpec(memory_space=HBM)] * 2,
        out_specs=tuple(vmem(chips)),
        scratch_shapes=[pltpu.VMEM((2, 2, half, half), jnp.bfloat16)] * 2
        + [pltpu.SemaphoreType.DMA((2, 2)), pltpu.SemaphoreType.DMA((chips, 2))],
        compiler_params=params(52),
        cost_estimate=SMALL,
    )(me, green, screen)


def bind_kernel(part, *refs):
    for place, piece in enumerate(refs[:-1]):
        refs[-1][place] = piece[part]


def bind(pieces, part):
    shape = (len(pieces),) + pieces[0].shape[1:]
    return pl.pallas_call(
        functools.partial(bind_kernel, part),
        out_shape=jax.ShapeDtypeStruct(shape, jnp.bfloat16),
        in_specs=vmem(len(pieces)),
        out_specs=vmem(1)[0],
        compiler_params=params(32),
        cost_estimate=SMALL,
    )(*pieces)


def conv_pieces_kernel(chips, part, me, index, *rest):
    same = rest[:chips][::-1]
    beside, other = rest[chips : chips + 2]
    outs = rest[chips + 2 : 2 * chips + 2]
    green, screen, sums, place = rest[2 * chips + 2 :]
    groups = 2 * chips
    rows, width = sums.shape[2:]
    for core in range(2):
        for d in range(chips):
            stored = me[0] ^ (2 * d + core)
            point = index[stored]
            place[point] = stored
            if core == 0:
                green[point] = same[d][part, 0]
                screen[point] = same[d][part, 1]
            elif d == 0:
                green[point] = beside[part, 0]
                screen[point] = beside[part, 1]
            else:
                green[point] = other[chips - 1 - d, 0]
                screen[point] = other[chips - 1 - d, 1]
    scale = groups**-0.5
    tall = 16
    for point in range(groups):

        @pl.when(((place[point] ^ me[0]) & 1) == 0)
        def _():
            total = point + groups // 2
            for first_row in range(0, rows, tall):
                for first_col in range(0, width, 128):
                    at = (slice(first_row, first_row + tall), slice(first_col, first_col + 128))
                    both_re = both_im = mixed = None
                    for p in range(max(0, total - groups + 1), min(groups - 1, total) + 1):
                        g_re = green[(p, 0) + at].astype(jnp.float32)
                        g_im = green[(p, 1) + at].astype(jnp.float32)
                        w_re = screen[(total - p, 0) + at].astype(jnp.float32)
                        w_im = screen[(total - p, 1) + at].astype(jnp.float32)
                        re = g_re * w_re
                        im = g_im * w_im
                        mix = g_re * w_im + g_im * w_re
                        both_re = re if both_re is None else both_re + re
                        both_im = im if both_im is None else both_im + im
                        mixed = mix if mixed is None else mixed + mix
                    s_re = -scale * mixed
                    s_im = scale * (both_re - both_im)
                    if part == 1:
                        first = lax.shift_right_logical(me[0], 1) * rows + first_row
                        at_rows, at_cols = grid_of((tall, 128), first)
                        diagonal = at_rows == at_cols + first_col
                        s_re = jnp.where(diagonal, -scale * both_re, s_re)
                        s_im = jnp.where(diagonal, -scale * both_im, s_im)
                    sums[(point, 0) + at] = s_re.astype(jnp.bfloat16)
                    sums[(point, 1) + at] = s_im.astype(jnp.bfloat16)

    for d in range(chips):
        outs[d][...] = sums[index[me[0] ^ (2 * d)]]


def conv_pieces(me, energy_index, same, beside, other, part):
    chips = len(same)
    shape = same[0].shape[2:]
    smem = pl.BlockSpec(memory_space=SMEM)
    return pl.pallas_call(
        functools.partial(conv_pieces_kernel, chips, part),
        out_shape=(jax.ShapeDtypeStruct(shape, jnp.bfloat16),) * chips,
        in_specs=[smem, smem] + vmem(chips + 2),
        out_specs=tuple(vmem(chips)),
        scratch_shapes=[pltpu.VMEM((2 * chips,) + shape, jnp.bfloat16)] * 3
        + [pltpu.SMEM((2 * chips,), jnp.int32)],
        compiler_params=params(32),
        cost_estimate=SMALL,
    )(me, energy_index, *same[::-1], beside, other)


def join_kernel(chips, me, *rest):
    pieces, out = rest[:chips][::-1], rest[chips]
    rows = pieces[0].shape[1]
    for d in range(chips):
        out[:, share_of(me[0], d, rows), :] = pieces[d][...]


def join(me, pieces):
    half = pieces[0].shape[-1]
    return pl.pallas_call(
        functools.partial(join_kernel, len(pieces)),
        out_shape=jax.ShapeDtypeStruct((2, half, half), jnp.bfloat16),
        in_specs=[pl.BlockSpec(memory_space=SMEM)] + vmem(len(pieces)),
        out_specs=vmem(1)[0],
        compiler_params=params(32),
        cost_estimate=SMALL,
    )(me, *pieces[::-1])


def swap(piece, d, groups):
    return lax.ppermute(piece, "energy", [(i, i ^ d) for i in range(groups)]) if d else piece


def after(value, *earlier):
    return lax.optimization_barrier((value, earlier))[0]


def gather_paired(g_lesser, w_lesser, energy_index, groups, send=lambda part: ()):
    me = lax.axis_index("energy").astype(jnp.int32).reshape(1)
    chips = groups // 2

    def over(pieces):
        return [swap(pieces[d], 2 * d, groups) for d in range(chips)]

    pieces = cut(me, g_lesser, w_lesser, chips)
    same = over(pieces)
    beside = swap(pieces[0], 1, groups)
    bound = [bind(after(same[:0:-1], beside), part) for part in range(2)]
    other = [swap(piece, 1, groups) for piece in bound]
    mine = conv_pieces(me, energy_index, same, beside, other[0], 0)
    shares = over(mine)
    own_cross = join(me, shares)
    sent = send(own_cross)
    mine = conv_pieces(me, energy_index, same, beside, after(other[1], own_cross), 1)
    own_tri = join(me, over(mine))
    return own_cross, own_tri


def gather_shared(g_lesser, w_lesser, energy_index, groups):
    half = g_lesser.shape[-1] // 2
    rows = half // groups
    cross, tri = (split_rows(packed, groups) for packed in pack(g_lesser, w_lesser, 1))
    offset = (lax.axis_index("energy") * rows).astype(jnp.int32).reshape(1)
    own = []
    for pieces, has_diagonal in ((cross, False), (tri, True)):
        shares = convolve(exchange(pieces), energy_index, offset, has_diagonal)
        own.append(jnp.moveaxis(exchange(shares), 0, 1).reshape(2, half, half))
    return own


def squares(cross, tri):
    return cross[0], cross[1], tri[0], tri[1]


def dot(a, b):
    return jnp.dot(a, b, preferred_element_type=jnp.float32)


def dot_t(a, b):
    return lax.dot_general(a, b, (((1,), (1,)), ((), ())), preferred_element_type=jnp.float32)


def product(cross, tri, retarded):
    c_re, c_im, t_re, t_im = squares(cross, tri)
    half = c_re.shape[0]
    rows, cols = grid_of((half, half))
    tr = t_re.astype(jnp.float32)
    ti = t_im.astype(jnp.float32)
    diagonal = rows == cols
    a_re = jnp.where(rows < cols, tr, 0.0).astype(jnp.bfloat16)
    a_im = jnp.where(rows < cols, ti, jnp.where(diagonal, 0.5 * tr, 0.0)).astype(jnp.bfloat16)
    d_re = jnp.where(rows > cols, tr, 0.0).astype(jnp.bfloat16)
    d_im = jnp.where(rows > cols, ti, jnp.where(diagonal, 0.5 * ti, 0.0)).astype(jnp.bfloat16)
    g_re = retarded[0]
    g_im = retarded[1]
    near = jnp.concatenate([g_re[:, :half], g_im[:, :half]], axis=1)
    far = jnp.concatenate([g_re, g_im], axis=1)
    l_re = jnp.concatenate(
        [
            dot(near, jnp.concatenate([a_re, -a_im], axis=0)),
            dot(far, jnp.concatenate([c_re, d_re, -c_im, -d_im], axis=0)),
        ],
        axis=1,
    ).astype(jnp.bfloat16)
    l_im = jnp.concatenate(
        [
            dot(near, jnp.concatenate([a_im, a_re], axis=0)),
            dot(far, jnp.concatenate([c_im, d_im, c_re, d_re], axis=0)),
        ],
        axis=1,
    ).astype(jnp.bfloat16)
    x_re = dot_t(jnp.concatenate([l_re, l_im], axis=1), far)
    x_im = dot_t(jnp.concatenate([l_im, -l_re], axis=1), far)
    return x_re, x_im


def own_kernel(where, cross, tri, retarded, sigma, total, block, sem):
    copy = pltpu.make_async_copy(retarded.at[0, :, 0, where[0]], block, sem)
    copy.start()
    c_re, c_im, t_re, t_im = squares(cross, tri)
    half = c_re.shape[0]
    rows, cols = grid_of((half, half))
    upper = rows < cols
    diagonal = rows == cols
    tr = t_re.astype(jnp.float32)
    ti = t_im.astype(jnp.float32)
    trt = tr.T
    tit = ti.T
    zero = jnp.zeros_like(tr)
    bf = jnp.bfloat16
    sigma[0, 0, 0, :half, half:] = c_re
    sigma[0, 1, 0, :half, half:] = c_im
    sigma[0, 0, 0, half:, :half] = (-(c_re.astype(jnp.float32).T)).astype(bf)
    sigma[0, 1, 0, half:, :half] = c_im.astype(jnp.float32).T.astype(bf)
    sigma[0, 0, 0, :half, :half] = jnp.where(upper, tr, jnp.where(diagonal, zero, -trt)).astype(bf)
    sigma[0, 1, 0, :half, :half] = jnp.where(upper, ti, jnp.where(diagonal, tr, tit)).astype(bf)
    sigma[0, 0, 0, half:, half:] = jnp.where(upper, -trt, jnp.where(diagonal, zero, tr)).astype(bf)
    sigma[0, 1, 0, half:, half:] = jnp.where(upper, tit, ti).astype(bf)
    copy.wait()
    total[0], total[1] = product(cross, tri, block)


def step_kernel(count, last, ahead, where, *rest):
    if last:
        block, total = rest[:2]
        sources = rest[2 : 2 + 2 * count]
        out = rest[-1]
    else:
        sources = rest[: 2 * count]
        rest = rest[2 * count :]
    if last:
        pass
    elif ahead:
        retarded, total, out, later, block, sems = rest
        fetch = pltpu.make_async_copy(retarded.at[0, :, 0, where[0]], block, sems.at[0])
        fetch.start()
        prefetch = pltpu.make_async_copy(retarded.at[0, :, 0, where[2]], later, sems.at[1])
        prefetch.start()
        fetch.wait()
    else:
        retarded, total, out, block, sems = rest
        fetch = pltpu.make_async_copy(retarded.at[0, :, 0, where[0]], block, sems.at[0])
        fetch.start()
        fetch.wait()
    for pick in range(count):

        @pl.when(where[1] == pick)
        def _():
            cross, tri = sources[pick], sources[count + pick]
            x_re, x_im = product(cross, tri, block)
            x_re += total[0]
            x_im += total[1]
            if last:
                out[0, 0, 0] = (x_re - x_re.T).astype(jnp.bfloat16)
                out[0, 1, 0] = (x_im + x_im.T).astype(jnp.bfloat16)
            else:
                out[0] = x_re
                out[1] = x_im

    if ahead:
        prefetch.wait()


def cost(width):
    return pl.CostEstimate(flops=14 * width**3, bytes_accessed=8 * width**2, transcendentals=0)


def own_product(block, own, retarded):
    width = retarded.shape[-1]
    return pl.pallas_call(
        own_kernel,
        out_shape=(
            jax.ShapeDtypeStruct((1, 2, 1, width, width), jnp.bfloat16),
            jax.ShapeDtypeStruct((2, width, width), jnp.float32),
        ),
        in_specs=[pl.BlockSpec(memory_space=SMEM)] + vmem(2) + [pl.BlockSpec(memory_space=HBM)],
        out_specs=tuple(vmem(2)),
        scratch_shapes=[pltpu.VMEM((2, width, width), jnp.bfloat16), pltpu.SemaphoreType.DMA],
        compiler_params=params(48),
        cost_estimate=cost(width),
    )(block.reshape(1), *own, retarded)


def step_product(block, pick, sources, retarded, total, later=None):
    width = retarded.shape[-1]
    flat = [source[part] for part in range(2) for source in sources]
    ahead = later is not None
    numbers = jnp.stack([block, pick] + ([later] if ahead else []))
    total_shape = jax.ShapeDtypeStruct((2, width, width), jnp.float32)
    block_shape = jax.ShapeDtypeStruct((2, width, width), jnp.bfloat16)
    return pl.pallas_call(
        functools.partial(step_kernel, len(sources), False, ahead),
        out_shape=(total_shape, block_shape) if ahead else total_shape,
        in_specs=[pl.BlockSpec(memory_space=SMEM)]
        + vmem(len(flat))
        + [pl.BlockSpec(memory_space=HBM)]
        + vmem(1),
        out_specs=tuple(vmem(2)) if ahead else vmem(1)[0],
        scratch_shapes=[pltpu.VMEM((2, width, width), jnp.bfloat16), pltpu.SemaphoreType.DMA((2,))],
        compiler_params=params(46),
        cost_estimate=cost(width),
    )(numbers, *flat, retarded, total)


def last_product(pick, sources, block, total):
    width = block.shape[-1]
    flat = [source[part] for part in range(2) for source in sources]
    return pl.pallas_call(
        functools.partial(step_kernel, len(sources), True, False),
        out_shape=jax.ShapeDtypeStruct((1, 2, 1, width, width), jnp.bfloat16),
        in_specs=[pl.BlockSpec(memory_space=SMEM)] + vmem(len(flat) + 2),
        out_specs=vmem(1)[0],
        compiler_params=params(48),
        cost_estimate=cost(width),
    )(jnp.stack([pick, pick]), block, total, *flat)


def exchange(pieces):
    return lax.all_to_all(pieces, "energy", split_axis=0, concat_axis=0, tiled=True)


def shards(g_lesser, w_lesser, g_retarded, energy_index):
    width = g_lesser.shape[-1]
    groups = lax.axis_size("energy")
    chain = lax.axis_size("space")
    here = lax.axis_index("space")
    paired = groups >= 4 and groups & (groups - 1) == 0 and (width // groups) % 16 == 0
    here = here.astype(jnp.int32)
    if chain == 4:
        return around_line(here, paired, g_lesser, w_lesser, energy_index, groups, g_retarded)
    gather = gather_paired if paired else gather_shared
    own = gather(g_lesser, w_lesser, energy_index, groups)
    everyone = [lax.all_gather(part, "space") for part in own]
    sigma_lesser, total = own_product(here, own, g_retarded)
    zero = jnp.int32(0)

    def source(block):
        return tuple(lax.dynamic_index_in_dim(part, block, 0, False) for part in everyone)

    for step in range(1, chain - 1):
        block = (here + step) % chain
        later = (block + 1) % chain
        total, held = step_product(block, zero, [source(block)], g_retarded, total, later)
    return (sigma_lesser, last_product(zero, [source(later)], held, total))


def around_line(here, paired, g_lesser, w_lesser, energy_index, groups, retarded):
    def swap(part, bits):
        return lax.ppermute(part, "space", [(i, i ^ bits) for i in range(4)])

    first, second = [], []

    def send(part):
        second.append(swap(part, 3))
        first.append(swap(part, 1))
        return first[-1], second[-1]

    if paired:
        own = gather_paired(g_lesser, w_lesser, energy_index, groups, send)
        second.append(swap(own[1], 3))
        first.append(swap(after(own[1], second[0], first[0]), 1))
    else:
        own = gather_shared(g_lesser, w_lesser, energy_index, groups)
        send(own[0]), send(own[1])
    zero = jnp.int32(0)
    sigma_lesser, total = own_product(here, own, retarded)
    third = [swap(second[0], 1), swap(second[1], 1)]
    total = step_product(here ^ 3, zero, [second], retarded, total)
    total, held = step_product(here ^ 1, zero, [first], retarded, total, here ^ 2)
    delta = last_product(zero, [third], held, total)
    return (sigma_lesser, delta)


def solution(mesh):
    return jax.shard_map(
        shards,
        mesh=mesh,
        in_specs=(
            P("energy", None, "space", None, None),
            P("energy", None, "space", None, None),
            P("energy", None, "space", None, None, None),
            P(),
        ),
        out_specs=(P("energy", None, "space", None, None), P("energy", None, "space", None, None)),
        check_vma=False,
    )
```

```python
import functools

import jax
import jax.numpy as jnp
from jax import lax
from jax.experimental import pallas as pl
from jax.experimental.pallas import tpu as pltpu
from jax.sharding import PartitionSpec as P


VMEM = pltpu.MemorySpace.VMEM
SMEM = pltpu.MemorySpace.SMEM
HBM = pltpu.MemorySpace.HBM

SMALL = pl.CostEstimate(flops=1, bytes_accessed=1, transcendentals=0)


def vmem(count):
    return [pl.BlockSpec(memory_space=VMEM)] * count


def params(mib):
    return pltpu.CompilerParams(vmem_limit_bytes=mib * 2**20)


def grid_of(shape, row_offset=0):
    rows = lax.broadcasted_iota(jnp.int32, shape, 0) + row_offset
    cols = lax.broadcasted_iota(jnp.int32, shape, 1)
    return rows, cols


def pack_kernel(green, screen, cross, tri):
    half = green.shape[-1] // 2
    rows, cols = grid_of((half, half))
    upper = rows < cols
    diagonal = rows == cols
    for place, source in enumerate((green, screen)):
        a_re = source[0, 0, 0, :half, :half].astype(jnp.float32)
        a_im = source[0, 1, 0, :half, :half].astype(jnp.float32)
        d_re = source[0, 0, 0, half:, half:].astype(jnp.float32)
        d_im = source[0, 1, 0, half:, half:].astype(jnp.float32)
        t_re = jnp.where(upper, a_re, jnp.where(diagonal, a_im, d_re)).astype(jnp.bfloat16)
        t_im = jnp.where(upper, a_im, d_im).astype(jnp.bfloat16)
        c_re = source[0, 0, 0, :half, half:]
        c_im = source[0, 1, 0, :half, half:]
        shape = cross.shape[:1] + cross.shape[3:]
        cross[:, place, 0] = c_re.reshape(shape)
        cross[:, place, 1] = c_im.reshape(shape)
        tri[:, place, 0] = t_re.reshape(shape)
        tri[:, place, 1] = t_im.reshape(shape)


def pack(green, screen, parts):
    half = green.shape[-1] // 2
    out = jax.ShapeDtypeStruct((parts, 2, 2, half // parts, half), jnp.bfloat16)
    return pl.pallas_call(
        pack_kernel,
        out_shape=(out, out),
        in_specs=vmem(2),
        out_specs=tuple(vmem(2)),
        compiler_params=params(24),
    )(green, screen)


def split_rows(packed, groups):
    _, fields, comps, half, width = packed.shape
    shaped = packed.reshape(fields, comps, groups, half // groups, width)
    return jnp.moveaxis(shaped, 2, 0)


def conv_kernel(has_diagonal, index, offset, pieces, out, green, screen, place):
    count, _, _, rows, width = pieces.shape

    def scatter(stored, carry):
        point = index[stored]
        place[point] = stored
        green[point] = pieces[stored, 0].astype(jnp.float32)
        screen[point] = pieces[stored, 1].astype(jnp.float32)
        return carry

    unroll = count <= 16
    lax.fori_loop(0, count, scatter, 0, unroll=unroll)
    scale = count**-0.5
    zero = jnp.zeros((rows, width), jnp.float32)

    def one(point, carry):
        total = point + count // 2

        def term(first, sums):
            both_re, both_im, mixed = sums
            g_re = green[first, 0]
            g_im = green[first, 1]
            w_re = screen[total - first, 0]
            w_im = screen[total - first, 1]
            return (
                both_re + g_re * w_re,
                both_im + g_im * w_im,
                mixed + g_re * w_im + g_im * w_re,
            )

        if unroll:
            sums = (zero, zero, zero)
            for first in range(max(0, total - count + 1), min(count - 1, total) + 1):
                sums = term(first, sums)
        else:
            low = jnp.maximum(0, total - count + 1)
            high = jnp.minimum(count - 1, total) + 1
            sums = lax.fori_loop(low, high, term, (zero, zero, zero))
        both_re, both_im, mixed = sums
        s_re = -scale * mixed
        s_im = scale * (both_re - both_im)
        if has_diagonal:
            at_rows, at_cols = grid_of((rows, width), offset[0])
            diagonal = at_rows == at_cols
            s_re = jnp.where(diagonal, -scale * both_re, s_re)
            s_im = jnp.where(diagonal, -scale * both_im, s_im)
        stored = place[point]
        out[stored, 0] = s_re.astype(jnp.bfloat16)
        out[stored, 1] = s_im.astype(jnp.bfloat16)
        return carry

    if unroll:
        for point in range(count):
            one(point, 0)
    else:
        lax.fori_loop(0, count, one, 0)


def convolve(pieces, energy_index, row_offset, has_diagonal):
    count, _, _, rows, width = pieces.shape
    smem = pl.BlockSpec(memory_space=SMEM)
    return pl.pallas_call(
        functools.partial(conv_kernel, has_diagonal),
        out_shape=jax.ShapeDtypeStruct((count, 2, rows, width), jnp.bfloat16),
        in_specs=[smem, smem] + vmem(1),
        out_specs=vmem(1)[0],
        scratch_shapes=[
            pltpu.VMEM((count, 2, rows, width), jnp.float32),
            pltpu.VMEM((count, 2, rows, width), jnp.float32),
            pltpu.SMEM((count,), jnp.int32),
        ],
        compiler_params=params(24),
    )(energy_index, row_offset, pieces)


def share_of(me, d, rows):
    return pl.ds(pl.multiple_of((lax.shift_right_logical(me, 1) ^ d) * rows, rows), rows)


def cut_kernel(chips, me, green, screen, *rest):
    outs = rest[:chips]
    near, far, sems, cross_sems = rest[chips:]
    half = near.shape[-1]
    rows = half // chips
    copies = []
    for field, source in enumerate((green, screen)):
        for place, (held, lines) in enumerate(((near, slice(0, half)), (far, slice(half, None)))):
            copy = pltpu.make_async_copy(
                source.at[0, :, 0, lines, lines], held.at[field], sems.at[field, place]
            )
            copy.start()
            copies.append(copy)
    cross_copies = []
    for d in range(chips):
        for field, source in enumerate((green, screen)):
            part = source.at[0, :, 0, share_of(me[0], d, rows), half:]
            copy = pltpu.make_async_copy(part, outs[d].at[0, field], cross_sems.at[d, field])
            copy.start()
            cross_copies.append(copy)
    at_rows, at_cols = grid_of((rows, half))
    for field in range(2):
        for copy in copies[2 * field : 2 * field + 2]:
            copy.wait()
        for d in range(chips):
            lines = share_of(me[0], d, rows)
            here = at_rows + (lax.shift_right_logical(me[0], 1) ^ d) * rows
            upper = here < at_cols
            diagonal = here == at_cols
            a_re = near[field, 0, lines, :].astype(jnp.float32)
            a_im = near[field, 1, lines, :].astype(jnp.float32)
            d_re = far[field, 0, lines, :].astype(jnp.float32)
            d_im = far[field, 1, lines, :].astype(jnp.float32)
            t_re = jnp.where(upper, a_re, jnp.where(diagonal, a_im, d_re))
            outs[d][1, field, 0] = t_re.astype(jnp.bfloat16)
            outs[d][1, field, 1] = jnp.where(upper, a_im, d_im).astype(jnp.bfloat16)
    for copy in cross_copies:
        copy.wait()


def cut(me, green, screen, chips):
    half = green.shape[-1] // 2
    piece = jax.ShapeDtypeStruct((2, 2, 2, half // chips, half), jnp.bfloat16)
    return pl.pallas_call(
        functools.partial(cut_kernel, chips),
        out_shape=(piece,) * chips,
        in_specs=[pl.BlockSpec(memory_space=SMEM)] + [pl.BlockSpec(memory_space=HBM)] * 2,
        out_specs=tuple(vmem(chips)),
        scratch_shapes=[pltpu.VMEM((2, 2, half, half), jnp.bfloat16)] * 2
        + [pltpu.SemaphoreType.DMA((2, 2)), pltpu.SemaphoreType.DMA((chips, 2))],
        compiler_params=params(52),
        cost_estimate=SMALL,
    )(me, green, screen)


def bind_kernel(part, *refs):
    for place, piece in enumerate(refs[:-1]):
        refs[-1][place] = piece[part]


def bind(pieces, part):
    shape = (len(pieces),) + pieces[0].shape[1:]
    return pl.pallas_call(
        functools.partial(bind_kernel, part),
        out_shape=jax.ShapeDtypeStruct(shape, jnp.bfloat16),
        in_specs=vmem(len(pieces)),
        out_specs=vmem(1)[0],
        compiler_params=params(32),
        cost_estimate=SMALL,
    )(*pieces)


def conv_pieces_kernel(chips, part, me, index, *rest):
    same = rest[:chips][::-1]
    beside, other = rest[chips : chips + 2]
    outs = rest[chips + 2 : 2 * chips + 2]
    green, screen, sums, place = rest[2 * chips + 2 :]
    groups = 2 * chips
    rows, width = sums.shape[2:]
    for core in range(2):
        for d in range(chips):
            stored = me[0] ^ (2 * d + core)
            point = index[stored]
            place[point] = stored
            if core == 0:
                green[point] = same[d][part, 0]
                screen[point] = same[d][part, 1]
            elif d == 0:
                green[point] = beside[part, 0]
                screen[point] = beside[part, 1]
            else:
                green[point] = other[chips - 1 - d, 0]
                screen[point] = other[chips - 1 - d, 1]
    scale = groups**-0.5
    tall = 16
    for point in range(groups):

        @pl.when(((place[point] ^ me[0]) & 1) == 0)
        def _():
            total = point + groups // 2
            for first_row in range(0, rows, tall):
                for first_col in range(0, width, 128):
                    at = (slice(first_row, first_row + tall), slice(first_col, first_col + 128))
                    both_re = both_im = mixed = None
                    for p in range(max(0, total - groups + 1), min(groups - 1, total) + 1):
                        g_re = green[(p, 0) + at].astype(jnp.float32)
                        g_im = green[(p, 1) + at].astype(jnp.float32)
                        w_re = screen[(total - p, 0) + at].astype(jnp.float32)
                        w_im = screen[(total - p, 1) + at].astype(jnp.float32)
                        re = g_re * w_re
                        im = g_im * w_im
                        mix = g_re * w_im + g_im * w_re
                        both_re = re if both_re is None else both_re + re
                        both_im = im if both_im is None else both_im + im
                        mixed = mix if mixed is None else mixed + mix
                    s_re = -scale * mixed
                    s_im = scale * (both_re - both_im)
                    if part == 1:
                        first = lax.shift_right_logical(me[0], 1) * rows + first_row
                        at_rows, at_cols = grid_of((tall, 128), first)
                        diagonal = at_rows == at_cols + first_col
                        s_re = jnp.where(diagonal, -scale * both_re, s_re)
                        s_im = jnp.where(diagonal, -scale * both_im, s_im)
                    sums[(point, 0) + at] = s_re.astype(jnp.bfloat16)
                    sums[(point, 1) + at] = s_im.astype(jnp.bfloat16)

    for d in range(chips):
        outs[d][...] = sums[index[me[0] ^ (2 * d)]]


def conv_pieces(me, energy_index, same, beside, other, part):
    chips = len(same)
    shape = same[0].shape[2:]
    smem = pl.BlockSpec(memory_space=SMEM)
    return pl.pallas_call(
        functools.partial(conv_pieces_kernel, chips, part),
        out_shape=(jax.ShapeDtypeStruct(shape, jnp.bfloat16),) * chips,
        in_specs=[smem, smem] + vmem(chips + 2),
        out_specs=tuple(vmem(chips)),
        scratch_shapes=[pltpu.VMEM((2 * chips,) + shape, jnp.bfloat16)] * 3
        + [pltpu.SMEM((2 * chips,), jnp.int32)],
        compiler_params=params(32),
        cost_estimate=SMALL,
    )(me, energy_index, *same[::-1], beside, other)


def join_kernel(chips, me, *rest):
    pieces, out = rest[:chips][::-1], rest[chips]
    rows = pieces[0].shape[1]
    for d in range(chips):
        out[:, share_of(me[0], d, rows), :] = pieces[d][...]


def join(me, pieces):
    half = pieces[0].shape[-1]
    return pl.pallas_call(
        functools.partial(join_kernel, len(pieces)),
        out_shape=jax.ShapeDtypeStruct((2, half, half), jnp.bfloat16),
        in_specs=[pl.BlockSpec(memory_space=SMEM)] + vmem(len(pieces)),
        out_specs=vmem(1)[0],
        compiler_params=params(32),
        cost_estimate=SMALL,
    )(me, *pieces[::-1])


def swap(piece, d, groups):
    return lax.ppermute(piece, "energy", [(i, i ^ d) for i in range(groups)]) if d else piece


def after(value, *earlier):
    return lax.optimization_barrier((value, earlier))[0]


def gather_paired(g_lesser, w_lesser, energy_index, groups, send):
    me = lax.axis_index("energy").astype(jnp.int32).reshape(1)
    chips = groups // 2

    def over(pieces):
        return [swap(pieces[d], 2 * d, groups) for d in range(chips)]

    pieces = cut(me, g_lesser, w_lesser, chips)
    same = over(pieces)
    beside = swap(pieces[0], 1, groups)
    bound = [bind(after(same[:0:-1], beside), part) for part in range(2)]
    other = [swap(piece, 1, groups) for piece in bound]
    mine = conv_pieces(me, energy_index, same, beside, other[1], 1)
    own_tri = join(me, over(mine))
    send(own_tri)
    mine = conv_pieces(me, energy_index, same, beside, after(other[0], own_tri), 0)
    own_cross = join(me, over(mine))
    return own_cross, own_tri


def gather_shared(g_lesser, w_lesser, energy_index, groups):
    half = g_lesser.shape[-1] // 2
    rows = half // groups
    cross, tri = (split_rows(packed, groups) for packed in pack(g_lesser, w_lesser, 1))
    offset = (lax.axis_index("energy") * rows).astype(jnp.int32).reshape(1)
    own = []
    for pieces, has_diagonal in ((cross, False), (tri, True)):
        shares = convolve(exchange(pieces), energy_index, offset, has_diagonal)
        own.append(jnp.moveaxis(exchange(shares), 0, 1).reshape(2, half, half))
    return own


def squares(cross, tri):
    return cross[0], cross[1], tri[0], tri[1]


def dot(a, b):
    return jnp.dot(a, b, preferred_element_type=jnp.float32)


def dot_t(a, b):
    return lax.dot_general(a, b, (((1,), (1,)), ((), ())), preferred_element_type=jnp.float32)


def product(cross, tri, retarded):
    return product_of(cross, tri, retarded)


def product_of(cross, tri, retarded):
    t_re, t_im = tri[0], tri[1]
    half = t_re.shape[0]
    rows, cols = grid_of((half, half))
    tr = t_re.astype(jnp.float32)
    ti = t_im.astype(jnp.float32)
    diagonal = rows == cols
    a_re = jnp.where(rows < cols, tr, 0.0).astype(jnp.bfloat16)
    a_im = jnp.where(rows < cols, ti, jnp.where(diagonal, 0.5 * tr, 0.0)).astype(jnp.bfloat16)
    d_re = jnp.where(rows > cols, tr, 0.0).astype(jnp.bfloat16)
    d_im = jnp.where(rows > cols, ti, jnp.where(diagonal, 0.5 * ti, 0.0)).astype(jnp.bfloat16)
    g_re = retarded[0]
    g_im = retarded[1]
    near = jnp.concatenate([g_re[:, :half], g_im[:, :half]], axis=1)
    all_g = jnp.concatenate([g_re, g_im], axis=1)
    if cross is None:
        far = jnp.concatenate([g_re[:, half:], g_im[:, half:]], axis=1)
        right_re = [d_re, -d_im]
        right_im = [d_im, d_re]
    else:
        c_re, c_im = cross[0], cross[1]
        far = all_g
        right_re = [c_re, d_re, -c_im, -d_im]
        right_im = [c_im, d_im, c_re, d_re]
    l_re = jnp.concatenate(
        [
            dot(near, jnp.concatenate([a_re, -a_im], axis=0)),
            dot(far, jnp.concatenate(right_re, axis=0)),
        ],
        axis=1,
    ).astype(jnp.bfloat16)
    l_im = jnp.concatenate(
        [
            dot(near, jnp.concatenate([a_im, a_re], axis=0)),
            dot(far, jnp.concatenate(right_im, axis=0)),
        ],
        axis=1,
    ).astype(jnp.bfloat16)
    x_re = dot_t(jnp.concatenate([l_re, l_im], axis=1), all_g)
    x_im = dot_t(jnp.concatenate([l_im, -l_re], axis=1), all_g)
    return x_re, x_im


def tri_product(tri, retarded):
    return product_of(None, tri, retarded)


def cross_product(cross, retarded):
    c_re, c_im = cross[0], cross[1]
    half = c_re.shape[0]
    g_re = retarded[0]
    g_im = retarded[1]
    near = jnp.concatenate([g_re[:, :half], g_im[:, :half]], axis=1)
    far = jnp.concatenate([g_re[:, half:], g_im[:, half:]], axis=1)
    l_re = dot(near, jnp.concatenate([c_re, -c_im], axis=0)).astype(jnp.bfloat16)
    l_im = dot(near, jnp.concatenate([c_im, c_re], axis=0)).astype(jnp.bfloat16)
    x_re = dot_t(jnp.concatenate([l_re, l_im], axis=1), far)
    x_im = dot_t(jnp.concatenate([l_im, -l_re], axis=1), far)
    return x_re, x_im


def own_kernel(where, cross, tri, retarded, sigma, total, block, sem):
    copy = pltpu.make_async_copy(retarded.at[0, :, 0, where[0]], block, sem)
    copy.start()
    c_re, c_im, t_re, t_im = squares(cross, tri)
    half = c_re.shape[0]
    rows, cols = grid_of((half, half))
    upper = rows < cols
    diagonal = rows == cols
    tr = t_re.astype(jnp.float32)
    ti = t_im.astype(jnp.float32)
    trt = tr.T
    tit = ti.T
    zero = jnp.zeros_like(tr)
    bf = jnp.bfloat16
    sigma[0, 0, 0, :half, half:] = c_re
    sigma[0, 1, 0, :half, half:] = c_im
    sigma[0, 0, 0, half:, :half] = (-(c_re.astype(jnp.float32).T)).astype(bf)
    sigma[0, 1, 0, half:, :half] = c_im.astype(jnp.float32).T.astype(bf)
    sigma[0, 0, 0, :half, :half] = jnp.where(upper, tr, jnp.where(diagonal, zero, -trt)).astype(bf)
    sigma[0, 1, 0, :half, :half] = jnp.where(upper, ti, jnp.where(diagonal, tr, tit)).astype(bf)
    sigma[0, 0, 0, half:, half:] = jnp.where(upper, -trt, jnp.where(diagonal, zero, tr)).astype(bf)
    sigma[0, 1, 0, half:, half:] = jnp.where(upper, tit, ti).astype(bf)
    copy.wait()
    total[0], total[1] = product(cross, tri, block)


def step_kernel(ahead, where, cross, tri, retarded, total, out, *rest):
    if ahead:
        later, block, sems = rest
    else:
        block, sems = rest
    fetch = pltpu.make_async_copy(retarded.at[0, :, 0, where[0]], block, sems.at[0])
    fetch.start()
    if ahead:
        prefetch = pltpu.make_async_copy(retarded.at[0, :, 0, where[1]], later, sems.at[1])
        prefetch.start()
    fetch.wait()
    x_re, x_im = product(cross, tri, block)
    out[0] = total[0] + x_re
    out[1] = total[1] + x_im
    if ahead:
        prefetch.wait()


def tri_kernel(tri, block, total, out):
    x_re, x_im = tri_product(tri, block)
    out[0] = total[0] + x_re
    out[1] = total[1] + x_im


def last_kernel(cross, block, total, out):
    x_re, x_im = cross_product(cross, block)
    x_re += total[0]
    x_im += total[1]
    out[0, 0, 0] = (x_re - x_re.T).astype(jnp.bfloat16)
    out[0, 1, 0] = (x_im + x_im.T).astype(jnp.bfloat16)


def cost(width):
    return pl.CostEstimate(flops=14 * width**3, bytes_accessed=8 * width**2, transcendentals=0)


def own_product(block, own, retarded):
    width = retarded.shape[-1]
    return pl.pallas_call(
        own_kernel,
        out_shape=(
            jax.ShapeDtypeStruct((1, 2, 1, width, width), jnp.bfloat16),
            jax.ShapeDtypeStruct((2, width, width), jnp.float32),
        ),
        in_specs=[pl.BlockSpec(memory_space=SMEM)] + vmem(2) + [pl.BlockSpec(memory_space=HBM)],
        out_specs=tuple(vmem(2)),
        scratch_shapes=[pltpu.VMEM((2, width, width), jnp.bfloat16), pltpu.SemaphoreType.DMA],
        compiler_params=params(48),
        cost_estimate=cost(width),
    )(block.reshape(1), *own, retarded)


def step_product(block, source, retarded, total, later=None):
    width = retarded.shape[-1]
    ahead = later is not None
    numbers = jnp.stack([block, later if ahead else block])
    total_shape = jax.ShapeDtypeStruct((2, width, width), jnp.float32)
    block_shape = jax.ShapeDtypeStruct((2, width, width), jnp.bfloat16)
    return pl.pallas_call(
        functools.partial(step_kernel, ahead),
        out_shape=(total_shape, block_shape) if ahead else total_shape,
        in_specs=[pl.BlockSpec(memory_space=SMEM)]
        + vmem(2)
        + [pl.BlockSpec(memory_space=HBM)]
        + vmem(1),
        out_specs=tuple(vmem(2)) if ahead else vmem(1)[0],
        scratch_shapes=[pltpu.VMEM((2, width, width), jnp.bfloat16), pltpu.SemaphoreType.DMA((2,))],
        compiler_params=params(46),
        cost_estimate=cost(width),
    )(numbers, *source, retarded, total)


def add_tri(tri, block, total):
    return pl.pallas_call(
        tri_kernel,
        out_shape=jax.ShapeDtypeStruct(total.shape, jnp.float32),
        in_specs=vmem(3),
        out_specs=vmem(1)[0],
        compiler_params=params(46),
        cost_estimate=cost(block.shape[-1]),
    )(tri, block, total)


def last_product(cross, block, total):
    width = block.shape[-1]
    return pl.pallas_call(
        last_kernel,
        out_shape=jax.ShapeDtypeStruct((1, 2, 1, width, width), jnp.bfloat16),
        in_specs=vmem(3),
        out_specs=vmem(1)[0],
        compiler_params=params(46),
        cost_estimate=cost(width),
    )(cross, block, total)


def exchange(pieces):
    return lax.all_to_all(pieces, "energy", split_axis=0, concat_axis=0, tiled=True)


def shards(g_lesser, w_lesser, g_retarded, energy_index):
    width = g_lesser.shape[-1]
    groups = lax.axis_size("energy")
    chain = lax.axis_size("space")
    here = lax.axis_index("space")
    paired = groups >= 4 and groups & (groups - 1) == 0 and (width // groups) % 16 == 0
    here = here.astype(jnp.int32)
    if chain == 4:
        return around_line(here, paired, g_lesser, w_lesser, energy_index, groups, g_retarded)
    if paired:
        own = gather_paired(g_lesser, w_lesser, energy_index, groups, lambda part: None)
    else:
        own = gather_shared(g_lesser, w_lesser, energy_index, groups)
    everyone = [lax.all_gather(part, "space") for part in own]
    sigma_lesser, total = own_product(here, own, g_retarded)

    def source(block):
        return tuple(lax.dynamic_index_in_dim(part, block, 0, False) for part in everyone)

    for step in range(1, chain - 1):
        block = (here + step) % chain
        later = (block + 1) % chain
        total, held = step_product(block, source(block), g_retarded, total, later)
    cross, tri = source(later)
    return (sigma_lesser, last_product(cross, held, add_tri(tri, held, total)))


def around_line(here, paired, g_lesser, w_lesser, energy_index, groups, retarded):
    def swap(part, bits):
        return lax.ppermute(part, "space", [(i, i ^ bits) for i in range(4)])

    first, second = [], []

    def send(part):
        first.append(swap(part, 1))
        second.append(swap(part, 3))

    if paired:
        own = gather_paired(g_lesser, w_lesser, energy_index, groups, send)
        second.append(swap(own[0], 3))
        first.append(swap(after(own[0], second[0], first[0]), 1))
    else:
        own = gather_shared(g_lesser, w_lesser, energy_index, groups)
        send(own[1]), send(own[0])
    sigma_lesser, total = own_product(here, own, retarded)
    third = [swap(after(second[0], first[0], total), 1), swap(second[1], 1)]
    total = step_product(here ^ 3, second[::-1], retarded, total)
    total, held = step_product(here ^ 1, first[::-1], retarded, total, here ^ 2)
    delta = last_product(third[1], held, add_tri(third[0], held, total))
    return (sigma_lesser, delta)


def solution(mesh):
    return jax.shard_map(
        shards,
        mesh=mesh,
        in_specs=(
            P("energy", None, "space", None, None),
            P("energy", None, "space", None, None),
            P("energy", None, "space", None, None, None),
            P(),
        ),
        out_specs=(P("energy", None, "space", None, None), P("energy", None, "space", None, None)),
        check_vma=False,
    )
```

```python
import functools

import jax
import jax.numpy as jnp
from jax import lax
from jax.experimental import pallas as pl
from jax.experimental.pallas import tpu as pltpu
from jax.sharding import PartitionSpec as P


VMEM = pltpu.MemorySpace.VMEM
SMEM = pltpu.MemorySpace.SMEM
HBM = pltpu.MemorySpace.HBM

SMALL = pl.CostEstimate(flops=1, bytes_accessed=1, transcendentals=0)


def vmem(count):
    return [pl.BlockSpec(memory_space=VMEM)] * count


def params(mib):
    return pltpu.CompilerParams(vmem_limit_bytes=mib * 2**20)


def grid_of(shape, row_offset=0):
    rows = lax.broadcasted_iota(jnp.int32, shape, 0) + row_offset
    cols = lax.broadcasted_iota(jnp.int32, shape, 1)
    return rows, cols


def pack_kernel(green, screen, cross, tri):
    half = green.shape[-1] // 2
    rows, cols = grid_of((half, half))
    upper = rows < cols
    diagonal = rows == cols
    for place, source in enumerate((green, screen)):
        a_re = source[0, 0, 0, :half, :half].astype(jnp.float32)
        a_im = source[0, 1, 0, :half, :half].astype(jnp.float32)
        d_re = source[0, 0, 0, half:, half:].astype(jnp.float32)
        d_im = source[0, 1, 0, half:, half:].astype(jnp.float32)
        t_re = jnp.where(upper, a_re, jnp.where(diagonal, a_im, d_re)).astype(jnp.bfloat16)
        t_im = jnp.where(upper, a_im, d_im).astype(jnp.bfloat16)
        c_re = source[0, 0, 0, :half, half:]
        c_im = source[0, 1, 0, :half, half:]
        shape = cross.shape[:1] + cross.shape[3:]
        cross[:, place, 0] = c_re.reshape(shape)
        cross[:, place, 1] = c_im.reshape(shape)
        tri[:, place, 0] = t_re.reshape(shape)
        tri[:, place, 1] = t_im.reshape(shape)


def pack(green, screen, parts):
    half = green.shape[-1] // 2
    out = jax.ShapeDtypeStruct((parts, 2, 2, half // parts, half), jnp.bfloat16)
    return pl.pallas_call(
        pack_kernel,
        out_shape=(out, out),
        in_specs=vmem(2),
        out_specs=tuple(vmem(2)),
        compiler_params=params(24),
    )(green, screen)


def split_rows(packed, groups):
    _, fields, comps, half, width = packed.shape
    shaped = packed.reshape(fields, comps, groups, half // groups, width)
    return jnp.moveaxis(shaped, 2, 0)


def conv_kernel(has_diagonal, index, offset, pieces, out, green, screen, place):
    count, _, _, rows, width = pieces.shape

    def scatter(stored, carry):
        point = index[stored]
        place[point] = stored
        green[point] = pieces[stored, 0].astype(jnp.float32)
        screen[point] = pieces[stored, 1].astype(jnp.float32)
        return carry

    unroll = count <= 16
    lax.fori_loop(0, count, scatter, 0, unroll=unroll)
    scale = count**-0.5
    zero = jnp.zeros((rows, width), jnp.float32)

    def one(point, carry):
        total = point + count // 2

        def term(first, sums):
            both_re, both_im, mixed = sums
            g_re = green[first, 0]
            g_im = green[first, 1]
            w_re = screen[total - first, 0]
            w_im = screen[total - first, 1]
            return (
                both_re + g_re * w_re,
                both_im + g_im * w_im,
                mixed + g_re * w_im + g_im * w_re,
            )

        if unroll:
            sums = (zero, zero, zero)
            for first in range(max(0, total - count + 1), min(count - 1, total) + 1):
                sums = term(first, sums)
        else:
            low = jnp.maximum(0, total - count + 1)
            high = jnp.minimum(count - 1, total) + 1
            sums = lax.fori_loop(low, high, term, (zero, zero, zero))
        both_re, both_im, mixed = sums
        s_re = -scale * mixed
        s_im = scale * (both_re - both_im)
        if has_diagonal:
            at_rows, at_cols = grid_of((rows, width), offset[0])
            diagonal = at_rows == at_cols
            s_re = jnp.where(diagonal, -scale * both_re, s_re)
            s_im = jnp.where(diagonal, -scale * both_im, s_im)
        stored = place[point]
        out[stored, 0] = s_re.astype(jnp.bfloat16)
        out[stored, 1] = s_im.astype(jnp.bfloat16)
        return carry

    if unroll:
        for point in range(count):
            one(point, 0)
    else:
        lax.fori_loop(0, count, one, 0)


def convolve(pieces, energy_index, row_offset, has_diagonal):
    count, _, _, rows, width = pieces.shape
    smem = pl.BlockSpec(memory_space=SMEM)
    return pl.pallas_call(
        functools.partial(conv_kernel, has_diagonal),
        out_shape=jax.ShapeDtypeStruct((count, 2, rows, width), jnp.bfloat16),
        in_specs=[smem, smem] + vmem(1),
        out_specs=vmem(1)[0],
        scratch_shapes=[
            pltpu.VMEM((count, 2, rows, width), jnp.float32),
            pltpu.VMEM((count, 2, rows, width), jnp.float32),
            pltpu.SMEM((count,), jnp.int32),
        ],
        compiler_params=params(24),
    )(energy_index, row_offset, pieces)


def share_of(me, d, rows):
    return pl.ds(pl.multiple_of((lax.shift_right_logical(me, 1) ^ d) * rows, rows), rows)


def cut_kernel(chips, me, green, screen, *rest):
    outs = rest[:chips]
    near, far, sems, cross_sems = rest[chips:]
    half = near.shape[-1]
    rows = half // chips
    copies = []
    for field, source in enumerate((green, screen)):
        for place, (held, lines) in enumerate(((near, slice(0, half)), (far, slice(half, None)))):
            copy = pltpu.make_async_copy(
                source.at[0, :, 0, lines, lines], held.at[field], sems.at[field, place]
            )
            copy.start()
            copies.append(copy)
    cross_copies = []
    for d in range(chips):
        for field, source in enumerate((green, screen)):
            part = source.at[0, :, 0, share_of(me[0], d, rows), half:]
            copy = pltpu.make_async_copy(part, outs[d].at[0, field], cross_sems.at[d, field])
            copy.start()
            cross_copies.append(copy)
    at_rows, at_cols = grid_of((rows, half))
    for field in range(2):
        for copy in copies[2 * field : 2 * field + 2]:
            copy.wait()
        for d in range(chips):
            lines = share_of(me[0], d, rows)
            here = at_rows + (lax.shift_right_logical(me[0], 1) ^ d) * rows
            upper = here < at_cols
            diagonal = here == at_cols
            a_re = near[field, 0, lines, :].astype(jnp.float32)
            a_im = near[field, 1, lines, :].astype(jnp.float32)
            d_re = far[field, 0, lines, :].astype(jnp.float32)
            d_im = far[field, 1, lines, :].astype(jnp.float32)
            t_re = jnp.where(upper, a_re, jnp.where(diagonal, a_im, d_re))
            outs[d][1, field, 0] = t_re.astype(jnp.bfloat16)
            outs[d][1, field, 1] = jnp.where(upper, a_im, d_im).astype(jnp.bfloat16)
    for copy in cross_copies:
        copy.wait()


def cut(me, green, screen, chips):
    half = green.shape[-1] // 2
    piece = jax.ShapeDtypeStruct((2, 2, 2, half // chips, half), jnp.bfloat16)
    return pl.pallas_call(
        functools.partial(cut_kernel, chips),
        out_shape=(piece,) * chips,
        in_specs=[pl.BlockSpec(memory_space=SMEM)] + [pl.BlockSpec(memory_space=HBM)] * 2,
        out_specs=tuple(vmem(chips)),
        scratch_shapes=[pltpu.VMEM((2, 2, half, half), jnp.bfloat16)] * 2
        + [pltpu.SemaphoreType.DMA((2, 2)), pltpu.SemaphoreType.DMA((chips, 2))],
        compiler_params=params(52),
        cost_estimate=SMALL,
    )(me, green, screen)


def bind_kernel(part, *refs):
    for place, piece in enumerate(refs[:-1]):
        refs[-1][place] = piece[part]


def bind(pieces, part):
    shape = (len(pieces),) + pieces[0].shape[1:]
    return pl.pallas_call(
        functools.partial(bind_kernel, part),
        out_shape=jax.ShapeDtypeStruct(shape, jnp.bfloat16),
        in_specs=vmem(len(pieces)),
        out_specs=vmem(1)[0],
        compiler_params=params(32),
        cost_estimate=SMALL,
    )(*pieces)


def conv_pieces_kernel(chips, part, me, index, *rest):
    same = rest[:chips][::-1]
    beside, other = rest[chips : chips + 2]
    outs = rest[chips + 2 : 2 * chips + 2]
    green, screen, sums, place = rest[2 * chips + 2 :]
    groups = 2 * chips
    rows, width = sums.shape[2:]
    for core in range(2):
        for d in range(chips):
            stored = me[0] ^ (2 * d + core)
            point = index[stored]
            place[point] = stored
            if core == 0:
                green[point] = same[d][part, 0]
                screen[point] = same[d][part, 1]
            elif d == 0:
                green[point] = beside[part, 0]
                screen[point] = beside[part, 1]
            else:
                green[point] = other[chips - 1 - d, 0]
                screen[point] = other[chips - 1 - d, 1]
    scale = groups**-0.5
    tall = 16
    for point in range(groups):

        @pl.when(((place[point] ^ me[0]) & 1) == 0)
        def _():
            total = point + groups // 2
            for first_row in range(0, rows, tall):
                for first_col in range(0, width, 128):
                    at = (slice(first_row, first_row + tall), slice(first_col, first_col + 128))
                    both_re = both_im = mixed = None
                    for p in range(max(0, total - groups + 1), min(groups - 1, total) + 1):
                        g_re = green[(p, 0) + at].astype(jnp.float32)
                        g_im = green[(p, 1) + at].astype(jnp.float32)
                        w_re = screen[(total - p, 0) + at].astype(jnp.float32)
                        w_im = screen[(total - p, 1) + at].astype(jnp.float32)
                        re = g_re * w_re
                        im = g_im * w_im
                        mix = g_re * w_im + g_im * w_re
                        both_re = re if both_re is None else both_re + re
                        both_im = im if both_im is None else both_im + im
                        mixed = mix if mixed is None else mixed + mix
                    s_re = -scale * mixed
                    s_im = scale * (both_re - both_im)
                    if part == 1:
                        first = lax.shift_right_logical(me[0], 1) * rows + first_row
                        at_rows, at_cols = grid_of((tall, 128), first)
                        diagonal = at_rows == at_cols + first_col
                        s_re = jnp.where(diagonal, -scale * both_re, s_re)
                        s_im = jnp.where(diagonal, -scale * both_im, s_im)
                    sums[(point, 0) + at] = s_re.astype(jnp.bfloat16)
                    sums[(point, 1) + at] = s_im.astype(jnp.bfloat16)

    for d in range(chips):
        outs[d][...] = sums[index[me[0] ^ (2 * d)]]


def conv_pieces(me, energy_index, same, beside, other, part):
    chips = len(same)
    shape = same[0].shape[2:]
    smem = pl.BlockSpec(memory_space=SMEM)
    return pl.pallas_call(
        functools.partial(conv_pieces_kernel, chips, part),
        out_shape=(jax.ShapeDtypeStruct(shape, jnp.bfloat16),) * chips,
        in_specs=[smem, smem] + vmem(chips + 2),
        out_specs=tuple(vmem(chips)),
        scratch_shapes=[pltpu.VMEM((2 * chips,) + shape, jnp.bfloat16)] * 3
        + [pltpu.SMEM((2 * chips,), jnp.int32)],
        compiler_params=params(32),
        cost_estimate=SMALL,
    )(me, energy_index, *same[::-1], beside, other)


def join_kernel(chips, me, *rest):
    pieces, out = rest[:chips][::-1], rest[chips]
    rows = pieces[0].shape[1]
    for d in range(chips):
        out[:, share_of(me[0], d, rows), :] = pieces[d][...]


def join(me, pieces):
    half = pieces[0].shape[-1]
    return pl.pallas_call(
        functools.partial(join_kernel, len(pieces)),
        out_shape=jax.ShapeDtypeStruct((2, half, half), jnp.bfloat16),
        in_specs=[pl.BlockSpec(memory_space=SMEM)] + vmem(len(pieces)),
        out_specs=vmem(1)[0],
        compiler_params=params(32),
        cost_estimate=SMALL,
    )(me, *pieces[::-1])


def swap(piece, d, groups):
    return lax.ppermute(piece, "energy", [(i, i ^ d) for i in range(groups)]) if d else piece


def after(value, *earlier):
    return lax.optimization_barrier((value, earlier))[0]


def gather_paired(g_lesser, w_lesser, energy_index, groups, send):
    me = lax.axis_index("energy").astype(jnp.int32).reshape(1)
    chips = groups // 2

    def over(pieces):
        return [swap(pieces[d], 2 * d, groups) for d in range(chips)]

    pieces = cut(me, g_lesser, w_lesser, chips)
    same = over(pieces)
    beside = swap(pieces[0], 1, groups)
    bound = [bind(after(same[:0:-1], beside), part) for part in range(2)]
    other = [swap(piece, 1, groups) for piece in bound]
    mine = conv_pieces(me, energy_index, same, beside, other[1], 1)
    own_tri = join(me, over(mine))
    send(own_tri)
    mine = conv_pieces(me, energy_index, same, beside, after(other[0], own_tri), 0)
    own_cross = join(me, over(mine))
    return own_cross, own_tri


def gather_shared(g_lesser, w_lesser, energy_index, groups):
    half = g_lesser.shape[-1] // 2
    rows = half // groups
    cross, tri = (split_rows(packed, groups) for packed in pack(g_lesser, w_lesser, 1))
    offset = (lax.axis_index("energy") * rows).astype(jnp.int32).reshape(1)
    own = []
    for pieces, has_diagonal in ((cross, False), (tri, True)):
        shares = convolve(exchange(pieces), energy_index, offset, has_diagonal)
        own.append(jnp.moveaxis(exchange(shares), 0, 1).reshape(2, half, half))
    return own


def squares(cross, tri):
    return cross[0], cross[1], tri[0], tri[1]


def dot(a, b):
    return jnp.dot(a, b, preferred_element_type=jnp.float32)


def dot_t(a, b):
    return lax.dot_general(a, b, (((1,), (1,)), ((), ())), preferred_element_type=jnp.float32)


def product(cross, tri, retarded):
    return product_of(cross, tri, retarded)


def product_of(cross, tri, retarded):
    t_re, t_im = tri[0], tri[1]
    half = t_re.shape[0]
    rows, cols = grid_of((half, half))
    tr = t_re.astype(jnp.float32)
    ti = t_im.astype(jnp.float32)
    diagonal = rows == cols
    a_re = jnp.where(rows < cols, tr, 0.0).astype(jnp.bfloat16)
    a_im = jnp.where(rows < cols, ti, jnp.where(diagonal, 0.5 * tr, 0.0)).astype(jnp.bfloat16)
    d_re = jnp.where(rows > cols, tr, 0.0).astype(jnp.bfloat16)
    d_im = jnp.where(rows > cols, ti, jnp.where(diagonal, 0.5 * ti, 0.0)).astype(jnp.bfloat16)
    g_re = retarded[0]
    g_im = retarded[1]
    near = jnp.concatenate([g_re[:, :half], g_im[:, :half]], axis=1)
    all_g = jnp.concatenate([g_re, g_im], axis=1)
    if cross is None:
        far = jnp.concatenate([g_re[:, half:], g_im[:, half:]], axis=1)
        right_re = [d_re, -d_im]
        right_im = [d_im, d_re]
    else:
        c_re, c_im = cross[0], cross[1]
        far = all_g
        right_re = [c_re, d_re, -c_im, -d_im]
        right_im = [c_im, d_im, c_re, d_re]
    l_re = jnp.concatenate(
        [
            dot(near, jnp.concatenate([a_re, -a_im], axis=0)),
            dot(far, jnp.concatenate(right_re, axis=0)),
        ],
        axis=1,
    ).astype(jnp.bfloat16)
    l_im = jnp.concatenate(
        [
            dot(near, jnp.concatenate([a_im, a_re], axis=0)),
            dot(far, jnp.concatenate(right_im, axis=0)),
        ],
        axis=1,
    ).astype(jnp.bfloat16)
    x_re = dot_t(jnp.concatenate([l_re, l_im], axis=1), all_g)
    x_im = dot_t(jnp.concatenate([l_im, -l_re], axis=1), all_g)
    return x_re, x_im


def tri_product(tri, retarded):
    return product_of(None, tri, retarded)


def cross_product(cross, retarded):
    c_re, c_im = cross[0], cross[1]
    half = c_re.shape[0]
    g_re = retarded[0]
    g_im = retarded[1]
    near = jnp.concatenate([g_re[:, :half], g_im[:, :half]], axis=1)
    far = jnp.concatenate([g_re[:, half:], g_im[:, half:]], axis=1)
    l_re = dot(near, jnp.concatenate([c_re, -c_im], axis=0)).astype(jnp.bfloat16)
    l_im = dot(near, jnp.concatenate([c_im, c_re], axis=0)).astype(jnp.bfloat16)
    x_re = dot_t(jnp.concatenate([l_re, l_im], axis=1), far)
    x_im = dot_t(jnp.concatenate([l_im, -l_re], axis=1), far)
    return x_re, x_im


def own_kernel(where, cross, tri, retarded, sigma, total, *rest):
    blocks, sems = rest[:-1], rest[-1]
    copies = [
        pltpu.make_async_copy(retarded.at[0, :, 0, where[place]], held, sems.at[place])
        for place, held in enumerate(blocks)
    ]
    for copy in copies:
        copy.start()
    c_re, c_im, t_re, t_im = squares(cross, tri)
    half = c_re.shape[0]
    rows, cols = grid_of((half, half))
    upper = rows < cols
    diagonal = rows == cols
    tr = t_re.astype(jnp.float32)
    ti = t_im.astype(jnp.float32)
    trt = tr.T
    tit = ti.T
    zero = jnp.zeros_like(tr)
    bf = jnp.bfloat16
    sigma[0, 0, 0, :half, half:] = c_re
    sigma[0, 1, 0, :half, half:] = c_im
    sigma[0, 0, 0, half:, :half] = (-(c_re.astype(jnp.float32).T)).astype(bf)
    sigma[0, 1, 0, half:, :half] = c_im.astype(jnp.float32).T.astype(bf)
    sigma[0, 0, 0, :half, :half] = jnp.where(upper, tr, jnp.where(diagonal, zero, -trt)).astype(bf)
    sigma[0, 1, 0, :half, :half] = jnp.where(upper, ti, jnp.where(diagonal, tr, tit)).astype(bf)
    sigma[0, 0, 0, half:, half:] = jnp.where(upper, -trt, jnp.where(diagonal, zero, tr)).astype(bf)
    sigma[0, 1, 0, half:, half:] = jnp.where(upper, tit, ti).astype(bf)
    for copy in copies:
        copy.wait()
    total[0], total[1] = product(cross, tri, blocks[0])


def part_kernel(part, square, block, total, out):
    x_re, x_im = part(square, block)
    out[0] = total[0] + x_re
    out[1] = total[1] + x_im


def last_kernel(cross, block, total, out):
    x_re, x_im = cross_product(cross, block)
    x_re += total[0]
    x_im += total[1]
    out[0, 0, 0] = (x_re - x_re.T).astype(jnp.bfloat16)
    out[0, 1, 0] = (x_im + x_im.T).astype(jnp.bfloat16)


def cost(width):
    return pl.CostEstimate(flops=14 * width**3, bytes_accessed=8 * width**2, transcendentals=0)


def own_product(blocks, own, retarded):
    width = retarded.shape[-1]
    count = len(blocks)
    block_shape = jax.ShapeDtypeStruct((2, width, width), jnp.bfloat16)
    sigma, total, *held = pl.pallas_call(
        own_kernel,
        out_shape=(
            jax.ShapeDtypeStruct((1, 2, 1, width, width), jnp.bfloat16),
            jax.ShapeDtypeStruct((2, width, width), jnp.float32),
        )
        + (block_shape,) * count,
        in_specs=[pl.BlockSpec(memory_space=SMEM)] + vmem(2) + [pl.BlockSpec(memory_space=HBM)],
        out_specs=tuple(vmem(2 + count)),
        scratch_shapes=[pltpu.SemaphoreType.DMA((count,))],
        compiler_params=params(44),
        cost_estimate=cost(width),
    )(jnp.stack(blocks), *own, retarded)
    return sigma, total, held


def add_part(part, square, block, total):
    width = block.shape[-1]
    return pl.pallas_call(
        functools.partial(part_kernel, part),
        out_shape=jax.ShapeDtypeStruct(total.shape, jnp.float32),
        in_specs=vmem(3),
        out_specs=vmem(1)[0],
        compiler_params=params(36),
        cost_estimate=cost(width),
    )(square, block, total)


def last_product(cross, block, total):
    width = block.shape[-1]
    return pl.pallas_call(
        last_kernel,
        out_shape=jax.ShapeDtypeStruct((1, 2, 1, width, width), jnp.bfloat16),
        in_specs=vmem(3),
        out_specs=vmem(1)[0],
        compiler_params=params(46),
        cost_estimate=cost(width),
    )(cross, block, total)


def exchange(pieces):
    return lax.all_to_all(pieces, "energy", split_axis=0, concat_axis=0, tiled=True)


def shards(g_lesser, w_lesser, g_retarded, energy_index):
    width = g_lesser.shape[-1]
    groups = lax.axis_size("energy")
    chain = lax.axis_size("space")
    here = lax.axis_index("space")
    paired = groups >= 4 and groups & (groups - 1) == 0 and (width // groups) % 16 == 0
    here = here.astype(jnp.int32)
    if chain == 4:
        return around_line(here, paired, g_lesser, w_lesser, energy_index, groups, g_retarded)
    if paired:
        own = gather_paired(g_lesser, w_lesser, energy_index, groups, lambda part: None)
    else:
        own = gather_shared(g_lesser, w_lesser, energy_index, groups)
    cross, tri = (lax.all_gather(part, "space") for part in own)
    blocks = [(here + step) % chain for step in range(chain)]
    sigma_lesser, total, held = own_product(blocks, own, g_retarded)

    def at(gathered, block):
        return lax.dynamic_index_in_dim(gathered, block, 0, False)

    for step in range(1, chain):
        total = add_part(tri_product, at(tri, blocks[step]), held[step], total)
        if step < chain - 1:
            total = add_part(cross_product, at(cross, blocks[step]), held[step], total)
    return (sigma_lesser, last_product(at(cross, blocks[-1]), held[-1], total))


def around_line(here, paired, g_lesser, w_lesser, energy_index, groups, retarded):
    def swap(part, bits):
        return lax.ppermute(part, "space", [(i, i ^ bits) for i in range(4)])

    first, second = [], []

    def send(part):
        first.append(swap(part, 1))
        second.append(swap(part, 3))

    if paired:
        own = gather_paired(g_lesser, w_lesser, energy_index, groups, send)
        second.append(swap(own[0], 3))
        first.append(swap(own[0], 1))
    else:
        own = gather_shared(g_lesser, w_lesser, energy_index, groups)
        send(own[1]), send(own[0])
    blocks = [here, here ^ 1, here ^ 3, here ^ 2]
    sigma_lesser, total, held = own_product(blocks, after(own, second[0], first[0]), retarded)
    third = [swap(after(second[0], total), 1), swap(second[1], 1)]
    total = add_part(tri_product, first[0], held[1], total)
    total = add_part(tri_product, second[0], held[2], total)
    total = add_part(cross_product, second[1], held[2], total)
    total = add_part(cross_product, first[1], held[1], total)
    total = add_part(tri_product, third[0], held[3], total)
    return (sigma_lesser, last_product(third[1], held[3], total))


def solution(mesh):
    return jax.shard_map(
        shards,
        mesh=mesh,
        in_specs=(
            P("energy", None, "space", None, None),
            P("energy", None, "space", None, None),
            P("energy", None, "space", None, None, None),
            P(),
        ),
        out_specs=(P("energy", None, "space", None, None), P("energy", None, "space", None, None)),
        check_vma=False,
    )
```

```python
import functools

import jax
import jax.numpy as jnp
from jax import lax
from jax.experimental import pallas as pl
from jax.experimental.pallas import tpu as pltpu
from jax.sharding import PartitionSpec as P


VMEM = pltpu.MemorySpace.VMEM
SMEM = pltpu.MemorySpace.SMEM
HBM = pltpu.MemorySpace.HBM

SMALL = pl.CostEstimate(flops=1, bytes_accessed=1, transcendentals=0)


def vmem(count):
    return [pl.BlockSpec(memory_space=VMEM)] * count


def params(mib):
    return pltpu.CompilerParams(vmem_limit_bytes=mib * 2**20)


def grid_of(shape, row_offset=0):
    rows = lax.broadcasted_iota(jnp.int32, shape, 0) + row_offset
    cols = lax.broadcasted_iota(jnp.int32, shape, 1)
    return rows, cols


def pack_kernel(green, screen, cross, tri):
    half = green.shape[-1] // 2
    rows, cols = grid_of((half, half))
    upper = rows < cols
    diagonal = rows == cols
    for place, source in enumerate((green, screen)):
        a_re = source[0, 0, 0, :half, :half].astype(jnp.float32)
        a_im = source[0, 1, 0, :half, :half].astype(jnp.float32)
        d_re = source[0, 0, 0, half:, half:].astype(jnp.float32)
        d_im = source[0, 1, 0, half:, half:].astype(jnp.float32)
        t_re = jnp.where(upper, a_re, jnp.where(diagonal, a_im, d_re)).astype(jnp.bfloat16)
        t_im = jnp.where(upper, a_im, d_im).astype(jnp.bfloat16)
        c_re = source[0, 0, 0, :half, half:]
        c_im = source[0, 1, 0, :half, half:]
        shape = cross.shape[:1] + cross.shape[3:]
        cross[:, place, 0] = c_re.reshape(shape)
        cross[:, place, 1] = c_im.reshape(shape)
        tri[:, place, 0] = t_re.reshape(shape)
        tri[:, place, 1] = t_im.reshape(shape)


def pack(green, screen, parts):
    half = green.shape[-1] // 2
    out = jax.ShapeDtypeStruct((parts, 2, 2, half // parts, half), jnp.bfloat16)
    return pl.pallas_call(
        pack_kernel,
        out_shape=(out, out),
        in_specs=vmem(2),
        out_specs=tuple(vmem(2)),
        compiler_params=params(24),
    )(green, screen)


def split_rows(packed, groups):
    _, fields, comps, half, width = packed.shape
    shaped = packed.reshape(fields, comps, groups, half // groups, width)
    return jnp.moveaxis(shaped, 2, 0)


def conv_kernel(has_diagonal, index, offset, pieces, out, green, screen, place):
    count, _, _, rows, width = pieces.shape

    def scatter(stored, carry):
        point = index[stored]
        place[point] = stored
        green[point] = pieces[stored, 0].astype(jnp.float32)
        screen[point] = pieces[stored, 1].astype(jnp.float32)
        return carry

    unroll = count <= 16
    lax.fori_loop(0, count, scatter, 0, unroll=unroll)
    scale = count**-0.5
    zero = jnp.zeros((rows, width), jnp.float32)

    def one(point, carry):
        total = point + count // 2

        def term(first, sums):
            both_re, both_im, mixed = sums
            g_re = green[first, 0]
            g_im = green[first, 1]
            w_re = screen[total - first, 0]
            w_im = screen[total - first, 1]
            return (
                both_re + g_re * w_re,
                both_im + g_im * w_im,
                mixed + g_re * w_im + g_im * w_re,
            )

        if unroll:
            sums = (zero, zero, zero)
            for first in range(max(0, total - count + 1), min(count - 1, total) + 1):
                sums = term(first, sums)
        else:
            low = jnp.maximum(0, total - count + 1)
            high = jnp.minimum(count - 1, total) + 1
            sums = lax.fori_loop(low, high, term, (zero, zero, zero))
        both_re, both_im, mixed = sums
        s_re = -scale * mixed
        s_im = scale * (both_re - both_im)
        if has_diagonal:
            at_rows, at_cols = grid_of((rows, width), offset[0])
            diagonal = at_rows == at_cols
            s_re = jnp.where(diagonal, -scale * both_re, s_re)
            s_im = jnp.where(diagonal, -scale * both_im, s_im)
        stored = place[point]
        out[stored, 0] = s_re.astype(jnp.bfloat16)
        out[stored, 1] = s_im.astype(jnp.bfloat16)
        return carry

    if unroll:
        for point in range(count):
            one(point, 0)
    else:
        lax.fori_loop(0, count, one, 0)


def convolve(pieces, energy_index, row_offset, has_diagonal):
    count, _, _, rows, width = pieces.shape
    smem = pl.BlockSpec(memory_space=SMEM)
    return pl.pallas_call(
        functools.partial(conv_kernel, has_diagonal),
        out_shape=jax.ShapeDtypeStruct((count, 2, rows, width), jnp.bfloat16),
        in_specs=[smem, smem] + vmem(1),
        out_specs=vmem(1)[0],
        scratch_shapes=[
            pltpu.VMEM((count, 2, rows, width), jnp.float32),
            pltpu.VMEM((count, 2, rows, width), jnp.float32),
            pltpu.SMEM((count,), jnp.int32),
        ],
        compiler_params=params(24),
    )(energy_index, row_offset, pieces)


def share_of(me, d, rows):
    return pl.ds(pl.multiple_of((lax.shift_right_logical(me, 1) ^ d) * rows, rows), rows)


def cut_kernel(chips, me, green, screen, *rest):
    outs = rest[:chips]
    near, far, sems, cross_sems = rest[chips:]
    half = near.shape[-1]
    rows = half // chips
    copies = []
    for field, source in enumerate((green, screen)):
        for place, (held, lines) in enumerate(((near, slice(0, half)), (far, slice(half, None)))):
            copy = pltpu.make_async_copy(
                source.at[0, :, 0, lines, lines], held.at[field], sems.at[field, place]
            )
            copy.start()
            copies.append(copy)
    cross_copies = []
    for d in range(chips):
        for field, source in enumerate((green, screen)):
            part = source.at[0, :, 0, share_of(me[0], d, rows), half:]
            copy = pltpu.make_async_copy(part, outs[d].at[0, field], cross_sems.at[d, field])
            copy.start()
            cross_copies.append(copy)
    at_rows, at_cols = grid_of((rows, half))
    for field in range(2):
        for copy in copies[2 * field : 2 * field + 2]:
            copy.wait()
        for d in range(chips):
            lines = share_of(me[0], d, rows)
            here = at_rows + (lax.shift_right_logical(me[0], 1) ^ d) * rows
            upper = here < at_cols
            diagonal = here == at_cols
            a_re = near[field, 0, lines, :].astype(jnp.float32)
            a_im = near[field, 1, lines, :].astype(jnp.float32)
            d_re = far[field, 0, lines, :].astype(jnp.float32)
            d_im = far[field, 1, lines, :].astype(jnp.float32)
            t_re = jnp.where(upper, a_re, jnp.where(diagonal, a_im, d_re))
            outs[d][1, field, 0] = t_re.astype(jnp.bfloat16)
            outs[d][1, field, 1] = jnp.where(upper, a_im, d_im).astype(jnp.bfloat16)
    for copy in cross_copies:
        copy.wait()


def cut(me, green, screen, chips):
    half = green.shape[-1] // 2
    piece = jax.ShapeDtypeStruct((2, 2, 2, half // chips, half), jnp.bfloat16)
    return pl.pallas_call(
        functools.partial(cut_kernel, chips),
        out_shape=(piece,) * chips,
        in_specs=[pl.BlockSpec(memory_space=SMEM)] + [pl.BlockSpec(memory_space=HBM)] * 2,
        out_specs=tuple(vmem(chips)),
        scratch_shapes=[pltpu.VMEM((2, 2, half, half), jnp.bfloat16)] * 2
        + [pltpu.SemaphoreType.DMA((2, 2)), pltpu.SemaphoreType.DMA((chips, 2))],
        compiler_params=params(52),
        cost_estimate=SMALL,
    )(me, green, screen)


def bind_kernel(part, *refs):
    for place, piece in enumerate(refs[:-1]):
        refs[-1][place] = piece[part]


def bind(pieces, part):
    shape = (len(pieces),) + pieces[0].shape[1:]
    return pl.pallas_call(
        functools.partial(bind_kernel, part),
        out_shape=jax.ShapeDtypeStruct(shape, jnp.bfloat16),
        in_specs=vmem(len(pieces)),
        out_specs=vmem(1)[0],
        compiler_params=params(32),
        cost_estimate=SMALL,
    )(*pieces)


def conv_pieces_kernel(chips, part, me, index, *rest):
    same = rest[:chips][::-1]
    beside, other = rest[chips : chips + 2]
    outs = rest[chips + 2 : 2 * chips + 2]
    green, screen, sums, place = rest[2 * chips + 2 :]
    groups = 2 * chips
    rows, width = sums.shape[2:]
    for core in range(2):
        for d in range(chips):
            stored = me[0] ^ (2 * d + core)
            point = index[stored]
            place[point] = stored
            if core == 0:
                green[point] = same[d][part, 0]
                screen[point] = same[d][part, 1]
            elif d == 0:
                green[point] = beside[part, 0]
                screen[point] = beside[part, 1]
            else:
                green[point] = other[chips - 1 - d, 0]
                screen[point] = other[chips - 1 - d, 1]
    scale = groups**-0.5
    tall = 16
    for point in range(groups):

        @pl.when(((place[point] ^ me[0]) & 1) == 0)
        def _():
            total = point + groups // 2
            for first_row in range(0, rows, tall):
                for first_col in range(0, width, 128):
                    at = (slice(first_row, first_row + tall), slice(first_col, first_col + 128))
                    both_re = both_im = mixed = None
                    for p in range(max(0, total - groups + 1), min(groups - 1, total) + 1):
                        g_re = green[(p, 0) + at].astype(jnp.float32)
                        g_im = green[(p, 1) + at].astype(jnp.float32)
                        w_re = screen[(total - p, 0) + at].astype(jnp.float32)
                        w_im = screen[(total - p, 1) + at].astype(jnp.float32)
                        re = g_re * w_re
                        im = g_im * w_im
                        mix = g_re * w_im + g_im * w_re
                        both_re = re if both_re is None else both_re + re
                        both_im = im if both_im is None else both_im + im
                        mixed = mix if mixed is None else mixed + mix
                    s_re = -scale * mixed
                    s_im = scale * (both_re - both_im)
                    if part == 1:
                        first = lax.shift_right_logical(me[0], 1) * rows + first_row
                        at_rows, at_cols = grid_of((tall, 128), first)
                        diagonal = at_rows == at_cols + first_col
                        s_re = jnp.where(diagonal, -scale * both_re, s_re)
                        s_im = jnp.where(diagonal, -scale * both_im, s_im)
                    sums[(point, 0) + at] = s_re.astype(jnp.bfloat16)
                    sums[(point, 1) + at] = s_im.astype(jnp.bfloat16)

    for d in range(chips):
        outs[d][...] = sums[index[me[0] ^ (2 * d)]]


def conv_pieces(me, energy_index, same, beside, other, part):
    chips = len(same)
    shape = same[0].shape[2:]
    smem = pl.BlockSpec(memory_space=SMEM)
    return pl.pallas_call(
        functools.partial(conv_pieces_kernel, chips, part),
        out_shape=(jax.ShapeDtypeStruct(shape, jnp.bfloat16),) * chips,
        in_specs=[smem, smem] + vmem(chips + 2),
        out_specs=tuple(vmem(chips)),
        scratch_shapes=[pltpu.VMEM((2 * chips,) + shape, jnp.bfloat16)] * 3
        + [pltpu.SMEM((2 * chips,), jnp.int32)],
        compiler_params=params(32),
        cost_estimate=SMALL,
    )(me, energy_index, *same[::-1], beside, other)


def join_kernel(chips, me, *rest):
    pieces, out = rest[:chips][::-1], rest[chips]
    rows = pieces[0].shape[1]
    for d in range(chips):
        out[:, share_of(me[0], d, rows), :] = pieces[d][...]


def join_apart_kernel(chips, me, *rest):
    pieces = rest[:chips][::-1]
    out, *apart = rest[chips:]
    rows = pieces[0].shape[1]
    for d in range(chips):
        lines = share_of(me[0], d, rows)
        out[:, lines, :] = pieces[d][...]
        for comp in range(2):
            apart[comp][lines, :] = pieces[d][comp]


def join_apart(me, pieces):
    half = pieces[0].shape[-1]
    one = jax.ShapeDtypeStruct((half, half), jnp.bfloat16)
    return pl.pallas_call(
        functools.partial(join_apart_kernel, len(pieces)),
        out_shape=(jax.ShapeDtypeStruct((2, half, half), jnp.bfloat16), one, one),
        in_specs=[pl.BlockSpec(memory_space=SMEM)] + vmem(len(pieces)),
        out_specs=tuple(vmem(3)),
        compiler_params=params(32),
        cost_estimate=SMALL,
    )(me, *pieces[::-1])


def join(me, pieces):
    half = pieces[0].shape[-1]
    return pl.pallas_call(
        functools.partial(join_kernel, len(pieces)),
        out_shape=jax.ShapeDtypeStruct((2, half, half), jnp.bfloat16),
        in_specs=[pl.BlockSpec(memory_space=SMEM)] + vmem(len(pieces)),
        out_specs=vmem(1)[0],
        compiler_params=params(32),
        cost_estimate=SMALL,
    )(me, *pieces[::-1])


def swap(piece, d, groups):
    return lax.ppermute(piece, "energy", [(i, i ^ d) for i in range(groups)]) if d else piece


def after(value, *earlier):
    return lax.optimization_barrier((value, earlier))[0]


def gather_paired(g_lesser, w_lesser, energy_index, groups, send):
    me = lax.axis_index("energy").astype(jnp.int32).reshape(1)
    chips = groups // 2

    def over(pieces):
        return [swap(pieces[d], 2 * d, groups) for d in range(chips)]

    pieces = cut(me, g_lesser, w_lesser, chips)
    same = over(pieces)
    beside = swap(pieces[0], 1, groups)
    bound = [bind(after(same[:0:-1], beside), part) for part in range(2)]
    other = [swap(piece, 1, groups) for piece in bound]
    mine = conv_pieces(me, energy_index, same, beside, other[1], 1)
    own_tri = join(me, over(mine))
    send(own_tri)
    mine = conv_pieces(me, energy_index, same, beside, after(other[0], own_tri), 0)
    own_cross, *apart = join_apart(me, over(mine))
    return own_cross, own_tri, apart


def gather_shared(g_lesser, w_lesser, energy_index, groups):
    half = g_lesser.shape[-1] // 2
    rows = half // groups
    cross, tri = (split_rows(packed, groups) for packed in pack(g_lesser, w_lesser, 1))
    offset = (lax.axis_index("energy") * rows).astype(jnp.int32).reshape(1)
    own = []
    for pieces, has_diagonal in ((cross, False), (tri, True)):
        shares = convolve(exchange(pieces), energy_index, offset, has_diagonal)
        own.append(jnp.moveaxis(exchange(shares), 0, 1).reshape(2, half, half))
    return own


def squares(cross, tri):
    return cross[0], cross[1], tri[0], tri[1]


def dot(a, b):
    return jnp.dot(a, b, preferred_element_type=jnp.float32)


def dot_t(a, b):
    return lax.dot_general(a, b, (((1,), (1,)), ((), ())), preferred_element_type=jnp.float32)


def product(cross, tri, retarded):
    return product_of(cross, tri, retarded)


def product_of(cross, tri, retarded):
    t_re, t_im = tri[0], tri[1]
    half = t_re.shape[0]
    rows, cols = grid_of((half, half))
    tr = t_re.astype(jnp.float32)
    ti = t_im.astype(jnp.float32)
    diagonal = rows == cols
    a_re = jnp.where(rows < cols, tr, 0.0).astype(jnp.bfloat16)
    a_im = jnp.where(rows < cols, ti, jnp.where(diagonal, 0.5 * tr, 0.0)).astype(jnp.bfloat16)
    d_re = jnp.where(rows > cols, tr, 0.0).astype(jnp.bfloat16)
    d_im = jnp.where(rows > cols, ti, jnp.where(diagonal, 0.5 * ti, 0.0)).astype(jnp.bfloat16)
    g_re = retarded[0]
    g_im = retarded[1]
    near = jnp.concatenate([g_re[:, :half], g_im[:, :half]], axis=1)
    all_g = jnp.concatenate([g_re, g_im], axis=1)
    if cross is None:
        far = jnp.concatenate([g_re[:, half:], g_im[:, half:]], axis=1)
        right_re = [d_re, -d_im]
        right_im = [d_im, d_re]
    else:
        c_re, c_im = cross[0], cross[1]
        far = all_g
        right_re = [c_re, d_re, -c_im, -d_im]
        right_im = [c_im, d_im, c_re, d_re]
    l_re = jnp.concatenate(
        [
            dot(near, jnp.concatenate([a_re, -a_im], axis=0)),
            dot(far, jnp.concatenate(right_re, axis=0)),
        ],
        axis=1,
    ).astype(jnp.bfloat16)
    l_im = jnp.concatenate(
        [
            dot(near, jnp.concatenate([a_im, a_re], axis=0)),
            dot(far, jnp.concatenate(right_im, axis=0)),
        ],
        axis=1,
    ).astype(jnp.bfloat16)
    x_re = dot_t(jnp.concatenate([l_re, l_im], axis=1), all_g)
    x_im = dot_t(jnp.concatenate([l_im, -l_re], axis=1), all_g)
    return x_re, x_im


def tri_product(tri, retarded):
    return product_of(None, tri, retarded)


def cross_left(cross, retarded):
    c_re, c_im = cross[0][...], cross[1][...]
    half = c_re.shape[0]
    g_re = retarded[0]
    g_im = retarded[1]
    near = jnp.concatenate([g_re[:, :half], g_im[:, :half]], axis=1)
    far = jnp.concatenate([g_re[:, half:], g_im[:, half:]], axis=1)
    l_re = dot(near, jnp.concatenate([c_re, -c_im], axis=0)).astype(jnp.bfloat16)
    l_im = dot(near, jnp.concatenate([c_im, c_re], axis=0)).astype(jnp.bfloat16)
    return l_re, l_im, far


def cross_product(cross, retarded):
    l_re, l_im, far = cross_left(cross, retarded)
    x_re = dot_t(jnp.concatenate([l_re, l_im], axis=1), far)
    x_im = dot_t(jnp.concatenate([l_im, -l_re], axis=1), far)
    return x_re, x_im


def own_kernel(where, cross, tri, retarded, sigma, total, *rest):
    blocks, sems = rest[:-1], rest[-1]
    copies = [
        pltpu.make_async_copy(retarded.at[0, :, 0, where[place]], held, sems.at[place])
        for place, held in enumerate(blocks)
    ]
    for copy in copies:
        copy.start()
    c_re, c_im, t_re, t_im = squares(cross, tri)
    half = c_re.shape[0]
    rows, cols = grid_of((half, half))
    upper = rows < cols
    diagonal = rows == cols
    tr = t_re.astype(jnp.float32)
    ti = t_im.astype(jnp.float32)
    trt = tr.T
    tit = ti.T
    zero = jnp.zeros_like(tr)
    bf = jnp.bfloat16
    sigma[0, 0, 0, :half, half:] = c_re
    sigma[0, 1, 0, :half, half:] = c_im
    sigma[0, 0, 0, half:, :half] = (-(c_re.astype(jnp.float32).T)).astype(bf)
    sigma[0, 1, 0, half:, :half] = c_im.astype(jnp.float32).T.astype(bf)
    sigma[0, 0, 0, :half, :half] = jnp.where(upper, tr, jnp.where(diagonal, zero, -trt)).astype(bf)
    sigma[0, 1, 0, :half, :half] = jnp.where(upper, ti, jnp.where(diagonal, tr, tit)).astype(bf)
    sigma[0, 0, 0, half:, half:] = jnp.where(upper, -trt, jnp.where(diagonal, zero, tr)).astype(bf)
    sigma[0, 1, 0, half:, half:] = jnp.where(upper, tit, ti).astype(bf)
    for copy in copies:
        copy.wait()
    total[0], total[1] = product(cross, tri, blocks[0])


def part_kernel(part, folded, *refs):
    *square, block, total, out = refs
    square = square if len(square) > 1 else square[0]
    x_re, x_im = part(square, block)
    x_re += total[0]
    x_im += total[1]
    if folded:
        x_re, x_im = x_re - x_re.T, x_im + x_im.T
    out[0] = x_re
    out[1] = x_im


def last_kernel(c_re, c_im, block, total, out):
    l_re, l_im, far = cross_left((c_re, c_im), block)
    half = far.shape[1] // 2
    f_re, f_im = far[:, :half], far[:, half:]

    def both(a, b):
        return dot_t(jnp.concatenate(a, axis=1), jnp.concatenate(b, axis=1))

    d_re = both([l_re, l_im, -f_re, -f_im], [f_re, f_im, l_re, l_im])
    d_im = both([l_im, -l_re, f_re, -f_im], [f_re, f_im, l_im, l_re])
    out[0, 0, 0] = (total[0] + d_re).astype(jnp.bfloat16)
    out[0, 1, 0] = (total[1] + d_im).astype(jnp.bfloat16)


def cost(width):
    return pl.CostEstimate(flops=14 * width**3, bytes_accessed=8 * width**2, transcendentals=0)


def own_product(blocks, own, retarded):
    width = retarded.shape[-1]
    count = len(blocks)
    block_shape = jax.ShapeDtypeStruct((2, width, width), jnp.bfloat16)
    sigma, total, *held = pl.pallas_call(
        own_kernel,
        out_shape=(
            jax.ShapeDtypeStruct((1, 2, 1, width, width), jnp.bfloat16),
            jax.ShapeDtypeStruct((2, width, width), jnp.float32),
        )
        + (block_shape,) * count,
        in_specs=[pl.BlockSpec(memory_space=SMEM)] + vmem(2) + [pl.BlockSpec(memory_space=HBM)],
        out_specs=tuple(vmem(2 + count)),
        scratch_shapes=[pltpu.SemaphoreType.DMA((count,))],
        compiler_params=params(44),
        cost_estimate=cost(width),
    )(jnp.stack(blocks), *own, retarded)
    return sigma, total, held


def add_part(part, square, block, total, folded=False):
    width = block.shape[-1]
    return pl.pallas_call(
        functools.partial(part_kernel, part, folded),
        out_shape=jax.ShapeDtypeStruct(total.shape, jnp.float32),
        in_specs=vmem(len(square) + 2),
        out_specs=vmem(1)[0],
        compiler_params=params(36),
        cost_estimate=cost(width),
    )(*square, block, total)


def last_product(cross, block, total):
    width = block.shape[-1]
    return pl.pallas_call(
        last_kernel,
        out_shape=jax.ShapeDtypeStruct((1, 2, 1, width, width), jnp.bfloat16),
        in_specs=vmem(4),
        out_specs=vmem(1)[0],
        compiler_params=params(46),
        cost_estimate=cost(width),
    )(*cross, block, total)


def exchange(pieces):
    return lax.all_to_all(pieces, "energy", split_axis=0, concat_axis=0, tiled=True)


def shards(g_lesser, w_lesser, g_retarded, energy_index):
    width = g_lesser.shape[-1]
    groups = lax.axis_size("energy")
    chain = lax.axis_size("space")
    here = lax.axis_index("space")
    paired = groups >= 4 and groups & (groups - 1) == 0 and (width // groups) % 16 == 0
    here = here.astype(jnp.int32)
    if chain == 4:
        return around_line(here, paired, g_lesser, w_lesser, energy_index, groups, g_retarded)
    if paired:
        *own, _ = gather_paired(g_lesser, w_lesser, energy_index, groups, lambda part: None)
    else:
        own = gather_shared(g_lesser, w_lesser, energy_index, groups)
    cross, tri = (lax.all_gather(part, "space") for part in own)
    blocks = [(here + step) % chain for step in range(chain)]
    sigma_lesser, total, held = own_product(blocks, own, g_retarded)

    def at(gathered, block):
        return lax.dynamic_index_in_dim(gathered, block, 0, False)

    for step in range(1, chain):
        square, block = at(tri, blocks[step]), held[step]
        total = add_part(tri_product, [square], block, total, step == chain - 1)
        square = at(cross, blocks[step])
        if step < chain - 1:
            total = add_part(cross_product, [square], block, total)
    return (sigma_lesser, last_product((square[0], square[1]), held[-1], total))


def around_line(here, paired, g_lesser, w_lesser, energy_index, groups, retarded):
    def swap(part, bits):
        return lax.ppermute(part, "space", [(i, i ^ bits) for i in range(4)])

    first, second = [], []

    def send(part):
        first.append(swap(part, 1))
        second.append(swap(part, 3))

    if paired:
        *own, apart = gather_paired(g_lesser, w_lesser, energy_index, groups, send)
    else:
        own = gather_shared(g_lesser, w_lesser, energy_index, groups)
        send(own[1])
        apart = [own[0][0], own[0][1]]
    far = [swap(comp, 3) for comp in apart]
    first.append(swap(own[0], 1))
    blocks = [here, here ^ 1, here ^ 3, here ^ 2]
    sigma_lesser, total, held = own_product(blocks, after(own, second[0], first[0]), retarded)
    third = swap(after(second[0], total), 1)
    last = [swap(after(far[0], total), 1)]
    total = add_part(tri_product, [first[0]], held[1], total)
    total = add_part(tri_product, [second[0]], held[2], total)
    last.append(swap(after(far[1], total), 1))
    total = add_part(cross_product, far, held[2], total)
    total = add_part(cross_product, [first[1]], held[1], total)
    total = add_part(tri_product, [third], held[3], total, True)
    return (sigma_lesser, last_product(last, held[3], total))


def solution(mesh):
    return jax.shard_map(
        shards,
        mesh=mesh,
        in_specs=(
            P("energy", None, "space", None, None),
            P("energy", None, "space", None, None),
            P("energy", None, "space", None, None, None),
            P(),
        ),
        out_specs=(P("energy", None, "space", None, None), P("energy", None, "space", None, None)),
        check_vma=False,
    )
```

```python
import functools

import jax
import jax.numpy as jnp
from jax import lax
from jax.experimental import pallas as pl
from jax.experimental.pallas import tpu as pltpu
from jax.sharding import PartitionSpec as P


VMEM = pltpu.MemorySpace.VMEM
SMEM = pltpu.MemorySpace.SMEM
HBM = pltpu.MemorySpace.HBM

SMALL = pl.CostEstimate(flops=1, bytes_accessed=1, transcendentals=0)


def vmem(count):
    return [pl.BlockSpec(memory_space=VMEM)] * count


def params(mib):
    return pltpu.CompilerParams(vmem_limit_bytes=mib * 2**20)


def grid_of(shape, row_offset=0):
    rows = lax.broadcasted_iota(jnp.int32, shape, 0) + row_offset
    cols = lax.broadcasted_iota(jnp.int32, shape, 1)
    return rows, cols


def pack_kernel(green, screen, cross, tri):
    half = green.shape[-1] // 2
    rows, cols = grid_of((half, half))
    upper = rows < cols
    diagonal = rows == cols
    for place, source in enumerate((green, screen)):
        a_re = source[0, 0, 0, :half, :half].astype(jnp.float32)
        a_im = source[0, 1, 0, :half, :half].astype(jnp.float32)
        d_re = source[0, 0, 0, half:, half:].astype(jnp.float32)
        d_im = source[0, 1, 0, half:, half:].astype(jnp.float32)
        t_re = jnp.where(upper, a_re, jnp.where(diagonal, a_im, d_re)).astype(jnp.bfloat16)
        t_im = jnp.where(upper, a_im, d_im).astype(jnp.bfloat16)
        c_re = source[0, 0, 0, :half, half:]
        c_im = source[0, 1, 0, :half, half:]
        shape = cross.shape[:1] + cross.shape[3:]
        cross[:, place, 0] = c_re.reshape(shape)
        cross[:, place, 1] = c_im.reshape(shape)
        tri[:, place, 0] = t_re.reshape(shape)
        tri[:, place, 1] = t_im.reshape(shape)


def pack(green, screen, parts):
    half = green.shape[-1] // 2
    out = jax.ShapeDtypeStruct((parts, 2, 2, half // parts, half), jnp.bfloat16)
    return pl.pallas_call(
        pack_kernel,
        out_shape=(out, out),
        in_specs=vmem(2),
        out_specs=tuple(vmem(2)),
        compiler_params=params(24),
    )(green, screen)


def split_rows(packed, groups):
    _, fields, comps, half, width = packed.shape
    shaped = packed.reshape(fields, comps, groups, half // groups, width)
    return jnp.moveaxis(shaped, 2, 0)


def conv_kernel(has_diagonal, index, offset, pieces, out, green, screen, place):
    count, _, _, rows, width = pieces.shape

    def scatter(stored, carry):
        point = index[stored]
        place[point] = stored
        green[point] = pieces[stored, 0].astype(jnp.float32)
        screen[point] = pieces[stored, 1].astype(jnp.float32)
        return carry

    unroll = count <= 16
    lax.fori_loop(0, count, scatter, 0, unroll=unroll)
    scale = count**-0.5
    zero = jnp.zeros((rows, width), jnp.float32)

    def one(point, carry):
        total = point + count // 2

        def term(first, sums):
            both_re, both_im, mixed = sums
            g_re = green[first, 0]
            g_im = green[first, 1]
            w_re = screen[total - first, 0]
            w_im = screen[total - first, 1]
            return (
                both_re + g_re * w_re,
                both_im + g_im * w_im,
                mixed + g_re * w_im + g_im * w_re,
            )

        if unroll:
            sums = (zero, zero, zero)
            for first in range(max(0, total - count + 1), min(count - 1, total) + 1):
                sums = term(first, sums)
        else:
            low = jnp.maximum(0, total - count + 1)
            high = jnp.minimum(count - 1, total) + 1
            sums = lax.fori_loop(low, high, term, (zero, zero, zero))
        both_re, both_im, mixed = sums
        s_re = -scale * mixed
        s_im = scale * (both_re - both_im)
        if has_diagonal:
            at_rows, at_cols = grid_of((rows, width), offset[0])
            diagonal = at_rows == at_cols
            s_re = jnp.where(diagonal, -scale * both_re, s_re)
            s_im = jnp.where(diagonal, -scale * both_im, s_im)
        stored = place[point]
        out[stored, 0] = s_re.astype(jnp.bfloat16)
        out[stored, 1] = s_im.astype(jnp.bfloat16)
        return carry

    if unroll:
        for point in range(count):
            one(point, 0)
    else:
        lax.fori_loop(0, count, one, 0)


def convolve(pieces, energy_index, row_offset, has_diagonal):
    count, _, _, rows, width = pieces.shape
    smem = pl.BlockSpec(memory_space=SMEM)
    return pl.pallas_call(
        functools.partial(conv_kernel, has_diagonal),
        out_shape=jax.ShapeDtypeStruct((count, 2, rows, width), jnp.bfloat16),
        in_specs=[smem, smem] + vmem(1),
        out_specs=vmem(1)[0],
        scratch_shapes=[
            pltpu.VMEM((count, 2, rows, width), jnp.float32),
            pltpu.VMEM((count, 2, rows, width), jnp.float32),
            pltpu.SMEM((count,), jnp.int32),
        ],
        compiler_params=params(24),
    )(energy_index, row_offset, pieces)


def share_of(me, d, rows):
    return pl.ds(pl.multiple_of((lax.shift_right_logical(me, 1) ^ d) * rows, rows), rows)


def cut_kernel(chips, me, green, screen, *rest):
    outs = rest[:chips]
    near, far, sems, cross_sems = rest[chips:]
    half = near.shape[-1]
    rows = half // chips
    copies = []
    for field, source in enumerate((green, screen)):
        for place, (held, lines) in enumerate(((near, slice(0, half)), (far, slice(half, None)))):
            copy = pltpu.make_async_copy(
                source.at[0, :, 0, lines, lines], held.at[field], sems.at[field, place]
            )
            copy.start()
            copies.append(copy)
    cross_copies = []
    for d in range(chips):
        for field, source in enumerate((green, screen)):
            part = source.at[0, :, 0, share_of(me[0], d, rows), half:]
            copy = pltpu.make_async_copy(part, outs[d].at[0, field], cross_sems.at[d, field])
            copy.start()
            cross_copies.append(copy)
    at_rows, at_cols = grid_of((rows, half))
    for field in range(2):
        for copy in copies[2 * field : 2 * field + 2]:
            copy.wait()
        for d in range(chips):
            lines = share_of(me[0], d, rows)
            here = at_rows + (lax.shift_right_logical(me[0], 1) ^ d) * rows
            upper = here < at_cols
            diagonal = here == at_cols
            a_re = near[field, 0, lines, :].astype(jnp.float32)
            a_im = near[field, 1, lines, :].astype(jnp.float32)
            d_re = far[field, 0, lines, :].astype(jnp.float32)
            d_im = far[field, 1, lines, :].astype(jnp.float32)
            t_re = jnp.where(upper, a_re, jnp.where(diagonal, a_im, d_re))
            outs[d][1, field, 0] = t_re.astype(jnp.bfloat16)
            outs[d][1, field, 1] = jnp.where(upper, a_im, d_im).astype(jnp.bfloat16)
    for copy in cross_copies:
        copy.wait()


def cut(me, green, screen, chips):
    half = green.shape[-1] // 2
    piece = jax.ShapeDtypeStruct((2, 2, 2, half // chips, half), jnp.bfloat16)
    return pl.pallas_call(
        functools.partial(cut_kernel, chips),
        out_shape=(piece,) * chips,
        in_specs=[pl.BlockSpec(memory_space=SMEM)] + [pl.BlockSpec(memory_space=HBM)] * 2,
        out_specs=tuple(vmem(chips)),
        scratch_shapes=[pltpu.VMEM((2, 2, half, half), jnp.bfloat16)] * 2
        + [pltpu.SemaphoreType.DMA((2, 2)), pltpu.SemaphoreType.DMA((chips, 2))],
        compiler_params=params(52),
        cost_estimate=SMALL,
    )(me, green, screen)


def bind_kernel(part, *refs):
    for place, piece in enumerate(refs[:-1]):
        refs[-1][place] = piece[part]


def bind(pieces, part):
    shape = (len(pieces),) + pieces[0].shape[1:]
    return pl.pallas_call(
        functools.partial(bind_kernel, part),
        out_shape=jax.ShapeDtypeStruct(shape, jnp.bfloat16),
        in_specs=vmem(len(pieces)),
        out_specs=vmem(1)[0],
        compiler_params=params(32),
        cost_estimate=SMALL,
    )(*pieces)


def conv_pieces_kernel(chips, part, me, index, *rest):
    same = rest[:chips][::-1]
    beside, other = rest[chips : chips + 2]
    outs = rest[chips + 2 : 2 * chips + 2]
    green, screen, sums, place = rest[2 * chips + 2 :]
    groups = 2 * chips
    rows, width = sums.shape[2:]
    for core in range(2):
        for d in range(chips):
            stored = me[0] ^ (2 * d + core)
            point = index[stored]
            place[point] = stored
            if core == 0:
                green[point] = same[d][part, 0]
                screen[point] = same[d][part, 1]
            elif d == 0:
                green[point] = beside[part, 0]
                screen[point] = beside[part, 1]
            else:
                green[point] = other[chips - 1 - d, 0]
                screen[point] = other[chips - 1 - d, 1]
    scale = groups**-0.5
    tall = 16
    for point in range(groups):

        @pl.when(((place[point] ^ me[0]) & 1) == 0)
        def _():
            total = point + groups // 2
            for first_row in range(0, rows, tall):
                for first_col in range(0, width, 128):
                    at = (slice(first_row, first_row + tall), slice(first_col, first_col + 128))
                    both_re = both_im = mixed = None
                    for p in range(max(0, total - groups + 1), min(groups - 1, total) + 1):
                        g_re = green[(p, 0) + at].astype(jnp.float32)
                        g_im = green[(p, 1) + at].astype(jnp.float32)
                        w_re = screen[(total - p, 0) + at].astype(jnp.float32)
                        w_im = screen[(total - p, 1) + at].astype(jnp.float32)
                        re = g_re * w_re
                        im = g_im * w_im
                        mix = g_re * w_im + g_im * w_re
                        both_re = re if both_re is None else both_re + re
                        both_im = im if both_im is None else both_im + im
                        mixed = mix if mixed is None else mixed + mix
                    s_re = -scale * mixed
                    s_im = scale * (both_re - both_im)
                    if part == 1:
                        first = lax.shift_right_logical(me[0], 1) * rows + first_row
                        at_rows, at_cols = grid_of((tall, 128), first)
                        diagonal = at_rows == at_cols + first_col
                        s_re = jnp.where(diagonal, -scale * both_re, s_re)
                        s_im = jnp.where(diagonal, -scale * both_im, s_im)
                    sums[(point, 0) + at] = s_re.astype(jnp.bfloat16)
                    sums[(point, 1) + at] = s_im.astype(jnp.bfloat16)

    for d in range(chips):
        outs[d][...] = sums[index[me[0] ^ (2 * d)]]


def conv_pieces(me, energy_index, same, beside, other, part):
    chips = len(same)
    shape = same[0].shape[2:]
    smem = pl.BlockSpec(memory_space=SMEM)
    return pl.pallas_call(
        functools.partial(conv_pieces_kernel, chips, part),
        out_shape=(jax.ShapeDtypeStruct(shape, jnp.bfloat16),) * chips,
        in_specs=[smem, smem] + vmem(chips + 2),
        out_specs=tuple(vmem(chips)),
        scratch_shapes=[pltpu.VMEM((2 * chips,) + shape, jnp.bfloat16)] * 3
        + [pltpu.SMEM((2 * chips,), jnp.int32)],
        compiler_params=params(32),
        cost_estimate=SMALL,
    )(me, energy_index, *same[::-1], beside, other)


def join_kernel(chips, me, *rest):
    pieces, out = rest[:chips][::-1], rest[chips]
    rows = pieces[0].shape[1]
    for d in range(chips):
        out[:, share_of(me[0], d, rows), :] = pieces[d][...]


def join_apart_kernel(chips, me, *rest):
    pieces = rest[:chips][::-1]
    out, *apart = rest[chips:]
    rows = pieces[0].shape[1]
    for d in range(chips):
        lines = share_of(me[0], d, rows)
        out[:, lines, :] = pieces[d][...]
        for comp in range(2):
            apart[comp][lines, :] = pieces[d][comp]


def join_apart(me, pieces):
    half = pieces[0].shape[-1]
    one = jax.ShapeDtypeStruct((half, half), jnp.bfloat16)
    return pl.pallas_call(
        functools.partial(join_apart_kernel, len(pieces)),
        out_shape=(jax.ShapeDtypeStruct((2, half, half), jnp.bfloat16), one, one),
        in_specs=[pl.BlockSpec(memory_space=SMEM)] + vmem(len(pieces)),
        out_specs=tuple(vmem(3)),
        compiler_params=params(32),
        cost_estimate=SMALL,
    )(me, *pieces[::-1])


def join(me, pieces):
    half = pieces[0].shape[-1]
    return pl.pallas_call(
        functools.partial(join_kernel, len(pieces)),
        out_shape=jax.ShapeDtypeStruct((2, half, half), jnp.bfloat16),
        in_specs=[pl.BlockSpec(memory_space=SMEM)] + vmem(len(pieces)),
        out_specs=vmem(1)[0],
        compiler_params=params(32),
        cost_estimate=SMALL,
    )(me, *pieces[::-1])


def swap(piece, d, groups):
    return lax.ppermute(piece, "energy", [(i, i ^ d) for i in range(groups)]) if d else piece


def after(value, *earlier):
    return lax.optimization_barrier((value, earlier))[0]


def gather_paired(g_lesser, w_lesser, energy_index, groups, send):
    me = lax.axis_index("energy").astype(jnp.int32).reshape(1)
    chips = groups // 2

    def over(pieces):
        return [swap(pieces[d], 2 * d, groups) for d in range(chips)]

    pieces = cut(me, g_lesser, w_lesser, chips)
    same = over(pieces)
    beside = swap(pieces[0], 1, groups)
    bound = [bind(after(same[:0:-1], beside), part) for part in range(2)]
    other = [swap(piece, 1, groups) for piece in bound]
    mine = conv_pieces(me, energy_index, same, beside, other[1], 1)
    own_tri = join(me, over(mine))
    send(own_tri)
    mine = conv_pieces(me, energy_index, same, beside, after(other[0], own_tri), 0)
    own_cross, *apart = join_apart(me, over(mine))
    return own_cross, own_tri, apart


def gather_shared(g_lesser, w_lesser, energy_index, groups):
    half = g_lesser.shape[-1] // 2
    rows = half // groups
    cross, tri = (split_rows(packed, groups) for packed in pack(g_lesser, w_lesser, 1))
    offset = (lax.axis_index("energy") * rows).astype(jnp.int32).reshape(1)
    own = []
    for pieces, has_diagonal in ((cross, False), (tri, True)):
        shares = convolve(exchange(pieces), energy_index, offset, has_diagonal)
        own.append(jnp.moveaxis(exchange(shares), 0, 1).reshape(2, half, half))
    return own


def squares(cross, tri):
    return cross[0], cross[1], tri[0], tri[1]


def dot(a, b):
    return jnp.dot(a, b, preferred_element_type=jnp.float32)


def dot_t(a, b):
    return lax.dot_general(a, b, (((1,), (1,)), ((), ())), preferred_element_type=jnp.float32)


def product(cross, tri, retarded):
    return product_of(cross, tri, retarded)


def product_of(cross, tri, retarded):
    t_re, t_im = tri[0], tri[1]
    half = t_re.shape[0]
    rows, cols = grid_of((half, half))
    tr = t_re.astype(jnp.float32)
    ti = t_im.astype(jnp.float32)
    diagonal = rows == cols
    a_re = jnp.where(rows < cols, tr, 0.0).astype(jnp.bfloat16)
    a_im = jnp.where(rows < cols, ti, jnp.where(diagonal, 0.5 * tr, 0.0)).astype(jnp.bfloat16)
    d_re = jnp.where(rows > cols, tr, 0.0).astype(jnp.bfloat16)
    d_im = jnp.where(rows > cols, ti, jnp.where(diagonal, 0.5 * ti, 0.0)).astype(jnp.bfloat16)
    g_re = retarded[0]
    g_im = retarded[1]
    near = jnp.concatenate([g_re[:, :half], g_im[:, :half]], axis=1)
    all_g = jnp.concatenate([g_re, g_im], axis=1)
    if cross is None:
        far = jnp.concatenate([g_re[:, half:], g_im[:, half:]], axis=1)
        right_re = [d_re, -d_im]
        right_im = [d_im, d_re]
    else:
        c_re, c_im = cross[0], cross[1]
        far = all_g
        right_re = [c_re, d_re, -c_im, -d_im]
        right_im = [c_im, d_im, c_re, d_re]
    l_re = jnp.concatenate(
        [
            dot(near, jnp.concatenate([a_re, -a_im], axis=0)),
            dot(far, jnp.concatenate(right_re, axis=0)),
        ],
        axis=1,
    ).astype(jnp.bfloat16)
    l_im = jnp.concatenate(
        [
            dot(near, jnp.concatenate([a_im, a_re], axis=0)),
            dot(far, jnp.concatenate(right_im, axis=0)),
        ],
        axis=1,
    ).astype(jnp.bfloat16)
    x_re = dot_t(jnp.concatenate([l_re, l_im], axis=1), all_g)
    x_im = dot_t(jnp.concatenate([l_im, -l_re], axis=1), all_g)
    return x_re, x_im


def tri_product(tri, retarded):
    return product_of(None, tri, retarded)


def cross_left(cross, retarded):
    c_re, c_im = cross[0][...], cross[1][...]
    half = c_re.shape[0]
    g_re = retarded[0]
    g_im = retarded[1]
    near = jnp.concatenate([g_re[:, :half], g_im[:, :half]], axis=1)
    far = jnp.concatenate([g_re[:, half:], g_im[:, half:]], axis=1)
    l_re = dot(near, jnp.concatenate([c_re, -c_im], axis=0)).astype(jnp.bfloat16)
    l_im = dot(near, jnp.concatenate([c_im, c_re], axis=0)).astype(jnp.bfloat16)
    return l_re, l_im, far


def cross_product(cross, retarded):
    l_re, l_im, far = cross_left(cross, retarded)
    x_re = dot_t(jnp.concatenate([l_re, l_im], axis=1), far)
    x_im = dot_t(jnp.concatenate([l_im, -l_re], axis=1), far)
    return x_re, x_im


def own_kernel(where, cross, tri, retarded, sigma, total, *rest):
    blocks, sems = rest[:-1], rest[-1]
    copies = [
        pltpu.make_async_copy(retarded.at[0, :, 0, where[place]], held, sems.at[place])
        for place, held in enumerate(blocks)
    ]
    for copy in copies:
        copy.start()
    c_re, c_im, t_re, t_im = squares(cross, tri)
    half = c_re.shape[0]
    rows, cols = grid_of((half, half))
    upper = rows < cols
    diagonal = rows == cols
    tr = t_re.astype(jnp.float32)
    ti = t_im.astype(jnp.float32)
    trt = tr.T
    tit = ti.T
    zero = jnp.zeros_like(tr)
    bf = jnp.bfloat16
    sigma[0, 0, 0, :half, half:] = c_re
    sigma[0, 1, 0, :half, half:] = c_im
    sigma[0, 0, 0, half:, :half] = (-(c_re.astype(jnp.float32).T)).astype(bf)
    sigma[0, 1, 0, half:, :half] = c_im.astype(jnp.float32).T.astype(bf)
    sigma[0, 0, 0, :half, :half] = jnp.where(upper, tr, jnp.where(diagonal, zero, -trt)).astype(bf)
    sigma[0, 1, 0, :half, :half] = jnp.where(upper, ti, jnp.where(diagonal, tr, tit)).astype(bf)
    sigma[0, 0, 0, half:, half:] = jnp.where(upper, -trt, jnp.where(diagonal, zero, tr)).astype(bf)
    sigma[0, 1, 0, half:, half:] = jnp.where(upper, tit, ti).astype(bf)
    for copy in copies:
        copy.wait()
    total[0], total[1] = product(cross, tri, blocks[0])


def part_kernel(part, *refs):
    *square, block, total, out = refs
    square = square if len(square) > 1 else square[0]
    x_re, x_im = part(square, block)
    x_re += total[0]
    x_im += total[1]
    out[0] = x_re
    out[1] = x_im


def last_kernel(c_re, c_im, block, total, out):
    x_re, x_im = cross_product((c_re, c_im), block)
    x_re += total[0]
    x_im += total[1]
    out[0, 0, 0] = (x_re - x_re.T).astype(jnp.bfloat16)
    out[0, 1, 0] = (x_im + x_im.T).astype(jnp.bfloat16)


def cost(width):
    return pl.CostEstimate(flops=14 * width**3, bytes_accessed=8 * width**2, transcendentals=0)


def own_product(blocks, own, retarded):
    width = retarded.shape[-1]
    count = len(blocks)
    block_shape = jax.ShapeDtypeStruct((2, width, width), jnp.bfloat16)
    sigma, total, *held = pl.pallas_call(
        own_kernel,
        out_shape=(
            jax.ShapeDtypeStruct((1, 2, 1, width, width), jnp.bfloat16),
            jax.ShapeDtypeStruct((2, width, width), jnp.float32),
        )
        + (block_shape,) * count,
        in_specs=[pl.BlockSpec(memory_space=SMEM)] + vmem(2) + [pl.BlockSpec(memory_space=HBM)],
        out_specs=tuple(vmem(2 + count)),
        scratch_shapes=[pltpu.SemaphoreType.DMA((count,))],
        compiler_params=params(44),
        cost_estimate=cost(width),
    )(jnp.stack(blocks), *own, retarded)
    return sigma, total, held


def add_part(part, square, block, total):
    width = block.shape[-1]
    return pl.pallas_call(
        functools.partial(part_kernel, part),
        out_shape=jax.ShapeDtypeStruct(total.shape, jnp.float32),
        in_specs=vmem(len(square) + 2),
        out_specs=vmem(1)[0],
        compiler_params=params(36),
        cost_estimate=cost(width),
    )(*square, block, total)


def last_product(cross, block, total):
    width = block.shape[-1]
    return pl.pallas_call(
        last_kernel,
        out_shape=jax.ShapeDtypeStruct((1, 2, 1, width, width), jnp.bfloat16),
        in_specs=vmem(4),
        out_specs=vmem(1)[0],
        compiler_params=params(46),
        cost_estimate=cost(width),
    )(*cross, block, total)


def exchange(pieces):
    return lax.all_to_all(pieces, "energy", split_axis=0, concat_axis=0, tiled=True)


def shards(g_lesser, w_lesser, g_retarded, energy_index):
    width = g_lesser.shape[-1]
    groups = lax.axis_size("energy")
    chain = lax.axis_size("space")
    here = lax.axis_index("space")
    paired = groups >= 4 and groups & (groups - 1) == 0 and (width // groups) % 16 == 0
    here = here.astype(jnp.int32)
    if chain == 4:
        return around_line(here, paired, g_lesser, w_lesser, energy_index, groups, g_retarded)
    if paired:
        *own, _ = gather_paired(g_lesser, w_lesser, energy_index, groups, lambda part: None)
    else:
        own = gather_shared(g_lesser, w_lesser, energy_index, groups)
    cross, tri = (lax.all_gather(part, "space") for part in own)
    blocks = [(here + step) % chain for step in range(chain)]
    sigma_lesser, total, held = own_product(blocks, own, g_retarded)

    def at(gathered, block):
        return lax.dynamic_index_in_dim(gathered, block, 0, False)

    for step in range(1, chain):
        square, block = at(tri, blocks[step]), held[step]
        total = add_part(tri_product, [square], block, total)
        square = at(cross, blocks[step])
        if step < chain - 1:
            total = add_part(cross_product, [square], block, total)
    return (sigma_lesser, last_product((square[0], square[1]), held[-1], total))


def around_line(here, paired, g_lesser, w_lesser, energy_index, groups, retarded):
    def swap(part, bits):
        return lax.ppermute(part, "space", [(i, i ^ bits) for i in range(4)])

    first, second = [], []

    def send(part):
        first.append(swap(part, 1))
        second.append(swap(part, 3))

    if paired:
        *own, apart = gather_paired(g_lesser, w_lesser, energy_index, groups, send)
    else:
        own = gather_shared(g_lesser, w_lesser, energy_index, groups)
        send(own[1])
        apart = [own[0][0], own[0][1]]
    far = [swap(comp, 3) for comp in apart]
    first.append(swap(after(own[0], first[0]), 1))
    blocks = [here, here ^ 1, here ^ 3, here ^ 2]
    sigma_lesser, total, held = own_product(blocks, after(own, first[0]), retarded)
    third = swap(after(second[0], total), 1)
    last = [swap(after(far[0], total), 1)]
    total = add_part(tri_product, [first[0]], held[1], total)
    total = add_part(tri_product, [second[0]], held[2], total)
    last.append(swap(after(far[1], total), 1))
    total = add_part(cross_product, far, held[2], total)
    total = add_part(cross_product, [first[1]], held[1], total)
    total = add_part(tri_product, [third], held[3], total)
    return (sigma_lesser, last_product(last, held[3], total))


def solution(mesh):
    return jax.shard_map(
        shards,
        mesh=mesh,
        in_specs=(
            P("energy", None, "space", None, None),
            P("energy", None, "space", None, None),
            P("energy", None, "space", None, None, None),
            P(),
        ),
        out_specs=(P("energy", None, "space", None, None), P("energy", None, "space", None, None)),
        check_vma=False,
    )
```

```python
import functools

import jax
import jax.numpy as jnp
from jax import lax
from jax.experimental import pallas as pl
from jax.experimental.pallas import tpu as pltpu
from jax.sharding import PartitionSpec as P


VMEM = pltpu.MemorySpace.VMEM
SMEM = pltpu.MemorySpace.SMEM
HBM = pltpu.MemorySpace.HBM

SMALL = pl.CostEstimate(flops=1, bytes_accessed=1, transcendentals=0)


def vmem(count):
    return [pl.BlockSpec(memory_space=VMEM)] * count


def params(mib):
    return pltpu.CompilerParams(vmem_limit_bytes=mib * 2**20)


def grid_of(shape, row_offset=0):
    rows = lax.broadcasted_iota(jnp.int32, shape, 0) + row_offset
    cols = lax.broadcasted_iota(jnp.int32, shape, 1)
    return rows, cols


def pack_kernel(green, screen, cross, tri):
    half = green.shape[-1] // 2
    rows, cols = grid_of((half, half))
    upper = rows < cols
    diagonal = rows == cols
    for place, source in enumerate((green, screen)):
        a_re = source[0, 0, 0, :half, :half].astype(jnp.float32)
        a_im = source[0, 1, 0, :half, :half].astype(jnp.float32)
        d_re = source[0, 0, 0, half:, half:].astype(jnp.float32)
        d_im = source[0, 1, 0, half:, half:].astype(jnp.float32)
        t_re = jnp.where(upper, a_re, jnp.where(diagonal, a_im, d_re)).astype(jnp.bfloat16)
        t_im = jnp.where(upper, a_im, d_im).astype(jnp.bfloat16)
        c_re = source[0, 0, 0, :half, half:]
        c_im = source[0, 1, 0, :half, half:]
        shape = cross.shape[:1] + cross.shape[3:]
        cross[:, place, 0] = c_re.reshape(shape)
        cross[:, place, 1] = c_im.reshape(shape)
        tri[:, place, 0] = t_re.reshape(shape)
        tri[:, place, 1] = t_im.reshape(shape)


def pack(green, screen, parts):
    half = green.shape[-1] // 2
    out = jax.ShapeDtypeStruct((parts, 2, 2, half // parts, half), jnp.bfloat16)
    return pl.pallas_call(
        pack_kernel,
        out_shape=(out, out),
        in_specs=vmem(2),
        out_specs=tuple(vmem(2)),
        compiler_params=params(24),
    )(green, screen)


def split_rows(packed, groups):
    _, fields, comps, half, width = packed.shape
    shaped = packed.reshape(fields, comps, groups, half // groups, width)
    return jnp.moveaxis(shaped, 2, 0)


def conv_kernel(has_diagonal, index, offset, pieces, out, green, screen, place):
    count, _, _, rows, width = pieces.shape

    def scatter(stored, carry):
        point = index[stored]
        place[point] = stored
        green[point] = pieces[stored, 0].astype(jnp.float32)
        screen[point] = pieces[stored, 1].astype(jnp.float32)
        return carry

    unroll = count <= 16
    lax.fori_loop(0, count, scatter, 0, unroll=unroll)
    scale = count**-0.5
    zero = jnp.zeros((rows, width), jnp.float32)

    def one(point, carry):
        total = point + count // 2

        def term(first, sums):
            both_re, both_im, mixed = sums
            g_re = green[first, 0]
            g_im = green[first, 1]
            w_re = screen[total - first, 0]
            w_im = screen[total - first, 1]
            return (
                both_re + g_re * w_re,
                both_im + g_im * w_im,
                mixed + g_re * w_im + g_im * w_re,
            )

        if unroll:
            sums = (zero, zero, zero)
            for first in range(max(0, total - count + 1), min(count - 1, total) + 1):
                sums = term(first, sums)
        else:
            low = jnp.maximum(0, total - count + 1)
            high = jnp.minimum(count - 1, total) + 1
            sums = lax.fori_loop(low, high, term, (zero, zero, zero))
        both_re, both_im, mixed = sums
        s_re = -scale * mixed
        s_im = scale * (both_re - both_im)
        if has_diagonal:
            at_rows, at_cols = grid_of((rows, width), offset[0])
            diagonal = at_rows == at_cols
            s_re = jnp.where(diagonal, -scale * both_re, s_re)
            s_im = jnp.where(diagonal, -scale * both_im, s_im)
        stored = place[point]
        out[stored, 0] = s_re.astype(jnp.bfloat16)
        out[stored, 1] = s_im.astype(jnp.bfloat16)
        return carry

    if unroll:
        for point in range(count):
            one(point, 0)
    else:
        lax.fori_loop(0, count, one, 0)


def convolve(pieces, energy_index, row_offset, has_diagonal):
    count, _, _, rows, width = pieces.shape
    smem = pl.BlockSpec(memory_space=SMEM)
    return pl.pallas_call(
        functools.partial(conv_kernel, has_diagonal),
        out_shape=jax.ShapeDtypeStruct((count, 2, rows, width), jnp.bfloat16),
        in_specs=[smem, smem] + vmem(1),
        out_specs=vmem(1)[0],
        scratch_shapes=[
            pltpu.VMEM((count, 2, rows, width), jnp.float32),
            pltpu.VMEM((count, 2, rows, width), jnp.float32),
            pltpu.SMEM((count,), jnp.int32),
        ],
        compiler_params=params(24),
    )(energy_index, row_offset, pieces)


def share_of(me, d, rows):
    return pl.ds(pl.multiple_of((lax.shift_right_logical(me, 1) ^ d) * rows, rows), rows)


def cut_kernel(chips, me, green, screen, *rest):
    outs = rest[:chips]
    near, far, sems, cross_sems = rest[chips:]
    half = near.shape[-1]
    rows = half // chips
    copies = []
    for field, source in enumerate((green, screen)):
        for place, (held, lines) in enumerate(((near, slice(0, half)), (far, slice(half, None)))):
            copy = pltpu.make_async_copy(
                source.at[0, :, 0, lines, lines], held.at[field], sems.at[field, place]
            )
            copy.start()
            copies.append(copy)
    cross_copies = []
    for d in range(chips):
        for field, source in enumerate((green, screen)):
            part = source.at[0, :, 0, share_of(me[0], d, rows), half:]
            copy = pltpu.make_async_copy(part, outs[d].at[0, field], cross_sems.at[d, field])
            copy.start()
            cross_copies.append(copy)
    at_rows, at_cols = grid_of((rows, half))
    for field in range(2):
        for copy in copies[2 * field : 2 * field + 2]:
            copy.wait()
        for d in range(chips):
            lines = share_of(me[0], d, rows)
            here = at_rows + (lax.shift_right_logical(me[0], 1) ^ d) * rows
            upper = here < at_cols
            diagonal = here == at_cols
            a_re = near[field, 0, lines, :].astype(jnp.float32)
            a_im = near[field, 1, lines, :].astype(jnp.float32)
            d_re = far[field, 0, lines, :].astype(jnp.float32)
            d_im = far[field, 1, lines, :].astype(jnp.float32)
            t_re = jnp.where(upper, a_re, jnp.where(diagonal, a_im, d_re))
            outs[d][1, field, 0] = t_re.astype(jnp.bfloat16)
            outs[d][1, field, 1] = jnp.where(upper, a_im, d_im).astype(jnp.bfloat16)
    for copy in cross_copies:
        copy.wait()


def cut(me, green, screen, chips):
    half = green.shape[-1] // 2
    piece = jax.ShapeDtypeStruct((2, 2, 2, half // chips, half), jnp.bfloat16)
    return pl.pallas_call(
        functools.partial(cut_kernel, chips),
        out_shape=(piece,) * chips,
        in_specs=[pl.BlockSpec(memory_space=SMEM)] + [pl.BlockSpec(memory_space=HBM)] * 2,
        out_specs=tuple(vmem(chips)),
        scratch_shapes=[pltpu.VMEM((2, 2, half, half), jnp.bfloat16)] * 2
        + [pltpu.SemaphoreType.DMA((2, 2)), pltpu.SemaphoreType.DMA((chips, 2))],
        compiler_params=params(52),
        cost_estimate=SMALL,
    )(me, green, screen)


def bind_kernel(part, *refs):
    for place, piece in enumerate(refs[:-1]):
        refs[-1][place] = piece[part]


def bind(pieces, part):
    shape = (len(pieces),) + pieces[0].shape[1:]
    return pl.pallas_call(
        functools.partial(bind_kernel, part),
        out_shape=jax.ShapeDtypeStruct(shape, jnp.bfloat16),
        in_specs=vmem(len(pieces)),
        out_specs=vmem(1)[0],
        compiler_params=params(32),
        cost_estimate=SMALL,
    )(*pieces)


def conv_pieces_kernel(chips, part, me, index, *rest):
    same = rest[:chips][::-1]
    beside, other = rest[chips : chips + 2]
    outs = rest[chips + 2 : 2 * chips + 2]
    green, screen, sums, place = rest[2 * chips + 2 :]
    groups = 2 * chips
    rows, width = sums.shape[2:]
    for core in range(2):
        for d in range(chips):
            stored = me[0] ^ (2 * d + core)
            point = index[stored]
            place[point] = stored
            if core == 0:
                green[point] = same[d][part, 0]
                screen[point] = same[d][part, 1]
            elif d == 0:
                green[point] = beside[part, 0]
                screen[point] = beside[part, 1]
            else:
                green[point] = other[chips - 1 - d, 0]
                screen[point] = other[chips - 1 - d, 1]
    scale = groups**-0.5
    tall = 16
    for point in range(groups):

        @pl.when(((place[point] ^ me[0]) & 1) == 0)
        def _():
            total = point + groups // 2
            for first_row in range(0, rows, tall):
                for first_col in range(0, width, 128):
                    at = (slice(first_row, first_row + tall), slice(first_col, first_col + 128))
                    both_re = both_im = mixed = None
                    for p in range(max(0, total - groups + 1), min(groups - 1, total) + 1):
                        g_re = green[(p, 0) + at].astype(jnp.float32)
                        g_im = green[(p, 1) + at].astype(jnp.float32)
                        w_re = screen[(total - p, 0) + at].astype(jnp.float32)
                        w_im = screen[(total - p, 1) + at].astype(jnp.float32)
                        re = g_re * w_re
                        im = g_im * w_im
                        mix = g_re * w_im + g_im * w_re
                        both_re = re if both_re is None else both_re + re
                        both_im = im if both_im is None else both_im + im
                        mixed = mix if mixed is None else mixed + mix
                    s_re = -scale * mixed
                    s_im = scale * (both_re - both_im)
                    if part == 1:
                        first = lax.shift_right_logical(me[0], 1) * rows + first_row
                        at_rows, at_cols = grid_of((tall, 128), first)
                        diagonal = at_rows == at_cols + first_col
                        s_re = jnp.where(diagonal, -scale * both_re, s_re)
                        s_im = jnp.where(diagonal, -scale * both_im, s_im)
                    sums[(point, 0) + at] = s_re.astype(jnp.bfloat16)
                    sums[(point, 1) + at] = s_im.astype(jnp.bfloat16)

    for d in range(chips):
        outs[d][...] = sums[index[me[0] ^ (2 * d)]]


def conv_pieces(me, energy_index, same, beside, other, part):
    chips = len(same)
    shape = same[0].shape[2:]
    smem = pl.BlockSpec(memory_space=SMEM)
    return pl.pallas_call(
        functools.partial(conv_pieces_kernel, chips, part),
        out_shape=(jax.ShapeDtypeStruct(shape, jnp.bfloat16),) * chips,
        in_specs=[smem, smem] + vmem(chips + 2),
        out_specs=tuple(vmem(chips)),
        scratch_shapes=[pltpu.VMEM((2 * chips,) + shape, jnp.bfloat16)] * 3
        + [pltpu.SMEM((2 * chips,), jnp.int32)],
        compiler_params=params(32),
        cost_estimate=SMALL,
    )(me, energy_index, *same[::-1], beside, other)


def join_kernel(chips, me, *rest):
    pieces, out = rest[:chips][::-1], rest[chips]
    rows = pieces[0].shape[1]
    for d in range(chips):
        out[:, share_of(me[0], d, rows), :] = pieces[d][...]


def join_apart_kernel(chips, me, *rest):
    pieces = rest[:chips][::-1]
    out, *apart = rest[chips:]
    rows = pieces[0].shape[1]
    for d in range(chips):
        lines = share_of(me[0], d, rows)
        out[:, lines, :] = pieces[d][...]
        for comp in range(2):
            apart[comp][lines, :] = pieces[d][comp]


def join_apart(me, pieces):
    half = pieces[0].shape[-1]
    one = jax.ShapeDtypeStruct((half, half), jnp.bfloat16)
    return pl.pallas_call(
        functools.partial(join_apart_kernel, len(pieces)),
        out_shape=(jax.ShapeDtypeStruct((2, half, half), jnp.bfloat16), one, one),
        in_specs=[pl.BlockSpec(memory_space=SMEM)] + vmem(len(pieces)),
        out_specs=tuple(vmem(3)),
        compiler_params=params(32),
        cost_estimate=SMALL,
    )(me, *pieces[::-1])


def join(me, pieces):
    half = pieces[0].shape[-1]
    return pl.pallas_call(
        functools.partial(join_kernel, len(pieces)),
        out_shape=jax.ShapeDtypeStruct((2, half, half), jnp.bfloat16),
        in_specs=[pl.BlockSpec(memory_space=SMEM)] + vmem(len(pieces)),
        out_specs=vmem(1)[0],
        compiler_params=params(32),
        cost_estimate=SMALL,
    )(me, *pieces[::-1])


def swap(piece, d, groups):
    return lax.ppermute(piece, "energy", [(i, i ^ d) for i in range(groups)]) if d else piece


def after(value, *earlier):
    return lax.optimization_barrier((value, earlier))[0]


def gather_paired(g_lesser, w_lesser, energy_index, groups, send):
    me = lax.axis_index("energy").astype(jnp.int32).reshape(1)
    chips = groups // 2

    def over(pieces):
        return [swap(pieces[d], 2 * d, groups) for d in range(chips)]

    pieces = cut(me, g_lesser, w_lesser, chips)
    same = over(pieces)
    beside = swap(pieces[0], 1, groups)
    bound = [bind(after(same[:0:-1], beside), part) for part in range(2)]
    other = [swap(piece, 1, groups) for piece in bound]
    mine = conv_pieces(me, energy_index, same, beside, other[1], 1)
    own_tri = join(me, over(mine))
    send(own_tri)
    mine = conv_pieces(me, energy_index, same, beside, after(other[0], own_tri), 0)
    own_cross, *apart = join_apart(me, over(mine))
    return own_cross, own_tri, apart


def gather_shared(g_lesser, w_lesser, energy_index, groups):
    half = g_lesser.shape[-1] // 2
    rows = half // groups
    cross, tri = (split_rows(packed, groups) for packed in pack(g_lesser, w_lesser, 1))
    offset = (lax.axis_index("energy") * rows).astype(jnp.int32).reshape(1)
    own = []
    for pieces, has_diagonal in ((cross, False), (tri, True)):
        shares = convolve(exchange(pieces), energy_index, offset, has_diagonal)
        own.append(jnp.moveaxis(exchange(shares), 0, 1).reshape(2, half, half))
    return own


def squares(cross, tri):
    return cross[0], cross[1], tri[0], tri[1]


def dot(a, b):
    return jnp.dot(a, b, preferred_element_type=jnp.float32)


def dot_t(a, b):
    return lax.dot_general(a, b, (((1,), (1,)), ((), ())), preferred_element_type=jnp.float32)


def product(cross, tri, retarded):
    return product_of(cross, tri, retarded)


def product_of(cross, tri, retarded):
    t_re, t_im = tri[0], tri[1]
    half = t_re.shape[0]
    rows, cols = grid_of((half, half))
    tr = t_re.astype(jnp.float32)
    ti = t_im.astype(jnp.float32)
    diagonal = rows == cols
    a_re = jnp.where(rows < cols, tr, 0.0).astype(jnp.bfloat16)
    a_im = jnp.where(rows < cols, ti, jnp.where(diagonal, 0.5 * tr, 0.0)).astype(jnp.bfloat16)
    d_re = jnp.where(rows > cols, tr, 0.0).astype(jnp.bfloat16)
    d_im = jnp.where(rows > cols, ti, jnp.where(diagonal, 0.5 * ti, 0.0)).astype(jnp.bfloat16)
    g_re = retarded[0]
    g_im = retarded[1]
    near = jnp.concatenate([g_re[:, :half], g_im[:, :half]], axis=1)
    all_g = jnp.concatenate([g_re, g_im], axis=1)
    if cross is None:
        far = jnp.concatenate([g_re[:, half:], g_im[:, half:]], axis=1)
        right_re = [d_re, -d_im]
        right_im = [d_im, d_re]
    else:
        c_re, c_im = cross[0], cross[1]
        far = all_g
        right_re = [c_re, d_re, -c_im, -d_im]
        right_im = [c_im, d_im, c_re, d_re]
    l_re = jnp.concatenate(
        [
            dot(near, jnp.concatenate([a_re, -a_im], axis=0)),
            dot(far, jnp.concatenate(right_re, axis=0)),
        ],
        axis=1,
    ).astype(jnp.bfloat16)
    l_im = jnp.concatenate(
        [
            dot(near, jnp.concatenate([a_im, a_re], axis=0)),
            dot(far, jnp.concatenate(right_im, axis=0)),
        ],
        axis=1,
    ).astype(jnp.bfloat16)
    x_re = dot_t(jnp.concatenate([l_re, l_im], axis=1), all_g)
    x_im = dot_t(jnp.concatenate([l_im, -l_re], axis=1), all_g)
    return x_re, x_im


def tri_product(tri, retarded):
    return product_of(None, tri, retarded)


def cross_left(cross, retarded):
    c_re, c_im = cross[0][...], cross[1][...]
    half = c_re.shape[0]
    g_re = retarded[0]
    g_im = retarded[1]
    near = jnp.concatenate([g_re[:, :half], g_im[:, :half]], axis=1)
    far = jnp.concatenate([g_re[:, half:], g_im[:, half:]], axis=1)
    l_re = dot(near, jnp.concatenate([c_re, -c_im], axis=0)).astype(jnp.bfloat16)
    l_im = dot(near, jnp.concatenate([c_im, c_re], axis=0)).astype(jnp.bfloat16)
    return l_re, l_im, far


def cross_product(cross, retarded):
    l_re, l_im, far = cross_left(cross, retarded)
    x_re = dot_t(jnp.concatenate([l_re, l_im], axis=1), far)
    x_im = dot_t(jnp.concatenate([l_im, -l_re], axis=1), far)
    return x_re, x_im


def own_kernel(where, cross, tri, retarded, sigma, total, *rest):
    blocks, sems = rest[:-1], rest[-1]
    copies = [
        pltpu.make_async_copy(retarded.at[0, :, 0, where[place]], held, sems.at[place])
        for place, held in enumerate(blocks)
    ]
    for copy in copies:
        copy.start()
    c_re, c_im, t_re, t_im = squares(cross, tri)
    half = c_re.shape[0]
    rows, cols = grid_of((half, half))
    upper = rows < cols
    diagonal = rows == cols
    tr = t_re.astype(jnp.float32)
    ti = t_im.astype(jnp.float32)
    trt = tr.T
    tit = ti.T
    zero = jnp.zeros_like(tr)
    bf = jnp.bfloat16
    sigma[0, 0, 0, :half, half:] = c_re
    sigma[0, 1, 0, :half, half:] = c_im
    sigma[0, 0, 0, half:, :half] = (-(c_re.astype(jnp.float32).T)).astype(bf)
    sigma[0, 1, 0, half:, :half] = c_im.astype(jnp.float32).T.astype(bf)
    sigma[0, 0, 0, :half, :half] = jnp.where(upper, tr, jnp.where(diagonal, zero, -trt)).astype(bf)
    sigma[0, 1, 0, :half, :half] = jnp.where(upper, ti, jnp.where(diagonal, tr, tit)).astype(bf)
    sigma[0, 0, 0, half:, half:] = jnp.where(upper, -trt, jnp.where(diagonal, zero, tr)).astype(bf)
    sigma[0, 1, 0, half:, half:] = jnp.where(upper, tit, ti).astype(bf)
    for copy in copies:
        copy.wait()
    total[0], total[1] = product(cross, tri, blocks[0])


def part_kernel(part, *refs):
    *square, block, total, out = refs
    square = square if len(square) > 1 else square[0]
    x_re, x_im = part(square, block)
    x_re += total[0]
    x_im += total[1]
    out[0] = x_re
    out[1] = x_im


def last_kernel(c_re, c_im, block, total, out):
    x_re, x_im = cross_product((c_re, c_im), block)
    x_re += total[0]
    x_im += total[1]
    out[0, 0, 0] = (x_re - x_re.T).astype(jnp.bfloat16)
    out[0, 1, 0] = (x_im + x_im.T).astype(jnp.bfloat16)


def cost(width):
    return pl.CostEstimate(flops=14 * width**3, bytes_accessed=8 * width**2, transcendentals=0)


def own_product(blocks, own, retarded):
    width = retarded.shape[-1]
    count = len(blocks)
    block_shape = jax.ShapeDtypeStruct((2, width, width), jnp.bfloat16)
    sigma, total, *held = pl.pallas_call(
        own_kernel,
        out_shape=(
            jax.ShapeDtypeStruct((1, 2, 1, width, width), jnp.bfloat16),
            jax.ShapeDtypeStruct((2, width, width), jnp.float32),
        )
        + (block_shape,) * count,
        in_specs=[pl.BlockSpec(memory_space=SMEM)] + vmem(2) + [pl.BlockSpec(memory_space=HBM)],
        out_specs=tuple(vmem(2 + count)),
        scratch_shapes=[pltpu.SemaphoreType.DMA((count,))],
        compiler_params=params(44),
        cost_estimate=cost(width),
    )(jnp.stack(blocks), *own, retarded)
    return sigma, total, held


def add_part(part, square, block, total):
    width = block.shape[-1]
    return pl.pallas_call(
        functools.partial(part_kernel, part),
        out_shape=jax.ShapeDtypeStruct(total.shape, jnp.float32),
        in_specs=vmem(len(square) + 2),
        out_specs=vmem(1)[0],
        compiler_params=params(36),
        cost_estimate=cost(width),
    )(*square, block, total)


def last_product(cross, block, total):
    width = block.shape[-1]
    return pl.pallas_call(
        last_kernel,
        out_shape=jax.ShapeDtypeStruct((1, 2, 1, width, width), jnp.bfloat16),
        in_specs=vmem(4),
        out_specs=vmem(1)[0],
        compiler_params=params(46),
        cost_estimate=cost(width),
    )(*cross, block, total)


def exchange(pieces):
    return lax.all_to_all(pieces, "energy", split_axis=0, concat_axis=0, tiled=True)


def shards(g_lesser, w_lesser, g_retarded, energy_index):
    width = g_lesser.shape[-1]
    groups = lax.axis_size("energy")
    chain = lax.axis_size("space")
    here = lax.axis_index("space")
    paired = groups >= 4 and groups & (groups - 1) == 0 and (width // groups) % 16 == 0
    here = here.astype(jnp.int32)
    if chain == 4:
        return around_line(here, paired, g_lesser, w_lesser, energy_index, groups, g_retarded)
    if paired:
        *own, _ = gather_paired(g_lesser, w_lesser, energy_index, groups, lambda part: None)
    else:
        own = gather_shared(g_lesser, w_lesser, energy_index, groups)
    cross, tri = (lax.all_gather(part, "space") for part in own)
    blocks = [(here + step) % chain for step in range(chain)]
    sigma_lesser, total, held = own_product(blocks, own, g_retarded)

    def at(gathered, block):
        return lax.dynamic_index_in_dim(gathered, block, 0, False)

    for step in range(1, chain):
        square, block = at(tri, blocks[step]), held[step]
        total = add_part(tri_product, [square], block, total)
        square = at(cross, blocks[step])
        if step < chain - 1:
            total = add_part(cross_product, [square], block, total)
    return (sigma_lesser, last_product((square[0], square[1]), held[-1], total))


def around_line(here, paired, g_lesser, w_lesser, energy_index, groups, retarded):
    def swap(part, bits):
        return lax.ppermute(part, "space", [(i, i ^ bits) for i in range(4)])

    first, second = [], []

    def send(part):
        first.append(swap(part, 1))
        second.append(swap(part, 3))

    if paired:
        *own, apart = gather_paired(g_lesser, w_lesser, energy_index, groups, send)
    else:
        own = gather_shared(g_lesser, w_lesser, energy_index, groups)
        send(own[1])
        apart = [own[0][0], own[0][1]]
    far = [swap(comp, 3) for comp in apart]
    first.append(swap(after(own[0], first[0]), 1))
    blocks = [here, here ^ 1, here ^ 3, here ^ 2]
    sigma_lesser, total, held = own_product(blocks, after(own, first[0]), retarded)
    third = swap(after(second[0], total), 1)
    total = add_part(tri_product, [first[0]], held[1], total)
    last = [swap(after(far[0], total), 1)]
    total = add_part(tri_product, [second[0]], held[2], total)
    last.append(swap(after(far[1], total), 1))
    total = add_part(cross_product, far, held[2], total)
    total = add_part(cross_product, [first[1]], held[1], total)
    total = add_part(tri_product, [third], held[3], total)
    return (sigma_lesser, last_product(last, held[3], total))


def solution(mesh):
    return jax.shard_map(
        shards,
        mesh=mesh,
        in_specs=(
            P("energy", None, "space", None, None),
            P("energy", None, "space", None, None),
            P("energy", None, "space", None, None, None),
            P(),
        ),
        out_specs=(P("energy", None, "space", None, None), P("energy", None, "space", None, None)),
        check_vma=False,
    )
```

```python
import functools

import jax
import jax.numpy as jnp
from jax import lax
from jax.experimental import pallas as pl
from jax.experimental.pallas import tpu as pltpu
from jax.sharding import PartitionSpec as P


VMEM = pltpu.MemorySpace.VMEM
SMEM = pltpu.MemorySpace.SMEM
HBM = pltpu.MemorySpace.HBM

SMALL = pl.CostEstimate(flops=1, bytes_accessed=1, transcendentals=0)


def vmem(count):
    return [pl.BlockSpec(memory_space=VMEM)] * count


def params(mib):
    return pltpu.CompilerParams(vmem_limit_bytes=mib * 2**20)


def grid_of(shape, row_offset=0):
    rows = lax.broadcasted_iota(jnp.int32, shape, 0) + row_offset
    cols = lax.broadcasted_iota(jnp.int32, shape, 1)
    return rows, cols


def pack_kernel(green, screen, cross, tri):
    half = green.shape[-1] // 2
    rows, cols = grid_of((half, half))
    upper = rows < cols
    diagonal = rows == cols
    for place, source in enumerate((green, screen)):
        a_re = source[0, 0, 0, :half, :half].astype(jnp.float32)
        a_im = source[0, 1, 0, :half, :half].astype(jnp.float32)
        d_re = source[0, 0, 0, half:, half:].astype(jnp.float32)
        d_im = source[0, 1, 0, half:, half:].astype(jnp.float32)
        t_re = jnp.where(upper, a_re, jnp.where(diagonal, a_im, d_re)).astype(jnp.bfloat16)
        t_im = jnp.where(upper, a_im, d_im).astype(jnp.bfloat16)
        c_re = source[0, 0, 0, :half, half:]
        c_im = source[0, 1, 0, :half, half:]
        shape = cross.shape[:1] + cross.shape[3:]
        cross[:, place, 0] = c_re.reshape(shape)
        cross[:, place, 1] = c_im.reshape(shape)
        tri[:, place, 0] = t_re.reshape(shape)
        tri[:, place, 1] = t_im.reshape(shape)


def pack(green, screen, parts):
    half = green.shape[-1] // 2
    out = jax.ShapeDtypeStruct((parts, 2, 2, half // parts, half), jnp.bfloat16)
    return pl.pallas_call(
        pack_kernel,
        out_shape=(out, out),
        in_specs=vmem(2),
        out_specs=tuple(vmem(2)),
        compiler_params=params(24),
    )(green, screen)


def split_rows(packed, groups):
    _, fields, comps, half, width = packed.shape
    shaped = packed.reshape(fields, comps, groups, half // groups, width)
    return jnp.moveaxis(shaped, 2, 0)


def conv_kernel(has_diagonal, index, offset, pieces, out, green, screen, place):
    count, _, _, rows, width = pieces.shape

    def scatter(stored, carry):
        point = index[stored]
        place[point] = stored
        green[point] = pieces[stored, 0].astype(jnp.float32)
        screen[point] = pieces[stored, 1].astype(jnp.float32)
        return carry

    unroll = count <= 16
    lax.fori_loop(0, count, scatter, 0, unroll=unroll)
    scale = count**-0.5
    zero = jnp.zeros((rows, width), jnp.float32)

    def one(point, carry):
        total = point + count // 2

        def term(first, sums):
            both_re, both_im, mixed = sums
            g_re = green[first, 0]
            g_im = green[first, 1]
            w_re = screen[total - first, 0]
            w_im = screen[total - first, 1]
            return (
                both_re + g_re * w_re,
                both_im + g_im * w_im,
                mixed + g_re * w_im + g_im * w_re,
            )

        if unroll:
            sums = (zero, zero, zero)
            for first in range(max(0, total - count + 1), min(count - 1, total) + 1):
                sums = term(first, sums)
        else:
            low = jnp.maximum(0, total - count + 1)
            high = jnp.minimum(count - 1, total) + 1
            sums = lax.fori_loop(low, high, term, (zero, zero, zero))
        both_re, both_im, mixed = sums
        s_re = -scale * mixed
        s_im = scale * (both_re - both_im)
        if has_diagonal:
            at_rows, at_cols = grid_of((rows, width), offset[0])
            diagonal = at_rows == at_cols
            s_re = jnp.where(diagonal, -scale * both_re, s_re)
            s_im = jnp.where(diagonal, -scale * both_im, s_im)
        stored = place[point]
        out[stored, 0] = s_re.astype(jnp.bfloat16)
        out[stored, 1] = s_im.astype(jnp.bfloat16)
        return carry

    if unroll:
        for point in range(count):
            one(point, 0)
    else:
        lax.fori_loop(0, count, one, 0)


def convolve(pieces, energy_index, row_offset, has_diagonal):
    count, _, _, rows, width = pieces.shape
    smem = pl.BlockSpec(memory_space=SMEM)
    return pl.pallas_call(
        functools.partial(conv_kernel, has_diagonal),
        out_shape=jax.ShapeDtypeStruct((count, 2, rows, width), jnp.bfloat16),
        in_specs=[smem, smem] + vmem(1),
        out_specs=vmem(1)[0],
        scratch_shapes=[
            pltpu.VMEM((count, 2, rows, width), jnp.float32),
            pltpu.VMEM((count, 2, rows, width), jnp.float32),
            pltpu.SMEM((count,), jnp.int32),
        ],
        compiler_params=params(24),
    )(energy_index, row_offset, pieces)


def share_of(me, d, rows):
    return pl.ds(pl.multiple_of((lax.shift_right_logical(me, 1) ^ d) * rows, rows), rows)


def cut_kernel(chips, wanted, me, green, screen, *rest):
    outs = rest[: len(wanted)]
    near, far, sems = rest[len(wanted) :]
    half = near.shape[-1]
    rows = half // chips
    copies = []
    for n, d in enumerate(wanted):
        lines = share_of(me[0], d, rows)
        below = pl.ds(pl.multiple_of(lines.start + half, rows), rows)
        for field, source in enumerate((green, screen)):
            parts = (
                (source.at[0, :, 0, lines, :half], near.at[n, field]),
                (source.at[0, :, 0, below, half:], far.at[n, field]),
                (source.at[0, :, 0, lines, half:], outs[n].at[0, field]),
            )
            for place, (part, held) in enumerate(parts):
                copies.append(pltpu.make_async_copy(part, held, sems.at[n, field, place]))
                copies[-1].start()
    for copy in copies:
        copy.wait()
    at_rows, at_cols = grid_of((rows, half))
    for n, d in enumerate(wanted):
        here = at_rows + (lax.shift_right_logical(me[0], 1) ^ d) * rows
        upper = here < at_cols
        diagonal = here == at_cols
        for field in range(2):
            a_re = near[n, field, 0].astype(jnp.float32)
            a_im = near[n, field, 1].astype(jnp.float32)
            d_re = far[n, field, 0].astype(jnp.float32)
            d_im = far[n, field, 1].astype(jnp.float32)
            t_re = jnp.where(upper, a_re, jnp.where(diagonal, a_im, d_re))
            outs[n][1, field, 0] = t_re.astype(jnp.bfloat16)
            outs[n][1, field, 1] = jnp.where(upper, a_im, d_im).astype(jnp.bfloat16)


def cut(me, green, screen, chips, wanted):
    half = green.shape[-1] // 2
    rows = half // chips
    piece = jax.ShapeDtypeStruct((2, 2, 2, rows, half), jnp.bfloat16)
    count = len(wanted)
    return pl.pallas_call(
        functools.partial(cut_kernel, chips, wanted),
        out_shape=(piece,) * count,
        in_specs=[pl.BlockSpec(memory_space=SMEM)] + [pl.BlockSpec(memory_space=HBM)] * 2,
        out_specs=tuple(vmem(count)),
        scratch_shapes=[pltpu.VMEM((count, 2, 2, rows, half), jnp.bfloat16)] * 2
        + [pltpu.SemaphoreType.DMA((count, 2, 3))],
        compiler_params=params(56),
        cost_estimate=SMALL,
    )(me, green, screen)


def bind_kernel(part, *refs):
    for place, piece in enumerate(refs[:-1]):
        refs[-1][place] = piece[part]


def bind(pieces, part):
    shape = (len(pieces),) + pieces[0].shape[1:]
    return pl.pallas_call(
        functools.partial(bind_kernel, part),
        out_shape=jax.ShapeDtypeStruct(shape, jnp.bfloat16),
        in_specs=vmem(len(pieces)),
        out_specs=vmem(1)[0],
        compiler_params=params(32),
        cost_estimate=SMALL,
    )(*pieces)


def conv_pieces_kernel(chips, part, me, index, *rest):
    same = rest[:chips][::-1]
    beside, other = rest[chips : chips + 2]
    outs = rest[chips + 2 : 2 * chips + 2]
    green, screen, sums, place = rest[2 * chips + 2 :]
    groups = 2 * chips
    rows, width = sums.shape[2:]
    for core in range(2):
        for d in range(chips):
            stored = me[0] ^ (2 * d + core)
            point = index[stored]
            place[point] = stored
            if core == 0:
                green[point] = same[d][part, 0]
                screen[point] = same[d][part, 1]
            elif d == 0:
                green[point] = beside[part, 0]
                screen[point] = beside[part, 1]
            else:
                green[point] = other[chips - 1 - d, 0]
                screen[point] = other[chips - 1 - d, 1]
    scale = groups**-0.5
    tall = 16
    for point in range(groups):

        @pl.when(((place[point] ^ me[0]) & 1) == 0)
        def _():
            total = point + groups // 2
            for first_row in range(0, rows, tall):
                for first_col in range(0, width, 128):
                    at = (slice(first_row, first_row + tall), slice(first_col, first_col + 128))
                    both_re = both_im = mixed = None
                    for p in range(max(0, total - groups + 1), min(groups - 1, total) + 1):
                        g_re = green[(p, 0) + at].astype(jnp.float32)
                        g_im = green[(p, 1) + at].astype(jnp.float32)
                        w_re = screen[(total - p, 0) + at].astype(jnp.float32)
                        w_im = screen[(total - p, 1) + at].astype(jnp.float32)
                        re = g_re * w_re
                        im = g_im * w_im
                        mix = g_re * w_im + g_im * w_re
                        both_re = re if both_re is None else both_re + re
                        both_im = im if both_im is None else both_im + im
                        mixed = mix if mixed is None else mixed + mix
                    s_re = -scale * mixed
                    s_im = scale * (both_re - both_im)
                    if part == 1:
                        first = lax.shift_right_logical(me[0], 1) * rows + first_row
                        at_rows, at_cols = grid_of((tall, 128), first)
                        diagonal = at_rows == at_cols + first_col
                        s_re = jnp.where(diagonal, -scale * both_re, s_re)
                        s_im = jnp.where(diagonal, -scale * both_im, s_im)
                    sums[(point, 0) + at] = s_re.astype(jnp.bfloat16)
                    sums[(point, 1) + at] = s_im.astype(jnp.bfloat16)

    for d in range(chips):
        outs[d][...] = sums[index[me[0] ^ (2 * d)]]


def conv_pieces(me, energy_index, same, beside, other, part):
    chips = len(same)
    shape = same[0].shape[2:]
    smem = pl.BlockSpec(memory_space=SMEM)
    return pl.pallas_call(
        functools.partial(conv_pieces_kernel, chips, part),
        out_shape=(jax.ShapeDtypeStruct(shape, jnp.bfloat16),) * chips,
        in_specs=[smem, smem] + vmem(chips + 2),
        out_specs=tuple(vmem(chips)),
        scratch_shapes=[pltpu.VMEM((2 * chips,) + shape, jnp.bfloat16)] * 3
        + [pltpu.SMEM((2 * chips,), jnp.int32)],
        compiler_params=params(32),
        cost_estimate=SMALL,
    )(me, energy_index, *same[::-1], beside, other)


def join_kernel(chips, me, *rest):
    pieces, out = rest[:chips][::-1], rest[chips]
    rows = pieces[0].shape[1]
    for d in range(chips):
        out[:, share_of(me[0], d, rows), :] = pieces[d][...]


def join(me, pieces):
    half = pieces[0].shape[-1]
    return pl.pallas_call(
        functools.partial(join_kernel, len(pieces)),
        out_shape=jax.ShapeDtypeStruct((2, half, half), jnp.bfloat16),
        in_specs=[pl.BlockSpec(memory_space=SMEM)] + vmem(len(pieces)),
        out_specs=vmem(1)[0],
        compiler_params=params(32),
        cost_estimate=SMALL,
    )(me, *pieces[::-1])


def swap(piece, d, groups):
    return lax.ppermute(piece, "energy", [(i, i ^ d) for i in range(groups)]) if d else piece


def after(value, *earlier):
    return lax.optimization_barrier((value, earlier))[0]


def gather_paired(g_lesser, w_lesser, energy_index, groups, send):
    me = lax.axis_index("energy").astype(jnp.int32).reshape(1)
    chips = groups // 2

    def over(pieces):
        return [swap(pieces[d], 2 * d, groups) for d in range(chips)]

    (farthest,) = cut(me, g_lesser, w_lesser, chips, (chips - 1,))
    pieces = cut(after(me, farthest), g_lesser, w_lesser, chips, tuple(range(chips - 1)))
    pieces = tuple(pieces) + (farthest,)
    same = over(pieces)
    beside = swap(pieces[0], 1, groups)
    bound = [bind(after(same[:0:-1], beside), part) for part in range(2)]
    other = [swap(piece, 1, groups) for piece in bound]
    mine = conv_pieces(me, energy_index, same, beside, other[1], 1)
    own_tri = join(me, over(mine))
    send(own_tri)
    mine = conv_pieces(me, energy_index, same, beside, after(other[0], own_tri), 0)
    own_cross = join(me, over(mine))
    return own_cross, own_tri


def gather_shared(g_lesser, w_lesser, energy_index, groups):
    half = g_lesser.shape[-1] // 2
    rows = half // groups
    cross, tri = (split_rows(packed, groups) for packed in pack(g_lesser, w_lesser, 1))
    offset = (lax.axis_index("energy") * rows).astype(jnp.int32).reshape(1)
    own = []
    for pieces, has_diagonal in ((cross, False), (tri, True)):
        shares = convolve(exchange(pieces), energy_index, offset, has_diagonal)
        own.append(jnp.moveaxis(exchange(shares), 0, 1).reshape(2, half, half))
    return own


def squares(cross, tri):
    return cross[0], cross[1], tri[0], tri[1]


def dot(a, b):
    return jnp.dot(a, b, preferred_element_type=jnp.float32)


def dot_t(a, b):
    return lax.dot_general(a, b, (((1,), (1,)), ((), ())), preferred_element_type=jnp.float32)


def product(cross, tri, retarded):
    return product_of(cross, tri, retarded)


def product_of(cross, tri, retarded):
    t_re, t_im = tri[0], tri[1]
    half = t_re.shape[0]
    rows, cols = grid_of((half, half))
    tr = t_re.astype(jnp.float32)
    ti = t_im.astype(jnp.float32)
    diagonal = rows == cols
    a_re = jnp.where(rows < cols, tr, 0.0).astype(jnp.bfloat16)
    a_im = jnp.where(rows < cols, ti, jnp.where(diagonal, 0.5 * tr, 0.0)).astype(jnp.bfloat16)
    d_re = jnp.where(rows > cols, tr, 0.0).astype(jnp.bfloat16)
    d_im = jnp.where(rows > cols, ti, jnp.where(diagonal, 0.5 * ti, 0.0)).astype(jnp.bfloat16)
    g_re = retarded[0]
    g_im = retarded[1]
    near = jnp.concatenate([g_re[:, :half], g_im[:, :half]], axis=1)
    all_g = jnp.concatenate([g_re, g_im], axis=1)
    if cross is None:
        far = jnp.concatenate([g_re[:, half:], g_im[:, half:]], axis=1)
        right_re = [d_re, -d_im]
        right_im = [d_im, d_re]
    else:
        c_re, c_im = cross[0], cross[1]
        far = all_g
        right_re = [c_re, d_re, -c_im, -d_im]
        right_im = [c_im, d_im, c_re, d_re]
    l_re = jnp.concatenate(
        [
            dot(near, jnp.concatenate([a_re, -a_im], axis=0)),
            dot(far, jnp.concatenate(right_re, axis=0)),
        ],
        axis=1,
    ).astype(jnp.bfloat16)
    l_im = jnp.concatenate(
        [
            dot(near, jnp.concatenate([a_im, a_re], axis=0)),
            dot(far, jnp.concatenate(right_im, axis=0)),
        ],
        axis=1,
    ).astype(jnp.bfloat16)
    x_re = dot_t(jnp.concatenate([l_re, l_im], axis=1), all_g)
    x_im = dot_t(jnp.concatenate([l_im, -l_re], axis=1), all_g)
    return x_re, x_im


def tri_product(tri, retarded):
    return product_of(None, tri, retarded)


def cross_product(cross, retarded):
    c_re, c_im = cross[0], cross[1]
    half = c_re.shape[0]
    g_re = retarded[0]
    g_im = retarded[1]
    near = jnp.concatenate([g_re[:, :half], g_im[:, :half]], axis=1)
    far = jnp.concatenate([g_re[:, half:], g_im[:, half:]], axis=1)
    l_re = dot(near, jnp.concatenate([c_re, -c_im], axis=0)).astype(jnp.bfloat16)
    l_im = dot(near, jnp.concatenate([c_im, c_re], axis=0)).astype(jnp.bfloat16)
    x_re = dot_t(jnp.concatenate([l_re, l_im], axis=1), far)
    x_im = dot_t(jnp.concatenate([l_im, -l_re], axis=1), far)
    return x_re, x_im


def own_kernel(where, cross, tri, retarded, sigma, total, block, sem):
    copy = pltpu.make_async_copy(retarded.at[0, :, 0, where[0]], block, sem)
    copy.start()
    c_re, c_im, t_re, t_im = squares(cross, tri)
    half = c_re.shape[0]
    rows, cols = grid_of((half, half))
    upper = rows < cols
    diagonal = rows == cols
    tr = t_re.astype(jnp.float32)
    ti = t_im.astype(jnp.float32)
    trt = tr.T
    tit = ti.T
    zero = jnp.zeros_like(tr)
    bf = jnp.bfloat16
    sigma[0, 0, 0, :half, half:] = c_re
    sigma[0, 1, 0, :half, half:] = c_im
    sigma[0, 0, 0, half:, :half] = (-(c_re.astype(jnp.float32).T)).astype(bf)
    sigma[0, 1, 0, half:, :half] = c_im.astype(jnp.float32).T.astype(bf)
    sigma[0, 0, 0, :half, :half] = jnp.where(upper, tr, jnp.where(diagonal, zero, -trt)).astype(bf)
    sigma[0, 1, 0, :half, :half] = jnp.where(upper, ti, jnp.where(diagonal, tr, tit)).astype(bf)
    sigma[0, 0, 0, half:, half:] = jnp.where(upper, -trt, jnp.where(diagonal, zero, tr)).astype(bf)
    sigma[0, 1, 0, half:, half:] = jnp.where(upper, tit, ti).astype(bf)
    copy.wait()
    total[0], total[1] = product(cross, tri, block)


def step_kernel(ahead, where, cross, tri, retarded, total, out, *rest):
    if ahead:
        later, block, sems = rest
    else:
        block, sems = rest
    fetch = pltpu.make_async_copy(retarded.at[0, :, 0, where[0]], block, sems.at[0])
    fetch.start()
    if ahead:
        prefetch = pltpu.make_async_copy(retarded.at[0, :, 0, where[1]], later, sems.at[1])
        prefetch.start()
    fetch.wait()
    x_re, x_im = product(cross, tri, block)
    out[0] = total[0] + x_re
    out[1] = total[1] + x_im
    if ahead:
        prefetch.wait()


def tri_kernel(tri, block, total, out):
    x_re, x_im = tri_product(tri, block)
    out[0] = total[0] + x_re
    out[1] = total[1] + x_im


def last_kernel(cross, block, total, out):
    x_re, x_im = cross_product(cross, block)
    x_re += total[0]
    x_im += total[1]
    out[0, 0, 0] = (x_re - x_re.T).astype(jnp.bfloat16)
    out[0, 1, 0] = (x_im + x_im.T).astype(jnp.bfloat16)


def cost(width):
    return pl.CostEstimate(flops=14 * width**3, bytes_accessed=8 * width**2, transcendentals=0)


def own_product(block, own, retarded):
    width = retarded.shape[-1]
    return pl.pallas_call(
        own_kernel,
        out_shape=(
            jax.ShapeDtypeStruct((1, 2, 1, width, width), jnp.bfloat16),
            jax.ShapeDtypeStruct((2, width, width), jnp.float32),
        ),
        in_specs=[pl.BlockSpec(memory_space=SMEM)] + vmem(2) + [pl.BlockSpec(memory_space=HBM)],
        out_specs=tuple(vmem(2)),
        scratch_shapes=[pltpu.VMEM((2, width, width), jnp.bfloat16), pltpu.SemaphoreType.DMA],
        compiler_params=params(48),
        cost_estimate=cost(width),
    )(block.reshape(1), *own, retarded)


def step_product(block, source, retarded, total, later=None):
    width = retarded.shape[-1]
    ahead = later is not None
    numbers = jnp.stack([block, later if ahead else block])
    total_shape = jax.ShapeDtypeStruct((2, width, width), jnp.float32)
    block_shape = jax.ShapeDtypeStruct((2, width, width), jnp.bfloat16)
    return pl.pallas_call(
        functools.partial(step_kernel, ahead),
        out_shape=(total_shape, block_shape) if ahead else total_shape,
        in_specs=[pl.BlockSpec(memory_space=SMEM)]
        + vmem(2)
        + [pl.BlockSpec(memory_space=HBM)]
        + vmem(1),
        out_specs=tuple(vmem(2)) if ahead else vmem(1)[0],
        scratch_shapes=[pltpu.VMEM((2, width, width), jnp.bfloat16), pltpu.SemaphoreType.DMA((2,))],
        compiler_params=params(46),
        cost_estimate=cost(width),
    )(numbers, *source, retarded, total)


def add_tri(tri, block, total):
    return pl.pallas_call(
        tri_kernel,
        out_shape=jax.ShapeDtypeStruct(total.shape, jnp.float32),
        in_specs=vmem(3),
        out_specs=vmem(1)[0],
        compiler_params=params(46),
        cost_estimate=cost(block.shape[-1]),
    )(tri, block, total)


def last_product(cross, block, total):
    width = block.shape[-1]
    return pl.pallas_call(
        last_kernel,
        out_shape=jax.ShapeDtypeStruct((1, 2, 1, width, width), jnp.bfloat16),
        in_specs=vmem(3),
        out_specs=vmem(1)[0],
        compiler_params=params(46),
        cost_estimate=cost(width),
    )(cross, block, total)


def exchange(pieces):
    return lax.all_to_all(pieces, "energy", split_axis=0, concat_axis=0, tiled=True)


def shards(g_lesser, w_lesser, g_retarded, energy_index):
    width = g_lesser.shape[-1]
    groups = lax.axis_size("energy")
    chain = lax.axis_size("space")
    here = lax.axis_index("space")
    paired = groups >= 4 and groups & (groups - 1) == 0 and (width // groups) % 16 == 0
    here = here.astype(jnp.int32)
    if chain == 4:
        return around_line(here, paired, g_lesser, w_lesser, energy_index, groups, g_retarded)
    if paired:
        own = gather_paired(g_lesser, w_lesser, energy_index, groups, lambda part: None)
    else:
        own = gather_shared(g_lesser, w_lesser, energy_index, groups)
    everyone = [lax.all_gather(part, "space") for part in own]
    sigma_lesser, total = own_product(here, own, g_retarded)

    def source(block):
        return tuple(lax.dynamic_index_in_dim(part, block, 0, False) for part in everyone)

    for step in range(1, chain - 1):
        block = (here + step) % chain
        later = (block + 1) % chain
        total, held = step_product(block, source(block), g_retarded, total, later)
    cross, tri = source(later)
    return (sigma_lesser, last_product(cross, held, add_tri(tri, held, total)))


def around_line(here, paired, g_lesser, w_lesser, energy_index, groups, retarded):
    def swap(part, bits):
        return lax.ppermute(part, "space", [(i, i ^ bits) for i in range(4)])

    first, second = [], []

    def send(part):
        first.append(swap(part, 1))
        second.append(swap(part, 3))

    if paired:
        own = gather_paired(g_lesser, w_lesser, energy_index, groups, send)
        second.append(swap(own[0], 3))
        first.append(swap(after(own[0], second[0], first[0]), 1))
    else:
        own = gather_shared(g_lesser, w_lesser, energy_index, groups)
        send(own[1]), send(own[0])
    sigma_lesser, total = own_product(here, own, retarded)
    third = [swap(after(second[0], first[0], total), 1), swap(second[1], 1)]
    total = step_product(here ^ 3, second[::-1], retarded, total)
    total, held = step_product(here ^ 1, first[::-1], retarded, total, here ^ 2)
    delta = last_product(third[1], held, add_tri(third[0], held, total))
    return (sigma_lesser, delta)


def solution(mesh):
    return jax.shard_map(
        shards,
        mesh=mesh,
        in_specs=(
            P("energy", None, "space", None, None),
            P("energy", None, "space", None, None),
            P("energy", None, "space", None, None, None),
            P(),
        ),
        out_specs=(P("energy", None, "space", None, None), P("energy", None, "space", None, None)),
        check_vma=False,
    )
```

```python
import functools

import jax
import jax.numpy as jnp
from jax import lax
from jax.experimental import pallas as pl
from jax.experimental.pallas import tpu as pltpu
from jax.sharding import PartitionSpec as P


VMEM = pltpu.MemorySpace.VMEM
SMEM = pltpu.MemorySpace.SMEM
HBM = pltpu.MemorySpace.HBM

SMALL = pl.CostEstimate(flops=1, bytes_accessed=1, transcendentals=0)


def vmem(count):
    return [pl.BlockSpec(memory_space=VMEM)] * count


def params(mib):
    return pltpu.CompilerParams(vmem_limit_bytes=mib * 2**20)


def grid_of(shape, row_offset=0):
    rows = lax.broadcasted_iota(jnp.int32, shape, 0) + row_offset
    cols = lax.broadcasted_iota(jnp.int32, shape, 1)
    return rows, cols


def pack_kernel(green, screen, cross, tri):
    half = green.shape[-1] // 2
    rows, cols = grid_of((half, half))
    upper = rows < cols
    diagonal = rows == cols
    for place, source in enumerate((green, screen)):
        a_re = source[0, 0, 0, :half, :half].astype(jnp.float32)
        a_im = source[0, 1, 0, :half, :half].astype(jnp.float32)
        d_re = source[0, 0, 0, half:, half:].astype(jnp.float32)
        d_im = source[0, 1, 0, half:, half:].astype(jnp.float32)
        t_re = jnp.where(upper, a_re, jnp.where(diagonal, a_im, d_re)).astype(jnp.bfloat16)
        t_im = jnp.where(upper, a_im, d_im).astype(jnp.bfloat16)
        c_re = source[0, 0, 0, :half, half:]
        c_im = source[0, 1, 0, :half, half:]
        shape = cross.shape[:1] + cross.shape[3:]
        cross[:, place, 0] = c_re.reshape(shape)
        cross[:, place, 1] = c_im.reshape(shape)
        tri[:, place, 0] = t_re.reshape(shape)
        tri[:, place, 1] = t_im.reshape(shape)


def pack(green, screen, parts):
    half = green.shape[-1] // 2
    out = jax.ShapeDtypeStruct((parts, 2, 2, half // parts, half), jnp.bfloat16)
    return pl.pallas_call(
        pack_kernel,
        out_shape=(out, out),
        in_specs=vmem(2),
        out_specs=tuple(vmem(2)),
        compiler_params=params(24),
    )(green, screen)


def split_rows(packed, groups):
    _, fields, comps, half, width = packed.shape
    shaped = packed.reshape(fields, comps, groups, half // groups, width)
    return jnp.moveaxis(shaped, 2, 0)


def conv_kernel(has_diagonal, index, offset, pieces, out, green, screen, place):
    count, _, _, rows, width = pieces.shape

    def scatter(stored, carry):
        point = index[stored]
        place[point] = stored
        green[point] = pieces[stored, 0].astype(jnp.float32)
        screen[point] = pieces[stored, 1].astype(jnp.float32)
        return carry

    unroll = count <= 16
    lax.fori_loop(0, count, scatter, 0, unroll=unroll)
    scale = count**-0.5
    zero = jnp.zeros((rows, width), jnp.float32)

    def one(point, carry):
        total = point + count // 2

        def term(first, sums):
            both_re, both_im, mixed = sums
            g_re = green[first, 0]
            g_im = green[first, 1]
            w_re = screen[total - first, 0]
            w_im = screen[total - first, 1]
            return (
                both_re + g_re * w_re,
                both_im + g_im * w_im,
                mixed + g_re * w_im + g_im * w_re,
            )

        if unroll:
            sums = (zero, zero, zero)
            for first in range(max(0, total - count + 1), min(count - 1, total) + 1):
                sums = term(first, sums)
        else:
            low = jnp.maximum(0, total - count + 1)
            high = jnp.minimum(count - 1, total) + 1
            sums = lax.fori_loop(low, high, term, (zero, zero, zero))
        both_re, both_im, mixed = sums
        s_re = -scale * mixed
        s_im = scale * (both_re - both_im)
        if has_diagonal:
            at_rows, at_cols = grid_of((rows, width), offset[0])
            diagonal = at_rows == at_cols
            s_re = jnp.where(diagonal, -scale * both_re, s_re)
            s_im = jnp.where(diagonal, -scale * both_im, s_im)
        stored = place[point]
        out[stored, 0] = s_re.astype(jnp.bfloat16)
        out[stored, 1] = s_im.astype(jnp.bfloat16)
        return carry

    if unroll:
        for point in range(count):
            one(point, 0)
    else:
        lax.fori_loop(0, count, one, 0)


def convolve(pieces, energy_index, row_offset, has_diagonal):
    count, _, _, rows, width = pieces.shape
    smem = pl.BlockSpec(memory_space=SMEM)
    return pl.pallas_call(
        functools.partial(conv_kernel, has_diagonal),
        out_shape=jax.ShapeDtypeStruct((count, 2, rows, width), jnp.bfloat16),
        in_specs=[smem, smem] + vmem(1),
        out_specs=vmem(1)[0],
        scratch_shapes=[
            pltpu.VMEM((count, 2, rows, width), jnp.float32),
            pltpu.VMEM((count, 2, rows, width), jnp.float32),
            pltpu.SMEM((count,), jnp.int32),
        ],
        compiler_params=params(24),
    )(energy_index, row_offset, pieces)


def share_of(me, d, rows):
    return pl.ds(pl.multiple_of((lax.shift_right_logical(me, 1) ^ d) * rows, rows), rows)


def cut_kernel(chips, wanted, me, green, screen, *rest):
    outs = rest[: len(wanted)]
    near, far, sems = rest[len(wanted) :]
    half = near.shape[-1]
    rows = half // chips
    copies = []
    for n, d in enumerate(wanted):
        lines = share_of(me[0], d, rows)
        below = pl.ds(pl.multiple_of(lines.start + half, rows), rows)
        for field, source in enumerate((green, screen)):
            parts = (
                (source.at[0, :, 0, lines, :half], near.at[n, field]),
                (source.at[0, :, 0, below, half:], far.at[n, field]),
                (source.at[0, :, 0, lines, half:], outs[n].at[0, field]),
            )
            for place, (part, held) in enumerate(parts):
                copies.append(pltpu.make_async_copy(part, held, sems.at[n, field, place]))
                copies[-1].start()
    for copy in copies:
        copy.wait()
    at_rows, at_cols = grid_of((rows, half))
    for n, d in enumerate(wanted):
        here = at_rows + (lax.shift_right_logical(me[0], 1) ^ d) * rows
        upper = here < at_cols
        diagonal = here == at_cols
        for field in range(2):
            a_re = near[n, field, 0].astype(jnp.float32)
            a_im = near[n, field, 1].astype(jnp.float32)
            d_re = far[n, field, 0].astype(jnp.float32)
            d_im = far[n, field, 1].astype(jnp.float32)
            t_re = jnp.where(upper, a_re, jnp.where(diagonal, a_im, d_re))
            outs[n][1, field, 0] = t_re.astype(jnp.bfloat16)
            outs[n][1, field, 1] = jnp.where(upper, a_im, d_im).astype(jnp.bfloat16)


def cut(me, green, screen, chips, wanted):
    half = green.shape[-1] // 2
    rows = half // chips
    piece = jax.ShapeDtypeStruct((2, 2, 2, rows, half), jnp.bfloat16)
    count = len(wanted)
    return pl.pallas_call(
        functools.partial(cut_kernel, chips, wanted),
        out_shape=(piece,) * count,
        in_specs=[pl.BlockSpec(memory_space=SMEM)] + [pl.BlockSpec(memory_space=HBM)] * 2,
        out_specs=tuple(vmem(count)),
        scratch_shapes=[pltpu.VMEM((count, 2, 2, rows, half), jnp.bfloat16)] * 2
        + [pltpu.SemaphoreType.DMA((count, 2, 3))],
        compiler_params=params(56),
        cost_estimate=SMALL,
    )(me, green, screen)


def bind_kernel(part, *refs):
    for place, piece in enumerate(refs[:-1]):
        refs[-1][place] = piece[part]


def bind(pieces, part):
    shape = (len(pieces),) + pieces[0].shape[1:]
    return pl.pallas_call(
        functools.partial(bind_kernel, part),
        out_shape=jax.ShapeDtypeStruct(shape, jnp.bfloat16),
        in_specs=vmem(len(pieces)),
        out_specs=vmem(1)[0],
        compiler_params=params(32),
        cost_estimate=SMALL,
    )(*pieces)


def conv_pieces_kernel(chips, part, me, index, *rest):
    same = rest[:chips][::-1]
    beside, other = rest[chips : chips + 2]
    outs = rest[chips + 2 : 2 * chips + 2]
    green, screen, sums, place = rest[2 * chips + 2 :]
    groups = 2 * chips
    rows, width = sums.shape[2:]
    for core in range(2):
        for d in range(chips):
            stored = me[0] ^ (2 * d + core)
            point = index[stored]
            place[point] = stored
            if core == 0:
                green[point] = same[d][part, 0]
                screen[point] = same[d][part, 1]
            elif d == 0:
                green[point] = beside[part, 0]
                screen[point] = beside[part, 1]
            else:
                green[point] = other[chips - 1 - d, 0]
                screen[point] = other[chips - 1 - d, 1]
    scale = groups**-0.5
    tall = 16
    for point in range(groups):

        @pl.when(((place[point] ^ me[0]) & 1) == 0)
        def _():
            total = point + groups // 2
            for first_row in range(0, rows, tall):
                for first_col in range(0, width, 128):
                    at = (slice(first_row, first_row + tall), slice(first_col, first_col + 128))
                    both_re = both_im = mixed = None
                    for p in range(max(0, total - groups + 1), min(groups - 1, total) + 1):
                        g_re = green[(p, 0) + at].astype(jnp.float32)
                        g_im = green[(p, 1) + at].astype(jnp.float32)
                        w_re = screen[(total - p, 0) + at].astype(jnp.float32)
                        w_im = screen[(total - p, 1) + at].astype(jnp.float32)
                        re = g_re * w_re
                        im = g_im * w_im
                        mix = g_re * w_im + g_im * w_re
                        both_re = re if both_re is None else both_re + re
                        both_im = im if both_im is None else both_im + im
                        mixed = mix if mixed is None else mixed + mix
                    s_re = -scale * mixed
                    s_im = scale * (both_re - both_im)
                    if part == 1:
                        first = lax.shift_right_logical(me[0], 1) * rows + first_row
                        at_rows, at_cols = grid_of((tall, 128), first)
                        diagonal = at_rows == at_cols + first_col
                        s_re = jnp.where(diagonal, -scale * both_re, s_re)
                        s_im = jnp.where(diagonal, -scale * both_im, s_im)
                    sums[(point, 0) + at] = s_re.astype(jnp.bfloat16)
                    sums[(point, 1) + at] = s_im.astype(jnp.bfloat16)

    for d in range(chips):
        outs[d][...] = sums[index[me[0] ^ (2 * d)]]


def conv_pieces(me, energy_index, same, beside, other, part):
    chips = len(same)
    shape = same[0].shape[2:]
    smem = pl.BlockSpec(memory_space=SMEM)
    return pl.pallas_call(
        functools.partial(conv_pieces_kernel, chips, part),
        out_shape=(jax.ShapeDtypeStruct(shape, jnp.bfloat16),) * chips,
        in_specs=[smem, smem] + vmem(chips + 2),
        out_specs=tuple(vmem(chips)),
        scratch_shapes=[pltpu.VMEM((2 * chips,) + shape, jnp.bfloat16)] * 3
        + [pltpu.SMEM((2 * chips,), jnp.int32)],
        compiler_params=params(32),
        cost_estimate=SMALL,
    )(me, energy_index, *same[::-1], beside, other)


def join_kernel(chips, me, *rest):
    pieces, out = rest[:chips][::-1], rest[chips]
    rows = pieces[0].shape[1]
    for d in range(chips):
        out[:, share_of(me[0], d, rows), :] = pieces[d][...]


def join_apart_kernel(chips, me, *rest):
    pieces = rest[:chips][::-1]
    out, *apart = rest[chips:]
    rows = pieces[0].shape[1]
    for d in range(chips):
        lines = share_of(me[0], d, rows)
        out[:, lines, :] = pieces[d][...]
        for comp in range(2):
            apart[comp][lines, :] = pieces[d][comp]


def join_apart(me, pieces):
    half = pieces[0].shape[-1]
    one = jax.ShapeDtypeStruct((half, half), jnp.bfloat16)
    return pl.pallas_call(
        functools.partial(join_apart_kernel, len(pieces)),
        out_shape=(jax.ShapeDtypeStruct((2, half, half), jnp.bfloat16), one, one),
        in_specs=[pl.BlockSpec(memory_space=SMEM)] + vmem(len(pieces)),
        out_specs=tuple(vmem(3)),
        compiler_params=params(32),
        cost_estimate=SMALL,
    )(me, *pieces[::-1])


def join(me, pieces):
    half = pieces[0].shape[-1]
    return pl.pallas_call(
        functools.partial(join_kernel, len(pieces)),
        out_shape=jax.ShapeDtypeStruct((2, half, half), jnp.bfloat16),
        in_specs=[pl.BlockSpec(memory_space=SMEM)] + vmem(len(pieces)),
        out_specs=vmem(1)[0],
        compiler_params=params(32),
        cost_estimate=SMALL,
    )(me, *pieces[::-1])


def swap(piece, d, groups):
    return lax.ppermute(piece, "energy", [(i, i ^ d) for i in range(groups)]) if d else piece


def after(value, *earlier):
    return lax.optimization_barrier((value, earlier))[0]


def gather_paired(g_lesser, w_lesser, energy_index, groups, send):
    me = lax.axis_index("energy").astype(jnp.int32).reshape(1)
    chips = groups // 2

    def over(pieces):
        return [swap(pieces[d], 2 * d, groups) for d in range(chips)]

    (farthest,) = cut(me, g_lesser, w_lesser, chips, (chips - 1,))
    pieces = cut(after(me, farthest), g_lesser, w_lesser, chips, tuple(range(chips - 1)))
    pieces = tuple(pieces) + (farthest,)
    same = over(pieces)
    beside = swap(pieces[0], 1, groups)
    bound = [bind(after(same[:0:-1], beside), part) for part in range(2)]
    other = [swap(piece, 1, groups) for piece in bound]
    mine = conv_pieces(me, energy_index, same, beside, other[1], 1)
    own_tri = join(me, over(mine))
    send(own_tri)
    mine = conv_pieces(me, energy_index, same, beside, after(other[0], own_tri), 0)
    own_cross, *apart = join_apart(me, over(mine))
    return own_cross, own_tri, apart


def gather_shared(g_lesser, w_lesser, energy_index, groups):
    half = g_lesser.shape[-1] // 2
    rows = half // groups
    cross, tri = (split_rows(packed, groups) for packed in pack(g_lesser, w_lesser, 1))
    offset = (lax.axis_index("energy") * rows).astype(jnp.int32).reshape(1)
    own = []
    for pieces, has_diagonal in ((cross, False), (tri, True)):
        shares = convolve(exchange(pieces), energy_index, offset, has_diagonal)
        own.append(jnp.moveaxis(exchange(shares), 0, 1).reshape(2, half, half))
    return own


def squares(cross, tri):
    return cross[0], cross[1], tri[0], tri[1]


def dot(a, b):
    return jnp.dot(a, b, preferred_element_type=jnp.float32)


def dot_t(a, b):
    return lax.dot_general(a, b, (((1,), (1,)), ((), ())), preferred_element_type=jnp.float32)


def product(cross, tri, retarded):
    return product_of(cross, tri, retarded)


def product_of(cross, tri, retarded):
    t_re, t_im = tri[0], tri[1]
    half = t_re.shape[0]
    rows, cols = grid_of((half, half))
    tr = t_re.astype(jnp.float32)
    ti = t_im.astype(jnp.float32)
    diagonal = rows == cols
    a_re = jnp.where(rows < cols, tr, 0.0).astype(jnp.bfloat16)
    a_im = jnp.where(rows < cols, ti, jnp.where(diagonal, 0.5 * tr, 0.0)).astype(jnp.bfloat16)
    d_re = jnp.where(rows > cols, tr, 0.0).astype(jnp.bfloat16)
    d_im = jnp.where(rows > cols, ti, jnp.where(diagonal, 0.5 * ti, 0.0)).astype(jnp.bfloat16)
    g_re = retarded[0]
    g_im = retarded[1]
    near = jnp.concatenate([g_re[:, :half], g_im[:, :half]], axis=1)
    all_g = jnp.concatenate([g_re, g_im], axis=1)
    if cross is None:
        far = jnp.concatenate([g_re[:, half:], g_im[:, half:]], axis=1)
        right_re = [d_re, -d_im]
        right_im = [d_im, d_re]
    else:
        c_re, c_im = cross[0], cross[1]
        far = all_g
        right_re = [c_re, d_re, -c_im, -d_im]
        right_im = [c_im, d_im, c_re, d_re]
    l_re = jnp.concatenate(
        [
            dot(near, jnp.concatenate([a_re, -a_im], axis=0)),
            dot(far, jnp.concatenate(right_re, axis=0)),
        ],
        axis=1,
    ).astype(jnp.bfloat16)
    l_im = jnp.concatenate(
        [
            dot(near, jnp.concatenate([a_im, a_re], axis=0)),
            dot(far, jnp.concatenate(right_im, axis=0)),
        ],
        axis=1,
    ).astype(jnp.bfloat16)
    x_re = dot_t(jnp.concatenate([l_re, l_im], axis=1), all_g)
    x_im = dot_t(jnp.concatenate([l_im, -l_re], axis=1), all_g)
    return x_re, x_im


def tri_product(tri, retarded):
    return product_of(None, tri, retarded)


def cross_left(cross, retarded):
    c_re, c_im = cross[0][...], cross[1][...]
    half = c_re.shape[0]
    g_re = retarded[0]
    g_im = retarded[1]
    near = jnp.concatenate([g_re[:, :half], g_im[:, :half]], axis=1)
    far = jnp.concatenate([g_re[:, half:], g_im[:, half:]], axis=1)
    l_re = dot(near, jnp.concatenate([c_re, -c_im], axis=0)).astype(jnp.bfloat16)
    l_im = dot(near, jnp.concatenate([c_im, c_re], axis=0)).astype(jnp.bfloat16)
    return l_re, l_im, far


def cross_product(cross, retarded):
    l_re, l_im, far = cross_left(cross, retarded)
    x_re = dot_t(jnp.concatenate([l_re, l_im], axis=1), far)
    x_im = dot_t(jnp.concatenate([l_im, -l_re], axis=1), far)
    return x_re, x_im


def own_kernel(where, cross, tri, retarded, sigma, total, *rest):
    blocks, sems = rest[:-1], rest[-1]
    copies = [
        pltpu.make_async_copy(retarded.at[0, :, 0, where[place]], held, sems.at[place])
        for place, held in enumerate(blocks)
    ]
    for copy in copies:
        copy.start()
    c_re, c_im, t_re, t_im = squares(cross, tri)
    half = c_re.shape[0]
    rows, cols = grid_of((half, half))
    upper = rows < cols
    diagonal = rows == cols
    tr = t_re.astype(jnp.float32)
    ti = t_im.astype(jnp.float32)
    trt = tr.T
    tit = ti.T
    zero = jnp.zeros_like(tr)
    bf = jnp.bfloat16
    sigma[0, 0, 0, :half, half:] = c_re
    sigma[0, 1, 0, :half, half:] = c_im
    sigma[0, 0, 0, half:, :half] = (-(c_re.astype(jnp.float32).T)).astype(bf)
    sigma[0, 1, 0, half:, :half] = c_im.astype(jnp.float32).T.astype(bf)
    sigma[0, 0, 0, :half, :half] = jnp.where(upper, tr, jnp.where(diagonal, zero, -trt)).astype(bf)
    sigma[0, 1, 0, :half, :half] = jnp.where(upper, ti, jnp.where(diagonal, tr, tit)).astype(bf)
    sigma[0, 0, 0, half:, half:] = jnp.where(upper, -trt, jnp.where(diagonal, zero, tr)).astype(bf)
    sigma[0, 1, 0, half:, half:] = jnp.where(upper, tit, ti).astype(bf)
    for copy in copies:
        copy.wait()
    total[0], total[1] = product(cross, tri, blocks[0])


def part_kernel(part, *refs):
    *square, block, total, out = refs
    square = square if len(square) > 1 else square[0]
    x_re, x_im = part(square, block)
    x_re += total[0]
    x_im += total[1]
    out[0] = x_re
    out[1] = x_im


def last_kernel(c_re, c_im, block, total, out):
    x_re, x_im = cross_product((c_re, c_im), block)
    x_re += total[0]
    x_im += total[1]
    out[0, 0, 0] = (x_re - x_re.T).astype(jnp.bfloat16)
    out[0, 1, 0] = (x_im + x_im.T).astype(jnp.bfloat16)


def cost(width):
    return pl.CostEstimate(flops=14 * width**3, bytes_accessed=8 * width**2, transcendentals=0)


def own_product(blocks, own, retarded):
    width = retarded.shape[-1]
    count = len(blocks)
    block_shape = jax.ShapeDtypeStruct((2, width, width), jnp.bfloat16)
    sigma, total, *held = pl.pallas_call(
        own_kernel,
        out_shape=(
            jax.ShapeDtypeStruct((1, 2, 1, width, width), jnp.bfloat16),
            jax.ShapeDtypeStruct((2, width, width), jnp.float32),
        )
        + (block_shape,) * count,
        in_specs=[pl.BlockSpec(memory_space=SMEM)] + vmem(2) + [pl.BlockSpec(memory_space=HBM)],
        out_specs=tuple(vmem(2 + count)),
        scratch_shapes=[pltpu.SemaphoreType.DMA((count,))],
        compiler_params=params(44),
        cost_estimate=cost(width),
    )(jnp.stack(blocks), *own, retarded)
    return sigma, total, held


def add_part(part, square, block, total):
    width = block.shape[-1]
    return pl.pallas_call(
        functools.partial(part_kernel, part),
        out_shape=jax.ShapeDtypeStruct(total.shape, jnp.float32),
        in_specs=vmem(len(square) + 2),
        out_specs=vmem(1)[0],
        compiler_params=params(36),
        cost_estimate=cost(width),
    )(*square, block, total)


def last_product(cross, block, total):
    width = block.shape[-1]
    return pl.pallas_call(
        last_kernel,
        out_shape=jax.ShapeDtypeStruct((1, 2, 1, width, width), jnp.bfloat16),
        in_specs=vmem(4),
        out_specs=vmem(1)[0],
        compiler_params=params(46),
        cost_estimate=cost(width),
    )(*cross, block, total)


def exchange(pieces):
    return lax.all_to_all(pieces, "energy", split_axis=0, concat_axis=0, tiled=True)


def shards(g_lesser, w_lesser, g_retarded, energy_index):
    width = g_lesser.shape[-1]
    groups = lax.axis_size("energy")
    chain = lax.axis_size("space")
    here = lax.axis_index("space")
    paired = groups >= 4 and groups & (groups - 1) == 0 and (width // groups) % 16 == 0
    here = here.astype(jnp.int32)
    if chain == 4:
        return around_line(here, paired, g_lesser, w_lesser, energy_index, groups, g_retarded)
    if paired:
        *own, _ = gather_paired(g_lesser, w_lesser, energy_index, groups, lambda part: None)
    else:
        own = gather_shared(g_lesser, w_lesser, energy_index, groups)
    cross, tri = (lax.all_gather(part, "space") for part in own)
    blocks = [(here + step) % chain for step in range(chain)]
    sigma_lesser, total, held = own_product(blocks, own, g_retarded)

    def at(gathered, block):
        return lax.dynamic_index_in_dim(gathered, block, 0, False)

    for step in range(1, chain):
        square, block = at(tri, blocks[step]), held[step]
        total = add_part(tri_product, [square], block, total)
        square = at(cross, blocks[step])
        if step < chain - 1:
            total = add_part(cross_product, [square], block, total)
    return (sigma_lesser, last_product((square[0], square[1]), held[-1], total))


def around_line(here, paired, g_lesser, w_lesser, energy_index, groups, retarded):
    def swap(part, bits):
        return lax.ppermute(part, "space", [(i, i ^ bits) for i in range(4)])

    first, second = [], []

    def send(part):
        first.append(swap(part, 1))
        second.append(swap(part, 3))

    if paired:
        *own, apart = gather_paired(g_lesser, w_lesser, energy_index, groups, send)
    else:
        own = gather_shared(g_lesser, w_lesser, energy_index, groups)
        send(own[1])
        apart = [own[0][0], own[0][1]]
    far = [swap(comp, 3) for comp in apart]
    first.append(swap(after(own[0], first[0]), 1))
    blocks = [here, here ^ 1, here ^ 3, here ^ 2]
    sigma_lesser, total, held = own_product(blocks, after(own, first[0]), retarded)
    third = swap(after(second[0], total), 1)
    total = add_part(tri_product, [first[0]], held[1], total)
    last = [swap(after(far[0], total), 1)]
    total = add_part(tri_product, [second[0]], held[2], total)
    last.append(swap(after(far[1], total), 1))
    total = add_part(cross_product, far, held[2], total)
    total = add_part(cross_product, [first[1]], held[1], total)
    total = add_part(tri_product, [third], held[3], total)
    return (sigma_lesser, last_product(last, held[3], total))


def solution(mesh):
    return jax.shard_map(
        shards,
        mesh=mesh,
        in_specs=(
            P("energy", None, "space", None, None),
            P("energy", None, "space", None, None),
            P("energy", None, "space", None, None, None),
            P(),
        ),
        out_specs=(P("energy", None, "space", None, None), P("energy", None, "space", None, None)),
        check_vma=False,
    )
```
